32 devices in a mesh: group: 2 (over y), area: 4 (over z), scen: 2 (over x), hour: 2 (over core).
Axes of the slice: x: 2, y: 2, z: 4, core: 2. Of those that a mesh axis runs over, the one named last changes fastest.
Arguments:
- ptdf: bfloat16 [16384, 512], P(('group', 'area')), parts along dimension 0, may hold values from -0.25 to 0.25
- angle_sens: bfloat16 [4096, 512], P(('group', 'area')), parts along dimension 0, may hold values from -0.25 to 0.25
- demand: float32 [48, 32, 2048], P(('group', 'hour'), 'scen', 'area'), parts along dimension 0, may hold values from -6 to 6
- gen_start: float32 [48, 2048], P(('group', 'hour'), 'area'), parts along dimension 0, may hold values from 0 to 2
- hedge_dual: float32 [48, 32, 2048], P(('group', 'hour'), 'scen', 'area'), parts along dimension 0, may hold values from -2 to 2
- gen_cost: float32 [4096], P(('group', 'area')), parts along dimension 0, may hold values from 0.1 to 1
- gen_max: float32 [4096], P(('group', 'area')), parts along dimension 0, may hold values from 1 to 3
- gen_ramp: float32 [4096], P(('group', 'area')), parts along dimension 0, may hold values from 0.05 to 0.5
- line_max: float32 [16384], P(('group', 'area')), parts along dimension 0, may hold values from 0.5 to 4
- tie_count: int32 [8, 4], P('group'), parts along dimension 0, may hold values from 0 to 16, as said below
- tie_low_bus: int32 [8, 64], P('group'), parts along dimension 0, may hold values from 0 to 511
- tie_high_bus: int32 [8, 64], P('group'), parts along dimension 0, may hold values from 0 to 511
- tie_susc: float32 [8, 64], P('group'), parts along dimension 0, may hold values from 0.5 to 2
Outputs:
- gen_mean: float32 [48, 2048], P(('group', 'hour'), 'area'), parts along dimension 0
- hedge_out: float32 [48, 32, 2048], P(('group', 'hour'), 'scen', 'area'), parts along dimension 0
- tie_flow: float32 [48, 32, 512], P(('group', 'hour'), 'scen', 'area'), parts along dimension 0
The draws below stay inside these ranges and needn't reach their ends.
There are 2 independent parts, one for each index of `group`. The reference program is written for one: setup_inputs(seed, part) draws one part's arguments, and reference() takes and returns one part's arrays. A program takes and returns all parts, laid end to end along the dimension named above; each array names one. Nothing has to cross between parts.
Inputs may be any that keep to these rules, and one draw needn't show every extreme that they name: `tie_count`: zero where a + k + 1 >= 4; some pair of areas one apart holds exactly 16.
All inputs are finite; a program needn't handle non-finite values.
Results may differ from the reference program's by a relative error of at most 0.0044.
Values sent between devices are 32-bit elements; how exact they have to be, the bound alone decides.
No kernel may reach another device: no remote copies, remote signals or barrier semaphores. Data moves between devices by JAX's collectives and lax.ppermute only.
A program may use at most 64 MiB of HBM per device.

```python
import math
import jax
import jax.numpy as jnp
from jax import lax

B = 512
L = 2048
HOURS = 24
REACH = 4
CAP = 16
ITERS = 2
A = 4
S = 32
RC = 64
SLOTS = 128


def draw_tie_count(key, part):
    key = jax.random.fold_in(key, 11)
    first_key, second_key = jax.random.split(key)
    counts = jax.random.randint(first_key, (A, REACH), 0, CAP + 1)
    area_ids = jnp.arange(A)[:, None]
    distance = jnp.arange(REACH)[None, :] + 1
    counts = jnp.where(area_ids + distance < A, counts, 0)
    chosen = jax.random.randint(second_key, (), 0, A - 1)
    counts = counts.at[chosen, 0].set(CAP)
    return counts.astype(jnp.int32)


def touch_ends(array, key, smallest, largest):
    spot = [jax.random.randint(jax.random.fold_in(key, axis), (), 0, length) for axis, length in enumerate(array.shape)]
    widest = array.shape.index(max(array.shape))
    neighbour = spot[:widest] + [(spot[widest] + 1) % array.shape[widest]] + spot[widest + 1:]
    return array.at[tuple(spot)].set(smallest).at[tuple(neighbour)].set(largest)


def shard_levels(key, shape, cuts, least, top_value):
    factor_of, own = 1.0, jax.random.fold_in(key, 6)
    for position, blocks in cuts:
        heights = jnp.exp(jax.random.uniform(jax.random.fold_in(own, position), (blocks,), jnp.float32, least / len(cuts), top_value / len(cuts)))
        factor_of = factor_of * jnp.repeat(heights, shape[position] // blocks).reshape([-1 if axis == position else 1 for axis in range(len(shape))])
    return factor_of


def gaussian(own_key, extent, deviation, bound, cuts=(), kind=jnp.bfloat16):
    values = deviation * jax.random.normal(own_key, extent, jnp.float32)
    if cuts:
        values = values * shard_levels(own_key, extent, cuts, -0.22, 0.18)
    return jnp.clip(values, -bound, bound).astype(kind)


def setup_inputs(seed: int = 0, part: int = 0) -> dict:
    keys = jax.random.split(jax.random.key(seed), 14)
    part_splits = jax.random.split(jax.random.fold_in(keys[13], part), 14)
    return {
        "ptdf": gaussian(part_splits[0], (A * L, B), B ** -0.5, 0.25, ((0, 4),)),
        "angle_sens": gaussian(part_splits[1], (A * B, B), B ** -0.5, 0.25, ((0, 4),)),
        "demand": gaussian(part_splits[2], (HOURS, S, A * B), 1.0, 6.0, ((0, 2), (1, 2), (2, 4)), jnp.float32),
        "gen_start": jnp.clip(2.0 * jax.random.uniform(part_splits[3], (HOURS, A * B), jnp.float32) ** shard_levels(part_splits[3], (HOURS, A * B), ((0, 2), (1, 4)), -0.2, 0.2), 0.0, 2.0),
        "hedge_dual": gaussian(part_splits[4], (HOURS, S, A * B), 0.3, 2.0, ((0, 2), (1, 2), (2, 4)), jnp.float32),
        "gen_cost": jnp.clip(jnp.exp(math.log(1.0) - 2.3025851 * jax.random.uniform(part_splits[5], (A * B,), jnp.float32) ** shard_levels(part_splits[5], (A * B,), ((0, 4),), -0.2, 0.2)), 0.1, 1.0),
        "gen_max": jnp.clip(1.0 + 2.0 * jax.random.uniform(part_splits[6], (A * B,), jnp.float32) ** shard_levels(part_splits[6], (A * B,), ((0, 4),), -0.2, 0.2), 1.0, 3.0),
        "gen_ramp": jnp.clip(jnp.exp(math.log(0.5) - 2.3025851 * jax.random.uniform(part_splits[7], (A * B,), jnp.float32) ** shard_levels(part_splits[7], (A * B,), ((0, 4),), -0.2, 0.2)), 0.05, 0.5),
        "line_max": jnp.clip(jnp.exp(math.log(4.0) - 2.0794415 * jax.random.uniform(part_splits[8], (A * L,), jnp.float32) ** shard_levels(part_splits[8], (A * L,), ((0, 4),), -0.2, 0.2)), 0.5, 4.0),
        "tie_count": draw_tie_count(jax.random.fold_in(jax.random.fold_in(keys[13], part), 71), part),
        "tie_low_bus": touch_ends(jax.random.randint(part_splits[10], (A, RC), 0, B), jax.random.fold_in(part_splits[10], 1), 0, B - 1).astype(jnp.int32),
        "tie_high_bus": touch_ends(jax.random.randint(part_splits[11], (A, RC), 0, B), jax.random.fold_in(part_splits[11], 1), 0, B - 1).astype(jnp.int32),
        "tie_susc": jnp.clip(jnp.exp(jax.random.uniform(part_splits[12], (A, RC), jnp.float32, math.log(0.5), math.log(2.0))), 0.5, 2.0),
    }


STEP_SIZE = 0.5


def ramp_force(mean_gen, limit):
    diffs = mean_gen[1:] - mean_gen[:-1]
    excess = diffs - jnp.clip(diffs, -limit, limit)
    zero_row = jnp.zeros((1, mean_gen.shape[1]), jnp.float32)
    padded = jnp.concatenate([zero_row, excess, zero_row], axis=0)
    return padded[:-1] - padded[1:]


def area_work(block):
    weights, angles, inject, limit = block
    flows = jnp.dot(inject, weights.T, preferred_element_type=jnp.float32)
    over = (flows - jnp.clip(flows, -limit, limit)).astype(jnp.bfloat16)
    theta = jnp.dot(inject, angles.T, preferred_element_type=jnp.float32)
    back = jnp.dot(over, weights, preferred_element_type=jnp.float32)
    return theta, back


def reference(ptdf, angle_sens, demand, gen_start, hedge_dual, gen_cost, gen_max, gen_ramp, line_max, tie_count, tie_low_bus, tie_high_bus, tie_susc):
    areas = A
    area_ids = jnp.arange(areas, dtype=jnp.int32)
    distance = jnp.arange(REACH, dtype=jnp.int32) + 1
    slot_ids = jnp.arange(CAP, dtype=jnp.int32)
    live = (slot_ids[None, None, :] < tie_count[:, :, None]) & ((area_ids[:, None] + distance[None, :]) < areas)[:, :, None]
    live = live.reshape(areas * RC).astype(jnp.float32)
    high_area = jnp.minimum(area_ids[:, None] + distance[None, :], areas - 1)
    high_area = jnp.broadcast_to(high_area[:, :, None], (areas, REACH, CAP)).reshape(areas, RC)
    low_index = (area_ids[:, None] * B + tie_low_bus).reshape(-1).astype(jnp.int32)
    high_index = (high_area * B + tie_high_bus).reshape(-1).astype(jnp.int32)
    susc = tie_susc.reshape(-1)

    gen = jnp.broadcast_to(gen_start[:, None, :], (HOURS, S, areas * B))
    gen_mean = gen_start
    hedge = hedge_dual
    tie_shape = (HOURS, S, areas * RC)
    flow = jnp.zeros(tie_shape, jnp.float32)
    dual_low = jnp.zeros(tie_shape, jnp.float32)
    dual_high = jnp.zeros(tie_shape, jnp.float32)
    peer_low = jnp.zeros(tie_shape, jnp.float32)
    peer_high = jnp.zeros(tie_shape, jnp.float32)
    blocks_h = ptdf.reshape(areas, L, B)
    blocks_s = angle_sens.reshape(areas, B, B)
    limits = line_max.reshape(areas, L)
    for step in range(ITERS):
        inject_add = jnp.zeros((HOURS, S, areas * B), jnp.float32)
        inject_add = inject_add.at[:, :, low_index].add(-live * flow)
        inject_add = inject_add.at[:, :, high_index].add(live * flow)
        inject = (gen - demand + inject_add).astype(jnp.bfloat16)
        inject_blocks = inject.reshape(HOURS * S, areas, B).transpose(1, 0, 2)
        theta, back = lax.map(area_work, (blocks_h, blocks_s, inject_blocks, limits))
        theta = theta.transpose(1, 0, 2).reshape(HOURS, S, areas * B)
        back = back.transpose(1, 0, 2).reshape(HOURS, S, areas * B)
        force = ramp_force(gen_mean, gen_ramp)
        grad = gen_cost + back + (gen - gen_mean[:, None, :] + hedge) + force[:, None, :]
        gen = jnp.clip(gen - STEP_SIZE * grad, 0.0, gen_max)
        gen_mean = jnp.sum(gen + hedge, axis=1) / S
        hedge = hedge + gen - gen_mean[:, None, :]
        own_low = live * theta[:, :, low_index]
        own_high = live * theta[:, :, high_index]
        est_low = live * susc * (own_low - peer_low)
        est_high = live * susc * (peer_high - own_high)
        flow = live * ((est_low + dual_low) + (est_high + dual_high)) * 0.5
        dual_low = dual_low + est_low - flow
        dual_high = dual_high + est_high - flow
        peer_low = own_high
        peer_high = own_low
    per_pair = flow.reshape(HOURS, S, areas, REACH, CAP)
    from_lower = []
    for k in range(REACH):
        shift_by = min(k + 1, areas)
        moved = jnp.pad(per_pair[:, :, :areas - shift_by, k, :], ((0, 0), (0, 0), (shift_by, 0), (0, 0)))
        from_lower.append(moved)
    from_lower = jnp.stack(from_lower, axis=3).reshape(HOURS, S, areas, RC)
    slots = jnp.concatenate([per_pair.reshape(HOURS, S, areas, RC), from_lower], axis=3)
    return gen_mean, hedge, slots.reshape(HOURS, S, areas * SLOTS)
```

```python
import functools

import jax
import jax.numpy as jnp
from jax import lax
from jax.experimental import pallas as pl
from jax.experimental.pallas import tpu as pltpu
from jax.sharding import PartitionSpec as P

HOURS = 24
REACH = 4
CAP = 16

STEP_SIZE = 0.5
LINE_CHUNK = 512

CONTRACT_LAST = (((1,), (1,)), ((), ()))
CONTRACT_FIRST = (((0,), (0,)), ((), ()))
VMEM = pl.BlockSpec(memory_space=pltpu.VMEM)


def partner_plan(areas):
    reach = min(REACH, areas - 1)
    if areas & (areas - 1) == 0 and areas - 1 <= REACH:
        flips = list(range(1, areas))
        routes = [[(a, a ^ f) for a in range(areas)] for f in flips]
        return routes, list(range(len(flips))), lambda here, i: here ^ flips[i]
    shifts = sorted({s % areas for d in range(1, reach + 1) for s in (d, -d)})
    routes = [[(a, (a + s) % areas) for a in range(areas)] for s in shifts]
    back = [shifts.index(areas - s) for s in shifts]
    return routes, back, lambda here, i: lax.rem(here + shifts[i], areas)


def block_facts(here, partner):
    low = partner > here
    distance = jnp.abs(partner - here)
    block = jnp.clip(distance - 1, 0, REACH - 1)
    in_reach = (distance >= 1) & (distance <= REACH)
    return low, jnp.minimum(here, partner), block, in_reach


def split_3(x):
    high = x.astype(jnp.bfloat16)
    rest = x - high.astype(jnp.float32)
    middle = rest.astype(jnp.bfloat16)
    rest = rest - middle.astype(jnp.float32)
    return jnp.concatenate([high, middle, rest.astype(jnp.bfloat16)], axis=0)


def write_ramp(mean_ref, before, after, limit, first_hour, padded_ref, excess_ref, ramp_ref):
    hours = mean_ref.shape[0]
    padded_ref[0:1, :] = before
    padded_ref[1 : hours + 1, :] = mean_ref[...]
    padded_ref[hours + 1 : hours + 2, :] = after
    diffs = padded_ref[1 : hours + 2, :] - padded_ref[0 : hours + 1, :]
    ids = first_hour + lax.broadcasted_iota(jnp.int32, diffs.shape, 0)
    valid = (ids >= 1) & (ids <= HOURS - 1)
    excess_ref[0 : hours + 1, :] = jnp.where(valid, diffs - jnp.clip(diffs, -limit, limit), 0.0)
    ramp_ref[...] = excess_ref[0:hours, :] - excess_ref[1 : hours + 1, :]


def line_work(inject_ref, ptdf_ref, line_max_ref, over_ref):
    inject = inject_ref[...]
    lines = ptdf_ref.shape[0]
    for at in range(0, lines, LINE_CHUNK):
        part = slice(at, at + LINE_CHUNK)
        flows = lax.dot_general(
            inject, ptdf_ref[part, :], CONTRACT_LAST, preferred_element_type=jnp.float32
        )
        limit = line_max_ref[:, part]
        over_ref[:, part] = (flows - jnp.clip(flows, -limit, limit)).astype(jnp.bfloat16)
    return jnp.dot(over_ref[...], ptdf_ref[...], preferred_element_type=jnp.float32)


def first_kernel(
    areas,
    blocks,
    partner_of,
    ptdf_ref,
    sens_ref,
    demand_ref,
    hedge_ref,
    start_ref,
    before_ref,
    after_ref,
    cost_ref,
    max_ref,
    limit_ref,
    line_max_ref,
    count_ref,
    low_bus_ref,
    high_bus_ref,
    susc_ref,
    *refs,
):
    own_refs = refs[:blocks]
    (gen_ref, hedged_ref, sums_ref, edge_ref, spread_ref, rows_ref, weight_ref) = refs[blocks : blocks + 7]
    (inject_ref, over_ref, onehot_ref, back_ref, padded_ref, excess_ref, ramp_ref) = refs[blocks + 7 :]
    hours, buses = start_ref.shape
    scens = demand_ref.shape[0] // hours
    here = lax.axis_index("area")
    first_hour = lax.axis_index("hour") * hours

    for i in range(blocks):
        partner = partner_of(here, i)
        low, row, block, in_reach = block_facts(here, partner)
        slots = slice(i * CAP, (i + 1) * CAP)
        pick = lax.broadcasted_iota(jnp.int32, (CAP, REACH * CAP), 1) == (
            block * CAP + lax.broadcasted_iota(jnp.int32, (CAP, REACH * CAP), 0)
        )
        table_row = pl.ds(row, 1)
        bus_row = jnp.where(low, low_bus_ref[table_row, :], high_bus_ref[table_row, :])
        bus = jnp.sum(jnp.where(pick, bus_row.astype(jnp.float32), 0.0), axis=1, keepdims=True)
        susc = jnp.sum(jnp.where(pick, susc_ref[table_row, :], 0.0), axis=1, keepdims=True)
        count_row = count_ref[table_row, :].astype(jnp.float32)
        is_block = lax.broadcasted_iota(jnp.int32, (CAP, REACH), 1) == block
        count = jnp.sum(jnp.where(is_block, count_row, 0.0), axis=1, keepdims=True)
        slot_ids = lax.broadcasted_iota(jnp.int32, (CAP, 1), 0).astype(jnp.float32)
        live = jnp.where((slot_ids < count) & in_reach, 1.0, 0.0)
        sign = jnp.where(low, 1.0, -1.0)
        bus_ids = lax.broadcasted_iota(jnp.int32, (CAP, buses), 1).astype(jnp.float32)
        onehot = jnp.where(bus_ids == bus, live, 0.0)
        onehot_ref[slots, :] = onehot.astype(jnp.bfloat16)
        spread_ref[slots, :] = (-sign * onehot).astype(jnp.bfloat16)
        weight_ref[slots, :] = jnp.broadcast_to(live * sign * susc, (CAP, 128))

    rows = jnp.dot(onehot_ref[...], sens_ref[...], preferred_element_type=jnp.float32)
    rows_ref[...] = rows.astype(jnp.bfloat16)

    for h in range(hours):
        part = slice(h * scens, (h + 1) * scens)
        inject_ref[part, :] = (start_ref[h : h + 1, :] - demand_ref[part, :]).astype(jnp.bfloat16)

    own = lax.dot_general(
        rows_ref[...], inject_ref[...], CONTRACT_LAST, preferred_element_type=jnp.float32
    )
    for i in range(blocks):
        own_refs[i][...] = own[i * CAP : (i + 1) * CAP, :]

    back_ref[...] = line_work(inject_ref, ptdf_ref, line_max_ref, over_ref)
    write_ramp(
        start_ref,
        before_ref[hours - 1 : hours, :],
        after_ref[0:1, :],
        limit_ref[...],
        first_hour,
        padded_ref,
        excess_ref,
        ramp_ref,
    )
    cost = cost_ref[...]
    top = max_ref[...]
    for h in range(hours):
        part = slice(h * scens, (h + 1) * scens)
        mean = start_ref[h : h + 1, :]
        hedge = hedge_ref[part, :]
        grad = cost + back_ref[part, :] + (mean - mean + hedge) + ramp_ref[h : h + 1, :]
        gen = jnp.clip(mean - STEP_SIZE * grad, 0.0, top)
        hedged = gen + hedge
        gen_ref[part, :] = gen
        hedged_ref[part, :] = hedged
        sums_ref[h : h + 1, :] = jnp.sum(hedged, axis=0, keepdims=True)
    edge_ref[0:1, :] = sums_ref[0:1, :]
    edge_ref[1:2, :] = sums_ref[hours - 1 : hours, :]


def second_kernel(blocks, terms, scen_total, ptdf_ref, demand_ref, gen_ref, hedged_ref, *refs):
    own_refs, refs = refs[:blocks], refs[blocks:]
    peer_refs, refs = refs[:blocks], refs[blocks:]
    sum_refs, refs = refs[:terms], refs[terms:]
    before_refs, refs = refs[:terms], refs[terms:]
    after_refs, refs = refs[:terms], refs[terms:]
    (spread_ref, rows_ref, weight_ref, cost_ref, max_ref, limit_ref, line_max_ref), refs = refs[:7], refs[7:]
    next_refs, refs = refs[:blocks], refs[blocks:]
    (hedged_out_ref, sums_out_ref, mine_ref, theirs_ref) = refs[:4]
    (inject_ref, over_ref, back_ref, mean_ref, padded_ref, excess_ref, ramp_ref) = refs[4:]
    hours, buses = mean_ref.shape
    width = demand_ref.shape[0]
    scens = width // hours
    first_hour = lax.axis_index("hour") * hours

    weight = weight_ref[:, 0:1]
    own = jnp.concatenate([ref[...] for ref in own_refs], axis=0)
    peer = jnp.concatenate([ref[...] for ref in peer_refs], axis=0)
    est_mine = weight * own
    est_theirs = -weight * peer
    flow = (est_mine + est_theirs) * 0.5
    dual_mine = est_mine - flow
    dual_theirs = est_theirs - flow
    spread = spread_ref[...]
    add = lax.dot_general(
        split_3(flow),
        jnp.concatenate([spread, spread, spread], axis=0),
        CONTRACT_FIRST,
        preferred_element_type=jnp.float32,
    )
    inject_ref[...] = (gen_ref[...] - demand_ref[...] + add).astype(jnp.bfloat16)

    own_next = lax.dot_general(
        rows_ref[...], inject_ref[...], CONTRACT_LAST, preferred_element_type=jnp.float32
    )
    for i in range(blocks):
        next_refs[i][...] = own_next[i * CAP : (i + 1) * CAP, :]
    mine_ref[...] = weight * (own_next - peer) + dual_mine
    theirs_ref[...] = weight * own + dual_theirs

    back_ref[...] = line_work(inject_ref, ptdf_ref, line_max_ref, over_ref)

    def agreed(parts):
        return functools.reduce(jnp.add, parts) / scen_total

    mean_ref[...] = agreed([ref[...] for ref in sum_refs])
    write_ramp(
        mean_ref,
        agreed([ref[1:2, :] for ref in before_refs]),
        agreed([ref[0:1, :] for ref in after_refs]),
        limit_ref[...],
        first_hour,
        padded_ref,
        excess_ref,
        ramp_ref,
    )
    cost = cost_ref[...]
    top = max_ref[...]
    for h in range(hours):
        part = slice(h * scens, (h + 1) * scens)
        mean = mean_ref[h : h + 1, :]
        gen = gen_ref[part, :]
        hedge = hedged_ref[part, :] - mean
        grad = cost + back_ref[part, :] + (gen - mean + hedge) + ramp_ref[h : h + 1, :]
        gen = jnp.clip(gen - STEP_SIZE * grad, 0.0, top)
        hedged = gen + hedge
        hedged_out_ref[part, :] = hedged
        sums_out_ref[h : h + 1, :] = jnp.sum(hedged, axis=0, keepdims=True)


def last_kernel(blocks, terms, partner_of, scen_total, hedged_ref, *refs):
    sum_refs, refs = refs[:terms], refs[terms:]
    peer_refs, refs = refs[:blocks], refs[blocks:]
    weight_ref, mine_ref, theirs_ref, mean_ref, hedge_ref, tie_ref = refs
    hours = mean_ref.shape[0]
    scens = hedged_ref.shape[0] // hours
    here = lax.axis_index("area")
    slots = tie_ref.shape[1]
    places = []
    for i in range(blocks):
        low, _, block, in_reach = block_facts(here, partner_of(here, i))
        first = block * CAP + jnp.where(low, 0, REACH * CAP)
        hit = lax.broadcasted_iota(jnp.int32, (CAP, slots), 1) == (
            first + lax.broadcasted_iota(jnp.int32, (CAP, slots), 0)
        )
        places.append(jnp.where(hit & in_reach, 1.0, 0.0).astype(jnp.bfloat16))
    peer = jnp.concatenate([ref[...] for ref in peer_refs], axis=0)
    flow = (mine_ref[...] + (theirs_ref[...] - weight_ref[:, 0:1] * peer)) * 0.5
    tie_ref[...] = lax.dot_general(
        split_3(flow),
        jnp.concatenate(places * 3, axis=0),
        CONTRACT_FIRST,
        preferred_element_type=jnp.float32,
    )
    mean_ref[...] = functools.reduce(jnp.add, [ref[...] for ref in sum_refs]) / scen_total
    for h in range(hours):
        part = slice(h * scens, (h + 1) * scens)
        hedge_ref[part, :] = hedged_ref[part, :] - mean_ref[h : h + 1, :]


def call(kernel, name, args, outs, scratch, flops):
    size = sum(x.size * x.dtype.itemsize for x in list(args) + list(outs))
    return pl.pallas_call(
        kernel,
        name=name,
        out_shape=outs,
        in_specs=[VMEM] * len(args),
        out_specs=[VMEM] * len(outs),
        scratch_shapes=scratch,
        compiler_params=pltpu.CompilerParams(vmem_limit_bytes=40 * 1024 * 1024),
        cost_estimate=pl.CostEstimate(flops=flops, bytes_accessed=size, transcendentals=0),
    )(*args)


def per_device(
    ptdf,
    angle_sens,
    demand,
    gen_start,
    hedge_dual,
    gen_cost,
    gen_max,
    gen_ramp,
    line_max,
    tie_count,
    tie_low_bus,
    tie_high_bus,
    tie_susc,
):
    hours, scens, buses = demand.shape
    lines = ptdf.shape[0]
    width = hours * scens
    areas = lax.axis_size("area")
    n_scen = lax.axis_size("scen")
    n_hour = lax.axis_size("hour")
    scen_total = scens * n_scen
    routes, returns, partner_of = partner_plan(areas)
    blocks = len(routes)
    slots = blocks * CAP
    f32, bf16 = jnp.float32, jnp.bfloat16
    up = [(i, (i + 1) % n_hour) for i in range(n_hour)]
    down = [(i, (i - 1) % n_hour) for i in range(n_hour)]

    def from_hours(x):
        before = lax.ppermute(x, "hour", up)
        return before, before if n_hour == 2 else lax.ppermute(x, "hour", down)

    def from_partners(parts):
        sent = [None] * blocks
        for i in reversed(range(blocks)):
            sent[i] = lax.ppermute(parts[i], "area", routes[i])
        return [sent[returns[i]] for i in range(blocks)]

    def shape(*dims, dtype=f32):
        return jax.ShapeDtypeStruct(dims, dtype)

    load = demand.reshape(width, buses)
    cost, top, limit, line_top = (x.reshape(1, -1) for x in (gen_cost, gen_max, gen_ramp, line_max))
    work = 4 * width * lines * buses + 2 * slots * buses * (width + buses)
    ramp_scratch = [
        pltpu.VMEM((hours + 4, buses), f32),
        pltpu.VMEM((hours + 4, buses), f32),
        pltpu.VMEM((hours, buses), f32),
    ]
    step_scratch = [pltpu.VMEM((width, buses), bf16), pltpu.VMEM((width, lines), bf16)]

    before, after = from_hours(gen_start)
    first = call(
        functools.partial(first_kernel, areas, blocks, partner_of),
        "first",
        (
            ptdf,
            angle_sens,
            load,
            hedge_dual.reshape(width, buses),
            gen_start,
            before,
            after,
            cost,
            top,
            limit,
            line_top,
            tie_count,
            tie_low_bus,
            tie_high_bus,
            tie_susc,
        ),
        [shape(CAP, width)] * blocks
        + [
            shape(width, buses),
            shape(width, buses),
            shape(hours, buses),
            shape(2, buses),
            shape(slots, buses, dtype=bf16),
            shape(slots, buses, dtype=bf16),
            shape(slots, 128),
        ],
        step_scratch + [pltpu.VMEM((slots, buses), bf16), pltpu.VMEM((width, buses), f32)] + ramp_scratch,
        work,
    )
    own = first[:blocks]
    gen, hedged, sums, edge, spread, rows, weight = first[blocks:]

    def from_scens(sums):
        if n_scen == 2:
            return [sums, lax.ppermute(sums, "scen", [(0, 1), (1, 0)])]
        return [lax.psum(sums, "scen")]

    peer = from_partners(own)
    if n_scen == 2 and n_hour == 2:
        sum_terms = from_scens(sums)
        edge_terms = [
            lax.ppermute(edge, "hour", up),
            lax.ppermute(edge, ("scen", "hour"), [(i, 3 - i) for i in range(4)]),
        ]
        before_terms, after_terms = edge_terms, edge_terms
    else:
        sum_terms = [lax.psum(sums, "scen")]
        edge = jnp.concatenate([sum_terms[0][:1], sum_terms[0][-1:]], axis=0)
        before, after = from_hours(edge)
        before_terms, after_terms = [before], [after]
    terms = len(sum_terms)

    second = call(
        functools.partial(second_kernel, blocks, terms, scen_total),
        "second",
        (
            ptdf,
            load,
            gen,
            hedged,
            *own,
            *peer,
            *sum_terms,
            *before_terms,
            *after_terms,
            spread,
            rows,
            weight,
            cost,
            top,
            limit,
            line_top,
        ),
        [shape(CAP, width)] * blocks
        + [shape(width, buses), shape(hours, buses), shape(slots, width), shape(slots, width)],
        step_scratch + [pltpu.VMEM((width, buses), f32), pltpu.VMEM((hours, buses), f32)] + ramp_scratch,
        work,
    )
    own = second[:blocks]
    hedged, sums, mine, theirs = second[blocks:]
    peer = from_partners(own)
    sum_terms = from_scens(sums)
    gen_mean, hedge, tie_flow = call(
        functools.partial(last_kernel, blocks, len(sum_terms), partner_of, scen_total),
        "last",
        (hedged, *sum_terms, *peer, weight, mine, theirs),
        [shape(hours, buses), shape(width, buses), shape(width, 2 * REACH * CAP)],
        [],
        6 * slots * width * 2 * REACH * CAP,
    )
    return (
        gen_mean,
        hedge.reshape(hours, scens, buses),
        tie_flow.reshape(hours, scens, 2 * REACH * CAP),
    )


def solution(mesh):
    return jax.shard_map(
        per_device,
        mesh=mesh,
        in_specs=(
            P(("group", "area"), None),
            P(("group", "area"), None),
            P(("group", "hour"), "scen", "area"),
            P(("group", "hour"), "area"),
            P(("group", "hour"), "scen", "area"),
            P(("group", "area")),
            P(("group", "area")),
            P(("group", "area")),
            P(("group", "area")),
            P("group", None),
            P("group", None),
            P("group", None),
            P("group", None),
        ),
        out_specs=(
            P(("group", "hour"), "area"),
            P(("group", "hour"), "scen", "area"),
            P(("group", "hour"), "scen", "area"),
        ),
        check_vma=False,
    )
```

```python
import functools

import jax
import jax.numpy as jnp
from jax import lax
from jax.experimental import pallas as pl
from jax.experimental.pallas import tpu as pltpu
from jax.sharding import PartitionSpec as P

HOURS = 24
REACH = 4
CAP = 16

STEP_SIZE = 0.5
LINE_CHUNK = 512

CONTRACT_LAST = (((1,), (1,)), ((), ()))
CONTRACT_FIRST = (((0,), (0,)), ((), ()))
VMEM = pl.BlockSpec(memory_space=pltpu.VMEM)
ANY = pl.BlockSpec(memory_space=pltpu.HBM)


def partner_plan(areas):
    if areas <= REACH + 1:

        def all_pairs(parts):
            return lax.all_to_all(parts, "area", split_axis=0, concat_axis=0, tiled=True)

        return areas, lambda here, i: i, all_pairs
    reach = min(REACH, areas - 1)
    shifts = sorted({s % areas for d in range(1, reach + 1) for s in (d, -d)})
    routes = [[(a, (a + s) % areas) for a in range(areas)] for s in shifts]

    def by_shift(parts):
        sent = [lax.ppermute(parts[i], "area", route) for i, route in enumerate(routes)]
        return jnp.stack([sent[shifts.index(areas - s)] for s in shifts])

    return len(shifts), lambda here, i: lax.rem(here + shifts[i], areas), by_shift


def block_facts(here, partner):
    low = partner > here
    distance = jnp.abs(partner - here)
    block = jnp.clip(distance - 1, 0, REACH - 1)
    in_reach = (distance >= 1) & (distance <= REACH)
    return low, jnp.minimum(here, partner), block, in_reach


def split_3(x):
    high = x.astype(jnp.bfloat16)
    rest = x - high.astype(jnp.float32)
    middle = rest.astype(jnp.bfloat16)
    rest = rest - middle.astype(jnp.float32)
    return jnp.concatenate([high, middle, rest.astype(jnp.bfloat16)], axis=0)


def write_ramp(mean_ref, before, after, limit, first_hour, padded_ref, excess_ref, ramp_ref):
    hours = mean_ref.shape[0]
    padded_ref[0:1, :] = before
    padded_ref[1 : hours + 1, :] = mean_ref[...]
    padded_ref[hours + 1 : hours + 2, :] = after
    diffs = padded_ref[1 : hours + 2, :] - padded_ref[0 : hours + 1, :]
    ids = first_hour + lax.broadcasted_iota(jnp.int32, diffs.shape, 0)
    valid = (ids >= 1) & (ids <= HOURS - 1)
    excess_ref[0 : hours + 1, :] = jnp.where(valid, diffs - jnp.clip(diffs, -limit, limit), 0.0)
    ramp_ref[...] = excess_ref[0:hours, :] - excess_ref[1 : hours + 1, :]


def line_work(inject_ref, ptdf_ref, line_max_ref, over_ref, arrived=None):
    inject = inject_ref[...]
    lines = ptdf_ref.shape[0]
    for at in range(0, lines, LINE_CHUNK):
        part = slice(at, at + LINE_CHUNK)
        if arrived is not None:
            arrived(at)
        flows = lax.dot_general(
            inject, ptdf_ref[part, :], CONTRACT_LAST, preferred_element_type=jnp.float32
        )
        limit = line_max_ref[:, part]
        over_ref[:, part] = (flows - jnp.clip(flows, -limit, limit)).astype(jnp.bfloat16)
    return jnp.dot(over_ref[...], ptdf_ref[...], preferred_element_type=jnp.float32)


def first_kernel(
    blocks,
    partner_of,
    ptdf_in,
    sens_in,
    demand_in,
    hedge_in,
    start_in,
    before_ref,
    after_ref,
    cost_in,
    max_in,
    limit_in,
    line_max_in,
    count_in,
    low_bus_in,
    high_bus_in,
    susc_in,
    own_ref,
    gen_ref,
    base_ref,
    hedged_ref,
    sums_ref,
    edge_ref,
    spread_ref,
    rows_ref,
    weight_ref,
    ptdf_ref,
    cost_ref,
    max_ref,
    limit_ref,
    line_max_ref,
    sens_ref,
    demand_ref,
    hedge_ref,
    start_ref,
    count_ref,
    low_bus_ref,
    high_bus_ref,
    susc_ref,
    inject_ref,
    over_ref,
    onehot_ref,
    back_ref,
    padded_ref,
    excess_ref,
    ramp_ref,
    copy_sems,
):
    hours, buses = start_ref.shape
    lines = ptdf_ref.shape[0]
    scens = demand_ref.shape[0] // hours
    here = lax.axis_index("area")
    first_hour = lax.axis_index("hour") * hours

    pairs = [
        (start_in, start_ref),
        (demand_in, demand_ref),
        (count_in, count_ref),
        (low_bus_in, low_bus_ref),
        (high_bus_in, high_bus_ref),
        (susc_in, susc_ref),
        (line_max_in, line_max_ref),
    ]
    chunks = range(0, lines, LINE_CHUNK)
    pairs += [(ptdf_in.at[pl.ds(at, LINE_CHUNK)], ptdf_ref.at[pl.ds(at, LINE_CHUNK)]) for at in chunks]
    pairs += [
        (sens_in, sens_ref),
        (hedge_in, hedge_ref),
        (cost_in, cost_ref),
        (max_in, max_ref),
        (limit_in, limit_ref),
    ]
    copies = [pltpu.make_async_copy(src, dst, copy_sems.at[i]) for i, (src, dst) in enumerate(pairs)]
    for copy in copies:
        copy.start()
    start_copy, demand_copy, *table_copies, line_copy = copies[:7]
    ptdf_copies = copies[7 : 7 + len(chunks)]
    sens_copy, *late_copies = copies[7 + len(chunks) :]

    start_copy.wait()
    demand_copy.wait()
    for h in range(hours):
        part = slice(h * scens, (h + 1) * scens)
        inject_ref[part, :] = (start_ref[h : h + 1, :] - demand_ref[part, :]).astype(jnp.bfloat16)

    for copy in table_copies:
        copy.wait()
    for i in range(blocks):
        partner = partner_of(here, i)
        low, row, block, in_reach = block_facts(here, partner)
        slots = slice(i * CAP, (i + 1) * CAP)
        pick = lax.broadcasted_iota(jnp.int32, (CAP, REACH * CAP), 1) == (
            block * CAP + lax.broadcasted_iota(jnp.int32, (CAP, REACH * CAP), 0)
        )
        table_row = pl.ds(row, 1)
        bus_row = jnp.where(low, low_bus_ref[table_row, :], high_bus_ref[table_row, :])
        bus = jnp.sum(jnp.where(pick, bus_row.astype(jnp.float32), 0.0), axis=1, keepdims=True)
        susc = jnp.sum(jnp.where(pick, susc_ref[table_row, :], 0.0), axis=1, keepdims=True)
        count_row = count_ref[table_row, :].astype(jnp.float32)
        is_block = lax.broadcasted_iota(jnp.int32, (CAP, REACH), 1) == block
        count = jnp.sum(jnp.where(is_block, count_row, 0.0), axis=1, keepdims=True)
        slot_ids = lax.broadcasted_iota(jnp.int32, (CAP, 1), 0).astype(jnp.float32)
        live = jnp.where((slot_ids < count) & in_reach, 1.0, 0.0)
        sign = jnp.where(low, 1.0, -1.0)
        bus_ids = lax.broadcasted_iota(jnp.int32, (CAP, buses), 1).astype(jnp.float32)
        onehot = jnp.where(bus_ids == bus, live, 0.0)
        onehot_ref[slots, :] = onehot.astype(jnp.bfloat16)
        spread_ref[slots, :] = (-sign * onehot).astype(jnp.bfloat16)
        weight_ref[slots, :] = jnp.broadcast_to(live * sign * susc, (CAP, 128))

    line_copy.wait()
    back_ref[...] = line_work(
        inject_ref, ptdf_ref, line_max_ref, over_ref, lambda at: ptdf_copies[at // LINE_CHUNK].wait()
    )
    sens_copy.wait()
    rows = jnp.dot(onehot_ref[...], sens_ref[...], preferred_element_type=jnp.float32)
    rows_ref[...] = rows.astype(jnp.bfloat16)
    own = lax.dot_general(
        rows_ref[...], inject_ref[...], CONTRACT_LAST, preferred_element_type=jnp.float32
    )
    for i in range(blocks):
        own_ref[i] = own[i * CAP : (i + 1) * CAP, :]

    for copy in late_copies:
        copy.wait()
    write_ramp(
        start_ref,
        before_ref[hours - 1 : hours, :],
        after_ref[0:1, :],
        limit_ref[...],
        first_hour,
        padded_ref,
        excess_ref,
        ramp_ref,
    )
    cost = cost_ref[...]
    top = max_ref[...]
    for h in range(hours):
        part = slice(h * scens, (h + 1) * scens)
        mean = start_ref[h : h + 1, :]
        hedge = hedge_ref[part, :]
        grad = cost + back_ref[part, :] + (mean - mean + hedge) + ramp_ref[h : h + 1, :]
        gen = jnp.clip(mean - STEP_SIZE * grad, 0.0, top)
        hedged = gen + hedge
        gen_ref[part, :] = gen
        base_ref[part, :] = gen - demand_ref[part, :]
        hedged_ref[part, :] = hedged
        sums_ref[h : h + 1, :] = jnp.sum(hedged, axis=0, keepdims=True)
    edge_ref[0:1, :] = sums_ref[0:1, :]
    edge_ref[1:2, :] = sums_ref[hours - 1 : hours, :]


def second_kernel(
    blocks, terms, scen_total, ptdf_ref, base_ref, gen_ref, hedged_ref, own_ref, peer_ref, *refs
):
    sum_refs, refs = refs[:terms], refs[terms:]
    before_refs, refs = refs[:terms], refs[terms:]
    after_refs, refs = refs[:terms], refs[terms:]
    (spread_ref, rows_ref, weight_ref, cost_ref, max_ref, limit_ref, line_max_ref), refs = refs[:7], refs[7:]
    (next_ref, hedged_out_ref, sums_out_ref, mine_ref, theirs_ref) = refs[:5]
    (inject_ref, over_ref, back_ref, mean_ref, padded_ref, excess_ref, ramp_ref) = refs[5:]
    hours, buses = mean_ref.shape
    width = base_ref.shape[0]
    scens = width // hours
    first_hour = lax.axis_index("hour") * hours

    weight = weight_ref[:, 0:1]
    own = own_ref[...].reshape(blocks * CAP, width)
    peer = peer_ref[...].reshape(blocks * CAP, width)
    est_mine = weight * own
    est_theirs = -weight * peer
    flow = (est_mine + est_theirs) * 0.5
    dual_mine = est_mine - flow
    dual_theirs = est_theirs - flow
    spread = spread_ref[...]
    add = lax.dot_general(
        split_3(flow),
        jnp.concatenate([spread, spread, spread], axis=0),
        CONTRACT_FIRST,
        preferred_element_type=jnp.float32,
    )
    inject_ref[...] = (base_ref[...] + add).astype(jnp.bfloat16)

    own_next = lax.dot_general(
        rows_ref[...], inject_ref[...], CONTRACT_LAST, preferred_element_type=jnp.float32
    )
    for i in range(blocks):
        next_ref[i] = own_next[i * CAP : (i + 1) * CAP, :]
    mine_ref[...] = weight * (own_next - peer) + dual_mine
    theirs_ref[...] = weight * own + dual_theirs

    back_ref[...] = line_work(inject_ref, ptdf_ref, line_max_ref, over_ref)

    def agreed(parts):
        return functools.reduce(jnp.add, parts) / scen_total

    mean_ref[...] = agreed([ref[...] for ref in sum_refs])
    write_ramp(
        mean_ref,
        agreed([ref[1:2, :] for ref in before_refs]),
        agreed([ref[0:1, :] for ref in after_refs]),
        limit_ref[...],
        first_hour,
        padded_ref,
        excess_ref,
        ramp_ref,
    )
    cost = cost_ref[...]
    top = max_ref[...]
    for h in range(hours):
        part = slice(h * scens, (h + 1) * scens)
        mean = mean_ref[h : h + 1, :]
        gen = gen_ref[part, :]
        hedge = hedged_ref[part, :] - mean
        grad = cost + back_ref[part, :] + (gen - mean + hedge) + ramp_ref[h : h + 1, :]
        gen = jnp.clip(gen - STEP_SIZE * grad, 0.0, top)
        hedged = gen + hedge
        hedged_out_ref[part, :] = hedged
        sums_out_ref[h : h + 1, :] = jnp.sum(hedged, axis=0, keepdims=True)


def last_kernel(blocks, terms, partner_of, scen_total, hedged_ref, *refs):
    sum_refs, refs = refs[:terms], refs[terms:]
    peer_ref, weight_ref, mine_ref, theirs_ref, mean_ref, hedge_ref, tie_ref = refs
    hours = mean_ref.shape[0]
    scens = hedged_ref.shape[0] // hours
    here = lax.axis_index("area")
    slots = tie_ref.shape[1]
    places = []
    for i in range(blocks):
        low, _, block, in_reach = block_facts(here, partner_of(here, i))
        first = block * CAP + jnp.where(low, 0, REACH * CAP)
        hit = lax.broadcasted_iota(jnp.int32, (CAP, slots), 1) == (
            first + lax.broadcasted_iota(jnp.int32, (CAP, slots), 0)
        )
        places.append(jnp.where(hit & in_reach, 1.0, 0.0).astype(jnp.bfloat16))
    peer = peer_ref[...].reshape(weight_ref.shape[0], hours * scens)
    flow = (mine_ref[...] + (theirs_ref[...] - weight_ref[:, 0:1] * peer)) * 0.5
    tie_ref[...] = lax.dot_general(
        split_3(flow),
        jnp.concatenate(places * 3, axis=0),
        CONTRACT_FIRST,
        preferred_element_type=jnp.float32,
    )
    mean_ref[...] = functools.reduce(jnp.add, [ref[...] for ref in sum_refs]) / scen_total
    for h in range(hours):
        part = slice(h * scens, (h + 1) * scens)
        hedge_ref[part, :] = hedged_ref[part, :] - mean_ref[h : h + 1, :]


def call(kernel, name, args, outs, scratch, flops, in_place=()):
    size = sum(x.size * x.dtype.itemsize for x in list(args) + list(outs))
    return pl.pallas_call(
        kernel,
        name=name,
        out_shape=outs,
        in_specs=[ANY if i in in_place else VMEM for i in range(len(args))],
        out_specs=[VMEM] * len(outs),
        scratch_shapes=scratch,
        compiler_params=pltpu.CompilerParams(vmem_limit_bytes=48 * 1024 * 1024),
        cost_estimate=pl.CostEstimate(flops=flops, bytes_accessed=size, transcendentals=0),
    )(*(pltpu.with_memory_space_constraint(x, pltpu.HBM) if i in in_place else x for i, x in enumerate(args)))


def per_device(
    ptdf,
    angle_sens,
    demand,
    gen_start,
    hedge_dual,
    gen_cost,
    gen_max,
    gen_ramp,
    line_max,
    tie_count,
    tie_low_bus,
    tie_high_bus,
    tie_susc,
):
    hours, scens, buses = demand.shape
    lines = ptdf.shape[0]
    width = hours * scens
    areas = lax.axis_size("area")
    n_scen = lax.axis_size("scen")
    n_hour = lax.axis_size("hour")
    scen_total = scens * n_scen
    blocks, partner_of, from_partners = partner_plan(areas)
    slots = blocks * CAP
    f32, bf16 = jnp.float32, jnp.bfloat16
    up = [(i, (i + 1) % n_hour) for i in range(n_hour)]
    down = [(i, (i - 1) % n_hour) for i in range(n_hour)]

    def from_hours(x):
        before = lax.ppermute(x, "hour", up)
        return before, before if n_hour == 2 else lax.ppermute(x, "hour", down)

    def shape(*dims, dtype=f32):
        return jax.ShapeDtypeStruct(dims, dtype)

    load = demand.reshape(width, buses)
    cost, top, limit, line_top = (x.reshape(1, -1) for x in (gen_cost, gen_max, gen_ramp, line_max))
    work = 4 * width * lines * buses + 2 * slots * buses * (width + buses)
    ramp_scratch = [
        pltpu.VMEM((hours + 4, buses), f32),
        pltpu.VMEM((hours + 4, buses), f32),
        pltpu.VMEM((hours, buses), f32),
    ]
    step_scratch = [pltpu.VMEM((width, buses), bf16), pltpu.VMEM((width, lines), bf16)]

    before, after = from_hours(gen_start)
    first = call(
        functools.partial(first_kernel, blocks, partner_of),
        "first",
        (
            ptdf,
            angle_sens,
            load,
            hedge_dual.reshape(width, buses),
            gen_start,
            before,
            after,
            cost,
            top,
            limit,
            line_top,
            tie_count,
            tie_low_bus,
            tie_high_bus,
            tie_susc,
        ),
        [
            shape(blocks, CAP, width),
            shape(width, buses),
            shape(width, buses),
            shape(width, buses),
            shape(hours, buses),
            shape(2, buses),
            shape(slots, buses, dtype=bf16),
            shape(slots, buses, dtype=bf16),
            shape(slots, 128),
            shape(lines, buses, dtype=bf16),
            shape(1, buses),
            shape(1, buses),
            shape(1, buses),
            shape(1, lines),
        ],
        [
            pltpu.VMEM(x.shape, x.dtype)
            for x in (angle_sens, load, load, gen_start, tie_count, tie_low_bus, tie_high_bus, tie_susc)
        ]
        + step_scratch
        + [pltpu.VMEM((slots, buses), bf16), pltpu.VMEM((width, buses), f32)]
        + ramp_scratch
        + [pltpu.SemaphoreType.DMA((12 + lines // LINE_CHUNK,))],
        work,
        set(range(15)) - {5, 6},
    )
    own, gen, base, hedged, sums, edge, spread, rows, weight, held, cost, top, limit, line_top = first

    def from_scens(sums):
        if n_scen == 2:
            return [sums, lax.ppermute(sums, "scen", [(0, 1), (1, 0)])]
        return [lax.psum(sums, "scen")]

    peer = from_partners(own)
    if n_scen == 2 and n_hour == 2:
        sum_terms = from_scens(sums)
        edge_terms = [
            lax.ppermute(edge, "hour", up),
            lax.ppermute(edge, ("scen", "hour"), [(i, 3 - i) for i in range(4)]),
        ]
        before_terms, after_terms = edge_terms, edge_terms
    else:
        sum_terms = [lax.psum(sums, "scen")]
        edge = jnp.concatenate([sum_terms[0][:1], sum_terms[0][-1:]], axis=0)
        before, after = from_hours(edge)
        before_terms, after_terms = [before], [after]
    terms = len(sum_terms)

    second = call(
        functools.partial(second_kernel, blocks, terms, scen_total),
        "second",
        (
            held,
            base,
            gen,
            hedged,
            own,
            peer,
            *sum_terms,
            *before_terms,
            *after_terms,
            spread,
            rows,
            weight,
            cost,
            top,
            limit,
            line_top,
        ),
        [shape(blocks, CAP, width), shape(width, buses), shape(hours, buses), shape(slots, width), shape(slots, width)],
        step_scratch + [pltpu.VMEM((width, buses), f32), pltpu.VMEM((hours, buses), f32)] + ramp_scratch,
        work,
    )
    own, hedged, sums, mine, theirs = second
    peer = from_partners(own)
    sum_terms = from_scens(sums)
    gen_mean, hedge, tie_flow = call(
        functools.partial(last_kernel, blocks, len(sum_terms), partner_of, scen_total),
        "last",
        (hedged, *sum_terms, peer, weight, mine, theirs),
        [shape(hours, buses), shape(width, buses), shape(width, 2 * REACH * CAP)],
        [],
        6 * slots * width * 2 * REACH * CAP,
    )
    return (
        gen_mean,
        hedge.reshape(hours, scens, buses),
        tie_flow.reshape(hours, scens, 2 * REACH * CAP),
    )


def solution(mesh):
    return jax.shard_map(
        per_device,
        mesh=mesh,
        in_specs=(
            P(("group", "area"), None),
            P(("group", "area"), None),
            P(("group", "hour"), "scen", "area"),
            P(("group", "hour"), "area"),
            P(("group", "hour"), "scen", "area"),
            P(("group", "area")),
            P(("group", "area")),
            P(("group", "area")),
            P(("group", "area")),
            P("group", None),
            P("group", None),
            P("group", None),
            P("group", None),
        ),
        out_specs=(
            P(("group", "hour"), "area"),
            P(("group", "hour"), "scen", "area"),
            P(("group", "hour"), "scen", "area"),
        ),
        check_vma=False,
    )
```

```python
import functools

import jax
import jax.numpy as jnp
from jax import lax
from jax.experimental import pallas as pl
from jax.experimental.pallas import tpu as pltpu
from jax.sharding import PartitionSpec as P

HOURS = 24
REACH = 4
CAP = 16

STEP_SIZE = 0.5
LINE_CHUNK = 512

CONTRACT_LAST = (((1,), (1,)), ((), ()))
CONTRACT_FIRST = (((0,), (0,)), ((), ()))
VMEM = pl.BlockSpec(memory_space=pltpu.VMEM)
ANY = pl.BlockSpec(memory_space=pltpu.HBM)


def partner_plan(areas):
    if areas & (areas - 1) == 0 and areas <= REACH + 1:
        flips = range(1, areas)

        def by_flip(parts):
            sent = {}
            for f in reversed(flips):
                sent[f] = lax.ppermute(parts[f - 1], "area", [(a, a ^ f) for a in range(areas)])
            return [sent[f] for f in flips]

        return len(flips), lambda here, i: here ^ flips[i], by_flip
    reach = min(REACH, areas - 1)
    shifts = sorted({s % areas for d in range(1, reach + 1) for s in (d, -d)})

    def by_shift(parts):
        sent = [
            lax.ppermute(part, "area", [(a, (a + s) % areas) for a in range(areas)])
            for part, s in zip(parts, shifts)
        ]
        return [sent[shifts.index(areas - s)] for s in shifts]

    return len(shifts), lambda here, i: lax.rem(here + shifts[i], areas), by_shift


def block_facts(here, partner):
    low = partner > here
    distance = jnp.abs(partner - here)
    block = jnp.clip(distance - 1, 0, REACH - 1)
    in_reach = (distance >= 1) & (distance <= REACH)
    return low, jnp.minimum(here, partner), block, in_reach


def split_3(x):
    high = x.astype(jnp.bfloat16)
    rest = x - high.astype(jnp.float32)
    middle = rest.astype(jnp.bfloat16)
    rest = rest - middle.astype(jnp.float32)
    return jnp.concatenate([high, middle, rest.astype(jnp.bfloat16)], axis=0)


def excess(diffs, limit):
    return diffs - jnp.clip(diffs, -limit, limit)


def write_ramp(mean_ref, beyond, limit, first_hour, padded_ref, excess_ref, ramp_ref):
    hours = ramp_ref.shape[0]
    padded_ref[0:1, :] = beyond
    padded_ref[1 : hours + 1, :] = mean_ref[0:hours, :]
    padded_ref[hours + 1 : hours + 2, :] = beyond
    diffs = padded_ref[1 : hours + 2, :] - padded_ref[0 : hours + 1, :]
    ids = first_hour + lax.broadcasted_iota(jnp.int32, diffs.shape, 0)
    valid = (ids >= 1) & (ids <= HOURS - 1)
    excess_ref[0 : hours + 1, :] = jnp.where(valid, excess(diffs, limit), 0.0)
    ramp_ref[...] = excess_ref[0:hours, :] - excess_ref[1 : hours + 1, :]


def line_work(inject_ref, ptdf_ref, line_max_ref, over_ref):
    inject = inject_ref[...]
    lines = ptdf_ref.shape[0]
    for at in range(0, lines, LINE_CHUNK):
        part = slice(at, at + LINE_CHUNK)
        flows = lax.dot_general(
            inject, ptdf_ref[part, :], CONTRACT_LAST, preferred_element_type=jnp.float32
        )
        limit = line_max_ref[:, part]
        over_ref[:, part] = (flows - jnp.clip(flows, -limit, limit)).astype(jnp.bfloat16)
    return jnp.dot(over_ref[...], ptdf_ref[...], preferred_element_type=jnp.float32)


def angle_kernel(
    blocks,
    partner_of,
    sens_in,
    demand_in,
    hedge_in,
    start_in,
    cost_in,
    max_in,
    limit_in,
    line_max_in,
    count_in,
    low_bus_in,
    high_bus_in,
    susc_in,
    ptdf_in,
    *refs,
):
    own_refs, refs = refs[:blocks], refs[blocks:]
    (
        edge_ref,
        inject_ref,
        spread_ref,
        rows_ref,
        weight_ref,
        demand_ref,
        hedge_ref,
        start_ref,
        cost_ref,
        max_ref,
        limit_ref,
        line_max_ref,
        ptdf_ref,
        sens_ref,
        count_ref,
        low_bus_ref,
        high_bus_ref,
        susc_ref,
        onehot_ref,
        copy_sems,
    ) = refs
    hours, buses = start_ref.shape
    scens = demand_ref.shape[0] // hours
    here = lax.axis_index("area")
    early = lax.axis_index("hour") == 0

    pairs = (
        (count_in, count_ref),
        (low_bus_in, low_bus_ref),
        (high_bus_in, high_bus_ref),
        (susc_in, susc_ref),
        (start_in, start_ref),
        (demand_in, demand_ref),
        (sens_in, sens_ref),
        (hedge_in, hedge_ref),
        (cost_in, cost_ref),
        (max_in, max_ref),
        (limit_in, limit_ref),
        (line_max_in, line_max_ref),
        (ptdf_in, ptdf_ref),
    )
    copies = [pltpu.make_async_copy(src, dst, copy_sems.at[i]) for i, (src, dst) in enumerate(pairs)]
    for copy in copies:
        copy.start()

    for copy in copies[:4]:
        copy.wait()
    for i in range(blocks):
        partner = partner_of(here, i)
        low, row, block, in_reach = block_facts(here, partner)
        slots = slice(i * CAP, (i + 1) * CAP)
        pick = lax.broadcasted_iota(jnp.int32, (CAP, REACH * CAP), 1) == (
            block * CAP + lax.broadcasted_iota(jnp.int32, (CAP, REACH * CAP), 0)
        )
        table_row = pl.ds(row, 1)
        bus_row = jnp.where(low, low_bus_ref[table_row, :], high_bus_ref[table_row, :])
        bus = jnp.sum(jnp.where(pick, bus_row.astype(jnp.float32), 0.0), axis=1, keepdims=True)
        susc = jnp.sum(jnp.where(pick, susc_ref[table_row, :], 0.0), axis=1, keepdims=True)
        count_row = count_ref[table_row, :].astype(jnp.float32)
        is_block = lax.broadcasted_iota(jnp.int32, (CAP, REACH), 1) == block
        count = jnp.sum(jnp.where(is_block, count_row, 0.0), axis=1, keepdims=True)
        slot_ids = lax.broadcasted_iota(jnp.int32, (CAP, 1), 0).astype(jnp.float32)
        live = jnp.where((slot_ids < count) & in_reach, 1.0, 0.0)
        sign = jnp.where(low, 1.0, -1.0)
        bus_ids = lax.broadcasted_iota(jnp.int32, (CAP, buses), 1).astype(jnp.float32)
        onehot = jnp.where(bus_ids == bus, live, 0.0)
        onehot_ref[slots, :] = onehot.astype(jnp.bfloat16)
        spread_ref[slots, :] = (-sign * onehot).astype(jnp.bfloat16)
        weight_ref[slots, :] = jnp.broadcast_to(live * sign * susc, (CAP, 128))

    for copy in copies[4:7]:
        copy.wait()
    for h in range(hours):
        part = slice(h * scens, (h + 1) * scens)
        inject_ref[part, :] = (start_ref[h : h + 1, :] - demand_ref[part, :]).astype(jnp.bfloat16)
    rows = jnp.dot(onehot_ref[...], sens_ref[...], preferred_element_type=jnp.float32)
    rows_ref[...] = rows.astype(jnp.bfloat16)
    own = lax.dot_general(
        rows_ref[...], inject_ref[...], CONTRACT_LAST, preferred_element_type=jnp.float32
    )
    for i in range(blocks):
        own_refs[i][...] = own[i * CAP : (i + 1) * CAP, :]

    for copy in copies[7:]:
        copy.wait()
    last = (hours - 1) * scens
    edge_ref[0:scens, :] = jnp.where(early, demand_ref[last:, :], demand_ref[0:scens, :])
    edge_ref[scens : 2 * scens, :] = jnp.where(early, hedge_ref[last:, :], hedge_ref[0:scens, :])
    at = 2 * scens
    edge_ref[at : at + 1, :] = jnp.where(early, start_ref[hours - 1 : hours, :], start_ref[0:1, :])
    edge_ref[at + 1 : at + 2, :] = jnp.where(
        early, start_ref[hours - 2 : hours - 1, :], start_ref[1:2, :]
    )


def first_kernel(
    ptdf_ref,
    own_inject_ref,
    demand_ref,
    hedge_ref,
    start_ref,
    edge_ref,
    cost_ref,
    max_ref,
    limit_ref,
    line_max_ref,
    gen_ref,
    base_ref,
    hedged_ref,
    sums_ref,
    inject_ref,
    over_ref,
    back_ref,
    padded_ref,
    excess_ref,
    ramp_ref,
):
    hours, buses = start_ref.shape
    width = demand_ref.shape[0]
    scens = width // hours
    at = 2 * scens
    early = lax.axis_index("hour") == 0
    first_hour = lax.axis_index("hour") * hours
    beyond = edge_ref[at : at + 1, :]
    limit = limit_ref[...]
    cost = cost_ref[...]
    top = max_ref[...]

    inject_ref[0:width, :] = own_inject_ref[...]
    inject_ref[width : width + scens, :] = (beyond - edge_ref[0:scens, :]).astype(jnp.bfloat16)
    back_ref[...] = line_work(inject_ref, ptdf_ref, line_max_ref, over_ref)
    write_ramp(start_ref, beyond, limit, first_hour, padded_ref, excess_ref, ramp_ref)

    def step(mean, hedge, back, ramp):
        grad = cost + back + (mean - mean + hedge) + ramp
        gen = jnp.clip(mean - STEP_SIZE * grad, 0.0, top)
        return gen, gen + hedge

    for h in range(hours):
        part = slice(h * scens, (h + 1) * scens)
        mean = start_ref[h : h + 1, :]
        gen, hedged = step(mean, hedge_ref[part, :], back_ref[part, :], ramp_ref[h : h + 1, :])
        gen_ref[part, :] = gen
        base_ref[part, :] = gen - demand_ref[part, :]
        hedged_ref[part, :] = hedged
        sums_ref[h : h + 1, :] = jnp.sum(hedged, axis=0, keepdims=True)
    near = jnp.where(early, start_ref[hours - 1 : hours, :], start_ref[0:1, :])
    ramp = excess(beyond - near, limit) + excess(beyond - edge_ref[at + 1 : at + 2, :], limit)
    _, hedged = step(beyond, edge_ref[scens:at, :], back_ref[width : width + scens, :], ramp)
    sums_ref[hours : hours + 1, :] = jnp.sum(hedged, axis=0, keepdims=True)
    spare = sums_ref.shape[0] - hours - 1
    sums_ref[hours + 1 :, :] = jnp.zeros((spare, buses), jnp.float32)


def second_kernel(
    blocks,
    terms,
    scen_total,
    ptdf_ref,
    base_ref,
    gen_ref,
    hedged_ref,
    spread_ref,
    rows_ref,
    weight_ref,
    *refs,
):
    (cost_ref, max_ref, limit_ref, line_max_ref), refs = refs[:4], refs[4:]
    own_refs, refs = refs[:blocks], refs[blocks:]
    peer_refs, refs = refs[:blocks], refs[blocks:]
    sum_refs, refs = refs[:terms], refs[terms:]
    next_refs, refs = refs[:blocks], refs[blocks:]
    (hedged_out_ref, sums_out_ref, mine_ref, theirs_ref) = refs[:4]
    (inject_ref, over_ref, back_ref, mean_ref, padded_ref, excess_ref, ramp_ref) = refs[4:]
    hours, buses = sums_out_ref.shape
    width = base_ref.shape[0]
    scens = width // hours
    first_hour = lax.axis_index("hour") * hours

    weight = weight_ref[:, 0:1]
    own = jnp.concatenate([ref[...] for ref in own_refs], axis=0)
    peer = jnp.concatenate([ref[...] for ref in peer_refs], axis=0)
    est_mine = weight * own
    est_theirs = -weight * peer
    flow = (est_mine + est_theirs) * 0.5
    dual_mine = est_mine - flow
    dual_theirs = est_theirs - flow
    spread = spread_ref[...]
    add = lax.dot_general(
        split_3(flow),
        jnp.concatenate([spread, spread, spread], axis=0),
        CONTRACT_FIRST,
        preferred_element_type=jnp.float32,
    )
    inject_ref[...] = (base_ref[...] + add).astype(jnp.bfloat16)

    own_next = lax.dot_general(
        rows_ref[...], inject_ref[...], CONTRACT_LAST, preferred_element_type=jnp.float32
    )
    for i in range(blocks):
        next_refs[i][...] = own_next[i * CAP : (i + 1) * CAP, :]
    mine_ref[...] = weight * (own_next - peer) + dual_mine
    theirs_ref[...] = weight * own + dual_theirs

    back_ref[...] = line_work(inject_ref, ptdf_ref, line_max_ref, over_ref)

    mean_ref[...] = functools.reduce(jnp.add, [ref[...] for ref in sum_refs]) / scen_total
    write_ramp(
        mean_ref, mean_ref[hours : hours + 1, :], limit_ref[...], first_hour, padded_ref, excess_ref, ramp_ref
    )
    cost = cost_ref[...]
    top = max_ref[...]
    for h in range(hours):
        part = slice(h * scens, (h + 1) * scens)
        mean = mean_ref[h : h + 1, :]
        gen = gen_ref[part, :]
        hedge = hedged_ref[part, :] - mean
        grad = cost + back_ref[part, :] + (gen - mean + hedge) + ramp_ref[h : h + 1, :]
        gen = jnp.clip(gen - STEP_SIZE * grad, 0.0, top)
        hedged = gen + hedge
        hedged_out_ref[part, :] = hedged
        sums_out_ref[h : h + 1, :] = jnp.sum(hedged, axis=0, keepdims=True)


def last_kernel(blocks, terms, partner_of, scen_total, hedged_ref, *refs):
    sum_refs, refs = refs[:terms], refs[terms:]
    peer_refs, refs = refs[:blocks], refs[blocks:]
    weight_ref, mine_ref, theirs_ref, mean_ref, hedge_ref, tie_ref = refs
    hours = mean_ref.shape[0]
    scens = hedged_ref.shape[0] // hours
    here = lax.axis_index("area")
    slots = tie_ref.shape[1]
    places = []
    for i in range(blocks):
        low, _, block, in_reach = block_facts(here, partner_of(here, i))
        first = block * CAP + jnp.where(low, 0, REACH * CAP)
        hit = lax.broadcasted_iota(jnp.int32, (CAP, slots), 1) == (
            first + lax.broadcasted_iota(jnp.int32, (CAP, slots), 0)
        )
        places.append(jnp.where(hit & in_reach, 1.0, 0.0).astype(jnp.bfloat16))
    peer = jnp.concatenate([ref[...] for ref in peer_refs], axis=0)
    flow = (mine_ref[...] + (theirs_ref[...] - weight_ref[:, 0:1] * peer)) * 0.5
    tie_ref[...] = lax.dot_general(
        split_3(flow),
        jnp.concatenate(places * 3, axis=0),
        CONTRACT_FIRST,
        preferred_element_type=jnp.float32,
    )
    mean_ref[...] = functools.reduce(jnp.add, [ref[...] for ref in sum_refs]) / scen_total
    for h in range(hours):
        part = slice(h * scens, (h + 1) * scens)
        hedge_ref[part, :] = hedged_ref[part, :] - mean_ref[h : h + 1, :]


def call(kernel, name, args, outs, scratch, flops, in_place=()):
    size = sum(x.size * x.dtype.itemsize for x in list(args) + list(outs))
    return pl.pallas_call(
        kernel,
        name=name,
        out_shape=outs,
        in_specs=[ANY if i in in_place else VMEM for i in range(len(args))],
        out_specs=[VMEM] * len(outs),
        scratch_shapes=scratch,
        compiler_params=pltpu.CompilerParams(vmem_limit_bytes=32 * 1024 * 1024),
        cost_estimate=pl.CostEstimate(flops=flops, bytes_accessed=size, transcendentals=0),
    )(*(pltpu.with_memory_space_constraint(x, pltpu.HBM) if i in in_place else x for i, x in enumerate(args)))


def per_device(
    ptdf,
    angle_sens,
    demand,
    gen_start,
    hedge_dual,
    gen_cost,
    gen_max,
    gen_ramp,
    line_max,
    tie_count,
    tie_low_bus,
    tie_high_bus,
    tie_susc,
):
    hours, scens, buses = demand.shape
    lines = ptdf.shape[0]
    width = hours * scens
    areas = lax.axis_size("area")
    n_scen = lax.axis_size("scen")
    assert lax.axis_size("hour") == 2 and hours >= 2
    scen_total = scens * n_scen
    blocks, partner_of, from_partners = partner_plan(areas)
    slots = blocks * CAP
    sum_rows = 8 * (hours // 8 + 1)
    f32, bf16 = jnp.float32, jnp.bfloat16

    def shape(*dims, dtype=f32):
        return jax.ShapeDtypeStruct(dims, dtype)

    def over_scens(sums):
        if n_scen == 2:
            return [sums, lax.ppermute(sums, "scen", [(0, 1), (1, 0)])]
        return [lax.psum(sums, "scen")]

    work = 4 * width * lines * buses

    def step_scratch(rows):
        return [
            pltpu.VMEM((rows, buses), bf16),
            pltpu.VMEM((rows, lines), bf16),
            pltpu.VMEM((rows, buses), f32),
        ]

    ramp_scratch = [
        pltpu.VMEM((hours + 4, buses), f32),
        pltpu.VMEM((hours + 4, buses), f32),
        pltpu.VMEM((hours, buses), f32),
    ]
    tables = (tie_count, tie_low_bus, tie_high_bus, tie_susc)
    vectors = [x.reshape(1, -1) for x in (gen_cost, gen_max, gen_ramp, line_max)]
    made = call(
        functools.partial(angle_kernel, blocks, partner_of),
        "angles",
        (
            angle_sens,
            demand.reshape(width, buses),
            hedge_dual.reshape(width, buses),
            gen_start,
            *vectors,
            *tables,
            ptdf,
        ),
        [shape(CAP, width)] * blocks
        + [
            shape(2 * scens + 8, buses),
            shape(width, buses, dtype=bf16),
            shape(slots, buses, dtype=bf16),
            shape(slots, buses, dtype=bf16),
            shape(slots, 128),
            shape(width, buses),
            shape(width, buses),
            shape(hours, buses),
            shape(1, buses),
            shape(1, buses),
            shape(1, buses),
            shape(1, lines),
            shape(lines, buses, dtype=bf16),
        ],
        [pltpu.VMEM(x.shape, x.dtype) for x in (angle_sens, *tables)]
        + [pltpu.VMEM((slots, buses), bf16), pltpu.SemaphoreType.DMA((13,))],
        2 * slots * buses * (width + buses),
        range(13),
    )
    own = made[:blocks]
    edge, inject, spread, rows, weight, load, hedge, start = made[blocks : blocks + 8]
    cost, top, limit, line_top, held = made[blocks + 8 :]
    edge = lax.ppermute(edge, "hour", [(0, 1), (1, 0)])
    peer = from_partners(own)
    gen, base, hedged, sums = call(
        first_kernel,
        "first",
        (held, inject, load, hedge, start, edge, cost, top, limit, line_top),
        [
            shape(width, buses),
            shape(width, buses),
            shape(width, buses),
            shape(sum_rows, buses),
        ],
        step_scratch(width + scens) + ramp_scratch,
        work,
    )
    sum_terms = over_scens(sums)
    terms = len(sum_terms)
    second = call(
        functools.partial(second_kernel, blocks, terms, scen_total),
        "second",
        (
            held,
            base,
            gen,
            hedged,
            spread,
            rows,
            weight,
            cost,
            top,
            limit,
            line_top,
            *own,
            *peer,
            *sum_terms,
        ),
        [shape(CAP, width)] * blocks
        + [shape(width, buses), shape(hours, buses), shape(slots, width), shape(slots, width)],
        step_scratch(width) + [pltpu.VMEM((sum_rows, buses), f32)] + ramp_scratch,
        work,
    )
    own = second[:blocks]
    hedged, sums, mine, theirs = second[blocks:]
    peer = from_partners(own)
    sum_terms = over_scens(sums)
    gen_mean, hedge, tie_flow = call(
        functools.partial(last_kernel, blocks, terms, partner_of, scen_total),
        "last",
        (hedged, *sum_terms, *peer, weight, mine, theirs),
        [shape(hours, buses), shape(width, buses), shape(width, 2 * REACH * CAP)],
        [],
        6 * slots * width * 2 * REACH * CAP,
    )
    return (
        gen_mean,
        hedge.reshape(hours, scens, buses),
        tie_flow.reshape(hours, scens, 2 * REACH * CAP),
    )


def solution(mesh):
    return jax.shard_map(
        per_device,
        mesh=mesh,
        in_specs=(
            P(("group", "area"), None),
            P(("group", "area"), None),
            P(("group", "hour"), "scen", "area"),
            P(("group", "hour"), "area"),
            P(("group", "hour"), "scen", "area"),
            P(("group", "area")),
            P(("group", "area")),
            P(("group", "area")),
            P(("group", "area")),
            P("group", None),
            P("group", None),
            P("group", None),
            P("group", None),
        ),
        out_specs=(
            P(("group", "hour"), "area"),
            P(("group", "hour"), "scen", "area"),
            P(("group", "hour"), "scen", "area"),
        ),
        check_vma=False,
    )
```

```python
import functools

import jax
import jax.numpy as jnp
from jax import lax
from jax.experimental import pallas as pl
from jax.experimental.pallas import tpu as pltpu
from jax.sharding import PartitionSpec as P

HOURS = 24
REACH = 4
CAP = 16

STEP_SIZE = 0.5
LINE_CHUNK = 512

CONTRACT_LAST = (((1,), (1,)), ((), ()))
CONTRACT_FIRST = (((0,), (0,)), ((), ()))
VMEM = pl.BlockSpec(memory_space=pltpu.VMEM)
ANY = pl.BlockSpec(memory_space=pltpu.HBM)


def partner_plan(areas):
    if areas & (areas - 1) == 0 and areas <= REACH + 1:
        blocks = areas - 1

        def gather(rows):
            return [lax.all_gather(rows, "area", axis=0, tiled=True)]

        def peer_rows(refs, here):
            first = [(here ^ (i + 1)) * (blocks * CAP) + i * CAP for i in range(blocks)]
            return jnp.concatenate([refs[0][pl.ds(pl.multiple_of(at, CAP), CAP), :] for at in first], axis=0)

        return blocks, 1, lambda here, i: here ^ (i + 1), gather, peer_rows
    reach = min(REACH, areas - 1)
    shifts = sorted({s % areas for d in range(1, reach + 1) for s in (d, -d)})
    blocks = len(shifts)

    def by_shift(rows):
        sent = [
            lax.ppermute(rows[i * CAP : (i + 1) * CAP], "area", [(a, (a + s) % areas) for a in range(areas)])
            for i, s in enumerate(shifts)
        ]
        return [sent[shifts.index(areas - s)] for s in shifts]

    def peer_blocks(refs, here):
        return jnp.concatenate([ref[...] for ref in refs], axis=0)

    return blocks, blocks, lambda here, i: lax.rem(here + shifts[i], areas), by_shift, peer_blocks


def block_facts(here, partner):
    low = partner > here
    distance = jnp.abs(partner - here)
    block = jnp.clip(distance - 1, 0, REACH - 1)
    in_reach = (distance >= 1) & (distance <= REACH)
    return low, jnp.minimum(here, partner), block, in_reach


def split_3(x):
    high = x.astype(jnp.bfloat16)
    rest = x - high.astype(jnp.float32)
    middle = rest.astype(jnp.bfloat16)
    rest = rest - middle.astype(jnp.float32)
    return jnp.concatenate([high, middle, rest.astype(jnp.bfloat16)], axis=0)


def excess(diffs, limit):
    return diffs - jnp.clip(diffs, -limit, limit)


def write_ramp(mean_ref, beyond, limit, first_hour, padded_ref, excess_ref, ramp_ref):
    hours = ramp_ref.shape[0]
    padded_ref[0:1, :] = beyond
    padded_ref[1 : hours + 1, :] = mean_ref[0:hours, :]
    padded_ref[hours + 1 : hours + 2, :] = beyond
    diffs = padded_ref[1 : hours + 2, :] - padded_ref[0 : hours + 1, :]
    ids = first_hour + lax.broadcasted_iota(jnp.int32, diffs.shape, 0)
    valid = (ids >= 1) & (ids <= HOURS - 1)
    excess_ref[0 : hours + 1, :] = jnp.where(valid, excess(diffs, limit), 0.0)
    ramp_ref[...] = excess_ref[0:hours, :] - excess_ref[1 : hours + 1, :]


def line_work(inject_ref, ptdf_ref, line_max_ref, over_ref):
    inject = inject_ref[...]
    lines = ptdf_ref.shape[0]
    for at in range(0, lines, LINE_CHUNK):
        part = slice(at, at + LINE_CHUNK)
        flows = lax.dot_general(
            inject, ptdf_ref[part, :], CONTRACT_LAST, preferred_element_type=jnp.float32
        )
        limit = line_max_ref[:, part]
        over_ref[:, part] = (flows - jnp.clip(flows, -limit, limit)).astype(jnp.bfloat16)
    return jnp.dot(over_ref[...], ptdf_ref[...], preferred_element_type=jnp.float32)


def angle_kernel(
    blocks,
    partner_of,
    sens_in,
    demand_in,
    hedge_in,
    start_in,
    cost_in,
    max_in,
    limit_in,
    line_max_in,
    count_in,
    low_bus_in,
    high_bus_in,
    susc_in,
    ptdf_in,
    *refs,
):
    (
        own_ref,
        edge_ref,
        inject_ref,
        spread_ref,
        rows_ref,
        weight_ref,
        demand_ref,
        hedge_ref,
        start_ref,
        cost_ref,
        max_ref,
        limit_ref,
        line_max_ref,
        ptdf_ref,
        sens_ref,
        count_ref,
        low_bus_ref,
        high_bus_ref,
        susc_ref,
        onehot_ref,
        copy_sems,
    ) = refs
    hours, buses = start_ref.shape
    scens = demand_ref.shape[0] // hours
    here = lax.axis_index("area")
    early = lax.axis_index("hour") == 0

    pairs = (
        (count_in, count_ref),
        (low_bus_in, low_bus_ref),
        (high_bus_in, high_bus_ref),
        (susc_in, susc_ref),
        (start_in, start_ref),
        (demand_in, demand_ref),
        (sens_in, sens_ref),
        (hedge_in, hedge_ref),
        (cost_in, cost_ref),
        (max_in, max_ref),
        (limit_in, limit_ref),
        (line_max_in, line_max_ref),
        (ptdf_in, ptdf_ref),
    )
    copies = [pltpu.make_async_copy(src, dst, copy_sems.at[i]) for i, (src, dst) in enumerate(pairs)]
    for copy in copies:
        copy.start()

    for copy in copies[:4]:
        copy.wait()
    for i in range(blocks):
        partner = partner_of(here, i)
        low, row, block, in_reach = block_facts(here, partner)
        slots = slice(i * CAP, (i + 1) * CAP)
        pick = lax.broadcasted_iota(jnp.int32, (CAP, REACH * CAP), 1) == (
            block * CAP + lax.broadcasted_iota(jnp.int32, (CAP, REACH * CAP), 0)
        )
        table_row = pl.ds(row, 1)
        bus_row = jnp.where(low, low_bus_ref[table_row, :], high_bus_ref[table_row, :])
        bus = jnp.sum(jnp.where(pick, bus_row.astype(jnp.float32), 0.0), axis=1, keepdims=True)
        susc = jnp.sum(jnp.where(pick, susc_ref[table_row, :], 0.0), axis=1, keepdims=True)
        count_row = count_ref[table_row, :].astype(jnp.float32)
        is_block = lax.broadcasted_iota(jnp.int32, (CAP, REACH), 1) == block
        count = jnp.sum(jnp.where(is_block, count_row, 0.0), axis=1, keepdims=True)
        slot_ids = lax.broadcasted_iota(jnp.int32, (CAP, 1), 0).astype(jnp.float32)
        live = jnp.where((slot_ids < count) & in_reach, 1.0, 0.0)
        sign = jnp.where(low, 1.0, -1.0)
        bus_ids = lax.broadcasted_iota(jnp.int32, (CAP, buses), 1).astype(jnp.float32)
        onehot = jnp.where(bus_ids == bus, live, 0.0)
        onehot_ref[slots, :] = onehot.astype(jnp.bfloat16)
        spread_ref[slots, :] = (-sign * onehot).astype(jnp.bfloat16)
        weight_ref[slots, :] = jnp.broadcast_to(live * sign * susc, (CAP, 128))

    for copy in copies[4:7]:
        copy.wait()
    for h in range(hours):
        part = slice(h * scens, (h + 1) * scens)
        inject_ref[part, :] = (start_ref[h : h + 1, :] - demand_ref[part, :]).astype(jnp.bfloat16)
    rows = jnp.dot(onehot_ref[...], sens_ref[...], preferred_element_type=jnp.float32)
    rows_ref[...] = rows.astype(jnp.bfloat16)
    own_ref[...] = lax.dot_general(
        rows_ref[...], inject_ref[...], CONTRACT_LAST, preferred_element_type=jnp.float32
    )

    for copy in copies[7:]:
        copy.wait()
    last = (hours - 1) * scens
    edge_ref[0:scens, :] = jnp.where(early, demand_ref[last:, :], demand_ref[0:scens, :])
    edge_ref[scens : 2 * scens, :] = jnp.where(early, hedge_ref[last:, :], hedge_ref[0:scens, :])
    at = 2 * scens
    edge_ref[at : at + 1, :] = jnp.where(early, start_ref[hours - 1 : hours, :], start_ref[0:1, :])
    edge_ref[at + 1 : at + 2, :] = jnp.where(
        early, start_ref[hours - 2 : hours - 1, :], start_ref[1:2, :]
    )


def first_kernel(
    ptdf_ref,
    own_inject_ref,
    demand_ref,
    hedge_ref,
    start_ref,
    edge_ref,
    cost_ref,
    max_ref,
    limit_ref,
    line_max_ref,
    gen_ref,
    base_ref,
    hedged_ref,
    sums_ref,
    inject_ref,
    over_ref,
    back_ref,
    padded_ref,
    excess_ref,
    ramp_ref,
):
    hours, buses = start_ref.shape
    width = demand_ref.shape[0]
    scens = width // hours
    at = 2 * scens
    early = lax.axis_index("hour") == 0
    first_hour = lax.axis_index("hour") * hours
    beyond = edge_ref[at : at + 1, :]
    limit = limit_ref[...]
    cost = cost_ref[...]
    top = max_ref[...]

    inject_ref[0:width, :] = own_inject_ref[...]
    inject_ref[width : width + scens, :] = (beyond - edge_ref[0:scens, :]).astype(jnp.bfloat16)
    back_ref[...] = line_work(inject_ref, ptdf_ref, line_max_ref, over_ref)
    write_ramp(start_ref, beyond, limit, first_hour, padded_ref, excess_ref, ramp_ref)

    def step(mean, hedge, back, ramp):
        grad = cost + back + (mean - mean + hedge) + ramp
        gen = jnp.clip(mean - STEP_SIZE * grad, 0.0, top)
        return gen, gen + hedge

    for h in range(hours):
        part = slice(h * scens, (h + 1) * scens)
        mean = start_ref[h : h + 1, :]
        gen, hedged = step(mean, hedge_ref[part, :], back_ref[part, :], ramp_ref[h : h + 1, :])
        gen_ref[part, :] = gen
        base_ref[part, :] = gen - demand_ref[part, :]
        hedged_ref[part, :] = hedged
        sums_ref[h : h + 1, :] = jnp.sum(hedged, axis=0, keepdims=True)
    near = jnp.where(early, start_ref[hours - 1 : hours, :], start_ref[0:1, :])
    ramp = excess(beyond - near, limit) + excess(beyond - edge_ref[at + 1 : at + 2, :], limit)
    _, hedged = step(beyond, edge_ref[scens:at, :], back_ref[width : width + scens, :], ramp)
    sums_ref[hours : hours + 1, :] = jnp.sum(hedged, axis=0, keepdims=True)
    spare = sums_ref.shape[0] - hours - 1
    sums_ref[hours + 1 :, :] = jnp.zeros((spare, buses), jnp.float32)


def second_kernel(
    peers,
    peer_rows,
    terms,
    scen_total,
    ptdf_ref,
    base_ref,
    gen_ref,
    hedged_ref,
    spread_ref,
    rows_ref,
    weight_ref,
    cost_ref,
    max_ref,
    limit_ref,
    line_max_ref,
    own_ref,
    *refs,
):
    peer_refs, refs = refs[:peers], refs[peers:]
    sum_refs, refs = refs[:terms], refs[terms:]
    (next_ref, hedged_out_ref, sums_out_ref, mine_ref, theirs_ref) = refs[:5]
    (inject_ref, over_ref, back_ref, mean_ref, padded_ref, excess_ref, ramp_ref) = refs[5:]
    hours, buses = sums_out_ref.shape
    width = base_ref.shape[0]
    scens = width // hours
    first_hour = lax.axis_index("hour") * hours

    weight = weight_ref[:, 0:1]
    own = own_ref[...]
    peer = peer_rows(peer_refs, lax.axis_index("area"))
    est_mine = weight * own
    est_theirs = -weight * peer
    flow = (est_mine + est_theirs) * 0.5
    dual_mine = est_mine - flow
    dual_theirs = est_theirs - flow
    spread = spread_ref[...]
    add = lax.dot_general(
        split_3(flow),
        jnp.concatenate([spread, spread, spread], axis=0),
        CONTRACT_FIRST,
        preferred_element_type=jnp.float32,
    )
    inject_ref[...] = (base_ref[...] + add).astype(jnp.bfloat16)

    own_next = lax.dot_general(
        rows_ref[...], inject_ref[...], CONTRACT_LAST, preferred_element_type=jnp.float32
    )
    next_ref[...] = own_next
    mine_ref[...] = weight * (own_next - peer) + dual_mine
    theirs_ref[...] = weight * own + dual_theirs

    back_ref[...] = line_work(inject_ref, ptdf_ref, line_max_ref, over_ref)

    mean_ref[...] = functools.reduce(jnp.add, [ref[...] for ref in sum_refs]) / scen_total
    write_ramp(
        mean_ref, mean_ref[hours : hours + 1, :], limit_ref[...], first_hour, padded_ref, excess_ref, ramp_ref
    )
    cost = cost_ref[...]
    top = max_ref[...]
    for h in range(hours):
        part = slice(h * scens, (h + 1) * scens)
        mean = mean_ref[h : h + 1, :]
        gen = gen_ref[part, :]
        hedge = hedged_ref[part, :] - mean
        grad = cost + back_ref[part, :] + (gen - mean + hedge) + ramp_ref[h : h + 1, :]
        gen = jnp.clip(gen - STEP_SIZE * grad, 0.0, top)
        hedged = gen + hedge
        hedged_out_ref[part, :] = hedged
        sums_out_ref[h : h + 1, :] = jnp.sum(hedged, axis=0, keepdims=True)


def last_kernel(blocks, peers, peer_rows, terms, partner_of, scen_total, hedged_ref, *refs):
    sum_refs, refs = refs[:terms], refs[terms:]
    peer_refs, refs = refs[:peers], refs[peers:]
    weight_ref, mine_ref, theirs_ref, mean_ref, hedge_ref, tie_ref = refs
    hours = mean_ref.shape[0]
    scens = hedged_ref.shape[0] // hours
    here = lax.axis_index("area")
    slots = tie_ref.shape[1]
    places = []
    for i in range(blocks):
        low, _, block, in_reach = block_facts(here, partner_of(here, i))
        first = block * CAP + jnp.where(low, 0, REACH * CAP)
        hit = lax.broadcasted_iota(jnp.int32, (CAP, slots), 1) == (
            first + lax.broadcasted_iota(jnp.int32, (CAP, slots), 0)
        )
        places.append(jnp.where(hit & in_reach, 1.0, 0.0).astype(jnp.bfloat16))
    peer = peer_rows(peer_refs, here)
    flow = (mine_ref[...] + (theirs_ref[...] - weight_ref[:, 0:1] * peer)) * 0.5
    tie_ref[...] = lax.dot_general(
        split_3(flow),
        jnp.concatenate(places * 3, axis=0),
        CONTRACT_FIRST,
        preferred_element_type=jnp.float32,
    )
    mean_ref[...] = functools.reduce(jnp.add, [ref[...] for ref in sum_refs]) / scen_total
    for h in range(hours):
        part = slice(h * scens, (h + 1) * scens)
        hedge_ref[part, :] = hedged_ref[part, :] - mean_ref[h : h + 1, :]


def call(kernel, name, args, outs, scratch, flops, in_place=()):
    size = sum(x.size * x.dtype.itemsize for x in list(args) + list(outs))
    return pl.pallas_call(
        kernel,
        name=name,
        out_shape=outs,
        in_specs=[ANY if i in in_place else VMEM for i in range(len(args))],
        out_specs=[VMEM] * len(outs),
        scratch_shapes=scratch,
        compiler_params=pltpu.CompilerParams(vmem_limit_bytes=32 * 1024 * 1024),
        cost_estimate=pl.CostEstimate(flops=flops, bytes_accessed=size, transcendentals=0),
    )(*(pltpu.with_memory_space_constraint(x, pltpu.HBM) if i in in_place else x for i, x in enumerate(args)))


def per_device(
    ptdf,
    angle_sens,
    demand,
    gen_start,
    hedge_dual,
    gen_cost,
    gen_max,
    gen_ramp,
    line_max,
    tie_count,
    tie_low_bus,
    tie_high_bus,
    tie_susc,
):
    hours, scens, buses = demand.shape
    lines = ptdf.shape[0]
    width = hours * scens
    areas = lax.axis_size("area")
    n_scen = lax.axis_size("scen")
    assert lax.axis_size("hour") == 2 and hours >= 2
    scen_total = scens * n_scen
    blocks, peers, partner_of, from_partners, peer_rows = partner_plan(areas)
    slots = blocks * CAP
    sum_rows = 8 * (hours // 8 + 1)
    f32, bf16 = jnp.float32, jnp.bfloat16

    def shape(*dims, dtype=f32):
        return jax.ShapeDtypeStruct(dims, dtype)

    def over_scens(sums):
        if n_scen == 2:
            return [sums, lax.ppermute(sums, "scen", [(0, 1), (1, 0)])]
        return [lax.psum(sums, "scen")]

    work = 4 * width * lines * buses

    def step_scratch(rows):
        return [
            pltpu.VMEM((rows, buses), bf16),
            pltpu.VMEM((rows, lines), bf16),
            pltpu.VMEM((rows, buses), f32),
        ]

    ramp_scratch = [
        pltpu.VMEM((hours + 4, buses), f32),
        pltpu.VMEM((hours + 4, buses), f32),
        pltpu.VMEM((hours, buses), f32),
    ]
    tables = (tie_count, tie_low_bus, tie_high_bus, tie_susc)
    vectors = [x.reshape(1, -1) for x in (gen_cost, gen_max, gen_ramp, line_max)]
    made = call(
        functools.partial(angle_kernel, blocks, partner_of),
        "angles",
        (
            angle_sens,
            demand.reshape(width, buses),
            hedge_dual.reshape(width, buses),
            gen_start,
            *vectors,
            *tables,
            ptdf,
        ),
        [
            shape(slots, width),
            shape(2 * scens + 8, buses),
            shape(width, buses, dtype=bf16),
            shape(slots, buses, dtype=bf16),
            shape(slots, buses, dtype=bf16),
            shape(slots, 128),
            shape(width, buses),
            shape(width, buses),
            shape(hours, buses),
            shape(1, buses),
            shape(1, buses),
            shape(1, buses),
            shape(1, lines),
            shape(lines, buses, dtype=bf16),
        ],
        [pltpu.VMEM(x.shape, x.dtype) for x in (angle_sens, *tables)]
        + [pltpu.VMEM((slots, buses), bf16), pltpu.SemaphoreType.DMA((13,))],
        2 * slots * buses * (width + buses),
        range(13),
    )
    own, edge, inject, spread, rows, weight, load, hedge, start = made[:9]
    cost, top, limit, line_top, held = made[9:]
    edge = lax.ppermute(edge, "hour", [(0, 1), (1, 0)])
    peer = from_partners(own)
    gen, base, hedged, sums = call(
        first_kernel,
        "first",
        (held, inject, load, hedge, start, edge, cost, top, limit, line_top),
        [
            shape(width, buses),
            shape(width, buses),
            shape(width, buses),
            shape(sum_rows, buses),
        ],
        step_scratch(width + scens) + ramp_scratch,
        work,
    )
    sum_terms = over_scens(sums)
    terms = len(sum_terms)
    second = call(
        functools.partial(second_kernel, peers, peer_rows, terms, scen_total),
        "second",
        (
            held,
            base,
            gen,
            hedged,
            spread,
            rows,
            weight,
            cost,
            top,
            limit,
            line_top,
            own,
            *peer,
            *sum_terms,
        ),
        [
            shape(slots, width),
            shape(width, buses),
            shape(hours, buses),
            shape(slots, width),
            shape(slots, width),
        ],
        step_scratch(width) + [pltpu.VMEM((sum_rows, buses), f32)] + ramp_scratch,
        work,
    )
    own, hedged, sums, mine, theirs = second
    peer = from_partners(own)
    sum_terms = over_scens(sums)
    gen_mean, hedge, tie_flow = call(
        functools.partial(last_kernel, blocks, peers, peer_rows, terms, partner_of, scen_total),
        "last",
        (hedged, *sum_terms, *peer, weight, mine, theirs),
        [shape(hours, buses), shape(width, buses), shape(width, 2 * REACH * CAP)],
        [],
        6 * slots * width * 2 * REACH * CAP,
    )
    return (
        gen_mean,
        hedge.reshape(hours, scens, buses),
        tie_flow.reshape(hours, scens, 2 * REACH * CAP),
    )


def solution(mesh):
    return jax.shard_map(
        per_device,
        mesh=mesh,
        in_specs=(
            P(("group", "area"), None),
            P(("group", "area"), None),
            P(("group", "hour"), "scen", "area"),
            P(("group", "hour"), "area"),
            P(("group", "hour"), "scen", "area"),
            P(("group", "area")),
            P(("group", "area")),
            P(("group", "area")),
            P(("group", "area")),
            P("group", None),
            P("group", None),
            P("group", None),
            P("group", None),
        ),
        out_specs=(
            P(("group", "hour"), "area"),
            P(("group", "hour"), "scen", "area"),
            P(("group", "hour"), "scen", "area"),
        ),
        check_vma=False,
    )
```

```python
import functools

import jax
import jax.numpy as jnp
from jax import lax
from jax.experimental import pallas as pl
from jax.experimental.pallas import tpu as pltpu
from jax.sharding import PartitionSpec as P

HOURS = 24
REACH = 4
CAP = 16

STEP_SIZE = 0.5
LINE_CHUNK = 512

CONTRACT_LAST = (((1,), (1,)), ((), ()))
CONTRACT_FIRST = (((0,), (0,)), ((), ()))
VMEM = pl.BlockSpec(memory_space=pltpu.VMEM)
ANY = pl.BlockSpec(memory_space=pltpu.HBM)


def partner_plan(areas):
    if areas & (areas - 1) == 0 and areas <= REACH + 1:
        flips = range(1, areas)

        def by_flip(parts):
            sent = {}
            for f in reversed(flips):
                sent[f] = lax.ppermute(parts[f - 1], "area", [(a, a ^ f) for a in range(areas)])
            return [sent[f] for f in flips]

        return len(flips), lambda here, i: here ^ flips[i], by_flip
    reach = min(REACH, areas - 1)
    shifts = sorted({s % areas for d in range(1, reach + 1) for s in (d, -d)})

    def by_shift(parts):
        sent = [
            lax.ppermute(part, "area", [(a, (a + s) % areas) for a in range(areas)])
            for part, s in zip(parts, shifts)
        ]
        return [sent[shifts.index(areas - s)] for s in shifts]

    return len(shifts), lambda here, i: lax.rem(here + shifts[i], areas), by_shift


def block_facts(here, partner):
    low = partner > here
    distance = jnp.abs(partner - here)
    block = jnp.clip(distance - 1, 0, REACH - 1)
    in_reach = (distance >= 1) & (distance <= REACH)
    return low, jnp.minimum(here, partner), block, in_reach


def split_3(x):
    high = x.astype(jnp.bfloat16)
    rest = x - high.astype(jnp.float32)
    middle = rest.astype(jnp.bfloat16)
    rest = rest - middle.astype(jnp.float32)
    return jnp.concatenate([high, middle, rest.astype(jnp.bfloat16)], axis=0)


def excess(diffs, limit):
    return diffs - jnp.clip(diffs, -limit, limit)


def write_ramp(mean_ref, beyond, limit, first_hour, padded_ref, excess_ref, ramp_ref):
    hours = ramp_ref.shape[0]
    padded_ref[0:1, :] = beyond
    padded_ref[1 : hours + 1, :] = mean_ref[0:hours, :]
    padded_ref[hours + 1 : hours + 2, :] = beyond
    diffs = padded_ref[1 : hours + 2, :] - padded_ref[0 : hours + 1, :]
    ids = first_hour + lax.broadcasted_iota(jnp.int32, diffs.shape, 0)
    valid = (ids >= 1) & (ids <= HOURS - 1)
    excess_ref[0 : hours + 1, :] = jnp.where(valid, excess(diffs, limit), 0.0)
    ramp_ref[...] = excess_ref[0:hours, :] - excess_ref[1 : hours + 1, :]


def line_work(inject_ref, ptdf_ref, line_max_ref, over_ref):
    inject = inject_ref[...]
    lines = ptdf_ref.shape[0]
    for at in range(0, lines, LINE_CHUNK):
        part = slice(at, at + LINE_CHUNK)
        flows = lax.dot_general(
            inject, ptdf_ref[part, :], CONTRACT_LAST, preferred_element_type=jnp.float32
        )
        limit = line_max_ref[:, part]
        over_ref[:, part] = (flows - jnp.clip(flows, -limit, limit)).astype(jnp.bfloat16)
    return jnp.dot(over_ref[...], ptdf_ref[...], preferred_element_type=jnp.float32)


def angle_kernel(
    blocks,
    partner_of,
    sens_in,
    demand_in,
    hedge_in,
    start_in,
    cost_in,
    max_in,
    limit_in,
    line_max_in,
    count_in,
    low_bus_in,
    high_bus_in,
    susc_in,
    ptdf_in,
    *refs,
):
    own_refs, refs = refs[:blocks], refs[blocks:]
    (
        edge_ref,
        inject_ref,
        spread_ref,
        rows_ref,
        weight_ref,
        demand_ref,
        hedge_ref,
        start_ref,
        cost_ref,
        max_ref,
        limit_ref,
        line_max_ref,
        ptdf_ref,
        sens_ref,
        count_ref,
        low_bus_ref,
        high_bus_ref,
        susc_ref,
        onehot_ref,
        copy_sems,
    ) = refs
    hours, buses = start_ref.shape
    scens = demand_ref.shape[0] // hours
    here = lax.axis_index("area")
    early = lax.axis_index("hour") == 0

    pairs = (
        (count_in, count_ref),
        (low_bus_in, low_bus_ref),
        (high_bus_in, high_bus_ref),
        (susc_in, susc_ref),
        (start_in, start_ref),
        (demand_in, demand_ref),
        (sens_in, sens_ref),
        (hedge_in, hedge_ref),
        (cost_in, cost_ref),
        (max_in, max_ref),
        (limit_in, limit_ref),
        (line_max_in, line_max_ref),
        (ptdf_in, ptdf_ref),
    )
    copies = [pltpu.make_async_copy(src, dst, copy_sems.at[i]) for i, (src, dst) in enumerate(pairs)]
    for copy in copies:
        copy.start()

    for copy in copies[:4]:
        copy.wait()
    for i in range(blocks):
        partner = partner_of(here, i)
        low, row, block, in_reach = block_facts(here, partner)
        slots = slice(i * CAP, (i + 1) * CAP)
        pick = lax.broadcasted_iota(jnp.int32, (CAP, REACH * CAP), 1) == (
            block * CAP + lax.broadcasted_iota(jnp.int32, (CAP, REACH * CAP), 0)
        )
        table_row = pl.ds(row, 1)
        bus_row = jnp.where(low, low_bus_ref[table_row, :], high_bus_ref[table_row, :])
        bus = jnp.sum(jnp.where(pick, bus_row.astype(jnp.float32), 0.0), axis=1, keepdims=True)
        susc = jnp.sum(jnp.where(pick, susc_ref[table_row, :], 0.0), axis=1, keepdims=True)
        count_row = count_ref[table_row, :].astype(jnp.float32)
        is_block = lax.broadcasted_iota(jnp.int32, (CAP, REACH), 1) == block
        count = jnp.sum(jnp.where(is_block, count_row, 0.0), axis=1, keepdims=True)
        slot_ids = lax.broadcasted_iota(jnp.int32, (CAP, 1), 0).astype(jnp.float32)
        live = jnp.where((slot_ids < count) & in_reach, 1.0, 0.0)
        sign = jnp.where(low, 1.0, -1.0)
        bus_ids = lax.broadcasted_iota(jnp.int32, (CAP, buses), 1).astype(jnp.float32)
        onehot = jnp.where(bus_ids == bus, live, 0.0)
        onehot_ref[slots, :] = onehot.astype(jnp.bfloat16)
        spread_ref[slots, :] = (-sign * onehot).astype(jnp.bfloat16)
        weight_ref[slots, :] = jnp.broadcast_to(live * sign * susc, (CAP, 128))

    for copy in copies[4:7]:
        copy.wait()
    for h in range(hours):
        part = slice(h * scens, (h + 1) * scens)
        inject_ref[part, :] = (start_ref[h : h + 1, :] - demand_ref[part, :]).astype(jnp.bfloat16)
    rows = jnp.dot(onehot_ref[...], sens_ref[...], preferred_element_type=jnp.float32)
    rows_ref[...] = rows.astype(jnp.bfloat16)
    own = lax.dot_general(
        rows_ref[...], inject_ref[...], CONTRACT_LAST, preferred_element_type=jnp.float32
    )
    for i in range(blocks):
        own_refs[i][...] = own[i * CAP : (i + 1) * CAP, :]

    for copy in copies[7:]:
        copy.wait()
    last = (hours - 1) * scens
    edge_ref[0:scens, :] = jnp.where(early, demand_ref[last:, :], demand_ref[0:scens, :])
    edge_ref[scens : 2 * scens, :] = jnp.where(early, hedge_ref[last:, :], hedge_ref[0:scens, :])
    at = 2 * scens
    edge_ref[at : at + 1, :] = jnp.where(early, start_ref[hours - 1 : hours, :], start_ref[0:1, :])
    edge_ref[at + 1 : at + 2, :] = jnp.where(
        early, start_ref[hours - 2 : hours - 1, :], start_ref[1:2, :]
    )


def first_kernel(
    ptdf_ref,
    own_inject_ref,
    demand_ref,
    hedge_ref,
    start_ref,
    edge_ref,
    cost_ref,
    max_ref,
    limit_ref,
    line_max_ref,
    gen_ref,
    base_ref,
    hedged_ref,
    sums_ref,
    inject_ref,
    over_ref,
    back_ref,
    padded_ref,
    excess_ref,
    ramp_ref,
):
    hours, buses = start_ref.shape
    width = demand_ref.shape[0]
    scens = width // hours
    at = 2 * scens
    early = lax.axis_index("hour") == 0
    first_hour = lax.axis_index("hour") * hours
    beyond = edge_ref[at : at + 1, :]
    limit = limit_ref[...]
    cost = cost_ref[...]
    top = max_ref[...]

    inject_ref[0:width, :] = own_inject_ref[...]
    inject_ref[width : width + scens, :] = (beyond - edge_ref[0:scens, :]).astype(jnp.bfloat16)
    back_ref[...] = line_work(inject_ref, ptdf_ref, line_max_ref, over_ref)
    write_ramp(start_ref, beyond, limit, first_hour, padded_ref, excess_ref, ramp_ref)

    def step(mean, hedge, back, ramp):
        grad = cost + back + (mean - mean + hedge) + ramp
        gen = jnp.clip(mean - STEP_SIZE * grad, 0.0, top)
        return gen, gen + hedge

    for h in range(hours):
        part = slice(h * scens, (h + 1) * scens)
        mean = start_ref[h : h + 1, :]
        gen, hedged = step(mean, hedge_ref[part, :], back_ref[part, :], ramp_ref[h : h + 1, :])
        gen_ref[part, :] = gen
        base_ref[part, :] = gen - demand_ref[part, :]
        hedged_ref[part, :] = hedged
        sums_ref[h : h + 1, :] = jnp.sum(hedged, axis=0, keepdims=True)
    near = jnp.where(early, start_ref[hours - 1 : hours, :], start_ref[0:1, :])
    ramp = excess(beyond - near, limit) + excess(beyond - edge_ref[at + 1 : at + 2, :], limit)
    _, hedged = step(beyond, edge_ref[scens:at, :], back_ref[width : width + scens, :], ramp)
    sums_ref[hours : hours + 1, :] = jnp.sum(hedged, axis=0, keepdims=True)
    spare = sums_ref.shape[0] - hours - 1
    sums_ref[hours + 1 :, :] = jnp.zeros((spare, buses), jnp.float32)


def tie_kernel(blocks, base_ref, spread_ref, rows_ref, weight_ref, *refs):
    own_refs, refs = refs[:blocks], refs[blocks:]
    peer_refs, refs = refs[:blocks], refs[blocks:]
    next_refs, (inject_ref, mine_ref, theirs_ref) = refs[:blocks], refs[blocks:]

    weight = weight_ref[:, 0:1]
    own = jnp.concatenate([ref[...] for ref in own_refs], axis=0)
    peer = jnp.concatenate([ref[...] for ref in peer_refs], axis=0)
    est_mine = weight * own
    est_theirs = -weight * peer
    flow = (est_mine + est_theirs) * 0.5
    dual_mine = est_mine - flow
    dual_theirs = est_theirs - flow
    spread = spread_ref[...]
    add = lax.dot_general(
        split_3(flow),
        jnp.concatenate([spread, spread, spread], axis=0),
        CONTRACT_FIRST,
        preferred_element_type=jnp.float32,
    )
    inject_ref[...] = (base_ref[...] + add).astype(jnp.bfloat16)

    own_next = lax.dot_general(
        rows_ref[...], inject_ref[...], CONTRACT_LAST, preferred_element_type=jnp.float32
    )
    for i in range(blocks):
        next_refs[i][...] = own_next[i * CAP : (i + 1) * CAP, :]
    mine_ref[...] = weight * (own_next - peer) + dual_mine
    theirs_ref[...] = weight * own + dual_theirs


def second_kernel(
    terms,
    scen_total,
    ptdf_ref,
    inject_ref,
    gen_ref,
    hedged_ref,
    cost_ref,
    max_ref,
    limit_ref,
    line_max_ref,
    *refs,
):
    sum_refs, refs = refs[:terms], refs[terms:]
    (hedged_out_ref, sums_out_ref, over_ref, back_ref, mean_ref, padded_ref, excess_ref, ramp_ref) = refs
    hours, buses = sums_out_ref.shape
    width = inject_ref.shape[0]
    scens = width // hours
    first_hour = lax.axis_index("hour") * hours

    back_ref[...] = line_work(inject_ref, ptdf_ref, line_max_ref, over_ref)
    mean_ref[...] = functools.reduce(jnp.add, [ref[...] for ref in sum_refs]) / scen_total
    write_ramp(
        mean_ref, mean_ref[hours : hours + 1, :], limit_ref[...], first_hour, padded_ref, excess_ref, ramp_ref
    )
    cost = cost_ref[...]
    top = max_ref[...]
    for h in range(hours):
        part = slice(h * scens, (h + 1) * scens)
        mean = mean_ref[h : h + 1, :]
        gen = gen_ref[part, :]
        hedge = hedged_ref[part, :] - mean
        grad = cost + back_ref[part, :] + (gen - mean + hedge) + ramp_ref[h : h + 1, :]
        gen = jnp.clip(gen - STEP_SIZE * grad, 0.0, top)
        hedged = gen + hedge
        hedged_out_ref[part, :] = hedged
        sums_out_ref[h : h + 1, :] = jnp.sum(hedged, axis=0, keepdims=True)


def flow_kernel(blocks, partner_of, *refs):
    peer_refs, (weight_ref, mine_ref, theirs_ref, tie_ref) = refs[:blocks], refs[blocks:]
    here = lax.axis_index("area")
    slots = tie_ref.shape[1]
    places = []
    for i in range(blocks):
        low, _, block, in_reach = block_facts(here, partner_of(here, i))
        first = block * CAP + jnp.where(low, 0, REACH * CAP)
        hit = lax.broadcasted_iota(jnp.int32, (CAP, slots), 1) == (
            first + lax.broadcasted_iota(jnp.int32, (CAP, slots), 0)
        )
        places.append(jnp.where(hit & in_reach, 1.0, 0.0).astype(jnp.bfloat16))
    peer = jnp.concatenate([ref[...] for ref in peer_refs], axis=0)
    flow = (mine_ref[...] + (theirs_ref[...] - weight_ref[:, 0:1] * peer)) * 0.5
    tie_ref[...] = lax.dot_general(
        split_3(flow),
        jnp.concatenate(places * 3, axis=0),
        CONTRACT_FIRST,
        preferred_element_type=jnp.float32,
    )


def agree_kernel(scen_total, hedged_ref, *refs):
    sum_refs, (mean_ref, hedge_ref) = refs[:-2], refs[-2:]
    hours = mean_ref.shape[0]
    scens = hedged_ref.shape[0] // hours
    mean_ref[...] = functools.reduce(jnp.add, [ref[...] for ref in sum_refs]) / scen_total
    for h in range(hours):
        part = slice(h * scens, (h + 1) * scens)
        hedge_ref[part, :] = hedged_ref[part, :] - mean_ref[h : h + 1, :]


def call(kernel, name, args, outs, scratch, flops, in_place=()):
    size = sum(x.size * x.dtype.itemsize for x in list(args) + list(outs))
    return pl.pallas_call(
        kernel,
        name=name,
        out_shape=outs,
        in_specs=[ANY if i in in_place else VMEM for i in range(len(args))],
        out_specs=[VMEM] * len(outs),
        scratch_shapes=scratch,
        compiler_params=pltpu.CompilerParams(vmem_limit_bytes=32 * 1024 * 1024),
        cost_estimate=pl.CostEstimate(flops=flops, bytes_accessed=size, transcendentals=0),
    )(*(pltpu.with_memory_space_constraint(x, pltpu.HBM) if i in in_place else x for i, x in enumerate(args)))


def per_device(
    ptdf,
    angle_sens,
    demand,
    gen_start,
    hedge_dual,
    gen_cost,
    gen_max,
    gen_ramp,
    line_max,
    tie_count,
    tie_low_bus,
    tie_high_bus,
    tie_susc,
):
    hours, scens, buses = demand.shape
    lines = ptdf.shape[0]
    width = hours * scens
    areas = lax.axis_size("area")
    n_scen = lax.axis_size("scen")
    assert lax.axis_size("hour") == 2 and hours >= 2
    scen_total = scens * n_scen
    blocks, partner_of, from_partners = partner_plan(areas)
    slots = blocks * CAP
    sum_rows = 8 * (hours // 8 + 1)
    f32, bf16 = jnp.float32, jnp.bfloat16

    def shape(*dims, dtype=f32):
        return jax.ShapeDtypeStruct(dims, dtype)

    def over_scens(sums):
        if n_scen == 2:
            return [sums, lax.ppermute(sums, "scen", [(0, 1), (1, 0)])]
        return [lax.psum(sums, "scen")]

    work = 4 * width * lines * buses

    def step_scratch(rows):
        return [
            pltpu.VMEM((rows, buses), bf16),
            pltpu.VMEM((rows, lines), bf16),
            pltpu.VMEM((rows, buses), f32),
        ]

    ramp_scratch = [
        pltpu.VMEM((hours + 4, buses), f32),
        pltpu.VMEM((hours + 4, buses), f32),
        pltpu.VMEM((hours, buses), f32),
    ]
    tables = (tie_count, tie_low_bus, tie_high_bus, tie_susc)
    vectors = [x.reshape(1, -1) for x in (gen_cost, gen_max, gen_ramp, line_max)]
    made = call(
        functools.partial(angle_kernel, blocks, partner_of),
        "angles",
        (
            angle_sens,
            demand.reshape(width, buses),
            hedge_dual.reshape(width, buses),
            gen_start,
            *vectors,
            *tables,
            ptdf,
        ),
        [shape(CAP, width)] * blocks
        + [
            shape(2 * scens + 8, buses),
            shape(width, buses, dtype=bf16),
            shape(slots, buses, dtype=bf16),
            shape(slots, buses, dtype=bf16),
            shape(slots, 128),
            shape(width, buses),
            shape(width, buses),
            shape(hours, buses),
            shape(1, buses),
            shape(1, buses),
            shape(1, buses),
            shape(1, lines),
            shape(lines, buses, dtype=bf16),
        ],
        [pltpu.VMEM(x.shape, x.dtype) for x in (angle_sens, *tables)]
        + [pltpu.VMEM((slots, buses), bf16), pltpu.SemaphoreType.DMA((13,))],
        2 * slots * buses * (width + buses),
        range(13),
    )
    own = made[:blocks]
    edge, inject, spread, rows, weight, load, hedge, start = made[blocks : blocks + 8]
    cost, top, limit, line_top, held = made[blocks + 8 :]
    edge = lax.ppermute(edge, "hour", [(0, 1), (1, 0)])
    peer = from_partners(own)
    gen, base, hedged, sums = call(
        first_kernel,
        "first",
        (held, inject, load, hedge, start, edge, cost, top, limit, line_top),
        [
            shape(width, buses),
            shape(width, buses),
            shape(width, buses),
            shape(sum_rows, buses),
        ],
        step_scratch(width + scens) + ramp_scratch,
        work,
    )
    sums, peer = lax.optimization_barrier((sums, peer))
    sum_terms = over_scens(sums)
    terms = len(sum_terms)
    tied = call(
        functools.partial(tie_kernel, blocks),
        "ties",
        (base, spread, rows, weight, *own, *peer),
        [shape(CAP, width)] * blocks
        + [shape(width, buses, dtype=bf16), shape(slots, width), shape(slots, width)],
        [],
        2 * slots * buses * 4 * width,
    )
    own = tied[:blocks]
    inject, mine, theirs = tied[blocks:]
    hedged, sums = call(
        functools.partial(second_kernel, terms, scen_total),
        "second",
        (held, inject, gen, hedged, cost, top, limit, line_top, *sum_terms),
        [shape(width, buses), shape(hours, buses)],
        step_scratch(width)[1:] + [pltpu.VMEM((sum_rows, buses), f32)] + ramp_scratch,
        work,
    )
    peer = from_partners(own)
    sums, peer = lax.optimization_barrier((sums, peer))
    sum_terms = over_scens(sums)
    (tie_flow,) = call(
        functools.partial(flow_kernel, blocks, partner_of),
        "flows",
        (*peer, weight, mine, theirs),
        [shape(width, 2 * REACH * CAP)],
        [],
        6 * slots * width * 2 * REACH * CAP,
    )
    sum_terms, tie_flow = lax.optimization_barrier((sum_terms, tie_flow))
    gen_mean, hedge = call(
        functools.partial(agree_kernel, scen_total),
        "agree",
        (hedged, *sum_terms),
        [shape(hours, buses), shape(width, buses)],
        [],
        2 * width * buses,
    )
    return (
        gen_mean,
        hedge.reshape(hours, scens, buses),
        tie_flow.reshape(hours, scens, 2 * REACH * CAP),
    )


def solution(mesh):
    return jax.shard_map(
        per_device,
        mesh=mesh,
        in_specs=(
            P(("group", "area"), None),
            P(("group", "area"), None),
            P(("group", "hour"), "scen", "area"),
            P(("group", "hour"), "area"),
            P(("group", "hour"), "scen", "area"),
            P(("group", "area")),
            P(("group", "area")),
            P(("group", "area")),
            P(("group", "area")),
            P("group", None),
            P("group", None),
            P("group", None),
            P("group", None),
        ),
        out_specs=(
            P(("group", "hour"), "area"),
            P(("group", "hour"), "scen", "area"),
            P(("group", "hour"), "scen", "area"),
        ),
        check_vma=False,
    )
```

```python
import functools

import jax
import jax.numpy as jnp
from jax import lax
from jax.experimental import pallas as pl
from jax.experimental.pallas import tpu as pltpu
from jax.sharding import PartitionSpec as P

HOURS = 24
REACH = 4
CAP = 16

STEP_SIZE = 0.5
LINE_CHUNK = 512
BETWEEN = 20_000_000_000

CONTRACT_LAST = (((1,), (1,)), ((), ()))
CONTRACT_FIRST = (((0,), (0,)), ((), ()))
VMEM = pl.BlockSpec(memory_space=pltpu.VMEM)
ANY = pl.BlockSpec(memory_space=pltpu.HBM)


def partner_plan(areas):
    if areas & (areas - 1) == 0 and areas <= REACH + 1:
        flips = range(1, areas)

        def by_flip(parts):
            sent = {}
            for f in reversed(flips):
                sent[f] = lax.ppermute(parts[f - 1], "area", [(a, a ^ f) for a in range(areas)])
            return [sent[f] for f in flips]

        return len(flips), lambda here, i: here ^ flips[i], by_flip
    reach = min(REACH, areas - 1)
    shifts = sorted({s % areas for d in range(1, reach + 1) for s in (d, -d)})

    def by_shift(parts):
        sent = [
            lax.ppermute(part, "area", [(a, (a + s) % areas) for a in range(areas)])
            for part, s in zip(parts, shifts)
        ]
        return [sent[shifts.index(areas - s)] for s in shifts]

    return len(shifts), lambda here, i: lax.rem(here + shifts[i], areas), by_shift


def block_facts(here, partner):
    low = partner > here
    distance = jnp.abs(partner - here)
    block = jnp.clip(distance - 1, 0, REACH - 1)
    in_reach = (distance >= 1) & (distance <= REACH)
    return low, jnp.minimum(here, partner), block, in_reach


def split_3(x):
    high = x.astype(jnp.bfloat16)
    rest = x - high.astype(jnp.float32)
    middle = rest.astype(jnp.bfloat16)
    rest = rest - middle.astype(jnp.float32)
    return jnp.concatenate([high, middle, rest.astype(jnp.bfloat16)], axis=0)


def excess(diffs, limit):
    return diffs - jnp.clip(diffs, -limit, limit)


def write_ramp(mean_ref, beyond, limit, first_hour, padded_ref, excess_ref, ramp_ref):
    hours = ramp_ref.shape[0]
    padded_ref[0:1, :] = beyond
    padded_ref[1 : hours + 1, :] = mean_ref[0:hours, :]
    padded_ref[hours + 1 : hours + 2, :] = beyond
    diffs = padded_ref[1 : hours + 2, :] - padded_ref[0 : hours + 1, :]
    ids = first_hour + lax.broadcasted_iota(jnp.int32, diffs.shape, 0)
    valid = (ids >= 1) & (ids <= HOURS - 1)
    excess_ref[0 : hours + 1, :] = jnp.where(valid, excess(diffs, limit), 0.0)
    ramp_ref[...] = excess_ref[0:hours, :] - excess_ref[1 : hours + 1, :]


def line_work(inject_ref, ptdf_ref, line_max_ref, over_ref):
    inject = inject_ref[...]
    lines = ptdf_ref.shape[0]
    for at in range(0, lines, LINE_CHUNK):
        part = slice(at, at + LINE_CHUNK)
        flows = lax.dot_general(
            inject, ptdf_ref[part, :], CONTRACT_LAST, preferred_element_type=jnp.float32
        )
        limit = line_max_ref[:, part]
        over_ref[:, part] = (flows - jnp.clip(flows, -limit, limit)).astype(jnp.bfloat16)
    return jnp.dot(over_ref[...], ptdf_ref[...], preferred_element_type=jnp.float32)


def angle_kernel(
    blocks,
    partner_of,
    sens_in,
    demand_in,
    hedge_in,
    start_in,
    cost_in,
    max_in,
    limit_in,
    line_max_in,
    count_in,
    low_bus_in,
    high_bus_in,
    susc_in,
    ptdf_in,
    *refs,
):
    own_refs, refs = refs[:blocks], refs[blocks:]
    (
        edge_ref,
        inject_ref,
        spread_ref,
        rows_ref,
        weight_ref,
        demand_ref,
        hedge_ref,
        start_ref,
        cost_ref,
        max_ref,
        limit_ref,
        line_max_ref,
        ptdf_ref,
        sens_ref,
        count_ref,
        low_bus_ref,
        high_bus_ref,
        susc_ref,
        onehot_ref,
        copy_sems,
    ) = refs
    hours, buses = start_ref.shape
    scens = demand_ref.shape[0] // hours
    here = lax.axis_index("area")
    early = lax.axis_index("hour") == 0

    pairs = (
        (count_in, count_ref),
        (low_bus_in, low_bus_ref),
        (high_bus_in, high_bus_ref),
        (susc_in, susc_ref),
        (start_in, start_ref),
        (demand_in, demand_ref),
        (sens_in, sens_ref),
        (hedge_in, hedge_ref),
        (cost_in, cost_ref),
        (max_in, max_ref),
        (limit_in, limit_ref),
        (line_max_in, line_max_ref),
        (ptdf_in, ptdf_ref),
    )
    copies = [pltpu.make_async_copy(src, dst, copy_sems.at[i]) for i, (src, dst) in enumerate(pairs)]
    for copy in copies:
        copy.start()

    for copy in copies[:4]:
        copy.wait()
    for i in range(blocks):
        partner = partner_of(here, i)
        low, row, block, in_reach = block_facts(here, partner)
        slots = slice(i * CAP, (i + 1) * CAP)
        pick = lax.broadcasted_iota(jnp.int32, (CAP, REACH * CAP), 1) == (
            block * CAP + lax.broadcasted_iota(jnp.int32, (CAP, REACH * CAP), 0)
        )
        table_row = pl.ds(row, 1)
        bus_row = jnp.where(low, low_bus_ref[table_row, :], high_bus_ref[table_row, :])
        bus = jnp.sum(jnp.where(pick, bus_row.astype(jnp.float32), 0.0), axis=1, keepdims=True)
        susc = jnp.sum(jnp.where(pick, susc_ref[table_row, :], 0.0), axis=1, keepdims=True)
        count_row = count_ref[table_row, :].astype(jnp.float32)
        is_block = lax.broadcasted_iota(jnp.int32, (CAP, REACH), 1) == block
        count = jnp.sum(jnp.where(is_block, count_row, 0.0), axis=1, keepdims=True)
        slot_ids = lax.broadcasted_iota(jnp.int32, (CAP, 1), 0).astype(jnp.float32)
        live = jnp.where((slot_ids < count) & in_reach, 1.0, 0.0)
        sign = jnp.where(low, 1.0, -1.0)
        bus_ids = lax.broadcasted_iota(jnp.int32, (CAP, buses), 1).astype(jnp.float32)
        onehot = jnp.where(bus_ids == bus, live, 0.0)
        onehot_ref[slots, :] = onehot.astype(jnp.bfloat16)
        spread_ref[slots, :] = (-sign * onehot).astype(jnp.bfloat16)
        weight_ref[slots, :] = jnp.broadcast_to(live * sign * susc, (CAP, 128))

    for copy in copies[4:7]:
        copy.wait()
    for h in range(hours):
        part = slice(h * scens, (h + 1) * scens)
        inject_ref[part, :] = (start_ref[h : h + 1, :] - demand_ref[part, :]).astype(jnp.bfloat16)
    rows = jnp.dot(onehot_ref[...], sens_ref[...], preferred_element_type=jnp.float32)
    rows_ref[...] = rows.astype(jnp.bfloat16)
    own = lax.dot_general(
        rows_ref[...], inject_ref[...], CONTRACT_LAST, preferred_element_type=jnp.float32
    )
    for i in range(blocks):
        own_refs[i][...] = own[i * CAP : (i + 1) * CAP, :]

    for copy in copies[7:]:
        copy.wait()
    last = (hours - 1) * scens
    edge_ref[0:scens, :] = jnp.where(early, demand_ref[last:, :], demand_ref[0:scens, :])
    edge_ref[scens : 2 * scens, :] = jnp.where(early, hedge_ref[last:, :], hedge_ref[0:scens, :])
    at = 2 * scens
    edge_ref[at : at + 1, :] = jnp.where(early, start_ref[hours - 1 : hours, :], start_ref[0:1, :])
    edge_ref[at + 1 : at + 2, :] = jnp.where(
        early, start_ref[hours - 2 : hours - 1, :], start_ref[1:2, :]
    )


def first_kernel(
    ptdf_ref,
    own_inject_ref,
    demand_ref,
    hedge_ref,
    start_ref,
    edge_ref,
    cost_ref,
    max_ref,
    limit_ref,
    line_max_ref,
    gen_ref,
    base_ref,
    hedged_ref,
    sums_ref,
    inject_ref,
    over_ref,
    back_ref,
    padded_ref,
    excess_ref,
    ramp_ref,
):
    hours, buses = start_ref.shape
    width = demand_ref.shape[0]
    scens = width // hours
    at = 2 * scens
    early = lax.axis_index("hour") == 0
    first_hour = lax.axis_index("hour") * hours
    beyond = edge_ref[at : at + 1, :]
    limit = limit_ref[...]
    cost = cost_ref[...]
    top = max_ref[...]

    inject_ref[0:width, :] = own_inject_ref[...]
    inject_ref[width : width + scens, :] = (beyond - edge_ref[0:scens, :]).astype(jnp.bfloat16)
    back_ref[...] = line_work(inject_ref, ptdf_ref, line_max_ref, over_ref)
    write_ramp(start_ref, beyond, limit, first_hour, padded_ref, excess_ref, ramp_ref)

    def step(mean, hedge, back, ramp):
        grad = cost + back + (mean - mean + hedge) + ramp
        gen = jnp.clip(mean - STEP_SIZE * grad, 0.0, top)
        return gen, gen + hedge

    for h in range(hours):
        part = slice(h * scens, (h + 1) * scens)
        mean = start_ref[h : h + 1, :]
        gen, hedged = step(mean, hedge_ref[part, :], back_ref[part, :], ramp_ref[h : h + 1, :])
        gen_ref[part, :] = gen
        base_ref[part, :] = gen - demand_ref[part, :]
        hedged_ref[part, :] = hedged
        sums_ref[h : h + 1, :] = jnp.sum(hedged, axis=0, keepdims=True)
    near = jnp.where(early, start_ref[hours - 1 : hours, :], start_ref[0:1, :])
    ramp = excess(beyond - near, limit) + excess(beyond - edge_ref[at + 1 : at + 2, :], limit)
    _, hedged = step(beyond, edge_ref[scens:at, :], back_ref[width : width + scens, :], ramp)
    sums_ref[hours : hours + 1, :] = jnp.sum(hedged, axis=0, keepdims=True)
    spare = sums_ref.shape[0] - hours - 1
    sums_ref[hours + 1 :, :] = jnp.zeros((spare, buses), jnp.float32)


def tie_kernel(blocks, base_ref, spread_ref, rows_ref, weight_ref, *refs):
    own_refs, refs = refs[:blocks], refs[blocks:]
    peer_refs, refs = refs[:blocks], refs[blocks:]
    next_refs, (inject_ref, mine_ref, theirs_ref) = refs[:blocks], refs[blocks:]

    weight = weight_ref[:, 0:1]
    own = jnp.concatenate([ref[...] for ref in own_refs], axis=0)
    peer = jnp.concatenate([ref[...] for ref in peer_refs], axis=0)
    est_mine = weight * own
    est_theirs = -weight * peer
    flow = (est_mine + est_theirs) * 0.5
    dual_mine = est_mine - flow
    dual_theirs = est_theirs - flow
    spread = spread_ref[...]
    add = lax.dot_general(
        split_3(flow),
        jnp.concatenate([spread, spread, spread], axis=0),
        CONTRACT_FIRST,
        preferred_element_type=jnp.float32,
    )
    inject_ref[...] = (base_ref[...] + add).astype(jnp.bfloat16)

    own_next = lax.dot_general(
        rows_ref[...], inject_ref[...], CONTRACT_LAST, preferred_element_type=jnp.float32
    )
    for i in range(blocks):
        next_refs[i][...] = own_next[i * CAP : (i + 1) * CAP, :]
    mine_ref[...] = weight * (own_next - peer) + dual_mine
    theirs_ref[...] = weight * own + dual_theirs


def second_kernel(
    terms,
    scen_total,
    ptdf_ref,
    inject_ref,
    gen_ref,
    hedged_ref,
    cost_ref,
    max_ref,
    limit_ref,
    line_max_ref,
    *refs,
):
    sum_refs, refs = refs[:terms], refs[terms:]
    (hedged_out_ref, sums_out_ref, over_ref, back_ref, mean_ref, padded_ref, excess_ref, ramp_ref) = refs
    hours, buses = sums_out_ref.shape
    width = inject_ref.shape[0]
    scens = width // hours
    first_hour = lax.axis_index("hour") * hours

    back_ref[...] = line_work(inject_ref, ptdf_ref, line_max_ref, over_ref)
    mean_ref[...] = functools.reduce(jnp.add, [ref[...] for ref in sum_refs]) / scen_total
    write_ramp(
        mean_ref, mean_ref[hours : hours + 1, :], limit_ref[...], first_hour, padded_ref, excess_ref, ramp_ref
    )
    cost = cost_ref[...]
    top = max_ref[...]
    for h in range(hours):
        part = slice(h * scens, (h + 1) * scens)
        mean = mean_ref[h : h + 1, :]
        gen = gen_ref[part, :]
        hedge = hedged_ref[part, :] - mean
        grad = cost + back_ref[part, :] + (gen - mean + hedge) + ramp_ref[h : h + 1, :]
        gen = jnp.clip(gen - STEP_SIZE * grad, 0.0, top)
        hedged = gen + hedge
        hedged_out_ref[part, :] = hedged
        sums_out_ref[h : h + 1, :] = jnp.sum(hedged, axis=0, keepdims=True)


def flow_kernel(blocks, partner_of, *refs):
    peer_refs, (weight_ref, mine_ref, theirs_ref, tie_ref) = refs[:blocks], refs[blocks:]
    here = lax.axis_index("area")
    slots = tie_ref.shape[1]
    places = []
    for i in range(blocks):
        low, _, block, in_reach = block_facts(here, partner_of(here, i))
        first = block * CAP + jnp.where(low, 0, REACH * CAP)
        hit = lax.broadcasted_iota(jnp.int32, (CAP, slots), 1) == (
            first + lax.broadcasted_iota(jnp.int32, (CAP, slots), 0)
        )
        places.append(jnp.where(hit & in_reach, 1.0, 0.0).astype(jnp.bfloat16))
    peer = jnp.concatenate([ref[...] for ref in peer_refs], axis=0)
    flow = (mine_ref[...] + (theirs_ref[...] - weight_ref[:, 0:1] * peer)) * 0.5
    tie_ref[...] = lax.dot_general(
        split_3(flow),
        jnp.concatenate(places * 3, axis=0),
        CONTRACT_FIRST,
        preferred_element_type=jnp.float32,
    )


def agree_kernel(scen_total, hedged_ref, *refs):
    sum_refs, (mean_ref, hedge_ref) = refs[:-2], refs[-2:]
    hours = mean_ref.shape[0]
    scens = hedged_ref.shape[0] // hours
    mean_ref[...] = functools.reduce(jnp.add, [ref[...] for ref in sum_refs]) / scen_total
    for h in range(hours):
        part = slice(h * scens, (h + 1) * scens)
        hedge_ref[part, :] = hedged_ref[part, :] - mean_ref[h : h + 1, :]


def call(kernel, name, args, outs, scratch, flops, in_place=()):
    size = sum(x.size * x.dtype.itemsize for x in list(args) + list(outs))
    return pl.pallas_call(
        kernel,
        name=name,
        out_shape=outs,
        in_specs=[ANY if i in in_place else VMEM for i in range(len(args))],
        out_specs=[VMEM] * len(outs),
        scratch_shapes=scratch,
        compiler_params=pltpu.CompilerParams(vmem_limit_bytes=32 * 1024 * 1024),
        cost_estimate=pl.CostEstimate(flops=flops, bytes_accessed=size, transcendentals=0),
    )(*(pltpu.with_memory_space_constraint(x, pltpu.HBM) if i in in_place else x for i, x in enumerate(args)))


def per_device(
    ptdf,
    angle_sens,
    demand,
    gen_start,
    hedge_dual,
    gen_cost,
    gen_max,
    gen_ramp,
    line_max,
    tie_count,
    tie_low_bus,
    tie_high_bus,
    tie_susc,
):
    hours, scens, buses = demand.shape
    lines = ptdf.shape[0]
    width = hours * scens
    areas = lax.axis_size("area")
    n_scen = lax.axis_size("scen")
    assert lax.axis_size("hour") == 2 and hours >= 2
    scen_total = scens * n_scen
    blocks, partner_of, from_partners = partner_plan(areas)
    slots = blocks * CAP
    sum_rows = 8 * (hours // 8 + 1)
    f32, bf16 = jnp.float32, jnp.bfloat16

    def shape(*dims, dtype=f32):
        return jax.ShapeDtypeStruct(dims, dtype)

    def over_scens(sums):
        if n_scen == 2:
            return [sums, lax.ppermute(sums, "scen", [(0, 1), (1, 0)])]
        return [lax.psum(sums, "scen")]

    work = 4 * width * lines * buses

    def step_scratch(rows):
        return [
            pltpu.VMEM((rows, buses), bf16),
            pltpu.VMEM((rows, lines), bf16),
            pltpu.VMEM((rows, buses), f32),
        ]

    ramp_scratch = [
        pltpu.VMEM((hours + 4, buses), f32),
        pltpu.VMEM((hours + 4, buses), f32),
        pltpu.VMEM((hours, buses), f32),
    ]
    tables = (tie_count, tie_low_bus, tie_high_bus, tie_susc)
    vectors = [x.reshape(1, -1) for x in (gen_cost, gen_max, gen_ramp, line_max)]
    made = call(
        functools.partial(angle_kernel, blocks, partner_of),
        "angles",
        (
            angle_sens,
            demand.reshape(width, buses),
            hedge_dual.reshape(width, buses),
            gen_start,
            *vectors,
            *tables,
            ptdf,
        ),
        [shape(CAP, width)] * blocks
        + [
            shape(2 * scens + 8, buses),
            shape(width, buses, dtype=bf16),
            shape(slots, buses, dtype=bf16),
            shape(slots, buses, dtype=bf16),
            shape(slots, 128),
            shape(width, buses),
            shape(width, buses),
            shape(hours, buses),
            shape(1, buses),
            shape(1, buses),
            shape(1, buses),
            shape(1, lines),
            shape(lines, buses, dtype=bf16),
        ],
        [pltpu.VMEM(x.shape, x.dtype) for x in (angle_sens, *tables)]
        + [pltpu.VMEM((slots, buses), bf16), pltpu.SemaphoreType.DMA((13,))],
        2 * slots * buses * (width + buses),
        range(13),
    )
    own = made[:blocks]
    edge, inject, spread, rows, weight, load, hedge, start = made[blocks : blocks + 8]
    cost, top, limit, line_top, held = made[blocks + 8 :]
    edge = lax.ppermute(edge, "hour", [(0, 1), (1, 0)])
    peer = from_partners(own)
    gen, base, hedged, sums = call(
        first_kernel,
        "first",
        (held, inject, load, hedge, start, edge, cost, top, limit, line_top),
        [
            shape(width, buses),
            shape(width, buses),
            shape(width, buses),
            shape(sum_rows, buses),
        ],
        step_scratch(width + scens) + ramp_scratch,
        work,
    )
    sum_terms = over_scens(sums)
    terms = len(sum_terms)
    tied = call(
        functools.partial(tie_kernel, blocks),
        "ties",
        (base, spread, rows, weight, *own, *peer),
        [shape(CAP, width)] * blocks
        + [shape(width, buses, dtype=bf16), shape(slots, width), shape(slots, width)],
        [],
        BETWEEN,
    )
    own = tied[:blocks]
    inject, mine, theirs = tied[blocks:]
    hedged, sums = call(
        functools.partial(second_kernel, terms, scen_total),
        "second",
        (held, inject, gen, hedged, cost, top, limit, line_top, *sum_terms),
        [shape(width, buses), shape(hours, buses)],
        step_scratch(width)[1:] + [pltpu.VMEM((sum_rows, buses), f32)] + ramp_scratch,
        work,
    )
    peer = from_partners(own)
    sum_terms = over_scens(sums)
    (tie_flow,) = call(
        functools.partial(flow_kernel, blocks, partner_of),
        "flows",
        (*peer, weight, mine, theirs),
        [shape(width, 2 * REACH * CAP)],
        [],
        BETWEEN,
    )
    sum_terms, tie_flow = lax.optimization_barrier((sum_terms, tie_flow))
    gen_mean, hedge = call(
        functools.partial(agree_kernel, scen_total),
        "agree",
        (hedged, *sum_terms),
        [shape(hours, buses), shape(width, buses)],
        [],
        2 * width * buses,
    )
    return (
        gen_mean,
        hedge.reshape(hours, scens, buses),
        tie_flow.reshape(hours, scens, 2 * REACH * CAP),
    )


def solution(mesh):
    return jax.shard_map(
        per_device,
        mesh=mesh,
        in_specs=(
            P(("group", "area"), None),
            P(("group", "area"), None),
            P(("group", "hour"), "scen", "area"),
            P(("group", "hour"), "area"),
            P(("group", "hour"), "scen", "area"),
            P(("group", "area")),
            P(("group", "area")),
            P(("group", "area")),
            P(("group", "area")),
            P("group", None),
            P("group", None),
            P("group", None),
            P("group", None),
        ),
        out_specs=(
            P(("group", "hour"), "area"),
            P(("group", "hour"), "scen", "area"),
            P(("group", "hour"), "scen", "area"),
        ),
        check_vma=False,
    )
```

```python
import functools

import jax
import jax.numpy as jnp
from jax import lax
from jax.experimental import pallas as pl
from jax.experimental.pallas import tpu as pltpu
from jax.sharding import PartitionSpec as P

HOURS = 24
REACH = 4
CAP = 16

STEP_SIZE = 0.5
LINE_CHUNK = 512
BETWEEN = 20_000_000_000

CONTRACT_LAST = (((1,), (1,)), ((), ()))
CONTRACT_FIRST = (((0,), (0,)), ((), ()))
VMEM = pl.BlockSpec(memory_space=pltpu.VMEM)
ANY = pl.BlockSpec(memory_space=pltpu.HBM)


def partner_plan(areas):
    if areas & (areas - 1) == 0 and areas <= REACH + 1:
        flips = range(1, areas)

        def by_flip(parts):
            sent = {}
            for f in reversed(flips):
                sent[f] = lax.ppermute(parts[f - 1], "area", [(a, a ^ f) for a in range(areas)])
            return [sent[f] for f in flips]

        return len(flips), lambda here, i: here ^ flips[i], by_flip
    reach = min(REACH, areas - 1)
    shifts = sorted({s % areas for d in range(1, reach + 1) for s in (d, -d)})

    def by_shift(parts):
        sent = [
            lax.ppermute(part, "area", [(a, (a + s) % areas) for a in range(areas)])
            for part, s in zip(parts, shifts)
        ]
        return [sent[shifts.index(areas - s)] for s in shifts]

    return len(shifts), lambda here, i: lax.rem(here + shifts[i], areas), by_shift


def block_facts(here, partner):
    low = partner > here
    distance = jnp.abs(partner - here)
    block = jnp.clip(distance - 1, 0, REACH - 1)
    in_reach = (distance >= 1) & (distance <= REACH)
    return low, jnp.minimum(here, partner), block, in_reach


def split_3(x):
    high = x.astype(jnp.bfloat16)
    rest = x - high.astype(jnp.float32)
    middle = rest.astype(jnp.bfloat16)
    rest = rest - middle.astype(jnp.float32)
    return jnp.concatenate([high, middle, rest.astype(jnp.bfloat16)], axis=0)


def excess(diffs, limit):
    return diffs - jnp.clip(diffs, -limit, limit)


def write_ramp(mean_ref, beyond, limit, first_hour, padded_ref, excess_ref, ramp_ref):
    hours = ramp_ref.shape[0]
    padded_ref[0:1, :] = beyond
    padded_ref[1 : hours + 1, :] = mean_ref[0:hours, :]
    padded_ref[hours + 1 : hours + 2, :] = beyond
    diffs = padded_ref[1 : hours + 2, :] - padded_ref[0 : hours + 1, :]
    ids = first_hour + lax.broadcasted_iota(jnp.int32, diffs.shape, 0)
    valid = (ids >= 1) & (ids <= HOURS - 1)
    excess_ref[0 : hours + 1, :] = jnp.where(valid, excess(diffs, limit), 0.0)
    ramp_ref[...] = excess_ref[0:hours, :] - excess_ref[1 : hours + 1, :]


def line_work(inject_ref, ptdf_ref, line_max_ref, over_ref):
    inject = inject_ref[...]
    lines = ptdf_ref.shape[0]
    for at in range(0, lines, LINE_CHUNK):
        part = slice(at, at + LINE_CHUNK)
        flows = lax.dot_general(
            inject, ptdf_ref[part, :], CONTRACT_LAST, preferred_element_type=jnp.float32
        )
        limit = line_max_ref[:, part]
        over_ref[:, part] = (flows - jnp.clip(flows, -limit, limit)).astype(jnp.bfloat16)
    return jnp.dot(over_ref[...], ptdf_ref[...], preferred_element_type=jnp.float32)


def angle_kernel(
    blocks,
    partner_of,
    sens_in,
    demand_in,
    hedge_in,
    start_in,
    cost_in,
    max_in,
    limit_in,
    line_max_in,
    count_in,
    low_bus_in,
    high_bus_in,
    susc_in,
    *refs,
):
    own_refs, refs = refs[:blocks], refs[blocks:]
    (
        edge_ref,
        inject_ref,
        spread_ref,
        rows_ref,
        weight_ref,
        demand_ref,
        start_ref,
        cost_ref,
        max_ref,
        limit_ref,
        line_max_ref,
        sens_ref,
        count_ref,
        low_bus_ref,
        high_bus_ref,
        susc_ref,
        onehot_ref,
        copy_sems,
    ) = refs
    hours, buses = start_ref.shape
    scens = demand_ref.shape[0] // hours
    here = lax.axis_index("area")
    early = lax.axis_index("hour") == 0
    last = (hours - 1) * scens
    edge_rows = pl.ds(pl.multiple_of((1 - lax.axis_index("hour")) * last, scens), scens)

    pairs = (
        (count_in, count_ref),
        (low_bus_in, low_bus_ref),
        (high_bus_in, high_bus_ref),
        (susc_in, susc_ref),
        (start_in, start_ref),
        (demand_in, demand_ref),
        (sens_in, sens_ref),
        (hedge_in.at[edge_rows], edge_ref.at[pl.ds(scens, scens)]),
        (cost_in, cost_ref),
        (max_in, max_ref),
        (limit_in, limit_ref),
        (line_max_in, line_max_ref),
    )
    copies = [pltpu.make_async_copy(src, dst, copy_sems.at[i]) for i, (src, dst) in enumerate(pairs)]
    for copy in copies:
        copy.start()

    for copy in copies[:4]:
        copy.wait()
    for i in range(blocks):
        partner = partner_of(here, i)
        low, row, block, in_reach = block_facts(here, partner)
        slots = slice(i * CAP, (i + 1) * CAP)
        pick = lax.broadcasted_iota(jnp.int32, (CAP, REACH * CAP), 1) == (
            block * CAP + lax.broadcasted_iota(jnp.int32, (CAP, REACH * CAP), 0)
        )
        table_row = pl.ds(row, 1)
        bus_row = jnp.where(low, low_bus_ref[table_row, :], high_bus_ref[table_row, :])
        bus = jnp.sum(jnp.where(pick, bus_row.astype(jnp.float32), 0.0), axis=1, keepdims=True)
        susc = jnp.sum(jnp.where(pick, susc_ref[table_row, :], 0.0), axis=1, keepdims=True)
        count_row = count_ref[table_row, :].astype(jnp.float32)
        is_block = lax.broadcasted_iota(jnp.int32, (CAP, REACH), 1) == block
        count = jnp.sum(jnp.where(is_block, count_row, 0.0), axis=1, keepdims=True)
        slot_ids = lax.broadcasted_iota(jnp.int32, (CAP, 1), 0).astype(jnp.float32)
        live = jnp.where((slot_ids < count) & in_reach, 1.0, 0.0)
        sign = jnp.where(low, 1.0, -1.0)
        bus_ids = lax.broadcasted_iota(jnp.int32, (CAP, buses), 1).astype(jnp.float32)
        onehot = jnp.where(bus_ids == bus, live, 0.0)
        onehot_ref[slots, :] = onehot.astype(jnp.bfloat16)
        spread_ref[slots, :] = (-sign * onehot).astype(jnp.bfloat16)
        weight_ref[slots, :] = jnp.broadcast_to(live * sign * susc, (CAP, 128))

    for copy in copies[4:7]:
        copy.wait()
    for h in range(hours):
        part = slice(h * scens, (h + 1) * scens)
        inject_ref[part, :] = (start_ref[h : h + 1, :] - demand_ref[part, :]).astype(jnp.bfloat16)
    rows = jnp.dot(onehot_ref[...], sens_ref[...], preferred_element_type=jnp.float32)
    rows_ref[...] = rows.astype(jnp.bfloat16)
    own = lax.dot_general(
        rows_ref[...], inject_ref[...], CONTRACT_LAST, preferred_element_type=jnp.float32
    )
    for i in range(blocks):
        own_refs[i][...] = own[i * CAP : (i + 1) * CAP, :]

    for copy in copies[7:]:
        copy.wait()
    edge_ref[0:scens, :] = jnp.where(early, demand_ref[last:, :], demand_ref[0:scens, :])
    at = 2 * scens
    edge_ref[at : at + 1, :] = jnp.where(early, start_ref[hours - 1 : hours, :], start_ref[0:1, :])
    edge_ref[at + 1 : at + 2, :] = jnp.where(
        early, start_ref[hours - 2 : hours - 1, :], start_ref[1:2, :]
    )


def first_kernel(
    ptdf_ref,
    own_inject_ref,
    demand_ref,
    hedge_ref,
    start_ref,
    edge_ref,
    cost_ref,
    max_ref,
    limit_ref,
    line_max_ref,
    gen_ref,
    base_ref,
    hedged_ref,
    sums_ref,
    inject_ref,
    over_ref,
    back_ref,
    padded_ref,
    excess_ref,
    ramp_ref,
):
    hours, buses = start_ref.shape
    width = demand_ref.shape[0]
    scens = width // hours
    at = 2 * scens
    early = lax.axis_index("hour") == 0
    first_hour = lax.axis_index("hour") * hours
    beyond = edge_ref[at : at + 1, :]
    limit = limit_ref[...]
    cost = cost_ref[...]
    top = max_ref[...]

    inject_ref[0:width, :] = own_inject_ref[...]
    inject_ref[width : width + scens, :] = (beyond - edge_ref[0:scens, :]).astype(jnp.bfloat16)
    back_ref[...] = line_work(inject_ref, ptdf_ref, line_max_ref, over_ref)
    write_ramp(start_ref, beyond, limit, first_hour, padded_ref, excess_ref, ramp_ref)

    def step(mean, hedge, back, ramp):
        grad = cost + back + (mean - mean + hedge) + ramp
        gen = jnp.clip(mean - STEP_SIZE * grad, 0.0, top)
        return gen, gen + hedge

    for h in range(hours):
        part = slice(h * scens, (h + 1) * scens)
        mean = start_ref[h : h + 1, :]
        gen, hedged = step(mean, hedge_ref[part, :], back_ref[part, :], ramp_ref[h : h + 1, :])
        gen_ref[part, :] = gen
        base_ref[part, :] = gen - demand_ref[part, :]
        hedged_ref[part, :] = hedged
        sums_ref[h : h + 1, :] = jnp.sum(hedged, axis=0, keepdims=True)
    near = jnp.where(early, start_ref[hours - 1 : hours, :], start_ref[0:1, :])
    ramp = excess(beyond - near, limit) + excess(beyond - edge_ref[at + 1 : at + 2, :], limit)
    _, hedged = step(beyond, edge_ref[scens:at, :], back_ref[width : width + scens, :], ramp)
    sums_ref[hours : hours + 1, :] = jnp.sum(hedged, axis=0, keepdims=True)
    spare = sums_ref.shape[0] - hours - 1
    sums_ref[hours + 1 :, :] = jnp.zeros((spare, buses), jnp.float32)


def tie_kernel(blocks, base_ref, spread_ref, rows_ref, weight_ref, *refs):
    own_refs, refs = refs[:blocks], refs[blocks:]
    peer_refs, refs = refs[:blocks], refs[blocks:]
    next_refs, (inject_ref, mine_ref, theirs_ref) = refs[:blocks], refs[blocks:]

    weight = weight_ref[:, 0:1]
    own = jnp.concatenate([ref[...] for ref in own_refs], axis=0)
    peer = jnp.concatenate([ref[...] for ref in peer_refs], axis=0)
    est_mine = weight * own
    est_theirs = -weight * peer
    flow = (est_mine + est_theirs) * 0.5
    dual_mine = est_mine - flow
    dual_theirs = est_theirs - flow
    spread = spread_ref[...]
    add = lax.dot_general(
        split_3(flow),
        jnp.concatenate([spread, spread, spread], axis=0),
        CONTRACT_FIRST,
        preferred_element_type=jnp.float32,
    )
    inject_ref[...] = (base_ref[...] + add).astype(jnp.bfloat16)

    own_next = lax.dot_general(
        rows_ref[...], inject_ref[...], CONTRACT_LAST, preferred_element_type=jnp.float32
    )
    for i in range(blocks):
        next_refs[i][...] = own_next[i * CAP : (i + 1) * CAP, :]
    mine_ref[...] = weight * (own_next - peer) + dual_mine
    theirs_ref[...] = weight * own + dual_theirs


def second_kernel(
    terms,
    scen_total,
    ptdf_ref,
    inject_ref,
    gen_ref,
    hedged_ref,
    cost_ref,
    max_ref,
    limit_ref,
    line_max_ref,
    *refs,
):
    sum_refs, refs = refs[:terms], refs[terms:]
    (hedged_out_ref, sums_out_ref, over_ref, back_ref, mean_ref, padded_ref, excess_ref, ramp_ref) = refs
    hours, buses = sums_out_ref.shape
    width = inject_ref.shape[0]
    scens = width // hours
    first_hour = lax.axis_index("hour") * hours

    back_ref[...] = line_work(inject_ref, ptdf_ref, line_max_ref, over_ref)
    mean_ref[...] = functools.reduce(jnp.add, [ref[...] for ref in sum_refs]) / scen_total
    write_ramp(
        mean_ref, mean_ref[hours : hours + 1, :], limit_ref[...], first_hour, padded_ref, excess_ref, ramp_ref
    )
    cost = cost_ref[...]
    top = max_ref[...]
    for h in range(hours):
        part = slice(h * scens, (h + 1) * scens)
        mean = mean_ref[h : h + 1, :]
        gen = gen_ref[part, :]
        hedge = hedged_ref[part, :] - mean
        grad = cost + back_ref[part, :] + (gen - mean + hedge) + ramp_ref[h : h + 1, :]
        gen = jnp.clip(gen - STEP_SIZE * grad, 0.0, top)
        hedged = gen + hedge
        hedged_out_ref[part, :] = hedged
        sums_out_ref[h : h + 1, :] = jnp.sum(hedged, axis=0, keepdims=True)


def flow_kernel(blocks, partner_of, *refs):
    peer_refs, (weight_ref, mine_ref, theirs_ref, tie_ref) = refs[:blocks], refs[blocks:]
    here = lax.axis_index("area")
    slots = tie_ref.shape[1]
    places = []
    for i in range(blocks):
        low, _, block, in_reach = block_facts(here, partner_of(here, i))
        first = block * CAP + jnp.where(low, 0, REACH * CAP)
        hit = lax.broadcasted_iota(jnp.int32, (CAP, slots), 1) == (
            first + lax.broadcasted_iota(jnp.int32, (CAP, slots), 0)
        )
        places.append(jnp.where(hit & in_reach, 1.0, 0.0).astype(jnp.bfloat16))
    peer = jnp.concatenate([ref[...] for ref in peer_refs], axis=0)
    flow = (mine_ref[...] + (theirs_ref[...] - weight_ref[:, 0:1] * peer)) * 0.5
    tie_ref[...] = lax.dot_general(
        split_3(flow),
        jnp.concatenate(places * 3, axis=0),
        CONTRACT_FIRST,
        preferred_element_type=jnp.float32,
    )


def agree_kernel(scen_total, hedged_ref, *refs):
    sum_refs, (mean_ref, hedge_ref) = refs[:-2], refs[-2:]
    hours = mean_ref.shape[0]
    scens = hedged_ref.shape[0] // hours
    mean_ref[...] = functools.reduce(jnp.add, [ref[...] for ref in sum_refs]) / scen_total
    for h in range(hours):
        part = slice(h * scens, (h + 1) * scens)
        hedge_ref[part, :] = hedged_ref[part, :] - mean_ref[h : h + 1, :]


def call(kernel, name, args, outs, scratch, flops, in_place=()):
    size = sum(x.size * x.dtype.itemsize for x in list(args) + list(outs))
    return pl.pallas_call(
        kernel,
        name=name,
        out_shape=outs,
        in_specs=[ANY if i in in_place else VMEM for i in range(len(args))],
        out_specs=[VMEM] * len(outs),
        scratch_shapes=scratch,
        compiler_params=pltpu.CompilerParams(vmem_limit_bytes=32 * 1024 * 1024),
        cost_estimate=pl.CostEstimate(flops=flops, bytes_accessed=size, transcendentals=0),
    )(*(pltpu.with_memory_space_constraint(x, pltpu.HBM) if i in in_place else x for i, x in enumerate(args)))


def per_device(
    ptdf,
    angle_sens,
    demand,
    gen_start,
    hedge_dual,
    gen_cost,
    gen_max,
    gen_ramp,
    line_max,
    tie_count,
    tie_low_bus,
    tie_high_bus,
    tie_susc,
):
    hours, scens, buses = demand.shape
    lines = ptdf.shape[0]
    width = hours * scens
    areas = lax.axis_size("area")
    n_scen = lax.axis_size("scen")
    assert lax.axis_size("hour") == 2 and hours >= 2
    scen_total = scens * n_scen
    blocks, partner_of, from_partners = partner_plan(areas)
    slots = blocks * CAP
    sum_rows = 8 * (hours // 8 + 1)
    f32, bf16 = jnp.float32, jnp.bfloat16

    def shape(*dims, dtype=f32):
        return jax.ShapeDtypeStruct(dims, dtype)

    def over_scens(sums):
        if n_scen == 2:
            return [sums, lax.ppermute(sums, "scen", [(0, 1), (1, 0)])]
        return [lax.psum(sums, "scen")]

    work = 4 * width * lines * buses

    def step_scratch(rows):
        return [
            pltpu.VMEM((rows, buses), bf16),
            pltpu.VMEM((rows, lines), bf16),
            pltpu.VMEM((rows, buses), f32),
        ]

    ramp_scratch = [
        pltpu.VMEM((hours + 4, buses), f32),
        pltpu.VMEM((hours + 4, buses), f32),
        pltpu.VMEM((hours, buses), f32),
    ]
    tables = (tie_count, tie_low_bus, tie_high_bus, tie_susc)
    vectors = [x.reshape(1, -1) for x in (gen_cost, gen_max, gen_ramp, line_max)]
    hedge = hedge_dual.reshape(width, buses)
    made = call(
        functools.partial(angle_kernel, blocks, partner_of),
        "angles",
        (
            angle_sens,
            demand.reshape(width, buses),
            hedge,
            gen_start,
            *vectors,
            *tables,
        ),
        [shape(CAP, width)] * blocks
        + [
            shape(2 * scens + 8, buses),
            shape(width, buses, dtype=bf16),
            shape(slots, buses, dtype=bf16),
            shape(slots, buses, dtype=bf16),
            shape(slots, 128),
            shape(width, buses),
            shape(hours, buses),
            shape(1, buses),
            shape(1, buses),
            shape(1, buses),
            shape(1, lines),
        ],
        [pltpu.VMEM(x.shape, x.dtype) for x in (angle_sens, *tables)]
        + [pltpu.VMEM((slots, buses), bf16), pltpu.SemaphoreType.DMA((12,))],
        BETWEEN,
        range(12),
    )
    own = made[:blocks]
    edge, inject, spread, rows, weight, load, start = made[blocks : blocks + 7]
    cost, top, limit, line_top = made[blocks + 7 :]
    edge = lax.ppermute(edge, "hour", [(0, 1), (1, 0)])
    peer = from_partners(own)
    gen, base, hedged, sums = call(
        first_kernel,
        "first",
        (ptdf, inject, load, hedge, start, edge, cost, top, limit, line_top),
        [
            shape(width, buses),
            shape(width, buses),
            shape(width, buses),
            shape(sum_rows, buses),
        ],
        step_scratch(width + scens) + ramp_scratch,
        work,
    )
    sum_terms = over_scens(sums)
    terms = len(sum_terms)
    tied = call(
        functools.partial(tie_kernel, blocks),
        "ties",
        (base, spread, rows, weight, *own, *peer),
        [shape(CAP, width)] * blocks
        + [shape(width, buses, dtype=bf16), shape(slots, width), shape(slots, width)],
        [],
        BETWEEN,
    )
    own = tied[:blocks]
    inject, mine, theirs = tied[blocks:]
    hedged, sums = call(
        functools.partial(second_kernel, terms, scen_total),
        "second",
        (ptdf, inject, gen, hedged, cost, top, limit, line_top, *sum_terms),
        [shape(width, buses), shape(hours, buses)],
        step_scratch(width)[1:] + [pltpu.VMEM((sum_rows, buses), f32)] + ramp_scratch,
        work,
    )
    peer = from_partners(own)
    sum_terms = over_scens(sums)
    (tie_flow,) = call(
        functools.partial(flow_kernel, blocks, partner_of),
        "flows",
        (*peer, weight, mine, theirs),
        [shape(width, 2 * REACH * CAP)],
        [],
        BETWEEN,
    )
    sum_terms, tie_flow = lax.optimization_barrier((sum_terms, tie_flow))
    gen_mean, hedge = call(
        functools.partial(agree_kernel, scen_total),
        "agree",
        (hedged, *sum_terms),
        [shape(hours, buses), shape(width, buses)],
        [],
        2 * width * buses,
    )
    return (
        gen_mean,
        hedge.reshape(hours, scens, buses),
        tie_flow.reshape(hours, scens, 2 * REACH * CAP),
    )


def solution(mesh):
    return jax.shard_map(
        per_device,
        mesh=mesh,
        in_specs=(
            P(("group", "area"), None),
            P(("group", "area"), None),
            P(("group", "hour"), "scen", "area"),
            P(("group", "hour"), "area"),
            P(("group", "hour"), "scen", "area"),
            P(("group", "area")),
            P(("group", "area")),
            P(("group", "area")),
            P(("group", "area")),
            P("group", None),
            P("group", None),
            P("group", None),
            P("group", None),
        ),
        out_specs=(
            P(("group", "hour"), "area"),
            P(("group", "hour"), "scen", "area"),
            P(("group", "hour"), "scen", "area"),
        ),
        check_vma=False,
    )
```

```python
import functools

import jax
import jax.numpy as jnp
from jax import lax
from jax.experimental import pallas as pl
from jax.experimental.pallas import tpu as pltpu
from jax.sharding import PartitionSpec as P

HOURS = 24
REACH = 4
CAP = 16

STEP_SIZE = 0.5
LINE_CHUNK = 512
BETWEEN = 20_000_000_000

CONTRACT_LAST = (((1,), (1,)), ((), ()))
CONTRACT_FIRST = (((0,), (0,)), ((), ()))
VMEM = pl.BlockSpec(memory_space=pltpu.VMEM)
ANY = pl.BlockSpec(memory_space=pltpu.HBM)


def partner_plan(areas):
    reach = min(REACH, areas - 1)
    shifts = sorted({s % areas for d in range(1, reach + 1) for s in (d, -d)})

    def by_shift(parts):
        sent = [
            lax.ppermute(part, "area", [(a, (a + s) % areas) for a in range(areas)])
            for part, s in zip(parts, shifts)
        ]
        return [sent[shifts.index(areas - s)] for s in shifts]

    return len(shifts), lambda here, i: lax.rem(here + shifts[i], areas), by_shift


def block_facts(here, partner):
    low = partner > here
    distance = jnp.abs(partner - here)
    block = jnp.clip(distance - 1, 0, REACH - 1)
    in_reach = (distance >= 1) & (distance <= REACH)
    return low, jnp.minimum(here, partner), block, in_reach


def split_3(x):
    high = x.astype(jnp.bfloat16)
    rest = x - high.astype(jnp.float32)
    middle = rest.astype(jnp.bfloat16)
    rest = rest - middle.astype(jnp.float32)
    return jnp.concatenate([high, middle, rest.astype(jnp.bfloat16)], axis=0)


def excess(diffs, limit):
    return diffs - jnp.clip(diffs, -limit, limit)


def write_ramp(mean_ref, beyond, limit, first_hour, padded_ref, excess_ref, ramp_ref):
    hours = ramp_ref.shape[0]
    padded_ref[0:1, :] = beyond
    padded_ref[1 : hours + 1, :] = mean_ref[0:hours, :]
    padded_ref[hours + 1 : hours + 2, :] = beyond
    diffs = padded_ref[1 : hours + 2, :] - padded_ref[0 : hours + 1, :]
    ids = first_hour + lax.broadcasted_iota(jnp.int32, diffs.shape, 0)
    valid = (ids >= 1) & (ids <= HOURS - 1)
    excess_ref[0 : hours + 1, :] = jnp.where(valid, excess(diffs, limit), 0.0)
    ramp_ref[...] = excess_ref[0:hours, :] - excess_ref[1 : hours + 1, :]


def line_work(inject_ref, ptdf_ref, line_max_ref, over_ref):
    inject = inject_ref[...]
    lines = ptdf_ref.shape[0]
    for at in range(0, lines, LINE_CHUNK):
        part = slice(at, at + LINE_CHUNK)
        flows = lax.dot_general(
            inject, ptdf_ref[part, :], CONTRACT_LAST, preferred_element_type=jnp.float32
        )
        limit = line_max_ref[:, part]
        over_ref[:, part] = (flows - jnp.clip(flows, -limit, limit)).astype(jnp.bfloat16)
    return jnp.dot(over_ref[...], ptdf_ref[...], preferred_element_type=jnp.float32)


def angle_kernel(
    blocks,
    partner_of,
    sens_in,
    demand_in,
    hedge_in,
    start_in,
    cost_in,
    max_in,
    limit_in,
    line_max_in,
    count_in,
    low_bus_in,
    high_bus_in,
    susc_in,
    *refs,
):
    own_refs, refs = refs[:blocks], refs[blocks:]
    (
        edge_ref,
        inject_ref,
        spread_ref,
        rows_ref,
        weight_ref,
        demand_ref,
        start_ref,
        cost_ref,
        max_ref,
        limit_ref,
        line_max_ref,
        sens_ref,
        count_ref,
        low_bus_ref,
        high_bus_ref,
        susc_ref,
        onehot_ref,
        copy_sems,
    ) = refs
    hours, buses = start_ref.shape
    scens = demand_ref.shape[0] // hours
    here = lax.axis_index("area")
    early = lax.axis_index("hour") == 0
    last = (hours - 1) * scens
    edge_rows = pl.ds(pl.multiple_of((1 - lax.axis_index("hour")) * last, scens), scens)

    pairs = (
        (count_in, count_ref),
        (low_bus_in, low_bus_ref),
        (high_bus_in, high_bus_ref),
        (susc_in, susc_ref),
        (start_in, start_ref),
        (demand_in, demand_ref),
        (sens_in, sens_ref),
        (hedge_in.at[edge_rows], edge_ref.at[pl.ds(scens, scens)]),
        (cost_in, cost_ref),
        (max_in, max_ref),
        (limit_in, limit_ref),
        (line_max_in, line_max_ref),
    )
    copies = [pltpu.make_async_copy(src, dst, copy_sems.at[i]) for i, (src, dst) in enumerate(pairs)]
    for copy in copies:
        copy.start()

    for copy in copies[:4]:
        copy.wait()
    for i in range(blocks):
        partner = partner_of(here, i)
        low, row, block, in_reach = block_facts(here, partner)
        slots = slice(i * CAP, (i + 1) * CAP)
        pick = lax.broadcasted_iota(jnp.int32, (CAP, REACH * CAP), 1) == (
            block * CAP + lax.broadcasted_iota(jnp.int32, (CAP, REACH * CAP), 0)
        )
        table_row = pl.ds(row, 1)
        bus_row = jnp.where(low, low_bus_ref[table_row, :], high_bus_ref[table_row, :])
        bus = jnp.sum(jnp.where(pick, bus_row.astype(jnp.float32), 0.0), axis=1, keepdims=True)
        susc = jnp.sum(jnp.where(pick, susc_ref[table_row, :], 0.0), axis=1, keepdims=True)
        count_row = count_ref[table_row, :].astype(jnp.float32)
        is_block = lax.broadcasted_iota(jnp.int32, (CAP, REACH), 1) == block
        count = jnp.sum(jnp.where(is_block, count_row, 0.0), axis=1, keepdims=True)
        slot_ids = lax.broadcasted_iota(jnp.int32, (CAP, 1), 0).astype(jnp.float32)
        live = jnp.where((slot_ids < count) & in_reach, 1.0, 0.0)
        sign = jnp.where(low, 1.0, -1.0)
        bus_ids = lax.broadcasted_iota(jnp.int32, (CAP, buses), 1).astype(jnp.float32)
        onehot = jnp.where(bus_ids == bus, live, 0.0)
        onehot_ref[slots, :] = onehot.astype(jnp.bfloat16)
        spread_ref[slots, :] = (-sign * onehot).astype(jnp.bfloat16)
        weight_ref[slots, :] = jnp.broadcast_to(live * sign * susc, (CAP, 128))

    for copy in copies[4:7]:
        copy.wait()
    for h in range(hours):
        part = slice(h * scens, (h + 1) * scens)
        inject_ref[part, :] = (start_ref[h : h + 1, :] - demand_ref[part, :]).astype(jnp.bfloat16)
    rows = jnp.dot(onehot_ref[...], sens_ref[...], preferred_element_type=jnp.float32)
    rows_ref[...] = rows.astype(jnp.bfloat16)
    own = lax.dot_general(
        rows_ref[...], inject_ref[...], CONTRACT_LAST, preferred_element_type=jnp.float32
    )
    for i in range(blocks):
        own_refs[i][...] = own[i * CAP : (i + 1) * CAP, :]

    for copy in copies[7:]:
        copy.wait()
    edge_ref[0:scens, :] = jnp.where(early, demand_ref[last:, :], demand_ref[0:scens, :])
    at = 2 * scens
    edge_ref[at : at + 1, :] = jnp.where(early, start_ref[hours - 1 : hours, :], start_ref[0:1, :])
    edge_ref[at + 1 : at + 2, :] = jnp.where(
        early, start_ref[hours - 2 : hours - 1, :], start_ref[1:2, :]
    )


def first_kernel(
    ptdf_ref,
    own_inject_ref,
    demand_ref,
    hedge_ref,
    start_ref,
    edge_ref,
    cost_ref,
    max_ref,
    limit_ref,
    line_max_ref,
    gen_ref,
    base_ref,
    hedged_ref,
    sums_ref,
    inject_ref,
    over_ref,
    back_ref,
    padded_ref,
    excess_ref,
    ramp_ref,
):
    hours, buses = start_ref.shape
    width = demand_ref.shape[0]
    scens = width // hours
    at = 2 * scens
    early = lax.axis_index("hour") == 0
    first_hour = lax.axis_index("hour") * hours
    beyond = edge_ref[at : at + 1, :]
    limit = limit_ref[...]
    cost = cost_ref[...]
    top = max_ref[...]

    inject_ref[0:width, :] = own_inject_ref[...]
    inject_ref[width : width + scens, :] = (beyond - edge_ref[0:scens, :]).astype(jnp.bfloat16)
    back_ref[...] = line_work(inject_ref, ptdf_ref, line_max_ref, over_ref)
    write_ramp(start_ref, beyond, limit, first_hour, padded_ref, excess_ref, ramp_ref)

    def step(mean, hedge, back, ramp):
        grad = cost + back + (mean - mean + hedge) + ramp
        gen = jnp.clip(mean - STEP_SIZE * grad, 0.0, top)
        return gen, gen + hedge

    for h in range(hours):
        part = slice(h * scens, (h + 1) * scens)
        mean = start_ref[h : h + 1, :]
        gen, hedged = step(mean, hedge_ref[part, :], back_ref[part, :], ramp_ref[h : h + 1, :])
        gen_ref[part, :] = gen
        base_ref[part, :] = gen - demand_ref[part, :]
        hedged_ref[part, :] = hedged
        sums_ref[h : h + 1, :] = jnp.sum(hedged, axis=0, keepdims=True)
    near = jnp.where(early, start_ref[hours - 1 : hours, :], start_ref[0:1, :])
    ramp = excess(beyond - near, limit) + excess(beyond - edge_ref[at + 1 : at + 2, :], limit)
    _, hedged = step(beyond, edge_ref[scens:at, :], back_ref[width : width + scens, :], ramp)
    sums_ref[hours : hours + 1, :] = jnp.sum(hedged, axis=0, keepdims=True)
    spare = sums_ref.shape[0] - hours - 1
    sums_ref[hours + 1 :, :] = jnp.zeros((spare, buses), jnp.float32)


def tie_kernel(blocks, base_ref, spread_ref, rows_ref, weight_ref, *refs):
    own_refs, refs = refs[:blocks], refs[blocks:]
    peer_refs, refs = refs[:blocks], refs[blocks:]
    next_refs, (inject_ref, mine_ref, theirs_ref) = refs[:blocks], refs[blocks:]

    weight = weight_ref[:, 0:1]
    own = jnp.concatenate([ref[...] for ref in own_refs], axis=0)
    peer = jnp.concatenate([ref[...] for ref in peer_refs], axis=0)
    est_mine = weight * own
    est_theirs = -weight * peer
    flow = (est_mine + est_theirs) * 0.5
    dual_mine = est_mine - flow
    dual_theirs = est_theirs - flow
    spread = spread_ref[...]
    add = lax.dot_general(
        split_3(flow),
        jnp.concatenate([spread, spread, spread], axis=0),
        CONTRACT_FIRST,
        preferred_element_type=jnp.float32,
    )
    inject_ref[...] = (base_ref[...] + add).astype(jnp.bfloat16)

    own_next = lax.dot_general(
        rows_ref[...], inject_ref[...], CONTRACT_LAST, preferred_element_type=jnp.float32
    )
    for i in range(blocks):
        next_refs[i][...] = own_next[i * CAP : (i + 1) * CAP, :]
    mine_ref[...] = weight * (own_next - peer) + dual_mine
    theirs_ref[...] = weight * own + dual_theirs


def second_kernel(
    terms,
    scen_total,
    ptdf_ref,
    inject_ref,
    gen_ref,
    hedged_ref,
    cost_ref,
    max_ref,
    limit_ref,
    line_max_ref,
    *refs,
):
    sum_refs, refs = refs[:terms], refs[terms:]
    (hedged_out_ref, sums_out_ref, over_ref, back_ref, mean_ref, padded_ref, excess_ref, ramp_ref) = refs
    hours, buses = sums_out_ref.shape
    width = inject_ref.shape[0]
    scens = width // hours
    first_hour = lax.axis_index("hour") * hours

    back_ref[...] = line_work(inject_ref, ptdf_ref, line_max_ref, over_ref)
    mean_ref[...] = functools.reduce(jnp.add, [ref[...] for ref in sum_refs]) / scen_total
    write_ramp(
        mean_ref, mean_ref[hours : hours + 1, :], limit_ref[...], first_hour, padded_ref, excess_ref, ramp_ref
    )
    cost = cost_ref[...]
    top = max_ref[...]
    for h in range(hours):
        part = slice(h * scens, (h + 1) * scens)
        mean = mean_ref[h : h + 1, :]
        gen = gen_ref[part, :]
        hedge = hedged_ref[part, :] - mean
        grad = cost + back_ref[part, :] + (gen - mean + hedge) + ramp_ref[h : h + 1, :]
        gen = jnp.clip(gen - STEP_SIZE * grad, 0.0, top)
        hedged = gen + hedge
        hedged_out_ref[part, :] = hedged
        sums_out_ref[h : h + 1, :] = jnp.sum(hedged, axis=0, keepdims=True)


def flow_kernel(blocks, partner_of, *refs):
    peer_refs, (weight_ref, mine_ref, theirs_ref, tie_ref) = refs[:blocks], refs[blocks:]
    here = lax.axis_index("area")
    slots = tie_ref.shape[1]
    places = []
    for i in range(blocks):
        low, _, block, in_reach = block_facts(here, partner_of(here, i))
        first = block * CAP + jnp.where(low, 0, REACH * CAP)
        hit = lax.broadcasted_iota(jnp.int32, (CAP, slots), 1) == (
            first + lax.broadcasted_iota(jnp.int32, (CAP, slots), 0)
        )
        places.append(jnp.where(hit & in_reach, 1.0, 0.0).astype(jnp.bfloat16))
    peer = jnp.concatenate([ref[...] for ref in peer_refs], axis=0)
    flow = (mine_ref[...] + (theirs_ref[...] - weight_ref[:, 0:1] * peer)) * 0.5
    tie_ref[...] = lax.dot_general(
        split_3(flow),
        jnp.concatenate(places * 3, axis=0),
        CONTRACT_FIRST,
        preferred_element_type=jnp.float32,
    )


def agree_kernel(scen_total, hedged_ref, *refs):
    sum_refs, (mean_ref, hedge_ref) = refs[:-2], refs[-2:]
    hours = mean_ref.shape[0]
    scens = hedged_ref.shape[0] // hours
    mean_ref[...] = functools.reduce(jnp.add, [ref[...] for ref in sum_refs]) / scen_total
    for h in range(hours):
        part = slice(h * scens, (h + 1) * scens)
        hedge_ref[part, :] = hedged_ref[part, :] - mean_ref[h : h + 1, :]


def call(kernel, name, args, outs, scratch, flops, in_place=()):
    size = sum(x.size * x.dtype.itemsize for x in list(args) + list(outs))
    return pl.pallas_call(
        kernel,
        name=name,
        out_shape=outs,
        in_specs=[ANY if i in in_place else VMEM for i in range(len(args))],
        out_specs=[VMEM] * len(outs),
        scratch_shapes=scratch,
        compiler_params=pltpu.CompilerParams(vmem_limit_bytes=32 * 1024 * 1024),
        cost_estimate=pl.CostEstimate(flops=flops, bytes_accessed=size, transcendentals=0),
    )(*(pltpu.with_memory_space_constraint(x, pltpu.HBM) if i in in_place else x for i, x in enumerate(args)))


def per_device(
    ptdf,
    angle_sens,
    demand,
    gen_start,
    hedge_dual,
    gen_cost,
    gen_max,
    gen_ramp,
    line_max,
    tie_count,
    tie_low_bus,
    tie_high_bus,
    tie_susc,
):
    hours, scens, buses = demand.shape
    lines = ptdf.shape[0]
    width = hours * scens
    areas = lax.axis_size("area")
    n_scen = lax.axis_size("scen")
    assert lax.axis_size("hour") == 2 and hours >= 2
    scen_total = scens * n_scen
    blocks, partner_of, from_partners = partner_plan(areas)
    slots = blocks * CAP
    sum_rows = 8 * (hours // 8 + 1)
    f32, bf16 = jnp.float32, jnp.bfloat16

    def shape(*dims, dtype=f32):
        return jax.ShapeDtypeStruct(dims, dtype)

    def over_scens(sums):
        if n_scen == 2:
            return [sums, lax.ppermute(sums, "scen", [(0, 1), (1, 0)])]
        return [lax.psum(sums, "scen")]

    work = 4 * width * lines * buses

    def step_scratch(rows):
        return [
            pltpu.VMEM((rows, buses), bf16),
            pltpu.VMEM((rows, lines), bf16),
            pltpu.VMEM((rows, buses), f32),
        ]

    ramp_scratch = [
        pltpu.VMEM((hours + 4, buses), f32),
        pltpu.VMEM((hours + 4, buses), f32),
        pltpu.VMEM((hours, buses), f32),
    ]
    tables = (tie_count, tie_low_bus, tie_high_bus, tie_susc)
    vectors = [x.reshape(1, -1) for x in (gen_cost, gen_max, gen_ramp, line_max)]
    hedge = hedge_dual.reshape(width, buses)
    made = call(
        functools.partial(angle_kernel, blocks, partner_of),
        "angles",
        (
            angle_sens,
            demand.reshape(width, buses),
            hedge,
            gen_start,
            *vectors,
            *tables,
        ),
        [shape(CAP, width)] * blocks
        + [
            shape(2 * scens + 8, buses),
            shape(width, buses, dtype=bf16),
            shape(slots, buses, dtype=bf16),
            shape(slots, buses, dtype=bf16),
            shape(slots, 128),
            shape(width, buses),
            shape(hours, buses),
            shape(1, buses),
            shape(1, buses),
            shape(1, buses),
            shape(1, lines),
        ],
        [pltpu.VMEM(x.shape, x.dtype) for x in (angle_sens, *tables)]
        + [pltpu.VMEM((slots, buses), bf16), pltpu.SemaphoreType.DMA((12,))],
        BETWEEN,
        range(12),
    )
    own = made[:blocks]
    edge, inject, spread, rows, weight, load, start = made[blocks : blocks + 7]
    cost, top, limit, line_top = made[blocks + 7 :]
    edge = lax.ppermute(edge, "hour", [(0, 1), (1, 0)])
    peer = from_partners(own)
    gen, base, hedged, sums = call(
        first_kernel,
        "first",
        (ptdf, inject, load, hedge, start, edge, cost, top, limit, line_top),
        [
            shape(width, buses),
            shape(width, buses),
            shape(width, buses),
            shape(sum_rows, buses),
        ],
        step_scratch(width + scens) + ramp_scratch,
        work,
    )
    sum_terms = over_scens(sums)
    terms = len(sum_terms)
    tied = call(
        functools.partial(tie_kernel, blocks),
        "ties",
        (base, spread, rows, weight, *own, *peer),
        [shape(CAP, width)] * blocks
        + [shape(width, buses, dtype=bf16), shape(slots, width), shape(slots, width)],
        [],
        BETWEEN,
    )
    own = tied[:blocks]
    inject, mine, theirs = tied[blocks:]
    hedged, sums = call(
        functools.partial(second_kernel, terms, scen_total),
        "second",
        (ptdf, inject, gen, hedged, cost, top, limit, line_top, *sum_terms),
        [shape(width, buses), shape(hours, buses)],
        step_scratch(width)[1:] + [pltpu.VMEM((sum_rows, buses), f32)] + ramp_scratch,
        work,
    )
    peer = from_partners(own)
    sum_terms = over_scens(sums)
    (tie_flow,) = call(
        functools.partial(flow_kernel, blocks, partner_of),
        "flows",
        (*peer, weight, mine, theirs),
        [shape(width, 2 * REACH * CAP)],
        [],
        BETWEEN,
    )
    sum_terms, tie_flow = lax.optimization_barrier((sum_terms, tie_flow))
    gen_mean, hedge = call(
        functools.partial(agree_kernel, scen_total),
        "agree",
        (hedged, *sum_terms),
        [shape(hours, buses), shape(width, buses)],
        [],
        2 * width * buses,
    )
    return (
        gen_mean,
        hedge.reshape(hours, scens, buses),
        tie_flow.reshape(hours, scens, 2 * REACH * CAP),
    )


def solution(mesh):
    return jax.shard_map(
        per_device,
        mesh=mesh,
        in_specs=(
            P(("group", "area"), None),
            P(("group", "area"), None),
            P(("group", "hour"), "scen", "area"),
            P(("group", "hour"), "area"),
            P(("group", "hour"), "scen", "area"),
            P(("group", "area")),
            P(("group", "area")),
            P(("group", "area")),
            P(("group", "area")),
            P("group", None),
            P("group", None),
            P("group", None),
            P("group", None),
        ),
        out_specs=(
            P(("group", "hour"), "area"),
            P(("group", "hour"), "scen", "area"),
            P(("group", "hour"), "scen", "area"),
        ),
        check_vma=False,
    )
```

```python
import functools

import jax
import jax.numpy as jnp
from jax import lax
from jax.experimental import pallas as pl
from jax.experimental.pallas import tpu as pltpu
from jax.sharding import PartitionSpec as P

HOURS = 24
REACH = 4
CAP = 16

STEP_SIZE = 0.5
LINE_CHUNK = 512
BETWEEN = 20_000_000_000

CONTRACT_LAST = (((1,), (1,)), ((), ()))
CONTRACT_FIRST = (((0,), (0,)), ((), ()))
VMEM = pl.BlockSpec(memory_space=pltpu.VMEM)
ANY = pl.BlockSpec(memory_space=pltpu.HBM)


def partner_plan(areas):
    if areas & (areas - 1) == 0 and areas <= REACH + 1:
        flips = [*range(2, areas), 1]

        def by_flip(parts):
            return [
                lax.ppermute(part, "area", [(a, a ^ f) for a in range(areas)]) for part, f in zip(parts, flips)
            ]

        return len(flips), lambda here, i: here ^ flips[i], by_flip
    reach = min(REACH, areas - 1)
    shifts = sorted({s % areas for d in range(1, reach + 1) for s in (d, -d)})

    def by_shift(parts):
        sent = [
            lax.ppermute(part, "area", [(a, (a + s) % areas) for a in range(areas)])
            for part, s in zip(parts, shifts)
        ]
        return [sent[shifts.index(areas - s)] for s in shifts]

    return len(shifts), lambda here, i: lax.rem(here + shifts[i], areas), by_shift


def block_facts(here, partner):
    low = partner > here
    distance = jnp.abs(partner - here)
    block = jnp.clip(distance - 1, 0, REACH - 1)
    in_reach = (distance >= 1) & (distance <= REACH)
    return low, jnp.minimum(here, partner), block, in_reach


def split_3(x):
    high = x.astype(jnp.bfloat16)
    rest = x - high.astype(jnp.float32)
    middle = rest.astype(jnp.bfloat16)
    rest = rest - middle.astype(jnp.float32)
    return jnp.concatenate([high, middle, rest.astype(jnp.bfloat16)], axis=0)


def excess(diffs, limit):
    return diffs - jnp.clip(diffs, -limit, limit)


def write_ramp(mean_ref, beyond, limit, first_hour, padded_ref, excess_ref, ramp_ref):
    hours = ramp_ref.shape[0]
    padded_ref[0:1, :] = beyond
    padded_ref[1 : hours + 1, :] = mean_ref[0:hours, :]
    padded_ref[hours + 1 : hours + 2, :] = beyond
    diffs = padded_ref[1 : hours + 2, :] - padded_ref[0 : hours + 1, :]
    ids = first_hour + lax.broadcasted_iota(jnp.int32, diffs.shape, 0)
    valid = (ids >= 1) & (ids <= HOURS - 1)
    excess_ref[0 : hours + 1, :] = jnp.where(valid, excess(diffs, limit), 0.0)
    ramp_ref[...] = excess_ref[0:hours, :] - excess_ref[1 : hours + 1, :]


def line_work(inject_ref, ptdf_ref, line_max_ref, over_ref):
    inject = inject_ref[...]
    lines = ptdf_ref.shape[0]
    for at in range(0, lines, LINE_CHUNK):
        part = slice(at, at + LINE_CHUNK)
        flows = lax.dot_general(
            inject, ptdf_ref[part, :], CONTRACT_LAST, preferred_element_type=jnp.float32
        )
        limit = line_max_ref[:, part]
        over_ref[:, part] = (flows - jnp.clip(flows, -limit, limit)).astype(jnp.bfloat16)
    return jnp.dot(over_ref[...], ptdf_ref[...], preferred_element_type=jnp.float32)


def angle_kernel(
    blocks,
    partner_of,
    sens_in,
    demand_in,
    hedge_in,
    start_in,
    cost_in,
    max_in,
    limit_in,
    line_max_in,
    count_in,
    low_bus_in,
    high_bus_in,
    susc_in,
    *refs,
):
    own_refs, refs = refs[:blocks], refs[blocks:]
    (
        edge_ref,
        inject_ref,
        spread_ref,
        rows_ref,
        weight_ref,
        demand_ref,
        start_ref,
        cost_ref,
        max_ref,
        limit_ref,
        line_max_ref,
        sens_ref,
        count_ref,
        low_bus_ref,
        high_bus_ref,
        susc_ref,
        onehot_ref,
        copy_sems,
    ) = refs
    hours, buses = start_ref.shape
    scens = demand_ref.shape[0] // hours
    here = lax.axis_index("area")
    early = lax.axis_index("hour") == 0
    last = (hours - 1) * scens
    edge_rows = pl.ds(pl.multiple_of((1 - lax.axis_index("hour")) * last, scens), scens)

    pairs = (
        (count_in, count_ref),
        (low_bus_in, low_bus_ref),
        (high_bus_in, high_bus_ref),
        (susc_in, susc_ref),
        (start_in, start_ref),
        (demand_in, demand_ref),
        (sens_in, sens_ref),
        (hedge_in.at[edge_rows], edge_ref.at[pl.ds(scens, scens)]),
        (cost_in, cost_ref),
        (max_in, max_ref),
        (limit_in, limit_ref),
        (line_max_in, line_max_ref),
    )
    copies = [pltpu.make_async_copy(src, dst, copy_sems.at[i]) for i, (src, dst) in enumerate(pairs)]
    for copy in copies:
        copy.start()

    for copy in copies[:4]:
        copy.wait()
    for i in range(blocks):
        partner = partner_of(here, i)
        low, row, block, in_reach = block_facts(here, partner)
        slots = slice(i * CAP, (i + 1) * CAP)
        pick = lax.broadcasted_iota(jnp.int32, (CAP, REACH * CAP), 1) == (
            block * CAP + lax.broadcasted_iota(jnp.int32, (CAP, REACH * CAP), 0)
        )
        table_row = pl.ds(row, 1)
        bus_row = jnp.where(low, low_bus_ref[table_row, :], high_bus_ref[table_row, :])
        bus = jnp.sum(jnp.where(pick, bus_row.astype(jnp.float32), 0.0), axis=1, keepdims=True)
        susc = jnp.sum(jnp.where(pick, susc_ref[table_row, :], 0.0), axis=1, keepdims=True)
        count_row = count_ref[table_row, :].astype(jnp.float32)
        is_block = lax.broadcasted_iota(jnp.int32, (CAP, REACH), 1) == block
        count = jnp.sum(jnp.where(is_block, count_row, 0.0), axis=1, keepdims=True)
        slot_ids = lax.broadcasted_iota(jnp.int32, (CAP, 1), 0).astype(jnp.float32)
        live = jnp.where((slot_ids < count) & in_reach, 1.0, 0.0)
        sign = jnp.where(low, 1.0, -1.0)
        bus_ids = lax.broadcasted_iota(jnp.int32, (CAP, buses), 1).astype(jnp.float32)
        onehot = jnp.where(bus_ids == bus, live, 0.0)
        onehot_ref[slots, :] = onehot.astype(jnp.bfloat16)
        spread_ref[slots, :] = (-sign * onehot).astype(jnp.bfloat16)
        weight_ref[slots, :] = jnp.broadcast_to(live * sign * susc, (CAP, 128))

    for copy in copies[4:7]:
        copy.wait()
    for h in range(hours):
        part = slice(h * scens, (h + 1) * scens)
        inject_ref[part, :] = (start_ref[h : h + 1, :] - demand_ref[part, :]).astype(jnp.bfloat16)
    rows = jnp.dot(onehot_ref[...], sens_ref[...], preferred_element_type=jnp.float32)
    rows_ref[...] = rows.astype(jnp.bfloat16)
    own = lax.dot_general(
        rows_ref[...], inject_ref[...], CONTRACT_LAST, preferred_element_type=jnp.float32
    )
    for i in range(blocks):
        own_refs[i][...] = own[i * CAP : (i + 1) * CAP, :]

    for copy in copies[7:]:
        copy.wait()
    edge_ref[0:scens, :] = jnp.where(early, demand_ref[last:, :], demand_ref[0:scens, :])
    at = 2 * scens
    edge_ref[at : at + 1, :] = jnp.where(early, start_ref[hours - 1 : hours, :], start_ref[0:1, :])
    edge_ref[at + 1 : at + 2, :] = jnp.where(
        early, start_ref[hours - 2 : hours - 1, :], start_ref[1:2, :]
    )


def first_kernel(
    ptdf_ref,
    own_inject_ref,
    demand_ref,
    hedge_ref,
    start_ref,
    edge_ref,
    cost_ref,
    max_ref,
    limit_ref,
    line_max_ref,
    gen_ref,
    base_ref,
    hedged_ref,
    sums_ref,
    inject_ref,
    over_ref,
    back_ref,
    padded_ref,
    excess_ref,
    ramp_ref,
):
    hours, buses = start_ref.shape
    width = demand_ref.shape[0]
    scens = width // hours
    at = 2 * scens
    early = lax.axis_index("hour") == 0
    first_hour = lax.axis_index("hour") * hours
    beyond = edge_ref[at : at + 1, :]
    limit = limit_ref[...]
    cost = cost_ref[...]
    top = max_ref[...]

    inject_ref[0:width, :] = own_inject_ref[...]
    inject_ref[width : width + scens, :] = (beyond - edge_ref[0:scens, :]).astype(jnp.bfloat16)
    back_ref[...] = line_work(inject_ref, ptdf_ref, line_max_ref, over_ref)
    write_ramp(start_ref, beyond, limit, first_hour, padded_ref, excess_ref, ramp_ref)

    def step(mean, hedge, back, ramp):
        grad = cost + back + (mean - mean + hedge) + ramp
        gen = jnp.clip(mean - STEP_SIZE * grad, 0.0, top)
        return gen, gen + hedge

    for h in range(hours):
        part = slice(h * scens, (h + 1) * scens)
        mean = start_ref[h : h + 1, :]
        gen, hedged = step(mean, hedge_ref[part, :], back_ref[part, :], ramp_ref[h : h + 1, :])
        gen_ref[part, :] = gen
        base_ref[part, :] = gen - demand_ref[part, :]
        hedged_ref[part, :] = hedged
        sums_ref[h : h + 1, :] = jnp.sum(hedged, axis=0, keepdims=True)
    near = jnp.where(early, start_ref[hours - 1 : hours, :], start_ref[0:1, :])
    ramp = excess(beyond - near, limit) + excess(beyond - edge_ref[at + 1 : at + 2, :], limit)
    _, hedged = step(beyond, edge_ref[scens:at, :], back_ref[width : width + scens, :], ramp)
    sums_ref[hours : hours + 1, :] = jnp.sum(hedged, axis=0, keepdims=True)
    spare = sums_ref.shape[0] - hours - 1
    sums_ref[hours + 1 :, :] = jnp.zeros((spare, buses), jnp.float32)


def tie_kernel(blocks, base_ref, spread_ref, rows_ref, weight_ref, *refs):
    own_refs, refs = refs[:blocks], refs[blocks:]
    peer_refs, refs = refs[:blocks], refs[blocks:]
    next_refs, (inject_ref, mine_ref, theirs_ref) = refs[:blocks], refs[blocks:]

    weight = weight_ref[:, 0:1]
    own = jnp.concatenate([ref[...] for ref in own_refs], axis=0)
    peer = jnp.concatenate([ref[...] for ref in peer_refs], axis=0)
    est_mine = weight * own
    est_theirs = -weight * peer
    flow = (est_mine + est_theirs) * 0.5
    dual_mine = est_mine - flow
    dual_theirs = est_theirs - flow
    spread = spread_ref[...]
    add = lax.dot_general(
        split_3(flow),
        jnp.concatenate([spread, spread, spread], axis=0),
        CONTRACT_FIRST,
        preferred_element_type=jnp.float32,
    )
    inject_ref[...] = (base_ref[...] + add).astype(jnp.bfloat16)

    own_next = lax.dot_general(
        rows_ref[...], inject_ref[...], CONTRACT_LAST, preferred_element_type=jnp.float32
    )
    for i in range(blocks):
        next_refs[i][...] = own_next[i * CAP : (i + 1) * CAP, :]
    mine_ref[...] = weight * (own_next - peer) + dual_mine
    theirs_ref[...] = weight * own + dual_theirs


def second_kernel(
    terms,
    scen_total,
    ptdf_ref,
    inject_ref,
    gen_ref,
    hedged_ref,
    cost_ref,
    max_ref,
    limit_ref,
    line_max_ref,
    *refs,
):
    sum_refs, refs = refs[:terms], refs[terms:]
    (hedged_out_ref, sums_out_ref, over_ref, back_ref, mean_ref, padded_ref, excess_ref, ramp_ref) = refs
    hours, buses = sums_out_ref.shape
    width = inject_ref.shape[0]
    scens = width // hours
    first_hour = lax.axis_index("hour") * hours

    back_ref[...] = line_work(inject_ref, ptdf_ref, line_max_ref, over_ref)
    mean_ref[...] = functools.reduce(jnp.add, [ref[...] for ref in sum_refs]) / scen_total
    write_ramp(
        mean_ref, mean_ref[hours : hours + 1, :], limit_ref[...], first_hour, padded_ref, excess_ref, ramp_ref
    )
    cost = cost_ref[...]
    top = max_ref[...]
    for h in range(hours):
        part = slice(h * scens, (h + 1) * scens)
        mean = mean_ref[h : h + 1, :]
        gen = gen_ref[part, :]
        hedge = hedged_ref[part, :] - mean
        grad = cost + back_ref[part, :] + (gen - mean + hedge) + ramp_ref[h : h + 1, :]
        gen = jnp.clip(gen - STEP_SIZE * grad, 0.0, top)
        hedged = gen + hedge
        hedged_out_ref[part, :] = hedged
        sums_out_ref[h : h + 1, :] = jnp.sum(hedged, axis=0, keepdims=True)


def flow_kernel(blocks, partner_of, *refs):
    peer_refs, (weight_ref, mine_ref, theirs_ref, tie_ref) = refs[:blocks], refs[blocks:]
    here = lax.axis_index("area")
    slots = tie_ref.shape[1]
    places = []
    for i in range(blocks):
        low, _, block, in_reach = block_facts(here, partner_of(here, i))
        first = block * CAP + jnp.where(low, 0, REACH * CAP)
        hit = lax.broadcasted_iota(jnp.int32, (CAP, slots), 1) == (
            first + lax.broadcasted_iota(jnp.int32, (CAP, slots), 0)
        )
        places.append(jnp.where(hit & in_reach, 1.0, 0.0).astype(jnp.bfloat16))
    peer = jnp.concatenate([ref[...] for ref in peer_refs], axis=0)
    flow = (mine_ref[...] + (theirs_ref[...] - weight_ref[:, 0:1] * peer)) * 0.5
    tie_ref[...] = lax.dot_general(
        split_3(flow),
        jnp.concatenate(places * 3, axis=0),
        CONTRACT_FIRST,
        preferred_element_type=jnp.float32,
    )


def agree_kernel(scen_total, hedged_ref, *refs):
    sum_refs, (mean_ref, hedge_ref) = refs[:-2], refs[-2:]
    hours = mean_ref.shape[0]
    scens = hedged_ref.shape[0] // hours
    mean_ref[...] = functools.reduce(jnp.add, [ref[...] for ref in sum_refs]) / scen_total
    for h in range(hours):
        part = slice(h * scens, (h + 1) * scens)
        hedge_ref[part, :] = hedged_ref[part, :] - mean_ref[h : h + 1, :]


def call(kernel, name, args, outs, scratch, flops, in_place=()):
    size = sum(x.size * x.dtype.itemsize for x in list(args) + list(outs))
    return pl.pallas_call(
        kernel,
        name=name,
        out_shape=outs,
        in_specs=[ANY if i in in_place else VMEM for i in range(len(args))],
        out_specs=[VMEM] * len(outs),
        scratch_shapes=scratch,
        compiler_params=pltpu.CompilerParams(vmem_limit_bytes=32 * 1024 * 1024),
        cost_estimate=pl.CostEstimate(flops=flops, bytes_accessed=size, transcendentals=0),
    )(*(pltpu.with_memory_space_constraint(x, pltpu.HBM) if i in in_place else x for i, x in enumerate(args)))


def per_device(
    ptdf,
    angle_sens,
    demand,
    gen_start,
    hedge_dual,
    gen_cost,
    gen_max,
    gen_ramp,
    line_max,
    tie_count,
    tie_low_bus,
    tie_high_bus,
    tie_susc,
):
    hours, scens, buses = demand.shape
    lines = ptdf.shape[0]
    width = hours * scens
    areas = lax.axis_size("area")
    n_scen = lax.axis_size("scen")
    assert lax.axis_size("hour") == 2 and hours >= 2
    scen_total = scens * n_scen
    blocks, partner_of, from_partners = partner_plan(areas)
    slots = blocks * CAP
    sum_rows = 8 * (hours // 8 + 1)
    f32, bf16 = jnp.float32, jnp.bfloat16

    def shape(*dims, dtype=f32):
        return jax.ShapeDtypeStruct(dims, dtype)

    def over_scens(sums):
        if n_scen == 2:
            return [sums, lax.ppermute(sums, "scen", [(0, 1), (1, 0)])]
        return [lax.psum(sums, "scen")]

    work = 4 * width * lines * buses

    def step_scratch(rows):
        return [
            pltpu.VMEM((rows, buses), bf16),
            pltpu.VMEM((rows, lines), bf16),
            pltpu.VMEM((rows, buses), f32),
        ]

    ramp_scratch = [
        pltpu.VMEM((hours + 4, buses), f32),
        pltpu.VMEM((hours + 4, buses), f32),
        pltpu.VMEM((hours, buses), f32),
    ]
    tables = (tie_count, tie_low_bus, tie_high_bus, tie_susc)
    vectors = [x.reshape(1, -1) for x in (gen_cost, gen_max, gen_ramp, line_max)]
    hedge = hedge_dual.reshape(width, buses)
    made = call(
        functools.partial(angle_kernel, blocks, partner_of),
        "angles",
        (
            angle_sens,
            demand.reshape(width, buses),
            hedge,
            gen_start,
            *vectors,
            *tables,
        ),
        [shape(CAP, width)] * blocks
        + [
            shape(2 * scens + 8, buses),
            shape(width, buses, dtype=bf16),
            shape(slots, buses, dtype=bf16),
            shape(slots, buses, dtype=bf16),
            shape(slots, 128),
            shape(width, buses),
            shape(hours, buses),
            shape(1, buses),
            shape(1, buses),
            shape(1, buses),
            shape(1, lines),
        ],
        [pltpu.VMEM(x.shape, x.dtype) for x in (angle_sens, *tables)]
        + [pltpu.VMEM((slots, buses), bf16), pltpu.SemaphoreType.DMA((12,))],
        BETWEEN,
        range(12),
    )
    own = made[:blocks]
    edge, inject, spread, rows, weight, load, start = made[blocks : blocks + 7]
    cost, top, limit, line_top = made[blocks + 7 :]
    edge = lax.ppermute(edge, "hour", [(0, 1), (1, 0)])
    peer = from_partners(own)
    gen, base, hedged, sums = call(
        first_kernel,
        "first",
        (ptdf, inject, load, hedge, start, edge, cost, top, limit, line_top),
        [
            shape(width, buses),
            shape(width, buses),
            shape(width, buses),
            shape(sum_rows, buses),
        ],
        step_scratch(width + scens) + ramp_scratch,
        work,
    )
    sum_terms = over_scens(sums)
    terms = len(sum_terms)
    tied = call(
        functools.partial(tie_kernel, blocks),
        "ties",
        (base, spread, rows, weight, *own, *peer),
        [shape(CAP, width)] * blocks
        + [shape(width, buses, dtype=bf16), shape(slots, width), shape(slots, width)],
        [],
        BETWEEN,
    )
    own = tied[:blocks]
    inject, mine, theirs = tied[blocks:]
    hedged, sums = call(
        functools.partial(second_kernel, terms, scen_total),
        "second",
        (ptdf, inject, gen, hedged, cost, top, limit, line_top, *sum_terms),
        [shape(width, buses), shape(hours, buses)],
        step_scratch(width)[1:] + [pltpu.VMEM((sum_rows, buses), f32)] + ramp_scratch,
        work,
    )
    peer = from_partners(own)
    sum_terms = over_scens(sums)
    (tie_flow,) = call(
        functools.partial(flow_kernel, blocks, partner_of),
        "flows",
        (*peer, weight, mine, theirs),
        [shape(width, 2 * REACH * CAP)],
        [],
        BETWEEN,
    )
    sum_terms, tie_flow = lax.optimization_barrier((sum_terms, tie_flow))
    gen_mean, hedge = call(
        functools.partial(agree_kernel, scen_total),
        "agree",
        (hedged, *sum_terms),
        [shape(hours, buses), shape(width, buses)],
        [],
        2 * width * buses,
    )
    return (
        gen_mean,
        hedge.reshape(hours, scens, buses),
        tie_flow.reshape(hours, scens, 2 * REACH * CAP),
    )


def solution(mesh):
    return jax.shard_map(
        per_device,
        mesh=mesh,
        in_specs=(
            P(("group", "area"), None),
            P(("group", "area"), None),
            P(("group", "hour"), "scen", "area"),
            P(("group", "hour"), "area"),
            P(("group", "hour"), "scen", "area"),
            P(("group", "area")),
            P(("group", "area")),
            P(("group", "area")),
            P(("group", "area")),
            P("group", None),
            P("group", None),
            P("group", None),
            P("group", None),
        ),
        out_specs=(
            P(("group", "hour"), "area"),
            P(("group", "hour"), "scen", "area"),
            P(("group", "hour"), "scen", "area"),
        ),
        check_vma=False,
    )
```

```python
import functools

import jax
import jax.numpy as jnp
from jax import lax
from jax.experimental import pallas as pl
from jax.experimental.pallas import tpu as pltpu
from jax.sharding import PartitionSpec as P

HOURS = 24
REACH = 4
CAP = 16

STEP_SIZE = 0.5
LINE_CHUNK = 512
BETWEEN = 20_000_000_000

CONTRACT_LAST = (((1,), (1,)), ((), ()))
CONTRACT_FIRST = (((0,), (0,)), ((), ()))
VMEM = pl.BlockSpec(memory_space=pltpu.VMEM)
ANY = pl.BlockSpec(memory_space=pltpu.HBM)


def partner_plan(areas):
    if areas == 4:
        targets = ((3, 2, 0, 1), (2, 3, 1, 0), (1, 0, 3, 2))

        def partner_of(here, i):
            return sum(jnp.where(here == a, target, 0) for a, target in enumerate(targets[i]))

        def by_target(parts):
            out, back, pair = (
                lax.ppermute(part, "area", list(enumerate(target))) for part, target in zip(parts, targets)
            )
            return [back, out, pair]

        return len(targets), partner_of, by_target
    reach = min(REACH, areas - 1)
    shifts = sorted({s % areas for d in range(1, reach + 1) for s in (d, -d)})

    def by_shift(parts):
        sent = [
            lax.ppermute(part, "area", [(a, (a + s) % areas) for a in range(areas)])
            for part, s in zip(parts, shifts)
        ]
        return [sent[shifts.index(areas - s)] for s in shifts]

    return len(shifts), lambda here, i: lax.rem(here + shifts[i], areas), by_shift


def block_facts(here, partner):
    low = partner > here
    distance = jnp.abs(partner - here)
    block = jnp.clip(distance - 1, 0, REACH - 1)
    in_reach = (distance >= 1) & (distance <= REACH)
    return low, jnp.minimum(here, partner), block, in_reach


def split_3(x):
    high = x.astype(jnp.bfloat16)
    rest = x - high.astype(jnp.float32)
    middle = rest.astype(jnp.bfloat16)
    rest = rest - middle.astype(jnp.float32)
    return jnp.concatenate([high, middle, rest.astype(jnp.bfloat16)], axis=0)


def excess(diffs, limit):
    return diffs - jnp.clip(diffs, -limit, limit)


def write_ramp(mean_ref, beyond, limit, first_hour, padded_ref, excess_ref, ramp_ref):
    hours = ramp_ref.shape[0]
    padded_ref[0:1, :] = beyond
    padded_ref[1 : hours + 1, :] = mean_ref[0:hours, :]
    padded_ref[hours + 1 : hours + 2, :] = beyond
    diffs = padded_ref[1 : hours + 2, :] - padded_ref[0 : hours + 1, :]
    ids = first_hour + lax.broadcasted_iota(jnp.int32, diffs.shape, 0)
    valid = (ids >= 1) & (ids <= HOURS - 1)
    excess_ref[0 : hours + 1, :] = jnp.where(valid, excess(diffs, limit), 0.0)
    ramp_ref[...] = excess_ref[0:hours, :] - excess_ref[1 : hours + 1, :]


def line_work(inject_ref, ptdf_ref, line_max_ref, over_ref):
    inject = inject_ref[...]
    lines = ptdf_ref.shape[0]
    for at in range(0, lines, LINE_CHUNK):
        part = slice(at, at + LINE_CHUNK)
        flows = lax.dot_general(
            inject, ptdf_ref[part, :], CONTRACT_LAST, preferred_element_type=jnp.float32
        )
        limit = line_max_ref[:, part]
        over_ref[:, part] = (flows - jnp.clip(flows, -limit, limit)).astype(jnp.bfloat16)
    return jnp.dot(over_ref[...], ptdf_ref[...], preferred_element_type=jnp.float32)


def angle_kernel(
    blocks,
    partner_of,
    sens_in,
    demand_in,
    hedge_in,
    start_in,
    cost_in,
    max_in,
    limit_in,
    line_max_in,
    count_in,
    low_bus_in,
    high_bus_in,
    susc_in,
    *refs,
):
    own_refs, refs = refs[:blocks], refs[blocks:]
    (
        edge_ref,
        inject_ref,
        spread_ref,
        rows_ref,
        weight_ref,
        demand_ref,
        start_ref,
        cost_ref,
        max_ref,
        limit_ref,
        line_max_ref,
        sens_ref,
        count_ref,
        low_bus_ref,
        high_bus_ref,
        susc_ref,
        onehot_ref,
        copy_sems,
    ) = refs
    hours, buses = start_ref.shape
    scens = demand_ref.shape[0] // hours
    here = lax.axis_index("area")
    early = lax.axis_index("hour") == 0
    last = (hours - 1) * scens
    edge_rows = pl.ds(pl.multiple_of((1 - lax.axis_index("hour")) * last, scens), scens)

    pairs = (
        (count_in, count_ref),
        (low_bus_in, low_bus_ref),
        (high_bus_in, high_bus_ref),
        (susc_in, susc_ref),
        (start_in, start_ref),
        (demand_in, demand_ref),
        (sens_in, sens_ref),
        (hedge_in.at[edge_rows], edge_ref.at[pl.ds(scens, scens)]),
        (cost_in, cost_ref),
        (max_in, max_ref),
        (limit_in, limit_ref),
        (line_max_in, line_max_ref),
    )
    copies = [pltpu.make_async_copy(src, dst, copy_sems.at[i]) for i, (src, dst) in enumerate(pairs)]
    for copy in copies:
        copy.start()

    for copy in copies[:4]:
        copy.wait()
    for i in range(blocks):
        partner = partner_of(here, i)
        low, row, block, in_reach = block_facts(here, partner)
        slots = slice(i * CAP, (i + 1) * CAP)
        pick = lax.broadcasted_iota(jnp.int32, (CAP, REACH * CAP), 1) == (
            block * CAP + lax.broadcasted_iota(jnp.int32, (CAP, REACH * CAP), 0)
        )
        table_row = pl.ds(row, 1)
        bus_row = jnp.where(low, low_bus_ref[table_row, :], high_bus_ref[table_row, :])
        bus = jnp.sum(jnp.where(pick, bus_row.astype(jnp.float32), 0.0), axis=1, keepdims=True)
        susc = jnp.sum(jnp.where(pick, susc_ref[table_row, :], 0.0), axis=1, keepdims=True)
        count_row = count_ref[table_row, :].astype(jnp.float32)
        is_block = lax.broadcasted_iota(jnp.int32, (CAP, REACH), 1) == block
        count = jnp.sum(jnp.where(is_block, count_row, 0.0), axis=1, keepdims=True)
        slot_ids = lax.broadcasted_iota(jnp.int32, (CAP, 1), 0).astype(jnp.float32)
        live = jnp.where((slot_ids < count) & in_reach, 1.0, 0.0)
        sign = jnp.where(low, 1.0, -1.0)
        bus_ids = lax.broadcasted_iota(jnp.int32, (CAP, buses), 1).astype(jnp.float32)
        onehot = jnp.where(bus_ids == bus, live, 0.0)
        onehot_ref[slots, :] = onehot.astype(jnp.bfloat16)
        spread_ref[slots, :] = (-sign * onehot).astype(jnp.bfloat16)
        weight_ref[slots, :] = jnp.broadcast_to(live * sign * susc, (CAP, 128))

    for copy in copies[4:7]:
        copy.wait()
    for h in range(hours):
        part = slice(h * scens, (h + 1) * scens)
        inject_ref[part, :] = (start_ref[h : h + 1, :] - demand_ref[part, :]).astype(jnp.bfloat16)
    rows = jnp.dot(onehot_ref[...], sens_ref[...], preferred_element_type=jnp.float32)
    rows_ref[...] = rows.astype(jnp.bfloat16)
    own = lax.dot_general(
        rows_ref[...], inject_ref[...], CONTRACT_LAST, preferred_element_type=jnp.float32
    )
    for i in range(blocks):
        own_refs[i][...] = own[i * CAP : (i + 1) * CAP, :]

    for copy in copies[7:]:
        copy.wait()
    edge_ref[0:scens, :] = jnp.where(early, demand_ref[last:, :], demand_ref[0:scens, :])
    at = 2 * scens
    edge_ref[at : at + 1, :] = jnp.where(early, start_ref[hours - 1 : hours, :], start_ref[0:1, :])
    edge_ref[at + 1 : at + 2, :] = jnp.where(
        early, start_ref[hours - 2 : hours - 1, :], start_ref[1:2, :]
    )


def first_kernel(
    ptdf_ref,
    own_inject_ref,
    demand_ref,
    hedge_ref,
    start_ref,
    edge_ref,
    cost_ref,
    max_ref,
    limit_ref,
    line_max_ref,
    gen_ref,
    base_ref,
    hedged_ref,
    sums_ref,
    inject_ref,
    over_ref,
    back_ref,
    padded_ref,
    excess_ref,
    ramp_ref,
):
    hours, buses = start_ref.shape
    width = demand_ref.shape[0]
    scens = width // hours
    at = 2 * scens
    early = lax.axis_index("hour") == 0
    first_hour = lax.axis_index("hour") * hours
    beyond = edge_ref[at : at + 1, :]
    limit = limit_ref[...]
    cost = cost_ref[...]
    top = max_ref[...]

    inject_ref[0:width, :] = own_inject_ref[...]
    inject_ref[width : width + scens, :] = (beyond - edge_ref[0:scens, :]).astype(jnp.bfloat16)
    back_ref[...] = line_work(inject_ref, ptdf_ref, line_max_ref, over_ref)
    write_ramp(start_ref, beyond, limit, first_hour, padded_ref, excess_ref, ramp_ref)

    def step(mean, hedge, back, ramp):
        grad = cost + back + (mean - mean + hedge) + ramp
        gen = jnp.clip(mean - STEP_SIZE * grad, 0.0, top)
        return gen, gen + hedge

    for h in range(hours):
        part = slice(h * scens, (h + 1) * scens)
        mean = start_ref[h : h + 1, :]
        gen, hedged = step(mean, hedge_ref[part, :], back_ref[part, :], ramp_ref[h : h + 1, :])
        gen_ref[part, :] = gen
        base_ref[part, :] = gen - demand_ref[part, :]
        hedged_ref[part, :] = hedged
        sums_ref[h : h + 1, :] = jnp.sum(hedged, axis=0, keepdims=True)
    near = jnp.where(early, start_ref[hours - 1 : hours, :], start_ref[0:1, :])
    ramp = excess(beyond - near, limit) + excess(beyond - edge_ref[at + 1 : at + 2, :], limit)
    _, hedged = step(beyond, edge_ref[scens:at, :], back_ref[width : width + scens, :], ramp)
    sums_ref[hours : hours + 1, :] = jnp.sum(hedged, axis=0, keepdims=True)
    spare = sums_ref.shape[0] - hours - 1
    sums_ref[hours + 1 :, :] = jnp.zeros((spare, buses), jnp.float32)


def tie_kernel(blocks, base_ref, spread_ref, rows_ref, weight_ref, *refs):
    own_refs, refs = refs[:blocks], refs[blocks:]
    peer_refs, refs = refs[:blocks], refs[blocks:]
    next_refs, (inject_ref, mine_ref, theirs_ref) = refs[:blocks], refs[blocks:]

    weight = weight_ref[:, 0:1]
    own = jnp.concatenate([ref[...] for ref in own_refs], axis=0)
    peer = jnp.concatenate([ref[...] for ref in peer_refs], axis=0)
    est_mine = weight * own
    est_theirs = -weight * peer
    flow = (est_mine + est_theirs) * 0.5
    dual_mine = est_mine - flow
    dual_theirs = est_theirs - flow
    spread = spread_ref[...]
    add = lax.dot_general(
        split_3(flow),
        jnp.concatenate([spread, spread, spread], axis=0),
        CONTRACT_FIRST,
        preferred_element_type=jnp.float32,
    )
    inject_ref[...] = (base_ref[...] + add).astype(jnp.bfloat16)

    own_next = lax.dot_general(
        rows_ref[...], inject_ref[...], CONTRACT_LAST, preferred_element_type=jnp.float32
    )
    for i in range(blocks):
        next_refs[i][...] = own_next[i * CAP : (i + 1) * CAP, :]
    mine_ref[...] = weight * (own_next - peer) + dual_mine
    theirs_ref[...] = weight * own + dual_theirs


def second_kernel(
    terms,
    scen_total,
    ptdf_ref,
    inject_ref,
    gen_ref,
    hedged_ref,
    cost_ref,
    max_ref,
    limit_ref,
    line_max_ref,
    *refs,
):
    sum_refs, refs = refs[:terms], refs[terms:]
    (hedged_out_ref, sums_out_ref, over_ref, back_ref, mean_ref, padded_ref, excess_ref, ramp_ref) = refs
    hours, buses = sums_out_ref.shape
    width = inject_ref.shape[0]
    scens = width // hours
    first_hour = lax.axis_index("hour") * hours

    back_ref[...] = line_work(inject_ref, ptdf_ref, line_max_ref, over_ref)
    mean_ref[...] = functools.reduce(jnp.add, [ref[...] for ref in sum_refs]) / scen_total
    write_ramp(
        mean_ref, mean_ref[hours : hours + 1, :], limit_ref[...], first_hour, padded_ref, excess_ref, ramp_ref
    )
    cost = cost_ref[...]
    top = max_ref[...]
    for h in range(hours):
        part = slice(h * scens, (h + 1) * scens)
        mean = mean_ref[h : h + 1, :]
        gen = gen_ref[part, :]
        hedge = hedged_ref[part, :] - mean
        grad = cost + back_ref[part, :] + (gen - mean + hedge) + ramp_ref[h : h + 1, :]
        gen = jnp.clip(gen - STEP_SIZE * grad, 0.0, top)
        hedged = gen + hedge
        hedged_out_ref[part, :] = hedged
        sums_out_ref[h : h + 1, :] = jnp.sum(hedged, axis=0, keepdims=True)


def flow_kernel(blocks, partner_of, *refs):
    peer_refs, (weight_ref, mine_ref, theirs_ref, tie_ref) = refs[:blocks], refs[blocks:]
    here = lax.axis_index("area")
    slots = tie_ref.shape[1]
    places = []
    for i in range(blocks):
        low, _, block, in_reach = block_facts(here, partner_of(here, i))
        first = block * CAP + jnp.where(low, 0, REACH * CAP)
        hit = lax.broadcasted_iota(jnp.int32, (CAP, slots), 1) == (
            first + lax.broadcasted_iota(jnp.int32, (CAP, slots), 0)
        )
        places.append(jnp.where(hit & in_reach, 1.0, 0.0).astype(jnp.bfloat16))
    peer = jnp.concatenate([ref[...] for ref in peer_refs], axis=0)
    flow = (mine_ref[...] + (theirs_ref[...] - weight_ref[:, 0:1] * peer)) * 0.5
    tie_ref[...] = lax.dot_general(
        split_3(flow),
        jnp.concatenate(places * 3, axis=0),
        CONTRACT_FIRST,
        preferred_element_type=jnp.float32,
    )


def agree_kernel(scen_total, hedged_ref, *refs):
    sum_refs, (mean_ref, hedge_ref) = refs[:-2], refs[-2:]
    hours = mean_ref.shape[0]
    scens = hedged_ref.shape[0] // hours
    mean_ref[...] = functools.reduce(jnp.add, [ref[...] for ref in sum_refs]) / scen_total
    for h in range(hours):
        part = slice(h * scens, (h + 1) * scens)
        hedge_ref[part, :] = hedged_ref[part, :] - mean_ref[h : h + 1, :]


def call(kernel, name, args, outs, scratch, flops, in_place=()):
    size = sum(x.size * x.dtype.itemsize for x in list(args) + list(outs))
    return pl.pallas_call(
        kernel,
        name=name,
        out_shape=outs,
        in_specs=[ANY if i in in_place else VMEM for i in range(len(args))],
        out_specs=[VMEM] * len(outs),
        scratch_shapes=scratch,
        compiler_params=pltpu.CompilerParams(vmem_limit_bytes=32 * 1024 * 1024),
        cost_estimate=pl.CostEstimate(flops=flops, bytes_accessed=size, transcendentals=0),
    )(*(pltpu.with_memory_space_constraint(x, pltpu.HBM) if i in in_place else x for i, x in enumerate(args)))


def per_device(
    ptdf,
    angle_sens,
    demand,
    gen_start,
    hedge_dual,
    gen_cost,
    gen_max,
    gen_ramp,
    line_max,
    tie_count,
    tie_low_bus,
    tie_high_bus,
    tie_susc,
):
    hours, scens, buses = demand.shape
    lines = ptdf.shape[0]
    width = hours * scens
    areas = lax.axis_size("area")
    n_scen = lax.axis_size("scen")
    assert lax.axis_size("hour") == 2 and hours >= 2
    scen_total = scens * n_scen
    blocks, partner_of, from_partners = partner_plan(areas)
    slots = blocks * CAP
    sum_rows = 8 * (hours // 8 + 1)
    f32, bf16 = jnp.float32, jnp.bfloat16

    def shape(*dims, dtype=f32):
        return jax.ShapeDtypeStruct(dims, dtype)

    def over_scens(sums):
        if n_scen == 2:
            return [sums, lax.ppermute(sums, "scen", [(0, 1), (1, 0)])]
        return [lax.psum(sums, "scen")]

    work = 4 * width * lines * buses

    def step_scratch(rows):
        return [
            pltpu.VMEM((rows, buses), bf16),
            pltpu.VMEM((rows, lines), bf16),
            pltpu.VMEM((rows, buses), f32),
        ]

    ramp_scratch = [
        pltpu.VMEM((hours + 4, buses), f32),
        pltpu.VMEM((hours + 4, buses), f32),
        pltpu.VMEM((hours, buses), f32),
    ]
    tables = (tie_count, tie_low_bus, tie_high_bus, tie_susc)
    vectors = [x.reshape(1, -1) for x in (gen_cost, gen_max, gen_ramp, line_max)]
    hedge = hedge_dual.reshape(width, buses)
    made = call(
        functools.partial(angle_kernel, blocks, partner_of),
        "angles",
        (
            angle_sens,
            demand.reshape(width, buses),
            hedge,
            gen_start,
            *vectors,
            *tables,
        ),
        [shape(CAP, width)] * blocks
        + [
            shape(2 * scens + 8, buses),
            shape(width, buses, dtype=bf16),
            shape(slots, buses, dtype=bf16),
            shape(slots, buses, dtype=bf16),
            shape(slots, 128),
            shape(width, buses),
            shape(hours, buses),
            shape(1, buses),
            shape(1, buses),
            shape(1, buses),
            shape(1, lines),
        ],
        [pltpu.VMEM(x.shape, x.dtype) for x in (angle_sens, *tables)]
        + [pltpu.VMEM((slots, buses), bf16), pltpu.SemaphoreType.DMA((12,))],
        BETWEEN,
        range(12),
    )
    own = made[:blocks]
    edge, inject, spread, rows, weight, load, start = made[blocks : blocks + 7]
    cost, top, limit, line_top = made[blocks + 7 :]
    edge = lax.ppermute(edge, "hour", [(0, 1), (1, 0)])
    peer = from_partners(own)
    gen, base, hedged, sums = call(
        first_kernel,
        "first",
        (ptdf, inject, load, hedge, start, edge, cost, top, limit, line_top),
        [
            shape(width, buses),
            shape(width, buses),
            shape(width, buses),
            shape(sum_rows, buses),
        ],
        step_scratch(width + scens) + ramp_scratch,
        work,
    )
    sum_terms = over_scens(sums)
    terms = len(sum_terms)
    tied = call(
        functools.partial(tie_kernel, blocks),
        "ties",
        (base, spread, rows, weight, *own, *peer),
        [shape(CAP, width)] * blocks
        + [shape(width, buses, dtype=bf16), shape(slots, width), shape(slots, width)],
        [],
        BETWEEN,
    )
    own = tied[:blocks]
    inject, mine, theirs = tied[blocks:]
    hedged, sums = call(
        functools.partial(second_kernel, terms, scen_total),
        "second",
        (ptdf, inject, gen, hedged, cost, top, limit, line_top, *sum_terms),
        [shape(width, buses), shape(hours, buses)],
        step_scratch(width)[1:] + [pltpu.VMEM((sum_rows, buses), f32)] + ramp_scratch,
        work,
    )
    peer = from_partners(own)
    sum_terms = over_scens(sums)
    (tie_flow,) = call(
        functools.partial(flow_kernel, blocks, partner_of),
        "flows",
        (*peer, weight, mine, theirs),
        [shape(width, 2 * REACH * CAP)],
        [],
        BETWEEN,
    )
    sum_terms, tie_flow = lax.optimization_barrier((sum_terms, tie_flow))
    gen_mean, hedge = call(
        functools.partial(agree_kernel, scen_total),
        "agree",
        (hedged, *sum_terms),
        [shape(hours, buses), shape(width, buses)],
        [],
        2 * width * buses,
    )
    return (
        gen_mean,
        hedge.reshape(hours, scens, buses),
        tie_flow.reshape(hours, scens, 2 * REACH * CAP),
    )


def solution(mesh):
    return jax.shard_map(
        per_device,
        mesh=mesh,
        in_specs=(
            P(("group", "area"), None),
            P(("group", "area"), None),
            P(("group", "hour"), "scen", "area"),
            P(("group", "hour"), "area"),
            P(("group", "hour"), "scen", "area"),
            P(("group", "area")),
            P(("group", "area")),
            P(("group", "area")),
            P(("group", "area")),
            P("group", None),
            P("group", None),
            P("group", None),
            P("group", None),
        ),
        out_specs=(
            P(("group", "hour"), "area"),
            P(("group", "hour"), "scen", "area"),
            P(("group", "hour"), "scen", "area"),
        ),
        check_vma=False,
    )
```

```python
import functools

import jax
import jax.numpy as jnp
from jax import lax
from jax.experimental import pallas as pl
from jax.experimental.pallas import tpu as pltpu
from jax.sharding import PartitionSpec as P

HOURS = 24
REACH = 4
CAP = 16

STEP_SIZE = 0.5
LINE_CHUNK = 512
LANES = 128
OUT_HOURS = 3
BETWEEN = 20_000_000_000

CONTRACT_LAST = (((1,), (1,)), ((), ()))
CONTRACT_FIRST = (((0,), (0,)), ((), ()))
VMEM = pl.BlockSpec(memory_space=pltpu.VMEM)
ANY = pl.BlockSpec(memory_space=pltpu.HBM)


def partner_plan(areas):
    if areas == 4:
        targets = ((3, 2, 0, 1), (2, 3, 1, 0), (1, 0, 3, 2))

        def partner_of(here, i):
            return sum(jnp.where(here == a, target, 0) for a, target in enumerate(targets[i]))

        def by_target(parts):
            out, back, pair = (
                lax.ppermute(part, "area", list(enumerate(target))) for part, target in zip(parts, targets)
            )
            return [back, out, pair]

        return len(targets), partner_of, by_target
    reach = min(REACH, areas - 1)
    shifts = sorted({s % areas for d in range(1, reach + 1) for s in (d, -d)})

    def by_shift(parts):
        sent = [
            lax.ppermute(part, "area", [(a, (a + s) % areas) for a in range(areas)])
            for part, s in zip(parts, shifts)
        ]
        return [sent[shifts.index(areas - s)] for s in shifts]

    return len(shifts), lambda here, i: lax.rem(here + shifts[i], areas), by_shift


def block_facts(here, partner):
    low = partner > here
    distance = jnp.abs(partner - here)
    block = jnp.clip(distance - 1, 0, REACH - 1)
    in_reach = (distance >= 1) & (distance <= REACH)
    return low, jnp.minimum(here, partner), block, in_reach


def split_3(x):
    high = x.astype(jnp.bfloat16)
    rest = x - high.astype(jnp.float32)
    middle = rest.astype(jnp.bfloat16)
    rest = rest - middle.astype(jnp.float32)
    return jnp.concatenate([high, middle, rest.astype(jnp.bfloat16)], axis=0)


def put_row(packed_ref, hours, h, row):
    for j in range(row.shape[1] // LANES):
        packed_ref[j * hours + h : j * hours + h + 1, :] = row[:, j * LANES : (j + 1) * LANES]


def agree(mean_ref, sum_refs, hours, scen_total):
    for j in range(mean_ref.shape[1] // LANES):
        parts = [ref[j * hours : (j + 1) * hours, :] for ref in sum_refs]
        mean_ref[0:hours, j * LANES : (j + 1) * LANES] = functools.reduce(jnp.add, parts) / scen_total


def excess(diffs, limit):
    return diffs - jnp.clip(diffs, -limit, limit)


def write_ramp(mean_ref, beyond, limit, first_hour, padded_ref, excess_ref, ramp_ref):
    hours = ramp_ref.shape[0]
    padded_ref[0:1, :] = beyond
    padded_ref[1 : hours + 1, :] = mean_ref[0:hours, :]
    padded_ref[hours + 1 : hours + 2, :] = beyond
    diffs = padded_ref[1 : hours + 2, :] - padded_ref[0 : hours + 1, :]
    ids = first_hour + lax.broadcasted_iota(jnp.int32, diffs.shape, 0)
    valid = (ids >= 1) & (ids <= HOURS - 1)
    excess_ref[0 : hours + 1, :] = jnp.where(valid, excess(diffs, limit), 0.0)
    ramp_ref[...] = excess_ref[0:hours, :] - excess_ref[1 : hours + 1, :]


def line_work(inject_ref, ptdf_ref, line_max_ref, over_ref):
    inject = inject_ref[...]
    lines = ptdf_ref.shape[0]
    for at in range(0, lines, LINE_CHUNK):
        part = slice(at, at + LINE_CHUNK)
        flows = lax.dot_general(
            inject, ptdf_ref[part, :], CONTRACT_LAST, preferred_element_type=jnp.float32
        )
        limit = line_max_ref[:, part]
        over_ref[:, part] = (flows - jnp.clip(flows, -limit, limit)).astype(jnp.bfloat16)
    return jnp.dot(over_ref[...], ptdf_ref[...], preferred_element_type=jnp.float32)


def angle_kernel(
    blocks,
    partner_of,
    sens_in,
    demand_in,
    hedge_in,
    start_in,
    cost_in,
    max_in,
    limit_in,
    line_max_in,
    count_in,
    low_bus_in,
    high_bus_in,
    susc_in,
    *refs,
):
    own_refs, refs = refs[:blocks], refs[blocks:]
    (
        edge_hedge_ref,
        inject_ref,
        spread_ref,
        rows_ref,
        weight_ref,
        demand_ref,
        start_ref,
        cost_ref,
        max_ref,
        limit_ref,
        line_max_ref,
        sens_ref,
        count_ref,
        low_bus_ref,
        high_bus_ref,
        susc_ref,
        onehot_ref,
        copy_sems,
    ) = refs
    hours, buses = start_ref.shape
    scens = demand_ref.shape[0] // hours
    here = lax.axis_index("area")
    last = (hours - 1) * scens
    edge_rows = pl.ds(pl.multiple_of((1 - lax.axis_index("hour")) * last, scens), scens)

    pairs = (
        (count_in, count_ref),
        (low_bus_in, low_bus_ref),
        (high_bus_in, high_bus_ref),
        (susc_in, susc_ref),
        (start_in, start_ref),
        (demand_in, demand_ref),
        (sens_in, sens_ref),
        (hedge_in.at[edge_rows], edge_hedge_ref),
        (cost_in, cost_ref),
        (max_in, max_ref),
        (limit_in, limit_ref),
        (line_max_in, line_max_ref),
    )
    copies = [pltpu.make_async_copy(src, dst, copy_sems.at[i]) for i, (src, dst) in enumerate(pairs)]
    for copy in copies:
        copy.start()

    for copy in copies[:4]:
        copy.wait()
    for i in range(blocks):
        partner = partner_of(here, i)
        low, row, block, in_reach = block_facts(here, partner)
        slots = slice(i * CAP, (i + 1) * CAP)
        pick = lax.broadcasted_iota(jnp.int32, (CAP, REACH * CAP), 1) == (
            block * CAP + lax.broadcasted_iota(jnp.int32, (CAP, REACH * CAP), 0)
        )
        table_row = pl.ds(row, 1)
        bus_row = jnp.where(low, low_bus_ref[table_row, :], high_bus_ref[table_row, :])
        bus = jnp.sum(jnp.where(pick, bus_row.astype(jnp.float32), 0.0), axis=1, keepdims=True)
        susc = jnp.sum(jnp.where(pick, susc_ref[table_row, :], 0.0), axis=1, keepdims=True)
        count_row = count_ref[table_row, :].astype(jnp.float32)
        is_block = lax.broadcasted_iota(jnp.int32, (CAP, REACH), 1) == block
        count = jnp.sum(jnp.where(is_block, count_row, 0.0), axis=1, keepdims=True)
        slot_ids = lax.broadcasted_iota(jnp.int32, (CAP, 1), 0).astype(jnp.float32)
        live = jnp.where((slot_ids < count) & in_reach, 1.0, 0.0)
        sign = jnp.where(low, 1.0, -1.0)
        bus_ids = lax.broadcasted_iota(jnp.int32, (CAP, buses), 1).astype(jnp.float32)
        onehot = jnp.where(bus_ids == bus, live, 0.0)
        onehot_ref[slots, :] = onehot.astype(jnp.bfloat16)
        spread_ref[slots, :] = (-sign * onehot).astype(jnp.bfloat16)
        weight_ref[slots, :] = jnp.broadcast_to(live * sign * susc, (CAP, 128))

    for copy in copies[4:7]:
        copy.wait()
    for h in range(hours):
        part = slice(h * scens, (h + 1) * scens)
        inject_ref[part, :] = (start_ref[h : h + 1, :] - demand_ref[part, :]).astype(jnp.bfloat16)
    rows = jnp.dot(onehot_ref[...], sens_ref[...], preferred_element_type=jnp.float32)
    rows_ref[...] = rows.astype(jnp.bfloat16)
    own = lax.dot_general(
        rows_ref[...], inject_ref[...], CONTRACT_LAST, preferred_element_type=jnp.float32
    )
    for i in range(blocks):
        own_refs[i][...] = own[i * CAP : (i + 1) * CAP, :]

    for copy in copies[7:]:
        copy.wait()


def edge_kernel(demand_ref, edge_hedge_ref, start_ref, edge_ref):
    scens = edge_hedge_ref.shape[0]
    hours = start_ref.shape[0]
    early = lax.axis_index("hour") == 0
    last = (hours - 1) * scens
    at = 2 * scens
    edge_ref[0:scens, :] = jnp.where(early, demand_ref[last:, :], demand_ref[0:scens, :])
    edge_ref[scens:at, :] = edge_hedge_ref[...]
    edge_ref[at : at + 1, :] = jnp.where(early, start_ref[hours - 1 : hours, :], start_ref[0:1, :])
    edge_ref[at + 1 : at + 2, :] = jnp.where(
        early, start_ref[hours - 2 : hours - 1, :], start_ref[1:2, :]
    )


def first_kernel(
    ptdf_ref,
    own_inject_ref,
    demand_ref,
    hedge_ref,
    start_ref,
    edge_ref,
    cost_ref,
    max_ref,
    limit_ref,
    line_max_ref,
    gen_ref,
    base_ref,
    hedged_ref,
    sums_ref,
    inject_ref,
    over_ref,
    back_ref,
    padded_ref,
    excess_ref,
    ramp_ref,
):
    hours, buses = start_ref.shape
    width = demand_ref.shape[0]
    scens = width // hours
    at = 2 * scens
    early = lax.axis_index("hour") == 0
    first_hour = lax.axis_index("hour") * hours
    beyond = edge_ref[at : at + 1, :]
    limit = limit_ref[...]
    cost = cost_ref[...]
    top = max_ref[...]

    inject_ref[0:width, :] = own_inject_ref[...]
    inject_ref[width : width + scens, :] = (beyond - edge_ref[0:scens, :]).astype(jnp.bfloat16)
    back_ref[...] = line_work(inject_ref, ptdf_ref, line_max_ref, over_ref)
    write_ramp(start_ref, beyond, limit, first_hour, padded_ref, excess_ref, ramp_ref)

    def step(mean, hedge, back, ramp):
        grad = cost + back + (mean - mean + hedge) + ramp
        gen = jnp.clip(mean - STEP_SIZE * grad, 0.0, top)
        return gen, gen + hedge

    for h in range(hours):
        part = slice(h * scens, (h + 1) * scens)
        mean = start_ref[h : h + 1, :]
        gen, hedged = step(mean, hedge_ref[part, :], back_ref[part, :], ramp_ref[h : h + 1, :])
        gen_ref[part, :] = gen
        base_ref[part, :] = gen - demand_ref[part, :]
        hedged_ref[part, :] = hedged
        put_row(sums_ref, hours + 1, h, jnp.sum(hedged, axis=0, keepdims=True))
    near = jnp.where(early, start_ref[hours - 1 : hours, :], start_ref[0:1, :])
    ramp = excess(beyond - near, limit) + excess(beyond - edge_ref[at + 1 : at + 2, :], limit)
    _, hedged = step(beyond, edge_ref[scens:at, :], back_ref[width : width + scens, :], ramp)
    put_row(sums_ref, hours + 1, hours, jnp.sum(hedged, axis=0, keepdims=True))
    used = (hours + 1) * (buses // LANES)
    if used < sums_ref.shape[0]:
        sums_ref[used:, :] = jnp.zeros((sums_ref.shape[0] - used, LANES), jnp.float32)


def tie_kernel(blocks, base_ref, spread_ref, rows_ref, weight_ref, *refs):
    own_refs, refs = refs[:blocks], refs[blocks:]
    peer_refs, refs = refs[:blocks], refs[blocks:]
    next_refs, (inject_ref, mine_ref, theirs_ref) = refs[:blocks], refs[blocks:]

    weight = weight_ref[:, 0:1]
    own = jnp.concatenate([ref[...] for ref in own_refs], axis=0)
    peer = jnp.concatenate([ref[...] for ref in peer_refs], axis=0)
    est_mine = weight * own
    est_theirs = -weight * peer
    flow = (est_mine + est_theirs) * 0.5
    dual_mine = est_mine - flow
    dual_theirs = est_theirs - flow
    spread = spread_ref[...]
    add = lax.dot_general(
        split_3(flow),
        jnp.concatenate([spread, spread, spread], axis=0),
        CONTRACT_FIRST,
        preferred_element_type=jnp.float32,
    )
    inject_ref[...] = (base_ref[...] + add).astype(jnp.bfloat16)

    own_next = lax.dot_general(
        rows_ref[...], inject_ref[...], CONTRACT_LAST, preferred_element_type=jnp.float32
    )
    for i in range(blocks):
        next_refs[i][...] = own_next[i * CAP : (i + 1) * CAP, :]
    mine_ref[...] = weight * (own_next - peer) + dual_mine
    theirs_ref[...] = weight * own + dual_theirs


def second_kernel(
    terms,
    scen_total,
    ptdf_ref,
    inject_ref,
    gen_ref,
    hedged_ref,
    cost_ref,
    max_ref,
    limit_ref,
    line_max_ref,
    *refs,
):
    sum_refs, refs = refs[:terms], refs[terms:]
    (hedged_out_ref, sums_out_ref, over_ref, back_ref, mean_ref, padded_ref, excess_ref, ramp_ref) = refs
    hours, buses = ramp_ref.shape
    width = inject_ref.shape[0]
    scens = width // hours
    first_hour = lax.axis_index("hour") * hours

    back_ref[...] = line_work(inject_ref, ptdf_ref, line_max_ref, over_ref)
    agree(mean_ref, sum_refs, hours + 1, scen_total)
    write_ramp(
        mean_ref, mean_ref[hours : hours + 1, :], limit_ref[...], first_hour, padded_ref, excess_ref, ramp_ref
    )
    cost = cost_ref[...]
    top = max_ref[...]
    for h in range(hours):
        part = slice(h * scens, (h + 1) * scens)
        mean = mean_ref[h : h + 1, :]
        gen = gen_ref[part, :]
        hedge = hedged_ref[part, :] - mean
        grad = cost + back_ref[part, :] + (gen - mean + hedge) + ramp_ref[h : h + 1, :]
        gen = jnp.clip(gen - STEP_SIZE * grad, 0.0, top)
        hedged = gen + hedge
        hedged_out_ref[part, :] = hedged
        put_row(sums_out_ref, hours, h, jnp.sum(hedged, axis=0, keepdims=True))


def flow_kernel(blocks, partner_of, *refs):
    peer_refs, (weight_ref, mine_ref, theirs_ref, tie_ref) = refs[:blocks], refs[blocks:]
    here = lax.axis_index("area")
    slots = tie_ref.shape[1]
    places = []
    for i in range(blocks):
        low, _, block, in_reach = block_facts(here, partner_of(here, i))
        first = block * CAP + jnp.where(low, 0, REACH * CAP)
        hit = lax.broadcasted_iota(jnp.int32, (CAP, slots), 1) == (
            first + lax.broadcasted_iota(jnp.int32, (CAP, slots), 0)
        )
        places.append(jnp.where(hit & in_reach, 1.0, 0.0).astype(jnp.bfloat16))
    peer = jnp.concatenate([ref[...] for ref in peer_refs], axis=0)
    flow = (mine_ref[...] + (theirs_ref[...] - weight_ref[:, 0:1] * peer)) * 0.5
    tie_ref[...] = lax.dot_general(
        split_3(flow),
        jnp.concatenate(places * 3, axis=0),
        CONTRACT_FIRST,
        preferred_element_type=jnp.float32,
    )


def agree_kernel(scen_total, hedged_ref, *refs):
    sum_refs, (mean_out, hedge_out, mean_ref, hedge_ref, copy_sems) = refs[:-5], refs[-5:]
    hours = mean_ref.shape[0]
    scens = hedged_ref.shape[0] // hours
    agree(mean_ref, sum_refs, hours, scen_total)
    copies = [pltpu.make_async_copy(mean_ref, mean_out, copy_sems.at[0])]
    copies[0].start()
    for i, first in enumerate(range(0, hours, OUT_HOURS)):
        for h in range(first, min(first + OUT_HOURS, hours)):
            part = slice(h * scens, (h + 1) * scens)
            hedge_ref[part, :] = hedged_ref[part, :] - mean_ref[h : h + 1, :]
        rows = pl.ds(first * scens, (min(first + OUT_HOURS, hours) - first) * scens)
        copies.append(pltpu.make_async_copy(hedge_ref.at[rows], hedge_out.at[rows], copy_sems.at[i + 1]))
        copies[-1].start()
    for copy in copies:
        copy.wait()


def call(kernel, name, args, outs, scratch, flops, in_place=(), outs_in_place=False):
    size = sum(x.size * x.dtype.itemsize for x in list(args) + list(outs))
    return pl.pallas_call(
        kernel,
        name=name,
        out_shape=outs,
        in_specs=[ANY if i in in_place else VMEM for i in range(len(args))],
        out_specs=[ANY if outs_in_place else VMEM] * len(outs),
        scratch_shapes=scratch,
        compiler_params=pltpu.CompilerParams(vmem_limit_bytes=32 * 1024 * 1024),
        cost_estimate=pl.CostEstimate(flops=flops, bytes_accessed=size, transcendentals=0),
    )(*(pltpu.with_memory_space_constraint(x, pltpu.HBM) if i in in_place else x for i, x in enumerate(args)))


def per_device(
    ptdf,
    angle_sens,
    demand,
    gen_start,
    hedge_dual,
    gen_cost,
    gen_max,
    gen_ramp,
    line_max,
    tie_count,
    tie_low_bus,
    tie_high_bus,
    tie_susc,
):
    hours, scens, buses = demand.shape
    lines = ptdf.shape[0]
    width = hours * scens
    areas = lax.axis_size("area")
    n_scen = lax.axis_size("scen")
    assert lax.axis_size("hour") == 2 and hours >= 2
    scen_total = scens * n_scen
    blocks, partner_of, from_partners = partner_plan(areas)
    slots = blocks * CAP
    pieces = buses // LANES
    sum_rows = 8 * pl.cdiv((hours + 1) * pieces, 8)
    f32, bf16 = jnp.float32, jnp.bfloat16

    def shape(*dims, dtype=f32):
        return jax.ShapeDtypeStruct(dims, dtype)

    def over_scens(sums):
        if n_scen == 2:
            return [sums, lax.ppermute(sums, "scen", [(0, 1), (1, 0)])]
        return [lax.psum(sums, "scen")]

    work = 4 * width * lines * buses

    def step_scratch(rows):
        return [
            pltpu.VMEM((rows, buses), bf16),
            pltpu.VMEM((rows, lines), bf16),
            pltpu.VMEM((rows, buses), f32),
        ]

    ramp_scratch = [
        pltpu.VMEM((hours + 4, buses), f32),
        pltpu.VMEM((hours + 4, buses), f32),
        pltpu.VMEM((hours, buses), f32),
    ]
    tables = (tie_count, tie_low_bus, tie_high_bus, tie_susc)
    vectors = [x.reshape(1, -1) for x in (gen_cost, gen_max, gen_ramp, line_max)]
    hedge = hedge_dual.reshape(width, buses)
    made = call(
        functools.partial(angle_kernel, blocks, partner_of),
        "angles",
        (
            angle_sens,
            demand.reshape(width, buses),
            hedge,
            gen_start,
            *vectors,
            *tables,
        ),
        [shape(CAP, width)] * blocks
        + [
            shape(scens, buses),
            shape(width, buses, dtype=bf16),
            shape(slots, buses, dtype=bf16),
            shape(slots, buses, dtype=bf16),
            shape(slots, 128),
            shape(width, buses),
            shape(hours, buses),
            shape(1, buses),
            shape(1, buses),
            shape(1, buses),
            shape(1, lines),
        ],
        [pltpu.VMEM(x.shape, x.dtype) for x in (angle_sens, *tables)]
        + [pltpu.VMEM((slots, buses), bf16), pltpu.SemaphoreType.DMA((12,))],
        2 * slots * buses * (width + buses),
        range(12),
    )
    own = made[:blocks]
    edge_hedge, inject, spread, rows, weight, load, start = made[blocks : blocks + 7]
    cost, top, limit, line_top = made[blocks + 7 :]
    (edge,) = call(edge_kernel, "edge", (load, edge_hedge, start), [shape(2 * scens + 8, buses)], [], BETWEEN)
    edge = lax.ppermute(edge, "hour", [(0, 1), (1, 0)])
    peer = from_partners(own)
    gen, base, hedged, sums = call(
        first_kernel,
        "first",
        (ptdf, inject, load, hedge, start, edge, cost, top, limit, line_top),
        [
            shape(width, buses),
            shape(width, buses),
            shape(width, buses),
            shape(sum_rows, LANES),
        ],
        step_scratch(width + scens) + ramp_scratch,
        work,
    )
    sum_terms = over_scens(sums)
    terms = len(sum_terms)
    tied = call(
        functools.partial(tie_kernel, blocks),
        "ties",
        (base, spread, rows, weight, *own, *peer),
        [shape(CAP, width)] * blocks
        + [shape(width, buses, dtype=bf16), shape(slots, width), shape(slots, width)],
        [],
        BETWEEN,
    )
    own = tied[:blocks]
    inject, mine, theirs = tied[blocks:]
    hedged, sums = call(
        functools.partial(second_kernel, terms, scen_total),
        "second",
        (ptdf, inject, gen, hedged, cost, top, limit, line_top, *sum_terms),
        [shape(width, buses), shape(hours * pieces, LANES)],
        step_scratch(width)[1:] + [pltpu.VMEM((8 * pl.cdiv(hours + 1, 8), buses), f32)] + ramp_scratch,
        work,
    )
    peer = from_partners(own)
    sum_terms = over_scens(sums)
    (tie_flow,) = call(
        functools.partial(flow_kernel, blocks, partner_of),
        "flows",
        (*peer, weight, mine, theirs),
        [shape(width, 2 * REACH * CAP)],
        [],
        BETWEEN,
    )
    sum_terms, tie_flow = lax.optimization_barrier((sum_terms, tie_flow))
    gen_mean, hedge = call(
        functools.partial(agree_kernel, scen_total),
        "agree",
        (hedged, *sum_terms),
        [shape(hours, buses), shape(width, buses)],
        [
            pltpu.VMEM((hours, buses), f32),
            pltpu.VMEM((width, buses), f32),
            pltpu.SemaphoreType.DMA((1 + pl.cdiv(hours, OUT_HOURS),)),
        ],
        2 * width * buses,
        outs_in_place=True,
    )
    return (
        gen_mean,
        hedge.reshape(hours, scens, buses),
        tie_flow.reshape(hours, scens, 2 * REACH * CAP),
    )


def solution(mesh):
    return jax.shard_map(
        per_device,
        mesh=mesh,
        in_specs=(
            P(("group", "area"), None),
            P(("group", "area"), None),
            P(("group", "hour"), "scen", "area"),
            P(("group", "hour"), "area"),
            P(("group", "hour"), "scen", "area"),
            P(("group", "area")),
            P(("group", "area")),
            P(("group", "area")),
            P(("group", "area")),
            P("group", None),
            P("group", None),
            P("group", None),
            P("group", None),
        ),
        out_specs=(
            P(("group", "hour"), "area"),
            P(("group", "hour"), "scen", "area"),
            P(("group", "hour"), "scen", "area"),
        ),
        check_vma=False,
    )
```

```python
import functools

import jax
import jax.numpy as jnp
from jax import lax
from jax.experimental import pallas as pl
from jax.experimental.pallas import tpu as pltpu
from jax.sharding import PartitionSpec as P

HOURS = 24
REACH = 4
CAP = 16

STEP_SIZE = 0.5
LINE_CHUNK = 512
LANES = 128
BETWEEN = 20_000_000_000

CONTRACT_LAST = (((1,), (1,)), ((), ()))
CONTRACT_FIRST = (((0,), (0,)), ((), ()))
VMEM = pl.BlockSpec(memory_space=pltpu.VMEM)
ANY = pl.BlockSpec(memory_space=pltpu.HBM)


TARGETS = ((3, 2, 0, 1), (2, 3, 1, 0), (1, 0, 3, 2))


def partner_plan(areas):
    if areas == 4:

        def partner_of(here, i):
            return sum(jnp.where(here == a, target, 0) for a, target in enumerate(TARGETS[i]))

        def by_target(parts):
            out, back, pair = (
                lax.ppermute(part, "area", list(enumerate(target))) for part, target in zip(parts, TARGETS)
            )
            return [back, out, pair]

        return len(TARGETS), partner_of, by_target
    reach = min(REACH, areas - 1)
    shifts = sorted({s % areas for d in range(1, reach + 1) for s in (d, -d)})

    def by_shift(parts):
        sent = [
            lax.ppermute(part, "area", [(a, (a + s) % areas) for a in range(areas)])
            for part, s in zip(parts, shifts)
        ]
        return [sent[shifts.index(areas - s)] for s in shifts]

    return len(shifts), lambda here, i: lax.rem(here + shifts[i], areas), by_shift


def by_flips(here, flip_3, flip_2):
    return jnp.where(here < 2, flip_3, flip_2), jnp.where(here < 2, flip_2, flip_3)


def block_facts(here, partner):
    low = partner > here
    distance = jnp.abs(partner - here)
    block = jnp.clip(distance - 1, 0, REACH - 1)
    in_reach = (distance >= 1) & (distance <= REACH)
    return low, jnp.minimum(here, partner), block, in_reach


def split_3(x):
    high = x.astype(jnp.bfloat16)
    rest = x - high.astype(jnp.float32)
    middle = rest.astype(jnp.bfloat16)
    rest = rest - middle.astype(jnp.float32)
    return jnp.concatenate([high, middle, rest.astype(jnp.bfloat16)], axis=0)


def put_row(packed_ref, hours, h, row):
    for j in range(row.shape[1] // LANES):
        packed_ref[j * hours + h : j * hours + h + 1, :] = row[:, j * LANES : (j + 1) * LANES]


def clear_rest(packed_ref, used):
    rows = packed_ref.shape[0]
    if used < rows:
        packed_ref[used:, :] = jnp.zeros((rows - used, LANES), jnp.float32)


def agree(mean_ref, sum_refs, hours, scen_total):
    for j in range(mean_ref.shape[1] // LANES):
        parts = [ref[j * hours : (j + 1) * hours, :] for ref in sum_refs]
        mean_ref[0:hours, j * LANES : (j + 1) * LANES] = functools.reduce(jnp.add, parts) / scen_total


def excess(diffs, limit):
    return diffs - jnp.clip(diffs, -limit, limit)


def write_ramp(mean_ref, beyond, limit, first_hour, padded_ref, excess_ref, ramp_ref):
    hours = ramp_ref.shape[0]
    padded_ref[0:1, :] = beyond
    padded_ref[1 : hours + 1, :] = mean_ref[0:hours, :]
    padded_ref[hours + 1 : hours + 2, :] = beyond
    diffs = padded_ref[1 : hours + 2, :] - padded_ref[0 : hours + 1, :]
    ids = first_hour + lax.broadcasted_iota(jnp.int32, diffs.shape, 0)
    valid = (ids >= 1) & (ids <= HOURS - 1)
    excess_ref[0 : hours + 1, :] = jnp.where(valid, excess(diffs, limit), 0.0)
    ramp_ref[...] = excess_ref[0:hours, :] - excess_ref[1 : hours + 1, :]


def line_work(inject_ref, ptdf_ref, line_max_ref, over_ref):
    inject = inject_ref[...]
    lines = ptdf_ref.shape[0]
    for at in range(0, lines, LINE_CHUNK):
        part = slice(at, at + LINE_CHUNK)
        flows = lax.dot_general(
            inject, ptdf_ref[part, :], CONTRACT_LAST, preferred_element_type=jnp.float32
        )
        limit = line_max_ref[:, part]
        over_ref[:, part] = (flows - jnp.clip(flows, -limit, limit)).astype(jnp.bfloat16)
    return jnp.dot(over_ref[...], ptdf_ref[...], preferred_element_type=jnp.float32)


def angle_kernel(
    blocks,
    partner_of,
    sens_in,
    demand_in,
    hedge_in,
    start_in,
    cost_in,
    max_in,
    limit_in,
    line_max_in,
    count_in,
    low_bus_in,
    high_bus_in,
    susc_in,
    *refs,
):
    own_refs, refs = refs[:blocks], refs[blocks:]
    (
        edge_hedge_ref,
        inject_ref,
        spread_ref,
        rows_ref,
        weight_ref,
        demand_ref,
        start_ref,
        cost_ref,
        max_ref,
        limit_ref,
        line_max_ref,
        sens_ref,
        count_ref,
        low_bus_ref,
        high_bus_ref,
        susc_ref,
        onehot_ref,
        copy_sems,
    ) = refs
    hours, buses = start_ref.shape
    scens = demand_ref.shape[0] // hours
    here = lax.axis_index("area")
    last = (hours - 1) * scens
    edge_rows = pl.ds(pl.multiple_of((1 - lax.axis_index("hour")) * last, scens), scens)

    pairs = (
        (count_in, count_ref),
        (low_bus_in, low_bus_ref),
        (high_bus_in, high_bus_ref),
        (susc_in, susc_ref),
        (start_in, start_ref),
        (demand_in, demand_ref),
        (sens_in, sens_ref),
        (hedge_in.at[edge_rows], edge_hedge_ref),
        (cost_in, cost_ref),
        (max_in, max_ref),
        (limit_in, limit_ref),
        (line_max_in, line_max_ref),
    )
    copies = [pltpu.make_async_copy(src, dst, copy_sems.at[i]) for i, (src, dst) in enumerate(pairs)]
    for copy in copies:
        copy.start()

    for copy in copies[:4]:
        copy.wait()
    for i in range(blocks):
        partner = partner_of(here, i)
        low, row, block, in_reach = block_facts(here, partner)
        slots = slice(i * CAP, (i + 1) * CAP)
        pick = lax.broadcasted_iota(jnp.int32, (CAP, REACH * CAP), 1) == (
            block * CAP + lax.broadcasted_iota(jnp.int32, (CAP, REACH * CAP), 0)
        )
        table_row = pl.ds(row, 1)
        bus_row = jnp.where(low, low_bus_ref[table_row, :], high_bus_ref[table_row, :])
        bus = jnp.sum(jnp.where(pick, bus_row.astype(jnp.float32), 0.0), axis=1, keepdims=True)
        susc = jnp.sum(jnp.where(pick, susc_ref[table_row, :], 0.0), axis=1, keepdims=True)
        count_row = count_ref[table_row, :].astype(jnp.float32)
        is_block = lax.broadcasted_iota(jnp.int32, (CAP, REACH), 1) == block
        count = jnp.sum(jnp.where(is_block, count_row, 0.0), axis=1, keepdims=True)
        slot_ids = lax.broadcasted_iota(jnp.int32, (CAP, 1), 0).astype(jnp.float32)
        live = jnp.where((slot_ids < count) & in_reach, 1.0, 0.0)
        sign = jnp.where(low, 1.0, -1.0)
        bus_ids = lax.broadcasted_iota(jnp.int32, (CAP, buses), 1).astype(jnp.float32)
        onehot = jnp.where(bus_ids == bus, live, 0.0)
        onehot_ref[slots, :] = onehot.astype(jnp.bfloat16)
        spread_ref[slots, :] = (-sign * onehot).astype(jnp.bfloat16)
        weight_ref[slots, :] = jnp.broadcast_to(live * sign * susc, (CAP, 128))

    for copy in copies[4:7]:
        copy.wait()
    for h in range(hours):
        part = slice(h * scens, (h + 1) * scens)
        inject_ref[part, :] = (start_ref[h : h + 1, :] - demand_ref[part, :]).astype(jnp.bfloat16)
    rows = jnp.dot(onehot_ref[...], sens_ref[...], preferred_element_type=jnp.float32)
    rows_ref[...] = rows.astype(jnp.bfloat16)
    own = lax.dot_general(
        rows_ref[...], inject_ref[...], CONTRACT_LAST, preferred_element_type=jnp.float32
    )
    for i in range(blocks):
        own_refs[i][...] = own[i * CAP : (i + 1) * CAP, :]

    for copy in copies[7:]:
        copy.wait()


def edge_kernel(demand_ref, edge_hedge_ref, start_ref, edge_ref):
    scens = edge_hedge_ref.shape[0]
    hours = start_ref.shape[0]
    early = lax.axis_index("hour") == 0
    last = (hours - 1) * scens
    at = 2 * scens
    edge_ref[0:scens, :] = jnp.where(early, demand_ref[last:, :], demand_ref[0:scens, :])
    edge_ref[scens:at, :] = edge_hedge_ref[...]
    edge_ref[at : at + 1, :] = jnp.where(early, start_ref[hours - 1 : hours, :], start_ref[0:1, :])
    edge_ref[at + 1 : at + 2, :] = jnp.where(
        early, start_ref[hours - 2 : hours - 1, :], start_ref[1:2, :]
    )


def first_kernel(
    ptdf_ref,
    own_inject_ref,
    demand_ref,
    hedge_ref,
    start_ref,
    edge_ref,
    cost_ref,
    max_ref,
    limit_ref,
    line_max_ref,
    gen_ref,
    base_ref,
    hedged_ref,
    sums_ref,
    inject_ref,
    over_ref,
    back_ref,
    padded_ref,
    excess_ref,
    ramp_ref,
):
    hours, buses = start_ref.shape
    width = demand_ref.shape[0]
    scens = width // hours
    at = 2 * scens
    early = lax.axis_index("hour") == 0
    first_hour = lax.axis_index("hour") * hours
    beyond = edge_ref[at : at + 1, :]
    limit = limit_ref[...]
    cost = cost_ref[...]
    top = max_ref[...]

    inject_ref[0:width, :] = own_inject_ref[...]
    inject_ref[width : width + scens, :] = (beyond - edge_ref[0:scens, :]).astype(jnp.bfloat16)
    back_ref[...] = line_work(inject_ref, ptdf_ref, line_max_ref, over_ref)
    write_ramp(start_ref, beyond, limit, first_hour, padded_ref, excess_ref, ramp_ref)

    def step(mean, hedge, back, ramp):
        grad = cost + back + (mean - mean + hedge) + ramp
        gen = jnp.clip(mean - STEP_SIZE * grad, 0.0, top)
        return gen, gen + hedge

    for h in range(hours):
        part = slice(h * scens, (h + 1) * scens)
        mean = start_ref[h : h + 1, :]
        gen, hedged = step(mean, hedge_ref[part, :], back_ref[part, :], ramp_ref[h : h + 1, :])
        gen_ref[part, :] = gen
        base_ref[part, :] = gen - demand_ref[part, :]
        hedged_ref[part, :] = hedged
        put_row(sums_ref, hours + 1, h, jnp.sum(hedged, axis=0, keepdims=True))
    near = jnp.where(early, start_ref[hours - 1 : hours, :], start_ref[0:1, :])
    ramp = excess(beyond - near, limit) + excess(beyond - edge_ref[at + 1 : at + 2, :], limit)
    _, hedged = step(beyond, edge_ref[scens:at, :], back_ref[width : width + scens, :], ramp)
    put_row(sums_ref, hours + 1, hours, jnp.sum(hedged, axis=0, keepdims=True))
    clear_rest(sums_ref, (hours + 1) * (buses // LANES))


def tie_kernel(blocks, relayed, base_ref, spread_ref, rows_ref, weight_ref, *refs):
    own_refs, refs = refs[:blocks], refs[blocks:]
    peer_refs, refs = refs[:blocks], refs[blocks:]
    *next_refs, inject_ref, mine_ref, theirs_ref = refs

    weight = weight_ref[:, 0:1]
    own = jnp.concatenate([ref[...] for ref in own_refs], axis=0)
    peer = jnp.concatenate([ref[...] for ref in peer_refs], axis=0)
    est_mine = weight * own
    est_theirs = -weight * peer
    flow = (est_mine + est_theirs) * 0.5
    dual_mine = est_mine - flow
    dual_theirs = est_theirs - flow
    spread = spread_ref[...]
    add = lax.dot_general(
        split_3(flow),
        jnp.concatenate([spread, spread, spread], axis=0),
        CONTRACT_FIRST,
        preferred_element_type=jnp.float32,
    )
    inject_ref[...] = (base_ref[...] + add).astype(jnp.bfloat16)

    own_next = lax.dot_general(
        rows_ref[...], inject_ref[...], CONTRACT_LAST, preferred_element_type=jnp.float32
    )
    parts = [own_next[i * CAP : (i + 1) * CAP, :] for i in range(blocks)]
    if relayed:
        far_ref, near_ref = next_refs
        flip_3, flip_2 = by_flips(lax.axis_index("area"), parts[0], parts[1])
        far_ref[0:CAP, :] = flip_2
        far_ref[CAP:, :] = flip_3
        near_ref[...] = parts[2]
    else:
        for ref, part in zip(next_refs, parts):
            ref[...] = part
    mine_ref[...] = weight * (own_next - peer) + dual_mine
    theirs_ref[...] = weight * own + dual_theirs


def second_kernel(
    terms,
    scen_total,
    ptdf_ref,
    inject_ref,
    gen_ref,
    hedged_ref,
    cost_ref,
    max_ref,
    limit_ref,
    line_max_ref,
    *refs,
):
    sum_refs, refs = refs[:terms], refs[terms:]
    (hedged_out_ref, sums_out_ref, over_ref, back_ref, mean_ref, padded_ref, excess_ref, ramp_ref) = refs
    hours, buses = ramp_ref.shape
    width = inject_ref.shape[0]
    scens = width // hours
    first_hour = lax.axis_index("hour") * hours

    back_ref[...] = line_work(inject_ref, ptdf_ref, line_max_ref, over_ref)
    agree(mean_ref, sum_refs, hours + 1, scen_total)
    write_ramp(
        mean_ref, mean_ref[hours : hours + 1, :], limit_ref[...], first_hour, padded_ref, excess_ref, ramp_ref
    )
    cost = cost_ref[...]
    top = max_ref[...]
    for h in range(hours):
        part = slice(h * scens, (h + 1) * scens)
        mean = mean_ref[h : h + 1, :]
        gen = gen_ref[part, :]
        hedge = hedged_ref[part, :] - mean
        grad = cost + back_ref[part, :] + (gen - mean + hedge) + ramp_ref[h : h + 1, :]
        gen = jnp.clip(gen - STEP_SIZE * grad, 0.0, top)
        hedged = gen + hedge
        hedged_out_ref[part, :] = hedged
        put_row(sums_out_ref, hours, h, jnp.sum(hedged, axis=0, keepdims=True))
    clear_rest(sums_out_ref, hours * (buses // LANES))


def relay_kernel(near_ref, far_ref, both_ref):
    both_ref[0:CAP, :] = near_ref[...]
    both_ref[CAP:, :] = far_ref[CAP:, :]


def last_kernel(blocks, terms, relayed, partner_of, scen_total, hedged_ref, *refs):
    *peer_refs, weight_ref, mine_ref, theirs_ref = refs[: -7 - terms]
    sum_refs = refs[-7 - terms : -7]
    mean_out, hedge_out, tie_out, mean_ref, hedge_ref, tie_ref, copy_sems = refs[-7:]
    hours = mean_ref.shape[0]
    scens = hedged_ref.shape[0] // hours
    here = lax.axis_index("area")
    slots = tie_ref.shape[1]
    copies = []

    def send(src, dst):
        copies.append(pltpu.make_async_copy(src, dst, copy_sems.at[len(copies)]))
        copies[-1].start()

    agree(mean_ref, sum_refs, hours, scen_total)
    send(mean_ref, mean_out)
    for h in range(hours):
        part = slice(h * scens, (h + 1) * scens)
        hedge_ref[part, :] = hedged_ref[part, :] - mean_ref[h : h + 1, :]
    send(hedge_ref, hedge_out)

    places = []
    for i in range(blocks):
        low, _, block, in_reach = block_facts(here, partner_of(here, i))
        first = block * CAP + jnp.where(low, 0, REACH * CAP)
        hit = lax.broadcasted_iota(jnp.int32, (CAP, slots), 1) == (
            first + lax.broadcasted_iota(jnp.int32, (CAP, slots), 0)
        )
        places.append(jnp.where(hit & in_reach, 1.0, 0.0).astype(jnp.bfloat16))
    if relayed:
        far_ref, both_ref = peer_refs
        peers = [*by_flips(here, both_ref[CAP:, :], far_ref[0:CAP, :]), both_ref[0:CAP, :]]
    else:
        peers = [ref[...] for ref in peer_refs]
    peer = jnp.concatenate(peers, axis=0)
    flow = (mine_ref[...] + (theirs_ref[...] - weight_ref[:, 0:1] * peer)) * 0.5
    tie_ref[...] = lax.dot_general(
        split_3(flow),
        jnp.concatenate(places * 3, axis=0),
        CONTRACT_FIRST,
        preferred_element_type=jnp.float32,
    )
    send(tie_ref, tie_out)
    for copy in copies:
        copy.wait()


def call(kernel, name, args, outs, scratch, flops, in_place=(), outs_in_place=False):
    size = sum(x.size * x.dtype.itemsize for x in list(args) + list(outs))
    return pl.pallas_call(
        kernel,
        name=name,
        out_shape=outs,
        in_specs=[ANY if i in in_place else VMEM for i in range(len(args))],
        out_specs=[ANY if outs_in_place else VMEM] * len(outs),
        scratch_shapes=scratch,
        compiler_params=pltpu.CompilerParams(vmem_limit_bytes=32 * 1024 * 1024),
        cost_estimate=pl.CostEstimate(flops=flops, bytes_accessed=size, transcendentals=0),
    )(*(pltpu.with_memory_space_constraint(x, pltpu.HBM) if i in in_place else x for i, x in enumerate(args)))


def per_device(
    ptdf,
    angle_sens,
    demand,
    gen_start,
    hedge_dual,
    gen_cost,
    gen_max,
    gen_ramp,
    line_max,
    tie_count,
    tie_low_bus,
    tie_high_bus,
    tie_susc,
):
    hours, scens, buses = demand.shape
    lines = ptdf.shape[0]
    width = hours * scens
    areas = lax.axis_size("area")
    n_scen = lax.axis_size("scen")
    assert lax.axis_size("hour") == 2 and hours >= 2
    scen_total = scens * n_scen
    blocks, partner_of, from_partners = partner_plan(areas)
    slots = blocks * CAP
    pieces = buses // LANES
    sum_rows = 8 * pl.cdiv((hours + 1) * pieces, 8)
    f32, bf16 = jnp.float32, jnp.bfloat16

    def shape(*dims, dtype=f32):
        return jax.ShapeDtypeStruct(dims, dtype)

    def over_scens(sums):
        if n_scen == 2:
            return [sums, lax.ppermute(sums, "scen", [(0, 1), (1, 0)])]
        return [lax.psum(sums, "scen")]

    work = 4 * width * lines * buses

    def step_scratch(rows):
        return [
            pltpu.VMEM((rows, buses), bf16),
            pltpu.VMEM((rows, lines), bf16),
            pltpu.VMEM((rows, buses), f32),
        ]

    ramp_scratch = [
        pltpu.VMEM((hours + 4, buses), f32),
        pltpu.VMEM((hours + 4, buses), f32),
        pltpu.VMEM((hours, buses), f32),
    ]
    tables = (tie_count, tie_low_bus, tie_high_bus, tie_susc)
    vectors = [x.reshape(1, -1) for x in (gen_cost, gen_max, gen_ramp, line_max)]
    hedge = hedge_dual.reshape(width, buses)
    made = call(
        functools.partial(angle_kernel, blocks, partner_of),
        "angles",
        (
            angle_sens,
            demand.reshape(width, buses),
            hedge,
            gen_start,
            *vectors,
            *tables,
        ),
        [shape(CAP, width)] * blocks
        + [
            shape(scens, buses),
            shape(width, buses, dtype=bf16),
            shape(slots, buses, dtype=bf16),
            shape(slots, buses, dtype=bf16),
            shape(slots, 128),
            shape(width, buses),
            shape(hours, buses),
            shape(1, buses),
            shape(1, buses),
            shape(1, buses),
            shape(1, lines),
        ],
        [pltpu.VMEM(x.shape, x.dtype) for x in (angle_sens, *tables)]
        + [pltpu.VMEM((slots, buses), bf16), pltpu.SemaphoreType.DMA((12,))],
        2 * slots * buses * (width + buses),
        range(12),
    )
    own = made[:blocks]
    edge_hedge, inject, spread, rows, weight, load, start = made[blocks : blocks + 7]
    cost, top, limit, line_top = made[blocks + 7 :]
    (edge,) = call(edge_kernel, "edge", (load, edge_hedge, start), [shape(2 * scens + 8, buses)], [], BETWEEN)
    edge = lax.ppermute(edge, "hour", [(0, 1), (1, 0)])
    peer = from_partners(own)
    gen, base, hedged, sums = call(
        first_kernel,
        "first",
        (ptdf, inject, load, hedge, start, edge, cost, top, limit, line_top),
        [
            shape(width, buses),
            shape(width, buses),
            shape(width, buses),
            shape(sum_rows, LANES),
        ],
        step_scratch(width + scens) + ramp_scratch,
        work,
    )
    sum_terms = over_scens(sums)
    terms = len(sum_terms)
    relayed = areas == 4
    tied = call(
        functools.partial(tie_kernel, blocks, relayed),
        "ties",
        (base, spread, rows, weight, *own, *peer),
        ([shape(2 * CAP, width), shape(CAP, width)] if relayed else [shape(CAP, width)] * blocks)
        + [shape(width, buses, dtype=bf16), shape(slots, width), shape(slots, width)],
        [],
        BETWEEN,
    )
    *own, inject, mine, theirs = tied
    hedged, sums = call(
        functools.partial(second_kernel, terms, scen_total),
        "second",
        (ptdf, inject, gen, hedged, cost, top, limit, line_top, *sum_terms),
        [shape(width, buses), shape(sum_rows, LANES)],
        step_scratch(width)[1:] + [pltpu.VMEM((8 * pl.cdiv(hours + 1, 8), buses), f32)] + ramp_scratch,
        work,
    )
    sum_terms = over_scens(sums)
    if relayed:
        far, near = own
        far = lax.ppermute(far, "area", [(a, a ^ 2) for a in range(areas)])
        arrived, _ = lax.optimization_barrier((far, sums))
        (both,) = call(relay_kernel, "relay", (near, arrived), [shape(2 * CAP, width)], [], BETWEEN)
        peer = [far, lax.ppermute(both, "area", [(a, a ^ 1) for a in range(areas)])]
    else:
        peer = from_partners(own)
    ends = [shape(hours, buses), shape(width, buses), shape(width, 2 * REACH * CAP)]
    gen_mean, hedge, tie_flow = call(
        functools.partial(last_kernel, blocks, terms, relayed, partner_of, scen_total),
        "last",
        (hedged, *peer, weight, mine, theirs, *sum_terms),
        ends,
        [pltpu.VMEM(x.shape, x.dtype) for x in ends] + [pltpu.SemaphoreType.DMA((len(ends),))],
        6 * slots * width * 2 * REACH * CAP,
        outs_in_place=True,
    )
    return (
        gen_mean,
        hedge.reshape(hours, scens, buses),
        tie_flow.reshape(hours, scens, 2 * REACH * CAP),
    )


def solution(mesh):
    return jax.shard_map(
        per_device,
        mesh=mesh,
        in_specs=(
            P(("group", "area"), None),
            P(("group", "area"), None),
            P(("group", "hour"), "scen", "area"),
            P(("group", "hour"), "area"),
            P(("group", "hour"), "scen", "area"),
            P(("group", "area")),
            P(("group", "area")),
            P(("group", "area")),
            P(("group", "area")),
            P("group", None),
            P("group", None),
            P("group", None),
            P("group", None),
        ),
        out_specs=(
            P(("group", "hour"), "area"),
            P(("group", "hour"), "scen", "area"),
            P(("group", "hour"), "scen", "area"),
        ),
        check_vma=False,
    )
```

```python
import functools

import jax
import jax.numpy as jnp
from jax import lax
from jax.experimental import pallas as pl
from jax.experimental.pallas import tpu as pltpu
from jax.sharding import PartitionSpec as P

HOURS = 24
REACH = 4
CAP = 16

STEP_SIZE = 0.5
LINE_CHUNK = 512
LANES = 128
BETWEEN = 20_000_000_000

CONTRACT_LAST = (((1,), (1,)), ((), ()))
CONTRACT_FIRST = (((0,), (0,)), ((), ()))
VMEM = pl.BlockSpec(memory_space=pltpu.VMEM)
ANY = pl.BlockSpec(memory_space=pltpu.HBM)


TARGETS = ((3, 2, 0, 1), (2, 3, 1, 0), (1, 0, 3, 2))


def partner_plan(areas):
    if areas == 4:

        def partner_of(here, i):
            return sum(jnp.where(here == a, target, 0) for a, target in enumerate(TARGETS[i]))

        def by_target(parts):
            out, back, pair = (
                lax.ppermute(part, "area", list(enumerate(target))) for part, target in zip(parts, TARGETS)
            )
            return [back, out, pair]

        return len(TARGETS), partner_of, by_target
    reach = min(REACH, areas - 1)
    shifts = sorted({s % areas for d in range(1, reach + 1) for s in (d, -d)})

    def by_shift(parts):
        sent = [
            lax.ppermute(part, "area", [(a, (a + s) % areas) for a in range(areas)])
            for part, s in zip(parts, shifts)
        ]
        return [sent[shifts.index(areas - s)] for s in shifts]

    return len(shifts), lambda here, i: lax.rem(here + shifts[i], areas), by_shift


def by_flips(here, flip_3, flip_2):
    return jnp.where(here < 2, flip_3, flip_2), jnp.where(here < 2, flip_2, flip_3)


def block_facts(here, partner):
    low = partner > here
    distance = jnp.abs(partner - here)
    block = jnp.clip(distance - 1, 0, REACH - 1)
    in_reach = (distance >= 1) & (distance <= REACH)
    return low, jnp.minimum(here, partner), block, in_reach


def fold(x):
    half = x.shape[0] // 2
    low = lax.broadcasted_iota(jnp.int32, (half, LANES), 1) < LANES // 2
    shared = jnp.where(low, x[0:half, LANES : 2 * LANES], x[half:, LANES : 2 * LANES])
    return jnp.concatenate([x[:, 0:LANES], shared], axis=0)


def unfold(packed):
    rows = 2 * packed.shape[0] // 3
    shared = packed[rows:, :]
    low = lax.broadcasted_iota(jnp.int32, shared.shape, 1) < LANES // 2
    turned = pltpu.roll(shared, LANES // 2, 1)
    rest = jnp.concatenate([jnp.where(low, shared, turned), jnp.where(low, turned, shared)], axis=0)
    return jnp.concatenate([packed[0:rows, :], rest], axis=1)


def repeat_rest(inject_ref, width):
    inject_ref[width:, :] = inject_ref[width - LANES // 2 : width, :]


def split_3(x):
    high = x.astype(jnp.bfloat16)
    rest = x - high.astype(jnp.float32)
    middle = rest.astype(jnp.bfloat16)
    rest = rest - middle.astype(jnp.float32)
    return jnp.concatenate([high, middle, rest.astype(jnp.bfloat16)], axis=0)


def put_row(packed_ref, hours, h, row):
    for j in range(row.shape[1] // LANES):
        packed_ref[j * hours + h : j * hours + h + 1, :] = row[:, j * LANES : (j + 1) * LANES]


def clear_rest(packed_ref, used):
    rows = packed_ref.shape[0]
    if used < rows:
        packed_ref[used:, :] = jnp.zeros((rows - used, LANES), jnp.float32)


def agree(mean_ref, sum_refs, hours, scen_total):
    for j in range(mean_ref.shape[1] // LANES):
        parts = [ref[j * hours : (j + 1) * hours, :] for ref in sum_refs]
        mean_ref[0:hours, j * LANES : (j + 1) * LANES] = functools.reduce(jnp.add, parts) / scen_total


def excess(diffs, limit):
    return diffs - jnp.clip(diffs, -limit, limit)


def write_ramp(mean_ref, beyond, limit, first_hour, padded_ref, excess_ref, ramp_ref):
    hours = ramp_ref.shape[0]
    padded_ref[0:1, :] = beyond
    padded_ref[1 : hours + 1, :] = mean_ref[0:hours, :]
    padded_ref[hours + 1 : hours + 2, :] = beyond
    diffs = padded_ref[1 : hours + 2, :] - padded_ref[0 : hours + 1, :]
    ids = first_hour + lax.broadcasted_iota(jnp.int32, diffs.shape, 0)
    valid = (ids >= 1) & (ids <= HOURS - 1)
    excess_ref[0 : hours + 1, :] = jnp.where(valid, excess(diffs, limit), 0.0)
    ramp_ref[...] = excess_ref[0:hours, :] - excess_ref[1 : hours + 1, :]


def line_work(inject_ref, ptdf_ref, line_max_ref, over_ref):
    inject = inject_ref[...]
    lines = ptdf_ref.shape[0]
    for at in range(0, lines, LINE_CHUNK):
        part = slice(at, at + LINE_CHUNK)
        flows = lax.dot_general(
            inject, ptdf_ref[part, :], CONTRACT_LAST, preferred_element_type=jnp.float32
        )
        limit = line_max_ref[:, part]
        over_ref[:, part] = (flows - jnp.clip(flows, -limit, limit)).astype(jnp.bfloat16)
    return jnp.dot(over_ref[...], ptdf_ref[...], preferred_element_type=jnp.float32)


def angle_kernel(
    blocks,
    partner_of,
    sens_in,
    demand_in,
    hedge_in,
    start_in,
    cost_in,
    max_in,
    limit_in,
    line_max_in,
    count_in,
    low_bus_in,
    high_bus_in,
    susc_in,
    *refs,
):
    own_refs, refs = refs[:blocks], refs[blocks:]
    (
        own_ref,
        edge_hedge_ref,
        inject_ref,
        spread_ref,
        rows_ref,
        weight_ref,
        demand_ref,
        start_ref,
        cost_ref,
        max_ref,
        limit_ref,
        line_max_ref,
        sens_ref,
        count_ref,
        low_bus_ref,
        high_bus_ref,
        susc_ref,
        onehot_ref,
        copy_sems,
    ) = refs
    hours, buses = start_ref.shape
    scens = demand_ref.shape[0] // hours
    here = lax.axis_index("area")
    last = (hours - 1) * scens
    edge_rows = pl.ds(pl.multiple_of((1 - lax.axis_index("hour")) * last, scens), scens)

    pairs = (
        (count_in, count_ref),
        (low_bus_in, low_bus_ref),
        (high_bus_in, high_bus_ref),
        (susc_in, susc_ref),
        (start_in, start_ref),
        (demand_in, demand_ref),
        (sens_in, sens_ref),
        (hedge_in.at[edge_rows], edge_hedge_ref),
        (cost_in, cost_ref),
        (max_in, max_ref),
        (limit_in, limit_ref),
        (line_max_in, line_max_ref),
    )
    copies = [pltpu.make_async_copy(src, dst, copy_sems.at[i]) for i, (src, dst) in enumerate(pairs)]
    for copy in copies:
        copy.start()

    for copy in copies[:4]:
        copy.wait()
    for i in range(blocks):
        partner = partner_of(here, i)
        low, row, block, in_reach = block_facts(here, partner)
        slots = slice(i * CAP, (i + 1) * CAP)
        pick = lax.broadcasted_iota(jnp.int32, (CAP, REACH * CAP), 1) == (
            block * CAP + lax.broadcasted_iota(jnp.int32, (CAP, REACH * CAP), 0)
        )
        table_row = pl.ds(row, 1)
        bus_row = jnp.where(low, low_bus_ref[table_row, :], high_bus_ref[table_row, :])
        bus = jnp.sum(jnp.where(pick, bus_row.astype(jnp.float32), 0.0), axis=1, keepdims=True)
        susc = jnp.sum(jnp.where(pick, susc_ref[table_row, :], 0.0), axis=1, keepdims=True)
        count_row = count_ref[table_row, :].astype(jnp.float32)
        is_block = lax.broadcasted_iota(jnp.int32, (CAP, REACH), 1) == block
        count = jnp.sum(jnp.where(is_block, count_row, 0.0), axis=1, keepdims=True)
        slot_ids = lax.broadcasted_iota(jnp.int32, (CAP, 1), 0).astype(jnp.float32)
        live = jnp.where((slot_ids < count) & in_reach, 1.0, 0.0)
        sign = jnp.where(low, 1.0, -1.0)
        bus_ids = lax.broadcasted_iota(jnp.int32, (CAP, buses), 1).astype(jnp.float32)
        onehot = jnp.where(bus_ids == bus, live, 0.0)
        onehot_ref[slots, :] = onehot.astype(jnp.bfloat16)
        spread_ref[slots, :] = (-sign * onehot).astype(jnp.bfloat16)
        weight_ref[slots, :] = jnp.broadcast_to(live * sign * susc, (CAP, 128))

    for copy in copies[4:7]:
        copy.wait()
    for h in range(hours):
        part = slice(h * scens, (h + 1) * scens)
        inject_ref[part, :] = (start_ref[h : h + 1, :] - demand_ref[part, :]).astype(jnp.bfloat16)
    repeat_rest(inject_ref, hours * scens)
    rows = jnp.dot(onehot_ref[...], sens_ref[...], preferred_element_type=jnp.float32)
    rows_ref[...] = rows.astype(jnp.bfloat16)
    own = lax.dot_general(
        rows_ref[...], inject_ref[...], CONTRACT_LAST, preferred_element_type=jnp.float32
    )
    own_ref[...] = own
    for i in range(blocks):
        own_refs[i][...] = fold(own[i * CAP : (i + 1) * CAP, :])

    for copy in copies[7:]:
        copy.wait()


def edge_kernel(demand_ref, edge_hedge_ref, start_ref, edge_ref):
    scens = edge_hedge_ref.shape[0]
    hours = start_ref.shape[0]
    early = lax.axis_index("hour") == 0
    last = (hours - 1) * scens
    at = 2 * scens
    edge_ref[0:scens, :] = jnp.where(early, demand_ref[last:, :], demand_ref[0:scens, :])
    edge_ref[scens:at, :] = edge_hedge_ref[...]
    edge_ref[at : at + 1, :] = jnp.where(early, start_ref[hours - 1 : hours, :], start_ref[0:1, :])
    edge_ref[at + 1 : at + 2, :] = jnp.where(
        early, start_ref[hours - 2 : hours - 1, :], start_ref[1:2, :]
    )


def first_kernel(
    ptdf_ref,
    own_inject_ref,
    demand_ref,
    hedge_ref,
    start_ref,
    edge_ref,
    cost_ref,
    max_ref,
    limit_ref,
    line_max_ref,
    gen_ref,
    base_ref,
    hedged_ref,
    sums_ref,
    inject_ref,
    over_ref,
    back_ref,
    padded_ref,
    excess_ref,
    ramp_ref,
):
    hours, buses = start_ref.shape
    width = demand_ref.shape[0]
    scens = width // hours
    at = 2 * scens
    early = lax.axis_index("hour") == 0
    first_hour = lax.axis_index("hour") * hours
    beyond = edge_ref[at : at + 1, :]
    limit = limit_ref[...]
    cost = cost_ref[...]
    top = max_ref[...]

    inject_ref[0:width, :] = own_inject_ref[0:width, :]
    inject_ref[width : width + scens, :] = (beyond - edge_ref[0:scens, :]).astype(jnp.bfloat16)
    back_ref[...] = line_work(inject_ref, ptdf_ref, line_max_ref, over_ref)
    write_ramp(start_ref, beyond, limit, first_hour, padded_ref, excess_ref, ramp_ref)

    def step(mean, hedge, back, ramp):
        grad = cost + back + (mean - mean + hedge) + ramp
        gen = jnp.clip(mean - STEP_SIZE * grad, 0.0, top)
        return gen, gen + hedge

    for h in range(hours):
        part = slice(h * scens, (h + 1) * scens)
        mean = start_ref[h : h + 1, :]
        gen, hedged = step(mean, hedge_ref[part, :], back_ref[part, :], ramp_ref[h : h + 1, :])
        gen_ref[part, :] = gen
        base_ref[part, :] = gen - demand_ref[part, :]
        hedged_ref[part, :] = hedged
        put_row(sums_ref, hours + 1, h, jnp.sum(hedged, axis=0, keepdims=True))
    near = jnp.where(early, start_ref[hours - 1 : hours, :], start_ref[0:1, :])
    ramp = excess(beyond - near, limit) + excess(beyond - edge_ref[at + 1 : at + 2, :], limit)
    _, hedged = step(beyond, edge_ref[scens:at, :], back_ref[width : width + scens, :], ramp)
    put_row(sums_ref, hours + 1, hours, jnp.sum(hedged, axis=0, keepdims=True))
    clear_rest(sums_ref, (hours + 1) * (buses // LANES))


def tie_kernel(blocks, relayed, base_ref, spread_ref, rows_ref, weight_ref, own_ref, *refs):
    peer_refs, refs = refs[:blocks], refs[blocks:]
    *next_refs, inject_ref, mine_ref, theirs_ref = refs
    width = base_ref.shape[0]

    weight = weight_ref[:, 0:1]
    own = own_ref[...]
    peer = jnp.concatenate([unfold(ref[...]) for ref in peer_refs], axis=0)
    est_mine = weight * own
    est_theirs = -weight * peer
    flow = (est_mine + est_theirs) * 0.5
    dual_mine = est_mine - flow
    dual_theirs = est_theirs - flow
    spread = spread_ref[...]
    add = lax.dot_general(
        split_3(flow),
        jnp.concatenate([spread, spread, spread], axis=0),
        CONTRACT_FIRST,
        preferred_element_type=jnp.float32,
    )
    inject_ref[0:width, :] = (base_ref[...] + add[0:width, :]).astype(jnp.bfloat16)
    repeat_rest(inject_ref, width)

    own_next = lax.dot_general(
        rows_ref[...], inject_ref[...], CONTRACT_LAST, preferred_element_type=jnp.float32
    )
    parts = [own_next[i * CAP : (i + 1) * CAP, :] for i in range(blocks)]
    if relayed:
        far_ref, near_ref = next_refs
        flip_3, flip_2 = by_flips(lax.axis_index("area"), parts[0], parts[1])
        far_ref[...] = fold(jnp.concatenate([flip_2, flip_3], axis=0))
        near_ref[...] = parts[2]
    else:
        for ref, part in zip(next_refs, parts):
            ref[...] = fold(part)
    mine_ref[...] = weight * (own_next - peer) + dual_mine
    theirs_ref[...] = weight * own + dual_theirs


def second_kernel(
    terms,
    scen_total,
    ptdf_ref,
    inject_ref,
    gen_ref,
    hedged_ref,
    cost_ref,
    max_ref,
    limit_ref,
    line_max_ref,
    *refs,
):
    sum_refs, refs = refs[:terms], refs[terms:]
    (hedged_out_ref, sums_out_ref, over_ref, back_ref, mean_ref, padded_ref, excess_ref, ramp_ref) = refs
    hours, buses = ramp_ref.shape
    width = back_ref.shape[0]
    scens = width // hours
    first_hour = lax.axis_index("hour") * hours

    back_ref[...] = line_work(inject_ref.at[0:width, :], ptdf_ref, line_max_ref, over_ref)
    agree(mean_ref, sum_refs, hours + 1, scen_total)
    write_ramp(
        mean_ref, mean_ref[hours : hours + 1, :], limit_ref[...], first_hour, padded_ref, excess_ref, ramp_ref
    )
    cost = cost_ref[...]
    top = max_ref[...]
    for h in range(hours):
        part = slice(h * scens, (h + 1) * scens)
        mean = mean_ref[h : h + 1, :]
        gen = gen_ref[part, :]
        hedge = hedged_ref[part, :] - mean
        grad = cost + back_ref[part, :] + (gen - mean + hedge) + ramp_ref[h : h + 1, :]
        gen = jnp.clip(gen - STEP_SIZE * grad, 0.0, top)
        hedged = gen + hedge
        hedged_out_ref[part, :] = hedged
        put_row(sums_out_ref, hours, h, jnp.sum(hedged, axis=0, keepdims=True))
    clear_rest(sums_out_ref, hours * (buses // LANES))


def relay_kernel(near_ref, far_ref, both_ref):
    low = lax.broadcasted_iota(jnp.int32, (CAP, LANES), 1) < LANES // 2
    both_ref[0:CAP, :] = near_ref[:, 0:LANES]
    both_ref[CAP : 2 * CAP, :] = far_ref[CAP : 2 * CAP, :]
    both_ref[2 * CAP :, :] = jnp.where(low, near_ref[:, LANES:], far_ref[2 * CAP :, :])


def last_kernel(blocks, terms, relayed, partner_of, scen_total, hedged_ref, *refs):
    *peer_refs, weight_ref, mine_ref, theirs_ref = refs[: -7 - terms]
    sum_refs = refs[-7 - terms : -7]
    mean_out, hedge_out, tie_out, mean_ref, hedge_ref, tie_ref, copy_sems = refs[-7:]
    hours = mean_ref.shape[0]
    scens = hedged_ref.shape[0] // hours
    here = lax.axis_index("area")
    slots = tie_ref.shape[1]
    copies = []

    def send(src, dst):
        copies.append(pltpu.make_async_copy(src, dst, copy_sems.at[len(copies)]))
        copies[-1].start()

    agree(mean_ref, sum_refs, hours, scen_total)
    send(mean_ref, mean_out)
    for h in range(hours):
        part = slice(h * scens, (h + 1) * scens)
        hedge_ref[part, :] = hedged_ref[part, :] - mean_ref[h : h + 1, :]
    send(hedge_ref, hedge_out)

    places = []
    for i in range(blocks):
        low, _, block, in_reach = block_facts(here, partner_of(here, i))
        first = block * CAP + jnp.where(low, 0, REACH * CAP)
        hit = lax.broadcasted_iota(jnp.int32, (CAP, slots), 1) == (
            first + lax.broadcasted_iota(jnp.int32, (CAP, slots), 0)
        )
        places.append(jnp.where(hit & in_reach, 1.0, 0.0).astype(jnp.bfloat16))
    if relayed:
        far, both = (unfold(ref[...]) for ref in peer_refs)
        peers = [*by_flips(here, both[CAP:, :], far[0:CAP, :]), both[0:CAP, :]]
    else:
        peers = [unfold(ref[...]) for ref in peer_refs]
    peer = jnp.concatenate(peers, axis=0)
    flow = (mine_ref[...] + (theirs_ref[...] - weight_ref[:, 0:1] * peer)) * 0.5
    placed = lax.dot_general(
        split_3(flow),
        jnp.concatenate(places * 3, axis=0),
        CONTRACT_FIRST,
        preferred_element_type=jnp.float32,
    )
    tie_ref[...] = placed[0 : hours * scens, :]
    send(tie_ref, tie_out)
    for copy in copies:
        copy.wait()


def call(kernel, name, args, outs, scratch, flops, in_place=(), outs_in_place=False):
    size = sum(x.size * x.dtype.itemsize for x in list(args) + list(outs))
    return pl.pallas_call(
        kernel,
        name=name,
        out_shape=outs,
        in_specs=[ANY if i in in_place else VMEM for i in range(len(args))],
        out_specs=[ANY if outs_in_place else VMEM] * len(outs),
        scratch_shapes=scratch,
        compiler_params=pltpu.CompilerParams(vmem_limit_bytes=32 * 1024 * 1024),
        cost_estimate=pl.CostEstimate(flops=flops, bytes_accessed=size, transcendentals=0),
    )(*(pltpu.with_memory_space_constraint(x, pltpu.HBM) if i in in_place else x for i, x in enumerate(args)))


def per_device(
    ptdf,
    angle_sens,
    demand,
    gen_start,
    hedge_dual,
    gen_cost,
    gen_max,
    gen_ramp,
    line_max,
    tie_count,
    tie_low_bus,
    tie_high_bus,
    tie_susc,
):
    hours, scens, buses = demand.shape
    lines = ptdf.shape[0]
    width = hours * scens
    areas = lax.axis_size("area")
    n_scen = lax.axis_size("scen")
    assert lax.axis_size("hour") == 2 and hours >= 2
    assert width % LANES == LANES // 2 and width < 2 * LANES
    columns = 2 * LANES
    block_rows = CAP * 3 // 2
    scen_total = scens * n_scen
    blocks, partner_of, from_partners = partner_plan(areas)
    slots = blocks * CAP
    pieces = buses // LANES
    sum_rows = 8 * pl.cdiv((hours + 1) * pieces, 8)
    f32, bf16 = jnp.float32, jnp.bfloat16

    def shape(*dims, dtype=f32):
        return jax.ShapeDtypeStruct(dims, dtype)

    def over_scens(sums):
        if n_scen == 2:
            return [sums, lax.ppermute(sums, "scen", [(0, 1), (1, 0)])]
        return [lax.psum(sums, "scen")]

    work = 4 * width * lines * buses

    def step_scratch(rows):
        return [
            pltpu.VMEM((rows, buses), bf16),
            pltpu.VMEM((rows, lines), bf16),
            pltpu.VMEM((rows, buses), f32),
        ]

    ramp_scratch = [
        pltpu.VMEM((hours + 4, buses), f32),
        pltpu.VMEM((hours + 4, buses), f32),
        pltpu.VMEM((hours, buses), f32),
    ]
    tables = (tie_count, tie_low_bus, tie_high_bus, tie_susc)
    vectors = [x.reshape(1, -1) for x in (gen_cost, gen_max, gen_ramp, line_max)]
    hedge = hedge_dual.reshape(width, buses)
    made = call(
        functools.partial(angle_kernel, blocks, partner_of),
        "angles",
        (
            angle_sens,
            demand.reshape(width, buses),
            hedge,
            gen_start,
            *vectors,
            *tables,
        ),
        [shape(block_rows, LANES)] * blocks
        + [
            shape(slots, columns),
            shape(scens, buses),
            shape(columns, buses, dtype=bf16),
            shape(slots, buses, dtype=bf16),
            shape(slots, buses, dtype=bf16),
            shape(slots, 128),
            shape(width, buses),
            shape(hours, buses),
            shape(1, buses),
            shape(1, buses),
            shape(1, buses),
            shape(1, lines),
        ],
        [pltpu.VMEM(x.shape, x.dtype) for x in (angle_sens, *tables)]
        + [pltpu.VMEM((slots, buses), bf16), pltpu.SemaphoreType.DMA((12,))],
        2 * slots * buses * (width + buses),
        range(12),
    )
    sent = made[:blocks]
    own, edge_hedge, inject, spread, rows, weight, load, start = made[blocks : blocks + 8]
    cost, top, limit, line_top = made[blocks + 8 :]
    (edge,) = call(edge_kernel, "edge", (load, edge_hedge, start), [shape(2 * scens + 8, buses)], [], BETWEEN)
    edge = lax.ppermute(edge, "hour", [(0, 1), (1, 0)])
    peer = from_partners(sent)
    gen, base, hedged, sums = call(
        first_kernel,
        "first",
        (ptdf, inject, load, hedge, start, edge, cost, top, limit, line_top),
        [
            shape(width, buses),
            shape(width, buses),
            shape(width, buses),
            shape(sum_rows, LANES),
        ],
        step_scratch(width + scens) + ramp_scratch,
        work,
    )
    sum_terms = over_scens(sums)
    terms = len(sum_terms)
    relayed = areas == 4
    tied = call(
        functools.partial(tie_kernel, blocks, relayed),
        "ties",
        (base, spread, rows, weight, own, *peer),
        (
            [shape(2 * block_rows, LANES), shape(CAP, columns)]
            if relayed
            else [shape(block_rows, LANES)] * blocks
        )
        + [shape(columns, buses, dtype=bf16), shape(slots, columns), shape(slots, columns)],
        [],
        BETWEEN,
    )
    *sent, inject, mine, theirs = tied
    hedged, sums = call(
        functools.partial(second_kernel, terms, scen_total),
        "second",
        (ptdf, inject, gen, hedged, cost, top, limit, line_top, *sum_terms),
        [shape(width, buses), shape(sum_rows, LANES)],
        step_scratch(width)[1:] + [pltpu.VMEM((8 * pl.cdiv(hours + 1, 8), buses), f32)] + ramp_scratch,
        work,
    )
    sum_terms = over_scens(sums)
    if relayed:
        far, near = sent
        far = lax.ppermute(far, "area", [(a, a ^ 2) for a in range(areas)])
        arrived, _ = lax.optimization_barrier((far, sums))
        (both,) = call(relay_kernel, "relay", (near, arrived), [shape(2 * block_rows, LANES)], [], BETWEEN)
        peer = [far, lax.ppermute(both, "area", [(a, a ^ 1) for a in range(areas)])]
    else:
        peer = from_partners(sent)
    ends = [shape(hours, buses), shape(width, buses), shape(width, 2 * REACH * CAP)]
    gen_mean, hedge, tie_flow = call(
        functools.partial(last_kernel, blocks, terms, relayed, partner_of, scen_total),
        "last",
        (hedged, *peer, weight, mine, theirs, *sum_terms),
        ends,
        [pltpu.VMEM(x.shape, x.dtype) for x in ends] + [pltpu.SemaphoreType.DMA((len(ends),))],
        6 * slots * width * 2 * REACH * CAP,
        outs_in_place=True,
    )
    return (
        gen_mean,
        hedge.reshape(hours, scens, buses),
        tie_flow.reshape(hours, scens, 2 * REACH * CAP),
    )


def solution(mesh):
    return jax.shard_map(
        per_device,
        mesh=mesh,
        in_specs=(
            P(("group", "area"), None),
            P(("group", "area"), None),
            P(("group", "hour"), "scen", "area"),
            P(("group", "hour"), "area"),
            P(("group", "hour"), "scen", "area"),
            P(("group", "area")),
            P(("group", "area")),
            P(("group", "area")),
            P(("group", "area")),
            P("group", None),
            P("group", None),
            P("group", None),
            P("group", None),
        ),
        out_specs=(
            P(("group", "hour"), "area"),
            P(("group", "hour"), "scen", "area"),
            P(("group", "hour"), "scen", "area"),
        ),
        check_vma=False,
    )
```

```python
import functools

import jax
import jax.numpy as jnp
from jax import lax
from jax.experimental import pallas as pl
from jax.experimental.pallas import tpu as pltpu
from jax.sharding import PartitionSpec as P

HOURS = 24
REACH = 4
CAP = 16

STEP_SIZE = 0.5
LINE_CHUNK = 512
LANES = 128
BETWEEN = 20_000_000_000

CONTRACT_LAST = (((1,), (1,)), ((), ()))
CONTRACT_FIRST = (((0,), (0,)), ((), ()))
VMEM = pl.BlockSpec(memory_space=pltpu.VMEM)
ANY = pl.BlockSpec(memory_space=pltpu.HBM)


TARGETS = ((3, 2, 0, 1), (2, 3, 1, 0), (1, 0, 3, 2))


def partner_plan(areas):
    if areas == 4:

        def partner_of(here, i):
            return sum(jnp.where(here == a, target, 0) for a, target in enumerate(TARGETS[i]))

        def by_target(parts):
            out, back, pair = (
                lax.ppermute(part, "area", list(enumerate(target))) for part, target in zip(parts, TARGETS)
            )
            return [back, out, pair]

        return len(TARGETS), partner_of, by_target
    reach = min(REACH, areas - 1)
    shifts = sorted({s % areas for d in range(1, reach + 1) for s in (d, -d)})

    def by_shift(parts):
        sent = [
            lax.ppermute(part, "area", [(a, (a + s) % areas) for a in range(areas)])
            for part, s in zip(parts, shifts)
        ]
        return [sent[shifts.index(areas - s)] for s in shifts]

    return len(shifts), lambda here, i: lax.rem(here + shifts[i], areas), by_shift


def by_flips(here, flip_3, flip_2):
    return jnp.where(here < 2, flip_3, flip_2), jnp.where(here < 2, flip_2, flip_3)


def block_facts(here, partner):
    low = partner > here
    distance = jnp.abs(partner - here)
    block = jnp.clip(distance - 1, 0, REACH - 1)
    in_reach = (distance >= 1) & (distance <= REACH)
    return low, jnp.minimum(here, partner), block, in_reach


def fold(x):
    half = x.shape[0] // 2
    low = lax.broadcasted_iota(jnp.int32, (half, LANES), 1) < LANES // 2
    shared = jnp.where(low, x[0:half, LANES : 2 * LANES], x[half:, LANES : 2 * LANES])
    return jnp.concatenate([x[:, 0:LANES], shared], axis=0)


def unfold(packed):
    rows = 2 * packed.shape[0] // 3
    shared = packed[rows:, :]
    low = lax.broadcasted_iota(jnp.int32, shared.shape, 1) < LANES // 2
    turned = pltpu.roll(shared, LANES // 2, 1)
    rest = jnp.concatenate([jnp.where(low, shared, turned), jnp.where(low, turned, shared)], axis=0)
    return jnp.concatenate([packed[0:rows, :], rest], axis=1)


def repeat_rest(inject_ref, width):
    inject_ref[width:, :] = inject_ref[width - LANES // 2 : width, :]


def split_3(x):
    high = x.astype(jnp.bfloat16)
    rest = x - high.astype(jnp.float32)
    middle = rest.astype(jnp.bfloat16)
    rest = rest - middle.astype(jnp.float32)
    return jnp.concatenate([high, middle, rest.astype(jnp.bfloat16)], axis=0)


def put_row(packed_ref, hours, h, row):
    for j in range(row.shape[1] // LANES):
        packed_ref[j * hours + h : j * hours + h + 1, :] = row[:, j * LANES : (j + 1) * LANES]


def clear_rest(packed_ref, used):
    rows = packed_ref.shape[0]
    if used < rows:
        packed_ref[used:, :] = jnp.zeros((rows - used, LANES), jnp.float32)


def agree(mean_ref, sum_refs, hours, scen_total):
    for j in range(mean_ref.shape[1] // LANES):
        parts = [ref[j * hours : (j + 1) * hours, :] for ref in sum_refs]
        mean_ref[0:hours, j * LANES : (j + 1) * LANES] = functools.reduce(jnp.add, parts) / scen_total


def excess(diffs, limit):
    return diffs - jnp.clip(diffs, -limit, limit)


def write_ramp(mean_ref, beyond, limit, first_hour, padded_ref, excess_ref, ramp_ref):
    hours = ramp_ref.shape[0]
    padded_ref[0:1, :] = beyond
    padded_ref[1 : hours + 1, :] = mean_ref[0:hours, :]
    padded_ref[hours + 1 : hours + 2, :] = beyond
    diffs = padded_ref[1 : hours + 2, :] - padded_ref[0 : hours + 1, :]
    ids = first_hour + lax.broadcasted_iota(jnp.int32, diffs.shape, 0)
    valid = (ids >= 1) & (ids <= HOURS - 1)
    excess_ref[0 : hours + 1, :] = jnp.where(valid, excess(diffs, limit), 0.0)
    ramp_ref[...] = excess_ref[0:hours, :] - excess_ref[1 : hours + 1, :]


def line_work(inject_ref, ptdf_ref, line_max_ref, over_ref):
    inject = inject_ref[...]
    lines = ptdf_ref.shape[0]
    for at in range(0, lines, LINE_CHUNK):
        part = slice(at, at + LINE_CHUNK)
        flows = lax.dot_general(
            inject, ptdf_ref[part, :], CONTRACT_LAST, preferred_element_type=jnp.float32
        )
        limit = line_max_ref[:, part]
        over_ref[:, part] = (flows - jnp.clip(flows, -limit, limit)).astype(jnp.bfloat16)
    return jnp.dot(over_ref[...], ptdf_ref[...], preferred_element_type=jnp.float32)


def angle_kernel(
    blocks,
    partner_of,
    sens_in,
    demand_in,
    hedge_in,
    start_in,
    cost_in,
    max_in,
    limit_in,
    line_max_in,
    count_in,
    low_bus_in,
    high_bus_in,
    susc_in,
    *refs,
):
    own_refs, refs = refs[:blocks], refs[blocks:]
    (
        own_ref,
        edge_hedge_ref,
        inject_ref,
        spread_ref,
        rows_ref,
        weight_ref,
        demand_ref,
        start_ref,
        cost_ref,
        max_ref,
        limit_ref,
        line_max_ref,
        sens_ref,
        count_ref,
        low_bus_ref,
        high_bus_ref,
        susc_ref,
        onehot_ref,
        copy_sems,
    ) = refs
    hours, buses = start_ref.shape
    scens = demand_ref.shape[0] // hours
    here = lax.axis_index("area")
    last = (hours - 1) * scens
    edge_rows = pl.ds(pl.multiple_of((1 - lax.axis_index("hour")) * last, scens), scens)

    pairs = (
        (count_in, count_ref),
        (low_bus_in, low_bus_ref),
        (high_bus_in, high_bus_ref),
        (susc_in, susc_ref),
        (start_in, start_ref),
        (demand_in, demand_ref),
        (sens_in, sens_ref),
        (hedge_in.at[edge_rows], edge_hedge_ref),
        (cost_in, cost_ref),
        (max_in, max_ref),
        (limit_in, limit_ref),
        (line_max_in, line_max_ref),
    )
    copies = [pltpu.make_async_copy(src, dst, copy_sems.at[i]) for i, (src, dst) in enumerate(pairs)]
    for copy in (*copies[4:7], *copies[:4], *copies[7:]):
        copy.start()

    for copy in copies[:4]:
        copy.wait()
    for i in range(blocks):
        partner = partner_of(here, i)
        low, row, block, in_reach = block_facts(here, partner)
        slots = slice(i * CAP, (i + 1) * CAP)
        pick = lax.broadcasted_iota(jnp.int32, (CAP, REACH * CAP), 1) == (
            block * CAP + lax.broadcasted_iota(jnp.int32, (CAP, REACH * CAP), 0)
        )
        table_row = pl.ds(row, 1)
        bus_row = jnp.where(low, low_bus_ref[table_row, :], high_bus_ref[table_row, :])
        bus = jnp.sum(jnp.where(pick, bus_row.astype(jnp.float32), 0.0), axis=1, keepdims=True)
        susc = jnp.sum(jnp.where(pick, susc_ref[table_row, :], 0.0), axis=1, keepdims=True)
        count_row = count_ref[table_row, :].astype(jnp.float32)
        is_block = lax.broadcasted_iota(jnp.int32, (CAP, REACH), 1) == block
        count = jnp.sum(jnp.where(is_block, count_row, 0.0), axis=1, keepdims=True)
        slot_ids = lax.broadcasted_iota(jnp.int32, (CAP, 1), 0).astype(jnp.float32)
        live = jnp.where((slot_ids < count) & in_reach, 1.0, 0.0)
        sign = jnp.where(low, 1.0, -1.0)
        bus_ids = lax.broadcasted_iota(jnp.int32, (CAP, buses), 1).astype(jnp.float32)
        onehot = jnp.where(bus_ids == bus, live, 0.0)
        onehot_ref[slots, :] = onehot.astype(jnp.bfloat16)
        spread_ref[slots, :] = (-sign * onehot).astype(jnp.bfloat16)
        weight_ref[slots, :] = jnp.broadcast_to(live * sign * susc, (CAP, 128))

    for copy in copies[4:7]:
        copy.wait()
    for h in range(hours):
        part = slice(h * scens, (h + 1) * scens)
        inject_ref[part, :] = (start_ref[h : h + 1, :] - demand_ref[part, :]).astype(jnp.bfloat16)
    repeat_rest(inject_ref, hours * scens)
    rows = jnp.dot(onehot_ref[...], sens_ref[...], preferred_element_type=jnp.float32)
    rows_ref[...] = rows.astype(jnp.bfloat16)
    own = lax.dot_general(
        rows_ref[...], inject_ref[...], CONTRACT_LAST, preferred_element_type=jnp.float32
    )
    own_ref[...] = own
    for i in range(blocks):
        own_refs[i][...] = fold(own[i * CAP : (i + 1) * CAP, :])

    for copy in copies[7:]:
        copy.wait()


def edge_kernel(demand_ref, edge_hedge_ref, start_ref, edge_ref):
    scens = edge_hedge_ref.shape[0]
    hours = start_ref.shape[0]
    early = lax.axis_index("hour") == 0
    last = (hours - 1) * scens
    at = 2 * scens
    edge_ref[0:scens, :] = jnp.where(early, demand_ref[last:, :], demand_ref[0:scens, :])
    edge_ref[scens:at, :] = edge_hedge_ref[...]
    edge_ref[at : at + 1, :] = jnp.where(early, start_ref[hours - 1 : hours, :], start_ref[0:1, :])
    edge_ref[at + 1 : at + 2, :] = jnp.where(
        early, start_ref[hours - 2 : hours - 1, :], start_ref[1:2, :]
    )


def first_kernel(
    ptdf_ref,
    own_inject_ref,
    demand_ref,
    hedge_ref,
    start_ref,
    edge_ref,
    cost_ref,
    max_ref,
    limit_ref,
    line_max_ref,
    gen_ref,
    base_ref,
    hedged_ref,
    sums_ref,
    inject_ref,
    over_ref,
    back_ref,
    padded_ref,
    excess_ref,
    ramp_ref,
):
    hours, buses = start_ref.shape
    width = demand_ref.shape[0]
    scens = width // hours
    at = 2 * scens
    early = lax.axis_index("hour") == 0
    first_hour = lax.axis_index("hour") * hours
    beyond = edge_ref[at : at + 1, :]
    limit = limit_ref[...]
    cost = cost_ref[...]
    top = max_ref[...]

    inject_ref[0:width, :] = own_inject_ref[0:width, :]
    inject_ref[width : width + scens, :] = (beyond - edge_ref[0:scens, :]).astype(jnp.bfloat16)
    back_ref[...] = line_work(inject_ref, ptdf_ref, line_max_ref, over_ref)
    write_ramp(start_ref, beyond, limit, first_hour, padded_ref, excess_ref, ramp_ref)

    def step(mean, hedge, back, ramp):
        grad = cost + back + (mean - mean + hedge) + ramp
        gen = jnp.clip(mean - STEP_SIZE * grad, 0.0, top)
        return gen, gen + hedge

    for h in range(hours):
        part = slice(h * scens, (h + 1) * scens)
        mean = start_ref[h : h + 1, :]
        gen, hedged = step(mean, hedge_ref[part, :], back_ref[part, :], ramp_ref[h : h + 1, :])
        gen_ref[part, :] = gen
        base_ref[part, :] = gen - demand_ref[part, :]
        hedged_ref[part, :] = hedged
        put_row(sums_ref, hours + 1, h, jnp.sum(hedged, axis=0, keepdims=True))
    near = jnp.where(early, start_ref[hours - 1 : hours, :], start_ref[0:1, :])
    ramp = excess(beyond - near, limit) + excess(beyond - edge_ref[at + 1 : at + 2, :], limit)
    _, hedged = step(beyond, edge_ref[scens:at, :], back_ref[width : width + scens, :], ramp)
    put_row(sums_ref, hours + 1, hours, jnp.sum(hedged, axis=0, keepdims=True))
    clear_rest(sums_ref, (hours + 1) * (buses // LANES))


def tie_kernel(blocks, relayed, base_ref, spread_ref, rows_ref, weight_ref, own_ref, *refs):
    peer_refs, refs = refs[:blocks], refs[blocks:]
    *next_refs, inject_ref, mine_ref, theirs_ref = refs
    width = base_ref.shape[0]

    weight = weight_ref[:, 0:1]
    own = own_ref[...]
    peer = jnp.concatenate([unfold(ref[...]) for ref in peer_refs], axis=0)
    est_mine = weight * own
    est_theirs = -weight * peer
    flow = (est_mine + est_theirs) * 0.5
    dual_mine = est_mine - flow
    dual_theirs = est_theirs - flow
    spread = spread_ref[...]
    add = lax.dot_general(
        split_3(flow),
        jnp.concatenate([spread, spread, spread], axis=0),
        CONTRACT_FIRST,
        preferred_element_type=jnp.float32,
    )
    inject_ref[0:width, :] = (base_ref[...] + add[0:width, :]).astype(jnp.bfloat16)
    repeat_rest(inject_ref, width)

    own_next = lax.dot_general(
        rows_ref[...], inject_ref[...], CONTRACT_LAST, preferred_element_type=jnp.float32
    )
    parts = [own_next[i * CAP : (i + 1) * CAP, :] for i in range(blocks)]
    if relayed:
        far_ref, near_ref = next_refs
        flip_3, flip_2 = by_flips(lax.axis_index("area"), parts[0], parts[1])
        far_ref[...] = fold(jnp.concatenate([flip_2, flip_3], axis=0))
        near_ref[...] = parts[2]
    else:
        for ref, part in zip(next_refs, parts):
            ref[...] = fold(part)
    mine_ref[...] = weight * (own_next - peer) + dual_mine
    theirs_ref[...] = weight * own + dual_theirs


def second_kernel(
    terms,
    scen_total,
    ptdf_ref,
    inject_ref,
    gen_ref,
    hedged_ref,
    cost_ref,
    max_ref,
    limit_ref,
    line_max_ref,
    *refs,
):
    sum_refs, refs = refs[:terms], refs[terms:]
    (hedged_out_ref, sums_out_ref, over_ref, back_ref, mean_ref, padded_ref, excess_ref, ramp_ref) = refs
    hours, buses = ramp_ref.shape
    width = back_ref.shape[0]
    scens = width // hours
    first_hour = lax.axis_index("hour") * hours

    back_ref[...] = line_work(inject_ref.at[0:width, :], ptdf_ref, line_max_ref, over_ref)
    agree(mean_ref, sum_refs, hours + 1, scen_total)
    write_ramp(
        mean_ref, mean_ref[hours : hours + 1, :], limit_ref[...], first_hour, padded_ref, excess_ref, ramp_ref
    )
    cost = cost_ref[...]
    top = max_ref[...]
    for h in range(hours):
        part = slice(h * scens, (h + 1) * scens)
        mean = mean_ref[h : h + 1, :]
        gen = gen_ref[part, :]
        hedge = hedged_ref[part, :] - mean
        grad = cost + back_ref[part, :] + (gen - mean + hedge) + ramp_ref[h : h + 1, :]
        gen = jnp.clip(gen - STEP_SIZE * grad, 0.0, top)
        hedged = gen + hedge
        hedged_out_ref[part, :] = hedged
        put_row(sums_out_ref, hours, h, jnp.sum(hedged, axis=0, keepdims=True))
    clear_rest(sums_out_ref, hours * (buses // LANES))


def relay_kernel(near_ref, far_ref, both_ref):
    low = lax.broadcasted_iota(jnp.int32, (CAP, LANES), 1) < LANES // 2
    both_ref[0:CAP, :] = near_ref[:, 0:LANES]
    both_ref[CAP : 2 * CAP, :] = far_ref[CAP : 2 * CAP, :]
    both_ref[2 * CAP :, :] = jnp.where(low, near_ref[:, LANES:], far_ref[2 * CAP :, :])


def agree_kernel(scen_total, hedged_ref, *refs):
    sum_refs, (mean_ref, hedge_ref) = refs[:-2], refs[-2:]
    hours = mean_ref.shape[0]
    scens = hedged_ref.shape[0] // hours
    agree(mean_ref, sum_refs, hours, scen_total)
    for h in range(hours):
        part = slice(h * scens, (h + 1) * scens)
        hedge_ref[part, :] = hedged_ref[part, :] - mean_ref[h : h + 1, :]


def flow_kernel(blocks, relayed, partner_of, *refs):
    *peer_refs, weight_ref, mine_ref, theirs_ref, tie_ref, placed_ref = refs
    here = lax.axis_index("area")
    placed_ref[...] = jnp.zeros_like(placed_ref)
    if relayed:
        far, both = (unfold(ref[...]) for ref in peer_refs)
        peers = [*by_flips(here, both[CAP:, :], far[0:CAP, :]), both[0:CAP, :]]
    else:
        peers = [unfold(ref[...]) for ref in peer_refs]
    for i in range(blocks):
        slots = slice(i * CAP, (i + 1) * CAP)
        flow = (mine_ref[slots, :] + (theirs_ref[slots, :] - weight_ref[slots, 0:1] * peers[i])) * 0.5
        low, _, block, in_reach = block_facts(here, partner_of(here, i))
        first = block * CAP + jnp.where(low, 0, REACH * CAP)

        @pl.when(in_reach)
        def _():
            placed_ref[pl.ds(pl.multiple_of(first, CAP), CAP), :] = flow

    tie_ref[...] = jnp.transpose(placed_ref[...])[0 : tie_ref.shape[0], :]


def call(kernel, name, args, outs, scratch, flops, in_place=()):
    size = sum(x.size * x.dtype.itemsize for x in list(args) + list(outs))
    return pl.pallas_call(
        kernel,
        name=name,
        out_shape=outs,
        in_specs=[ANY if i in in_place else VMEM for i in range(len(args))],
        out_specs=[VMEM] * len(outs),
        scratch_shapes=scratch,
        compiler_params=pltpu.CompilerParams(vmem_limit_bytes=32 * 1024 * 1024),
        cost_estimate=pl.CostEstimate(flops=flops, bytes_accessed=size, transcendentals=0),
    )(*(pltpu.with_memory_space_constraint(x, pltpu.HBM) if i in in_place else x for i, x in enumerate(args)))


def per_device(
    ptdf,
    angle_sens,
    demand,
    gen_start,
    hedge_dual,
    gen_cost,
    gen_max,
    gen_ramp,
    line_max,
    tie_count,
    tie_low_bus,
    tie_high_bus,
    tie_susc,
):
    hours, scens, buses = demand.shape
    lines = ptdf.shape[0]
    width = hours * scens
    areas = lax.axis_size("area")
    n_scen = lax.axis_size("scen")
    assert lax.axis_size("hour") == 2 and hours >= 2
    assert width % LANES == LANES // 2 and width < 2 * LANES
    columns = 2 * LANES
    block_rows = CAP * 3 // 2
    scen_total = scens * n_scen
    blocks, partner_of, from_partners = partner_plan(areas)
    slots = blocks * CAP
    pieces = buses // LANES
    sum_rows = 8 * pl.cdiv((hours + 1) * pieces, 8)
    f32, bf16 = jnp.float32, jnp.bfloat16

    def shape(*dims, dtype=f32):
        return jax.ShapeDtypeStruct(dims, dtype)

    def over_scens(sums):
        if n_scen == 2:
            return [sums, lax.ppermute(sums, "scen", [(0, 1), (1, 0)])]
        return [lax.psum(sums, "scen")]

    work = 4 * width * lines * buses

    def step_scratch(rows):
        return [
            pltpu.VMEM((rows, buses), bf16),
            pltpu.VMEM((rows, lines), bf16),
            pltpu.VMEM((rows, buses), f32),
        ]

    ramp_scratch = [
        pltpu.VMEM((hours + 4, buses), f32),
        pltpu.VMEM((hours + 4, buses), f32),
        pltpu.VMEM((hours, buses), f32),
    ]
    tables = (tie_count, tie_low_bus, tie_high_bus, tie_susc)
    vectors = [x.reshape(1, -1) for x in (gen_cost, gen_max, gen_ramp, line_max)]
    hedge = hedge_dual.reshape(width, buses)
    made = call(
        functools.partial(angle_kernel, blocks, partner_of),
        "angles",
        (
            angle_sens,
            demand.reshape(width, buses),
            hedge,
            gen_start,
            *vectors,
            *tables,
        ),
        [shape(block_rows, LANES)] * blocks
        + [
            shape(slots, columns),
            shape(scens, buses),
            shape(columns, buses, dtype=bf16),
            shape(slots, buses, dtype=bf16),
            shape(slots, buses, dtype=bf16),
            shape(slots, 128),
            shape(width, buses),
            shape(hours, buses),
            shape(1, buses),
            shape(1, buses),
            shape(1, buses),
            shape(1, lines),
        ],
        [pltpu.VMEM(x.shape, x.dtype) for x in (angle_sens, *tables)]
        + [pltpu.VMEM((slots, buses), bf16), pltpu.SemaphoreType.DMA((12,))],
        2 * slots * buses * (width + buses),
        range(12),
    )
    sent = made[:blocks]
    own, edge_hedge, inject, spread, rows, weight, load, start = made[blocks : blocks + 8]
    cost, top, limit, line_top = made[blocks + 8 :]
    (edge,) = call(edge_kernel, "edge", (load, edge_hedge, start), [shape(2 * scens + 8, buses)], [], BETWEEN)
    edge = lax.ppermute(edge, "hour", [(0, 1), (1, 0)])
    peer = from_partners(sent)
    gen, base, hedged, sums = call(
        first_kernel,
        "first",
        (ptdf, inject, load, hedge, start, edge, cost, top, limit, line_top),
        [
            shape(width, buses),
            shape(width, buses),
            shape(width, buses),
            shape(sum_rows, LANES),
        ],
        step_scratch(width + scens) + ramp_scratch,
        work,
    )
    sum_terms = over_scens(sums)
    terms = len(sum_terms)
    relayed = areas == 4
    tied = call(
        functools.partial(tie_kernel, blocks, relayed),
        "ties",
        (base, spread, rows, weight, own, *peer),
        (
            [shape(2 * block_rows, LANES), shape(CAP, columns)]
            if relayed
            else [shape(block_rows, LANES)] * blocks
        )
        + [shape(columns, buses, dtype=bf16), shape(slots, columns), shape(slots, columns)],
        [],
        BETWEEN,
    )
    *sent, inject, mine, theirs = tied
    hedged, sums = call(
        functools.partial(second_kernel, terms, scen_total),
        "second",
        (ptdf, inject, gen, hedged, cost, top, limit, line_top, *sum_terms),
        [shape(width, buses), shape(sum_rows, LANES)],
        step_scratch(width)[1:] + [pltpu.VMEM((8 * pl.cdiv(hours + 1, 8), buses), f32)] + ramp_scratch,
        work,
    )
    sum_terms = over_scens(sums)
    if relayed:
        far, near = sent
        far = lax.ppermute(far, "area", [(a, a ^ 2) for a in range(areas)])
        arrived, _ = lax.optimization_barrier((far, sums))
        (both,) = call(relay_kernel, "relay", (near, arrived), [shape(2 * block_rows, LANES)], [], BETWEEN)
        peer = [far, lax.ppermute(both, "area", [(a, a ^ 1) for a in range(areas)])]
    else:
        peer = from_partners(sent)
    gen_mean, hedge = call(
        functools.partial(agree_kernel, scen_total),
        "agree",
        (hedged, *sum_terms),
        [shape(hours, buses), shape(width, buses)],
        [],
        BETWEEN,
    )
    peer, gen_mean = lax.optimization_barrier((peer, gen_mean))
    (tie_flow,) = call(
        functools.partial(flow_kernel, blocks, relayed, partner_of),
        "flows",
        (*peer, weight, mine, theirs),
        [shape(width, 2 * REACH * CAP)],
        [pltpu.VMEM((2 * REACH * CAP, columns), f32)],
        slots * columns,
    )
    return (
        gen_mean,
        hedge.reshape(hours, scens, buses),
        tie_flow.reshape(hours, scens, 2 * REACH * CAP),
    )


def solution(mesh):
    return jax.shard_map(
        per_device,
        mesh=mesh,
        in_specs=(
            P(("group", "area"), None),
            P(("group", "area"), None),
            P(("group", "hour"), "scen", "area"),
            P(("group", "hour"), "area"),
            P(("group", "hour"), "scen", "area"),
            P(("group", "area")),
            P(("group", "area")),
            P(("group", "area")),
            P(("group", "area")),
            P("group", None),
            P("group", None),
            P("group", None),
            P("group", None),
        ),
        out_specs=(
            P(("group", "hour"), "area"),
            P(("group", "hour"), "scen", "area"),
            P(("group", "hour"), "scen", "area"),
        ),
        check_vma=False,
    )
```

```python
import functools

import jax
import jax.numpy as jnp
from jax import lax
from jax.experimental import pallas as pl
from jax.experimental.pallas import tpu as pltpu
from jax.sharding import PartitionSpec as P

HOURS = 24
REACH = 4
CAP = 16

STEP_SIZE = 0.5
LINE_CHUNK = 512
LANES = 128
PIECES = 4
BETWEEN = 20_000_000_000

CONTRACT_LAST = (((1,), (1,)), ((), ()))
CONTRACT_FIRST = (((0,), (0,)), ((), ()))
VMEM = pl.BlockSpec(memory_space=pltpu.VMEM)
ANY = pl.BlockSpec(memory_space=pltpu.HBM)


TARGETS = ((3, 2, 0, 1), (2, 3, 1, 0), (1, 0, 3, 2))


def partner_plan(areas):
    if areas == 4:

        def partner_of(here, i):
            return sum(jnp.where(here == a, target, 0) for a, target in enumerate(TARGETS[i]))

        def by_target(parts):
            out, back, pair = (
                lax.ppermute(part, "area", list(enumerate(target))) for part, target in zip(parts, TARGETS)
            )
            return [back, out, pair]

        return len(TARGETS), partner_of, by_target
    reach = min(REACH, areas - 1)
    shifts = sorted({s % areas for d in range(1, reach + 1) for s in (d, -d)})

    def by_shift(parts):
        sent = [
            lax.ppermute(part, "area", [(a, (a + s) % areas) for a in range(areas)])
            for part, s in zip(parts, shifts)
        ]
        return [sent[shifts.index(areas - s)] for s in shifts]

    return len(shifts), lambda here, i: lax.rem(here + shifts[i], areas), by_shift


def by_flips(here, flip_3, flip_2):
    return jnp.where(here < 2, flip_3, flip_2), jnp.where(here < 2, flip_2, flip_3)


def block_facts(here, partner):
    low = partner > here
    distance = jnp.abs(partner - here)
    block = jnp.clip(distance - 1, 0, REACH - 1)
    in_reach = (distance >= 1) & (distance <= REACH)
    return low, jnp.minimum(here, partner), block, in_reach


def fold(x):
    half = x.shape[0] // 2
    low = lax.broadcasted_iota(jnp.int32, (half, LANES), 1) < LANES // 2
    shared = jnp.where(low, x[0:half, LANES : 2 * LANES], x[half:, LANES : 2 * LANES])
    return jnp.concatenate([x[:, 0:LANES], shared], axis=0)


def unfold(packed):
    rows = 2 * packed.shape[0] // 3
    shared = packed[rows:, :]
    low = lax.broadcasted_iota(jnp.int32, shared.shape, 1) < LANES // 2
    turned = pltpu.roll(shared, LANES // 2, 1)
    rest = jnp.concatenate([jnp.where(low, shared, turned), jnp.where(low, turned, shared)], axis=0)
    return jnp.concatenate([packed[0:rows, :], rest], axis=1)


def repeat_rest(inject_ref, width):
    inject_ref[width:, :] = inject_ref[width - LANES // 2 : width, :]


def split_3(x):
    high = x.astype(jnp.bfloat16)
    rest = x - high.astype(jnp.float32)
    middle = rest.astype(jnp.bfloat16)
    rest = rest - middle.astype(jnp.float32)
    return jnp.concatenate([high, middle, rest.astype(jnp.bfloat16)], axis=0)


def put_row(packed_ref, hours, h, row):
    for j in range(row.shape[1] // LANES):
        packed_ref[j * hours + h : j * hours + h + 1, :] = row[:, j * LANES : (j + 1) * LANES]


def clear_rest(packed_ref, used):
    rows = packed_ref.shape[0]
    if used < rows:
        packed_ref[used:, :] = jnp.zeros((rows - used, LANES), jnp.float32)


def agree(mean_ref, sum_refs, hours, scen_total):
    for j in range(mean_ref.shape[1] // LANES):
        parts = [ref[j * hours : (j + 1) * hours, :] for ref in sum_refs]
        mean_ref[0:hours, j * LANES : (j + 1) * LANES] = functools.reduce(jnp.add, parts) / scen_total


def excess(diffs, limit):
    return diffs - jnp.clip(diffs, -limit, limit)


def write_ramp(mean_ref, beyond, limit, first_hour, padded_ref, excess_ref, ramp_ref):
    hours = ramp_ref.shape[0]
    padded_ref[0:1, :] = beyond
    padded_ref[1 : hours + 1, :] = mean_ref[0:hours, :]
    padded_ref[hours + 1 : hours + 2, :] = beyond
    diffs = padded_ref[1 : hours + 2, :] - padded_ref[0 : hours + 1, :]
    ids = first_hour + lax.broadcasted_iota(jnp.int32, diffs.shape, 0)
    valid = (ids >= 1) & (ids <= HOURS - 1)
    excess_ref[0 : hours + 1, :] = jnp.where(valid, excess(diffs, limit), 0.0)
    ramp_ref[...] = excess_ref[0:hours, :] - excess_ref[1 : hours + 1, :]


def line_work(inject_ref, ptdf_ref, line_max_ref, over_ref):
    inject = inject_ref[...]
    lines = ptdf_ref.shape[0]
    for at in range(0, lines, LINE_CHUNK):
        part = slice(at, at + LINE_CHUNK)
        flows = lax.dot_general(
            inject, ptdf_ref[part, :], CONTRACT_LAST, preferred_element_type=jnp.float32
        )
        limit = line_max_ref[:, part]
        over_ref[:, part] = (flows - jnp.clip(flows, -limit, limit)).astype(jnp.bfloat16)
    return jnp.dot(over_ref[...], ptdf_ref[...], preferred_element_type=jnp.float32)


def angle_kernel(
    blocks,
    partner_of,
    sens_in,
    demand_in,
    hedge_in,
    start_in,
    cost_in,
    max_in,
    limit_in,
    line_max_in,
    count_in,
    low_bus_in,
    high_bus_in,
    susc_in,
    *refs,
):
    own_refs, refs = refs[:blocks], refs[blocks:]
    (
        own_ref,
        edge_hedge_ref,
        inject_ref,
        spread_ref,
        rows_ref,
        weight_ref,
        demand_ref,
        start_ref,
        cost_ref,
        max_ref,
        limit_ref,
        line_max_ref,
        sens_ref,
        count_ref,
        low_bus_ref,
        high_bus_ref,
        susc_ref,
        onehot_ref,
        copy_sems,
    ) = refs
    hours, buses = start_ref.shape
    scens = demand_ref.shape[0] // hours
    here = lax.axis_index("area")
    last = (hours - 1) * scens
    edge_rows = pl.ds(pl.multiple_of((1 - lax.axis_index("hour")) * last, scens), scens)

    piece = buses // PIECES
    hours_piece = hours // PIECES

    def rows_of(source, target, first, count):
        return source.at[pl.ds(first, count)], target.at[pl.ds(first, count)]

    tables = (
        (count_in, count_ref),
        (low_bus_in, low_bus_ref),
        (high_bus_in, high_bus_ref),
        (susc_in, susc_ref),
        (start_in, start_ref),
    )
    loads = [
        rows_of(demand_in, demand_ref, p * hours_piece * scens, hours_piece * scens) for p in range(PIECES)
    ]
    angles = [rows_of(sens_in, sens_ref, p * piece, piece) for p in range(PIECES)]
    later = (
        (hedge_in.at[edge_rows], edge_hedge_ref),
        (cost_in, cost_ref),
        (max_in, max_ref),
        (limit_in, limit_ref),
        (line_max_in, line_max_ref),
    )
    sems = iter(range(len(tables) + len(loads) + len(angles) + len(later)))

    def copies_of(pairs):
        return [pltpu.make_async_copy(src, dst, copy_sems.at[next(sems)]) for src, dst in pairs]

    tables, loads, angles, later = (copies_of(pairs) for pairs in (tables, loads, angles, later))
    for copy in (*tables, *loads, *angles):
        copy.start()
    for copy in tables:
        copy.wait()
    for i in range(blocks):
        partner = partner_of(here, i)
        low, row, block, in_reach = block_facts(here, partner)
        slots = slice(i * CAP, (i + 1) * CAP)
        pick = lax.broadcasted_iota(jnp.int32, (CAP, REACH * CAP), 1) == (
            block * CAP + lax.broadcasted_iota(jnp.int32, (CAP, REACH * CAP), 0)
        )
        table_row = pl.ds(row, 1)
        bus_row = jnp.where(low, low_bus_ref[table_row, :], high_bus_ref[table_row, :])
        bus = jnp.sum(jnp.where(pick, bus_row.astype(jnp.float32), 0.0), axis=1, keepdims=True)
        susc = jnp.sum(jnp.where(pick, susc_ref[table_row, :], 0.0), axis=1, keepdims=True)
        count_row = count_ref[table_row, :].astype(jnp.float32)
        is_block = lax.broadcasted_iota(jnp.int32, (CAP, REACH), 1) == block
        count = jnp.sum(jnp.where(is_block, count_row, 0.0), axis=1, keepdims=True)
        slot_ids = lax.broadcasted_iota(jnp.int32, (CAP, 1), 0).astype(jnp.float32)
        live = jnp.where((slot_ids < count) & in_reach, 1.0, 0.0)
        sign = jnp.where(low, 1.0, -1.0)
        bus_ids = lax.broadcasted_iota(jnp.int32, (CAP, buses), 1).astype(jnp.float32)
        onehot = jnp.where(bus_ids == bus, live, 0.0)
        onehot_ref[slots, :] = onehot.astype(jnp.bfloat16)
        spread_ref[slots, :] = (-sign * onehot).astype(jnp.bfloat16)
        weight_ref[slots, :] = jnp.broadcast_to(live * sign * susc, (CAP, 128))

    for copy in later:
        copy.start()
    for p, load in enumerate(loads):
        load.wait()
        for h in range(p * hours_piece, (p + 1) * hours_piece):
            part = slice(h * scens, (h + 1) * scens)
            inject_ref[part, :] = (start_ref[h : h + 1, :] - demand_ref[part, :]).astype(jnp.bfloat16)
    repeat_rest(inject_ref, hours * scens)
    rows = 0.0
    for p, angle in enumerate(angles):
        angle.wait()
        part = slice(p * piece, (p + 1) * piece)
        rows = rows + jnp.dot(
            onehot_ref[:, part], sens_ref[part, :], preferred_element_type=jnp.float32
        )
    rows_ref[...] = rows.astype(jnp.bfloat16)
    own = lax.dot_general(
        rows_ref[...], inject_ref[...], CONTRACT_LAST, preferred_element_type=jnp.float32
    )
    own_ref[...] = own
    for i in range(blocks):
        own_refs[i][...] = fold(own[i * CAP : (i + 1) * CAP, :])

    for copy in later:
        copy.wait()


def edge_kernel(demand_ref, edge_hedge_ref, start_ref, edge_ref):
    scens = edge_hedge_ref.shape[0]
    hours = start_ref.shape[0]
    early = lax.axis_index("hour") == 0
    last = (hours - 1) * scens
    at = 2 * scens
    edge_ref[0:scens, :] = jnp.where(early, demand_ref[last:, :], demand_ref[0:scens, :])
    edge_ref[scens:at, :] = edge_hedge_ref[...]
    edge_ref[at : at + 1, :] = jnp.where(early, start_ref[hours - 1 : hours, :], start_ref[0:1, :])
    edge_ref[at + 1 : at + 2, :] = jnp.where(
        early, start_ref[hours - 2 : hours - 1, :], start_ref[1:2, :]
    )


def first_kernel(
    ptdf_ref,
    own_inject_ref,
    demand_ref,
    hedge_ref,
    start_ref,
    edge_ref,
    cost_ref,
    max_ref,
    limit_ref,
    line_max_ref,
    gen_ref,
    base_ref,
    hedged_ref,
    sums_ref,
    inject_ref,
    over_ref,
    back_ref,
    padded_ref,
    excess_ref,
    ramp_ref,
):
    hours, buses = start_ref.shape
    width = demand_ref.shape[0]
    scens = width // hours
    at = 2 * scens
    early = lax.axis_index("hour") == 0
    first_hour = lax.axis_index("hour") * hours
    beyond = edge_ref[at : at + 1, :]
    limit = limit_ref[...]
    cost = cost_ref[...]
    top = max_ref[...]

    inject_ref[0:width, :] = own_inject_ref[0:width, :]
    inject_ref[width : width + scens, :] = (beyond - edge_ref[0:scens, :]).astype(jnp.bfloat16)
    back_ref[...] = line_work(inject_ref, ptdf_ref, line_max_ref, over_ref)
    write_ramp(start_ref, beyond, limit, first_hour, padded_ref, excess_ref, ramp_ref)

    def step(mean, hedge, back, ramp):
        grad = cost + back + (mean - mean + hedge) + ramp
        gen = jnp.clip(mean - STEP_SIZE * grad, 0.0, top)
        return gen, gen + hedge

    for h in range(hours):
        part = slice(h * scens, (h + 1) * scens)
        mean = start_ref[h : h + 1, :]
        gen, hedged = step(mean, hedge_ref[part, :], back_ref[part, :], ramp_ref[h : h + 1, :])
        gen_ref[part, :] = gen
        base_ref[part, :] = gen - demand_ref[part, :]
        hedged_ref[part, :] = hedged
        put_row(sums_ref, hours + 1, h, jnp.sum(hedged, axis=0, keepdims=True))
    near = jnp.where(early, start_ref[hours - 1 : hours, :], start_ref[0:1, :])
    ramp = excess(beyond - near, limit) + excess(beyond - edge_ref[at + 1 : at + 2, :], limit)
    _, hedged = step(beyond, edge_ref[scens:at, :], back_ref[width : width + scens, :], ramp)
    put_row(sums_ref, hours + 1, hours, jnp.sum(hedged, axis=0, keepdims=True))
    clear_rest(sums_ref, (hours + 1) * (buses // LANES))


def tie_kernel(blocks, relayed, base_ref, spread_ref, rows_ref, weight_ref, own_ref, *refs):
    peer_refs, refs = refs[:blocks], refs[blocks:]
    *next_refs, inject_ref, mine_ref, theirs_ref = refs
    width = base_ref.shape[0]

    weight = weight_ref[:, 0:1]
    own = own_ref[...]
    peer = jnp.concatenate([unfold(ref[...]) for ref in peer_refs], axis=0)
    est_mine = weight * own
    est_theirs = -weight * peer
    flow = (est_mine + est_theirs) * 0.5
    dual_mine = est_mine - flow
    dual_theirs = est_theirs - flow
    spread = spread_ref[...]
    add = lax.dot_general(
        split_3(flow),
        jnp.concatenate([spread, spread, spread], axis=0),
        CONTRACT_FIRST,
        preferred_element_type=jnp.float32,
    )
    inject_ref[0:width, :] = (base_ref[...] + add[0:width, :]).astype(jnp.bfloat16)
    repeat_rest(inject_ref, width)

    own_next = lax.dot_general(
        rows_ref[...], inject_ref[...], CONTRACT_LAST, preferred_element_type=jnp.float32
    )
    parts = [own_next[i * CAP : (i + 1) * CAP, :] for i in range(blocks)]
    if relayed:
        far_ref, near_ref = next_refs
        flip_3, flip_2 = by_flips(lax.axis_index("area"), parts[0], parts[1])
        far_ref[...] = fold(jnp.concatenate([flip_2, flip_3], axis=0))
        near_ref[...] = parts[2]
    else:
        for ref, part in zip(next_refs, parts):
            ref[...] = fold(part)
    mine_ref[...] = weight * (own_next - peer) + dual_mine
    theirs_ref[...] = weight * own + dual_theirs


def second_kernel(
    terms,
    scen_total,
    ptdf_ref,
    inject_ref,
    gen_ref,
    hedged_ref,
    cost_ref,
    max_ref,
    limit_ref,
    line_max_ref,
    *refs,
):
    sum_refs, refs = refs[:terms], refs[terms:]
    (hedged_out_ref, sums_out_ref, over_ref, back_ref, mean_ref, padded_ref, excess_ref, ramp_ref) = refs
    hours, buses = ramp_ref.shape
    width = back_ref.shape[0]
    scens = width // hours
    first_hour = lax.axis_index("hour") * hours

    back_ref[...] = line_work(inject_ref.at[0:width, :], ptdf_ref, line_max_ref, over_ref)
    agree(mean_ref, sum_refs, hours + 1, scen_total)
    write_ramp(
        mean_ref, mean_ref[hours : hours + 1, :], limit_ref[...], first_hour, padded_ref, excess_ref, ramp_ref
    )
    cost = cost_ref[...]
    top = max_ref[...]
    for h in range(hours):
        part = slice(h * scens, (h + 1) * scens)
        mean = mean_ref[h : h + 1, :]
        gen = gen_ref[part, :]
        hedge = hedged_ref[part, :] - mean
        grad = cost + back_ref[part, :] + (gen - mean + hedge) + ramp_ref[h : h + 1, :]
        gen = jnp.clip(gen - STEP_SIZE * grad, 0.0, top)
        hedged = gen + hedge
        hedged_out_ref[part, :] = hedged
        put_row(sums_out_ref, hours, h, jnp.sum(hedged, axis=0, keepdims=True))
    clear_rest(sums_out_ref, hours * (buses // LANES))


def relay_kernel(near_ref, far_ref, both_ref):
    low = lax.broadcasted_iota(jnp.int32, (CAP, LANES), 1) < LANES // 2
    both_ref[0:CAP, :] = near_ref[:, 0:LANES]
    both_ref[CAP : 2 * CAP, :] = far_ref[CAP : 2 * CAP, :]
    both_ref[2 * CAP :, :] = jnp.where(low, near_ref[:, LANES:], far_ref[2 * CAP :, :])


def last_kernel(blocks, terms, relayed, partner_of, scen_total, hedged_ref, *refs):
    *peer_refs, weight_ref, mine_ref, theirs_ref = refs[: -8 - terms]
    sum_refs = refs[-8 - terms : -8]
    mean_out, hedge_out, tie_out, mean_ref, hedge_ref, tie_ref, placed_ref, copy_sems = refs[-8:]
    hours = mean_ref.shape[0]
    scens = hedged_ref.shape[0] // hours
    copies = []

    def send(src, dst):
        copies.append(pltpu.make_async_copy(src, dst, copy_sems.at[len(copies)]))
        copies[-1].start()

    agree(mean_ref, sum_refs, hours, scen_total)
    for h in range(hours):
        part = slice(h * scens, (h + 1) * scens)
        hedge_ref[part, :] = hedged_ref[part, :] - mean_ref[h : h + 1, :]
    send(hedge_ref, hedge_out)
    send(mean_ref, mean_out)

    here = lax.axis_index("area")
    placed_ref[...] = jnp.zeros_like(placed_ref)
    if relayed:
        far, both = (unfold(ref[...]) for ref in peer_refs)
        peers = [*by_flips(here, both[CAP:, :], far[0:CAP, :]), both[0:CAP, :]]
    else:
        peers = [unfold(ref[...]) for ref in peer_refs]
    for i in range(blocks):
        slots = slice(i * CAP, (i + 1) * CAP)
        flow = (mine_ref[slots, :] + (theirs_ref[slots, :] - weight_ref[slots, 0:1] * peers[i])) * 0.5
        low, _, block, in_reach = block_facts(here, partner_of(here, i))
        first = block * CAP + jnp.where(low, 0, REACH * CAP)

        @pl.when(in_reach)
        def _():
            placed_ref[pl.ds(pl.multiple_of(first, CAP), CAP), :] = flow

    tie_ref[...] = jnp.transpose(placed_ref[...])[0 : tie_ref.shape[0], :]
    send(tie_ref, tie_out)
    for copy in copies:
        copy.wait()


def call(kernel, name, args, outs, scratch, flops, in_place=(), outs_in_place=False):
    size = sum(x.size * x.dtype.itemsize for x in list(args) + list(outs))
    return pl.pallas_call(
        kernel,
        name=name,
        out_shape=outs,
        in_specs=[ANY if i in in_place else VMEM for i in range(len(args))],
        out_specs=[ANY if outs_in_place else VMEM] * len(outs),
        scratch_shapes=scratch,
        compiler_params=pltpu.CompilerParams(vmem_limit_bytes=32 * 1024 * 1024),
        cost_estimate=pl.CostEstimate(flops=flops, bytes_accessed=size, transcendentals=0),
    )(*(pltpu.with_memory_space_constraint(x, pltpu.HBM) if i in in_place else x for i, x in enumerate(args)))


def per_device(
    ptdf,
    angle_sens,
    demand,
    gen_start,
    hedge_dual,
    gen_cost,
    gen_max,
    gen_ramp,
    line_max,
    tie_count,
    tie_low_bus,
    tie_high_bus,
    tie_susc,
):
    hours, scens, buses = demand.shape
    lines = ptdf.shape[0]
    width = hours * scens
    areas = lax.axis_size("area")
    n_scen = lax.axis_size("scen")
    assert lax.axis_size("hour") == 2 and hours >= 2
    assert hours % PIECES == 0 and buses % (PIECES * LANES) == 0
    assert width % LANES == LANES // 2 and width < 2 * LANES
    columns = 2 * LANES
    block_rows = CAP * 3 // 2
    scen_total = scens * n_scen
    blocks, partner_of, from_partners = partner_plan(areas)
    slots = blocks * CAP
    pieces = buses // LANES
    sum_rows = 8 * pl.cdiv((hours + 1) * pieces, 8)
    f32, bf16 = jnp.float32, jnp.bfloat16

    def shape(*dims, dtype=f32):
        return jax.ShapeDtypeStruct(dims, dtype)

    def over_scens(sums):
        if n_scen == 2:
            return [sums, lax.ppermute(sums, "scen", [(0, 1), (1, 0)])]
        return [lax.psum(sums, "scen")]

    work = 4 * width * lines * buses

    def step_scratch(rows):
        return [
            pltpu.VMEM((rows, buses), bf16),
            pltpu.VMEM((rows, lines), bf16),
            pltpu.VMEM((rows, buses), f32),
        ]

    ramp_scratch = [
        pltpu.VMEM((hours + 4, buses), f32),
        pltpu.VMEM((hours + 4, buses), f32),
        pltpu.VMEM((hours, buses), f32),
    ]
    tables = (tie_count, tie_low_bus, tie_high_bus, tie_susc)
    vectors = [x.reshape(1, -1) for x in (gen_cost, gen_max, gen_ramp, line_max)]
    hedge = hedge_dual.reshape(width, buses)
    made = call(
        functools.partial(angle_kernel, blocks, partner_of),
        "angles",
        (
            angle_sens,
            demand.reshape(width, buses),
            hedge,
            gen_start,
            *vectors,
            *tables,
        ),
        [shape(block_rows, LANES)] * blocks
        + [
            shape(slots, columns),
            shape(scens, buses),
            shape(columns, buses, dtype=bf16),
            shape(slots, buses, dtype=bf16),
            shape(slots, buses, dtype=bf16),
            shape(slots, 128),
            shape(width, buses),
            shape(hours, buses),
            shape(1, buses),
            shape(1, buses),
            shape(1, buses),
            shape(1, lines),
        ],
        [pltpu.VMEM(x.shape, x.dtype) for x in (angle_sens, *tables)]
        + [pltpu.VMEM((slots, buses), bf16), pltpu.SemaphoreType.DMA((10 + 2 * PIECES,))],
        2 * slots * buses * (width + buses),
        range(12),
    )
    sent = made[:blocks]
    own, edge_hedge, inject, spread, rows, weight, load, start = made[blocks : blocks + 8]
    cost, top, limit, line_top = made[blocks + 8 :]
    (edge,) = call(edge_kernel, "edge", (load, edge_hedge, start), [shape(2 * scens + 8, buses)], [], BETWEEN)
    edge = lax.ppermute(edge, "hour", [(0, 1), (1, 0)])
    peer = from_partners(sent)
    gen, base, hedged, sums = call(
        first_kernel,
        "first",
        (ptdf, inject, load, hedge, start, edge, cost, top, limit, line_top),
        [
            shape(width, buses),
            shape(width, buses),
            shape(width, buses),
            shape(sum_rows, LANES),
        ],
        step_scratch(width + scens) + ramp_scratch,
        work,
    )
    sum_terms = over_scens(sums)
    terms = len(sum_terms)
    relayed = areas == 4
    tied = call(
        functools.partial(tie_kernel, blocks, relayed),
        "ties",
        (base, spread, rows, weight, own, *peer),
        (
            [shape(2 * block_rows, LANES), shape(CAP, columns)]
            if relayed
            else [shape(block_rows, LANES)] * blocks
        )
        + [shape(columns, buses, dtype=bf16), shape(slots, columns), shape(slots, columns)],
        [],
        BETWEEN,
    )
    *sent, inject, mine, theirs = tied
    hedged, sums = call(
        functools.partial(second_kernel, terms, scen_total),
        "second",
        (ptdf, inject, gen, hedged, cost, top, limit, line_top, *sum_terms),
        [shape(width, buses), shape(sum_rows, LANES)],
        step_scratch(width)[1:] + [pltpu.VMEM((8 * pl.cdiv(hours + 1, 8), buses), f32)] + ramp_scratch,
        work,
    )
    sum_terms = over_scens(sums)
    if relayed:
        far, near = sent
        far = lax.ppermute(far, "area", [(a, a ^ 2) for a in range(areas)])
        arrived, _ = lax.optimization_barrier((far, sums))
        (both,) = call(relay_kernel, "relay", (near, arrived), [shape(2 * block_rows, LANES)], [], BETWEEN)
        peer = [far, lax.ppermute(both, "area", [(a, a ^ 1) for a in range(areas)])]
    else:
        peer = from_partners(sent)
    ends = [shape(hours, buses), shape(width, buses), shape(width, 2 * REACH * CAP)]
    gen_mean, hedge, tie_flow = call(
        functools.partial(last_kernel, blocks, terms, relayed, partner_of, scen_total),
        "last",
        (hedged, *peer, weight, mine, theirs, *sum_terms),
        ends,
        [pltpu.VMEM(x.shape, x.dtype) for x in ends]
        + [pltpu.VMEM((2 * REACH * CAP, columns), f32), pltpu.SemaphoreType.DMA((len(ends),))],
        slots * columns,
        outs_in_place=True,
    )
    return (
        gen_mean,
        hedge.reshape(hours, scens, buses),
        tie_flow.reshape(hours, scens, 2 * REACH * CAP),
    )


def solution(mesh):
    return jax.shard_map(
        per_device,
        mesh=mesh,
        in_specs=(
            P(("group", "area"), None),
            P(("group", "area"), None),
            P(("group", "hour"), "scen", "area"),
            P(("group", "hour"), "area"),
            P(("group", "hour"), "scen", "area"),
            P(("group", "area")),
            P(("group", "area")),
            P(("group", "area")),
            P(("group", "area")),
            P("group", None),
            P("group", None),
            P("group", None),
            P("group", None),
        ),
        out_specs=(
            P(("group", "hour"), "area"),
            P(("group", "hour"), "scen", "area"),
            P(("group", "hour"), "scen", "area"),
        ),
        check_vma=False,
    )
```

```python
import functools

import jax
import jax.numpy as jnp
from jax import lax
from jax.experimental import pallas as pl
from jax.experimental.pallas import tpu as pltpu
from jax.sharding import PartitionSpec as P

HOURS = 24
REACH = 4
CAP = 16

STEP_SIZE = 0.5
LINE_CHUNK = 512
LANES = 128
BETWEEN = 20_000_000_000

CONTRACT_LAST = (((1,), (1,)), ((), ()))
CONTRACT_FIRST = (((0,), (0,)), ((), ()))
VMEM = pl.BlockSpec(memory_space=pltpu.VMEM)
ANY = pl.BlockSpec(memory_space=pltpu.HBM)


TARGETS = ((3, 2, 0, 1), (2, 3, 1, 0), (1, 0, 3, 2))


def partner_plan(areas):
    if areas == 4:

        def partner_of(here, i):
            return sum(jnp.where(here == a, target, 0) for a, target in enumerate(TARGETS[i]))

        def by_target(parts):
            out, back, pair = (
                lax.ppermute(part, "area", list(enumerate(target))) for part, target in zip(parts, TARGETS)
            )
            return [back, out, pair]

        return len(TARGETS), partner_of, by_target
    reach = min(REACH, areas - 1)
    shifts = sorted({s % areas for d in range(1, reach + 1) for s in (d, -d)})

    def by_shift(parts):
        sent = [
            lax.ppermute(part, "area", [(a, (a + s) % areas) for a in range(areas)])
            for part, s in zip(parts, shifts)
        ]
        return [sent[shifts.index(areas - s)] for s in shifts]

    return len(shifts), lambda here, i: lax.rem(here + shifts[i], areas), by_shift


def by_flips(here, flip_3, flip_2):
    return jnp.where(here < 2, flip_3, flip_2), jnp.where(here < 2, flip_2, flip_3)


def block_facts(here, partner):
    low = partner > here
    distance = jnp.abs(partner - here)
    block = jnp.clip(distance - 1, 0, REACH - 1)
    in_reach = (distance >= 1) & (distance <= REACH)
    return low, jnp.minimum(here, partner), block, in_reach


def fold(x):
    half = x.shape[0] // 2
    low = lax.broadcasted_iota(jnp.int32, (half, LANES), 1) < LANES // 2
    shared = jnp.where(low, x[0:half, LANES : 2 * LANES], x[half:, LANES : 2 * LANES])
    return jnp.concatenate([x[:, 0:LANES], shared], axis=0)


def unfold(packed):
    rows = 2 * packed.shape[0] // 3
    shared = packed[rows:, :]
    low = lax.broadcasted_iota(jnp.int32, shared.shape, 1) < LANES // 2
    turned = pltpu.roll(shared, LANES // 2, 1)
    rest = jnp.concatenate([jnp.where(low, shared, turned), jnp.where(low, turned, shared)], axis=0)
    return jnp.concatenate([packed[0:rows, :], rest], axis=1)


def repeat_rest(inject_ref, width):
    inject_ref[width:, :] = inject_ref[width - LANES // 2 : width, :]


def split_3(x):
    high = x.astype(jnp.bfloat16)
    rest = x - high.astype(jnp.float32)
    middle = rest.astype(jnp.bfloat16)
    rest = rest - middle.astype(jnp.float32)
    return jnp.concatenate([high, middle, rest.astype(jnp.bfloat16)], axis=0)


def put_row(packed_ref, hours, h, row):
    for j in range(row.shape[1] // LANES):
        packed_ref[j * hours + h : j * hours + h + 1, :] = row[:, j * LANES : (j + 1) * LANES]


def clear_rest(packed_ref, used):
    rows = packed_ref.shape[0]
    if used < rows:
        packed_ref[used:, :] = jnp.zeros((rows - used, LANES), jnp.float32)


def agree(mean_ref, sum_refs, hours, scen_total):
    for j in range(mean_ref.shape[1] // LANES):
        parts = [ref[j * hours : (j + 1) * hours, :] for ref in sum_refs]
        mean_ref[0:hours, j * LANES : (j + 1) * LANES] = functools.reduce(jnp.add, parts) / scen_total


def excess(diffs, limit):
    return diffs - jnp.clip(diffs, -limit, limit)


def write_ramp(mean_ref, beyond, limit, first_hour, padded_ref, excess_ref, ramp_ref):
    hours = ramp_ref.shape[0]
    padded_ref[0:1, :] = beyond
    padded_ref[1 : hours + 1, :] = mean_ref[0:hours, :]
    padded_ref[hours + 1 : hours + 2, :] = beyond
    diffs = padded_ref[1 : hours + 2, :] - padded_ref[0 : hours + 1, :]
    ids = first_hour + lax.broadcasted_iota(jnp.int32, diffs.shape, 0)
    valid = (ids >= 1) & (ids <= HOURS - 1)
    excess_ref[0 : hours + 1, :] = jnp.where(valid, excess(diffs, limit), 0.0)
    ramp_ref[...] = excess_ref[0:hours, :] - excess_ref[1 : hours + 1, :]


def line_work(inject_ref, ptdf_ref, line_max_ref, over_ref):
    inject = inject_ref[...]
    lines = ptdf_ref.shape[0]
    for at in range(0, lines, LINE_CHUNK):
        part = slice(at, at + LINE_CHUNK)
        flows = lax.dot_general(
            inject, ptdf_ref[part, :], CONTRACT_LAST, preferred_element_type=jnp.float32
        )
        limit = line_max_ref[:, part]
        over_ref[:, part] = (flows - jnp.clip(flows, -limit, limit)).astype(jnp.bfloat16)
    return jnp.dot(over_ref[...], ptdf_ref[...], preferred_element_type=jnp.float32)


def angle_kernel(
    blocks,
    partner_of,
    sens_in,
    demand_in,
    hedge_in,
    start_in,
    count_in,
    low_bus_in,
    high_bus_in,
    susc_in,
    *refs,
):
    own_refs, refs = refs[:blocks], refs[blocks:]
    (
        own_ref,
        edge_hedge_ref,
        inject_ref,
        spread_ref,
        rows_ref,
        weight_ref,
        demand_ref,
        start_ref,
        sens_ref,
        count_ref,
        low_bus_ref,
        high_bus_ref,
        susc_ref,
        onehot_ref,
        copy_sems,
    ) = refs
    hours, buses = start_ref.shape
    scens = demand_ref.shape[0] // hours
    here = lax.axis_index("area")
    last = (hours - 1) * scens
    edge_rows = pl.ds(pl.multiple_of((1 - lax.axis_index("hour")) * last, scens), scens)

    pairs = (
        (sens_in, sens_ref),
        (demand_in, demand_ref),
        (start_in, start_ref),
        (count_in, count_ref),
        (low_bus_in, low_bus_ref),
        (high_bus_in, high_bus_ref),
        (susc_in, susc_ref),
        (hedge_in.at[edge_rows], edge_hedge_ref),
    )
    copies = [pltpu.make_async_copy(src, dst, copy_sems.at[i]) for i, (src, dst) in enumerate(pairs)]
    for copy in copies:
        copy.start()
    for copy in copies[3:7]:
        copy.wait()
    for i in range(blocks):
        partner = partner_of(here, i)
        low, row, block, in_reach = block_facts(here, partner)
        slots = slice(i * CAP, (i + 1) * CAP)
        pick = lax.broadcasted_iota(jnp.int32, (CAP, REACH * CAP), 1) == (
            block * CAP + lax.broadcasted_iota(jnp.int32, (CAP, REACH * CAP), 0)
        )
        table_row = pl.ds(row, 1)
        bus_row = jnp.where(low, low_bus_ref[table_row, :], high_bus_ref[table_row, :])
        bus = jnp.sum(jnp.where(pick, bus_row.astype(jnp.float32), 0.0), axis=1, keepdims=True)
        susc = jnp.sum(jnp.where(pick, susc_ref[table_row, :], 0.0), axis=1, keepdims=True)
        count_row = count_ref[table_row, :].astype(jnp.float32)
        is_block = lax.broadcasted_iota(jnp.int32, (CAP, REACH), 1) == block
        count = jnp.sum(jnp.where(is_block, count_row, 0.0), axis=1, keepdims=True)
        slot_ids = lax.broadcasted_iota(jnp.int32, (CAP, 1), 0).astype(jnp.float32)
        live = jnp.where((slot_ids < count) & in_reach, 1.0, 0.0)
        sign = jnp.where(low, 1.0, -1.0)
        bus_ids = lax.broadcasted_iota(jnp.int32, (CAP, buses), 1).astype(jnp.float32)
        onehot = jnp.where(bus_ids == bus, live, 0.0)
        onehot_ref[slots, :] = onehot.astype(jnp.bfloat16)
        spread_ref[slots, :] = (-sign * onehot).astype(jnp.bfloat16)
        weight_ref[slots, :] = jnp.broadcast_to(live * sign * susc, (CAP, 128))

    for copy in copies[:3]:
        copy.wait()
    for h in range(hours):
        part = slice(h * scens, (h + 1) * scens)
        inject_ref[part, :] = (start_ref[h : h + 1, :] - demand_ref[part, :]).astype(jnp.bfloat16)
    repeat_rest(inject_ref, hours * scens)
    rows = jnp.dot(onehot_ref[...], sens_ref[...], preferred_element_type=jnp.float32)
    rows_ref[...] = rows.astype(jnp.bfloat16)
    own = lax.dot_general(
        rows_ref[...], inject_ref[...], CONTRACT_LAST, preferred_element_type=jnp.float32
    )
    own_ref[...] = own
    for i in range(blocks):
        own_refs[i][...] = fold(own[i * CAP : (i + 1) * CAP, :])

    copies[7].wait()


def edge_kernel(demand_ref, edge_hedge_ref, start_ref, edge_ref):
    scens = edge_hedge_ref.shape[0]
    hours = start_ref.shape[0]
    early = lax.axis_index("hour") == 0
    last = (hours - 1) * scens
    at = 2 * scens
    edge_ref[0:scens, :] = jnp.where(early, demand_ref[last:, :], demand_ref[0:scens, :])
    edge_ref[scens:at, :] = edge_hedge_ref[...]
    edge_ref[at : at + 1, :] = jnp.where(early, start_ref[hours - 1 : hours, :], start_ref[0:1, :])
    edge_ref[at + 1 : at + 2, :] = jnp.where(
        early, start_ref[hours - 2 : hours - 1, :], start_ref[1:2, :]
    )


def first_kernel(
    ptdf_ref,
    own_inject_ref,
    demand_ref,
    hedge_ref,
    start_ref,
    edge_ref,
    cost_ref,
    max_ref,
    limit_ref,
    line_max_ref,
    gen_ref,
    base_ref,
    hedged_ref,
    sums_ref,
    inject_ref,
    over_ref,
    back_ref,
    padded_ref,
    excess_ref,
    ramp_ref,
):
    hours, buses = start_ref.shape
    width = demand_ref.shape[0]
    scens = width // hours
    at = 2 * scens
    early = lax.axis_index("hour") == 0
    first_hour = lax.axis_index("hour") * hours
    beyond = edge_ref[at : at + 1, :]
    limit = limit_ref[...]
    cost = cost_ref[...]
    top = max_ref[...]

    inject_ref[0:width, :] = own_inject_ref[0:width, :]
    inject_ref[width : width + scens, :] = (beyond - edge_ref[0:scens, :]).astype(jnp.bfloat16)
    back_ref[...] = line_work(inject_ref, ptdf_ref, line_max_ref, over_ref)
    write_ramp(start_ref, beyond, limit, first_hour, padded_ref, excess_ref, ramp_ref)

    def step(mean, hedge, back, ramp):
        grad = cost + back + (mean - mean + hedge) + ramp
        gen = jnp.clip(mean - STEP_SIZE * grad, 0.0, top)
        return gen, gen + hedge

    for h in range(hours):
        part = slice(h * scens, (h + 1) * scens)
        mean = start_ref[h : h + 1, :]
        gen, hedged = step(mean, hedge_ref[part, :], back_ref[part, :], ramp_ref[h : h + 1, :])
        gen_ref[part, :] = gen
        base_ref[part, :] = gen - demand_ref[part, :]
        hedged_ref[part, :] = hedged
        put_row(sums_ref, hours + 1, h, jnp.sum(hedged, axis=0, keepdims=True))
    near = jnp.where(early, start_ref[hours - 1 : hours, :], start_ref[0:1, :])
    ramp = excess(beyond - near, limit) + excess(beyond - edge_ref[at + 1 : at + 2, :], limit)
    _, hedged = step(beyond, edge_ref[scens:at, :], back_ref[width : width + scens, :], ramp)
    put_row(sums_ref, hours + 1, hours, jnp.sum(hedged, axis=0, keepdims=True))
    clear_rest(sums_ref, (hours + 1) * (buses // LANES))


def tie_kernel(blocks, relayed, base_ref, spread_ref, rows_ref, weight_ref, own_ref, *refs):
    peer_refs, refs = refs[:blocks], refs[blocks:]
    *next_refs, inject_ref, mine_ref, theirs_ref = refs
    width = base_ref.shape[0]

    weight = weight_ref[:, 0:1]
    own = own_ref[...]
    peer = jnp.concatenate([unfold(ref[...]) for ref in peer_refs], axis=0)
    est_mine = weight * own
    est_theirs = -weight * peer
    flow = (est_mine + est_theirs) * 0.5
    dual_mine = est_mine - flow
    dual_theirs = est_theirs - flow
    spread = spread_ref[...]
    add = lax.dot_general(
        split_3(flow),
        jnp.concatenate([spread, spread, spread], axis=0),
        CONTRACT_FIRST,
        preferred_element_type=jnp.float32,
    )
    inject_ref[0:width, :] = (base_ref[...] + add[0:width, :]).astype(jnp.bfloat16)
    repeat_rest(inject_ref, width)

    own_next = lax.dot_general(
        rows_ref[...], inject_ref[...], CONTRACT_LAST, preferred_element_type=jnp.float32
    )
    parts = [own_next[i * CAP : (i + 1) * CAP, :] for i in range(blocks)]
    if relayed:
        far_ref, near_ref = next_refs
        flip_3, flip_2 = by_flips(lax.axis_index("area"), parts[0], parts[1])
        far_ref[...] = fold(jnp.concatenate([flip_2, flip_3], axis=0))
        near_ref[...] = parts[2]
    else:
        for ref, part in zip(next_refs, parts):
            ref[...] = fold(part)
    mine_ref[...] = weight * (own_next - peer) + dual_mine
    theirs_ref[...] = weight * own + dual_theirs


def second_kernel(
    terms,
    scen_total,
    ptdf_ref,
    inject_ref,
    gen_ref,
    hedged_ref,
    cost_ref,
    max_ref,
    limit_ref,
    line_max_ref,
    *refs,
):
    sum_refs, refs = refs[:terms], refs[terms:]
    (hedged_out_ref, sums_out_ref, over_ref, back_ref, mean_ref, padded_ref, excess_ref, ramp_ref) = refs
    hours, buses = ramp_ref.shape
    width = back_ref.shape[0]
    scens = width // hours
    first_hour = lax.axis_index("hour") * hours

    back_ref[...] = line_work(inject_ref.at[0:width, :], ptdf_ref, line_max_ref, over_ref)
    agree(mean_ref, sum_refs, hours + 1, scen_total)
    write_ramp(
        mean_ref, mean_ref[hours : hours + 1, :], limit_ref[...], first_hour, padded_ref, excess_ref, ramp_ref
    )
    cost = cost_ref[...]
    top = max_ref[...]
    for h in range(hours):
        part = slice(h * scens, (h + 1) * scens)
        mean = mean_ref[h : h + 1, :]
        gen = gen_ref[part, :]
        hedge = hedged_ref[part, :] - mean
        grad = cost + back_ref[part, :] + (gen - mean + hedge) + ramp_ref[h : h + 1, :]
        gen = jnp.clip(gen - STEP_SIZE * grad, 0.0, top)
        hedged = gen + hedge
        hedged_out_ref[part, :] = hedged
        put_row(sums_out_ref, hours, h, jnp.sum(hedged, axis=0, keepdims=True))
    clear_rest(sums_out_ref, hours * (buses // LANES))


def relay_kernel(near_ref, far_ref, both_ref):
    low = lax.broadcasted_iota(jnp.int32, (CAP, LANES), 1) < LANES // 2
    both_ref[0:CAP, :] = near_ref[:, 0:LANES]
    both_ref[CAP : 2 * CAP, :] = far_ref[CAP : 2 * CAP, :]
    both_ref[2 * CAP :, :] = jnp.where(low, near_ref[:, LANES:], far_ref[2 * CAP :, :])


def last_kernel(blocks, terms, relayed, partner_of, scen_total, hedged_ref, *refs):
    *peer_refs, weight_ref, mine_ref, theirs_ref = refs[: -8 - terms]
    sum_refs = refs[-8 - terms : -8]
    mean_out, hedge_out, tie_out, mean_ref, hedge_ref, tie_ref, placed_ref, copy_sems = refs[-8:]
    hours = mean_ref.shape[0]
    scens = hedged_ref.shape[0] // hours
    copies = []

    def send(src, dst):
        copies.append(pltpu.make_async_copy(src, dst, copy_sems.at[len(copies)]))
        copies[-1].start()

    agree(mean_ref, sum_refs, hours, scen_total)
    for h in range(hours):
        part = slice(h * scens, (h + 1) * scens)
        hedge_ref[part, :] = hedged_ref[part, :] - mean_ref[h : h + 1, :]
    send(hedge_ref, hedge_out)
    send(mean_ref, mean_out)

    here = lax.axis_index("area")
    placed_ref[...] = jnp.zeros_like(placed_ref)
    if relayed:
        far, both = (unfold(ref[...]) for ref in peer_refs)
        peers = [*by_flips(here, both[CAP:, :], far[0:CAP, :]), both[0:CAP, :]]
    else:
        peers = [unfold(ref[...]) for ref in peer_refs]
    for i in range(blocks):
        slots = slice(i * CAP, (i + 1) * CAP)
        flow = (mine_ref[slots, :] + (theirs_ref[slots, :] - weight_ref[slots, 0:1] * peers[i])) * 0.5
        low, _, block, in_reach = block_facts(here, partner_of(here, i))
        first = block * CAP + jnp.where(low, 0, REACH * CAP)

        @pl.when(in_reach)
        def _():
            placed_ref[pl.ds(pl.multiple_of(first, CAP), CAP), :] = flow

    tie_ref[...] = jnp.transpose(placed_ref[...])[0 : tie_ref.shape[0], :]
    send(tie_ref, tie_out)
    for copy in copies:
        copy.wait()


def call(kernel, name, args, outs, scratch, flops, in_place=(), outs_in_place=False):
    size = sum(x.size * x.dtype.itemsize for x in list(args) + list(outs))
    return pl.pallas_call(
        kernel,
        name=name,
        out_shape=outs,
        in_specs=[ANY if i in in_place else VMEM for i in range(len(args))],
        out_specs=[ANY if outs_in_place else VMEM] * len(outs),
        scratch_shapes=scratch,
        compiler_params=pltpu.CompilerParams(vmem_limit_bytes=32 * 1024 * 1024),
        cost_estimate=pl.CostEstimate(flops=flops, bytes_accessed=size, transcendentals=0),
    )(*(pltpu.with_memory_space_constraint(x, pltpu.HBM) if i in in_place else x for i, x in enumerate(args)))


def per_device(
    ptdf,
    angle_sens,
    demand,
    gen_start,
    hedge_dual,
    gen_cost,
    gen_max,
    gen_ramp,
    line_max,
    tie_count,
    tie_low_bus,
    tie_high_bus,
    tie_susc,
):
    hours, scens, buses = demand.shape
    lines = ptdf.shape[0]
    width = hours * scens
    areas = lax.axis_size("area")
    n_scen = lax.axis_size("scen")
    assert lax.axis_size("hour") == 2 and hours >= 2
    assert width % LANES == LANES // 2 and width < 2 * LANES
    columns = 2 * LANES
    block_rows = CAP * 3 // 2
    scen_total = scens * n_scen
    blocks, partner_of, from_partners = partner_plan(areas)
    slots = blocks * CAP
    pieces = buses // LANES
    sum_rows = 8 * pl.cdiv((hours + 1) * pieces, 8)
    f32, bf16 = jnp.float32, jnp.bfloat16

    def shape(*dims, dtype=f32):
        return jax.ShapeDtypeStruct(dims, dtype)

    def over_scens(sums):
        if n_scen == 2:
            return [sums, lax.ppermute(sums, "scen", [(0, 1), (1, 0)])]
        return [lax.psum(sums, "scen")]

    work = 4 * width * lines * buses

    def step_scratch(rows):
        return [
            pltpu.VMEM((rows, buses), bf16),
            pltpu.VMEM((rows, lines), bf16),
            pltpu.VMEM((rows, buses), f32),
        ]

    ramp_scratch = [
        pltpu.VMEM((hours + 4, buses), f32),
        pltpu.VMEM((hours + 4, buses), f32),
        pltpu.VMEM((hours, buses), f32),
    ]
    tables = (tie_count, tie_low_bus, tie_high_bus, tie_susc)
    vectors = [x.reshape(1, -1) for x in (gen_cost, gen_max, gen_ramp, line_max)]
    hedge = hedge_dual.reshape(width, buses)
    made = call(
        functools.partial(angle_kernel, blocks, partner_of),
        "angles",
        (
            angle_sens,
            demand.reshape(width, buses),
            hedge,
            gen_start,
            *tables,
        ),
        [shape(block_rows, LANES)] * blocks
        + [
            shape(slots, columns),
            shape(scens, buses),
            shape(columns, buses, dtype=bf16),
            shape(slots, buses, dtype=bf16),
            shape(slots, buses, dtype=bf16),
            shape(slots, 128),
            shape(width, buses),
            shape(hours, buses),
        ],
        [pltpu.VMEM(x.shape, x.dtype) for x in (angle_sens, *tables)]
        + [pltpu.VMEM((slots, buses), bf16), pltpu.SemaphoreType.DMA((8,))],
        2 * slots * buses * (width + buses),
        range(8),
    )
    sent = made[:blocks]
    own, edge_hedge, inject, spread, rows, weight, load, start = made[blocks:]
    (edge,) = call(edge_kernel, "edge", (load, edge_hedge, start), [shape(2 * scens + 8, buses)], [], BETWEEN)
    edge = lax.ppermute(edge, "hour", [(0, 1), (1, 0)])
    peer = from_partners(sent)
    gen, base, hedged, sums = call(
        first_kernel,
        "first",
        (ptdf, inject, load, hedge, start, edge, *vectors),
        [
            shape(width, buses),
            shape(width, buses),
            shape(width, buses),
            shape(sum_rows, LANES),
        ],
        step_scratch(width + scens) + ramp_scratch,
        work,
    )
    sum_terms = over_scens(sums)
    terms = len(sum_terms)
    relayed = areas == 4
    tied = call(
        functools.partial(tie_kernel, blocks, relayed),
        "ties",
        (base, spread, rows, weight, own, *peer),
        (
            [shape(2 * block_rows, LANES), shape(CAP, columns)]
            if relayed
            else [shape(block_rows, LANES)] * blocks
        )
        + [shape(columns, buses, dtype=bf16), shape(slots, columns), shape(slots, columns)],
        [],
        BETWEEN,
    )
    *sent, inject, mine, theirs = tied
    hedged, sums = call(
        functools.partial(second_kernel, terms, scen_total),
        "second",
        (ptdf, inject, gen, hedged, *vectors, *sum_terms),
        [shape(width, buses), shape(sum_rows, LANES)],
        step_scratch(width)[1:] + [pltpu.VMEM((8 * pl.cdiv(hours + 1, 8), buses), f32)] + ramp_scratch,
        work,
    )
    sum_terms = over_scens(sums)
    if relayed:
        far, near = sent
        far = lax.ppermute(far, "area", [(a, a ^ 2) for a in range(areas)])
        arrived, _ = lax.optimization_barrier((far, sums))
        (both,) = call(relay_kernel, "relay", (near, arrived), [shape(2 * block_rows, LANES)], [], BETWEEN)
        peer = [far, lax.ppermute(both, "area", [(a, a ^ 1) for a in range(areas)])]
    else:
        peer = from_partners(sent)
    ends = [shape(hours, buses), shape(width, buses), shape(width, 2 * REACH * CAP)]
    gen_mean, hedge, tie_flow = call(
        functools.partial(last_kernel, blocks, terms, relayed, partner_of, scen_total),
        "last",
        (hedged, *peer, weight, mine, theirs, *sum_terms),
        ends,
        [pltpu.VMEM(x.shape, x.dtype) for x in ends]
        + [pltpu.VMEM((2 * REACH * CAP, columns), f32), pltpu.SemaphoreType.DMA((len(ends),))],
        slots * columns,
        outs_in_place=True,
    )
    return (
        gen_mean,
        hedge.reshape(hours, scens, buses),
        tie_flow.reshape(hours, scens, 2 * REACH * CAP),
    )


def solution(mesh):
    return jax.shard_map(
        per_device,
        mesh=mesh,
        in_specs=(
            P(("group", "area"), None),
            P(("group", "area"), None),
            P(("group", "hour"), "scen", "area"),
            P(("group", "hour"), "area"),
            P(("group", "hour"), "scen", "area"),
            P(("group", "area")),
            P(("group", "area")),
            P(("group", "area")),
            P(("group", "area")),
            P("group", None),
            P("group", None),
            P("group", None),
            P("group", None),
        ),
        out_specs=(
            P(("group", "hour"), "area"),
            P(("group", "hour"), "scen", "area"),
            P(("group", "hour"), "scen", "area"),
        ),
        check_vma=False,
    )
```

```python
import functools

import jax
import jax.numpy as jnp
from jax import lax
from jax.experimental import pallas as pl
from jax.experimental.pallas import tpu as pltpu
from jax.sharding import PartitionSpec as P

HOURS = 24
REACH = 4
CAP = 16

STEP_SIZE = 0.5
LINE_CHUNK = 512
LANES = 128
BETWEEN = 20_000_000_000

CONTRACT_LAST = (((1,), (1,)), ((), ()))
CONTRACT_FIRST = (((0,), (0,)), ((), ()))
VMEM = pl.BlockSpec(memory_space=pltpu.VMEM)
ANY = pl.BlockSpec(memory_space=pltpu.HBM)


TARGETS = ((3, 2, 0, 1), (2, 3, 1, 0), (1, 0, 3, 2))


def partner_plan(areas):
    if areas == 4:

        def partner_of(here, i):
            return sum(jnp.where(here == a, target, 0) for a, target in enumerate(TARGETS[i]))

        def by_target(parts):
            out, back, pair = (
                lax.ppermute(part, "area", list(enumerate(target))) for part, target in zip(parts, TARGETS)
            )
            return [back, out, pair]

        return len(TARGETS), partner_of, by_target
    reach = min(REACH, areas - 1)
    shifts = sorted({s % areas for d in range(1, reach + 1) for s in (d, -d)})

    def by_shift(parts):
        sent = [
            lax.ppermute(part, "area", [(a, (a + s) % areas) for a in range(areas)])
            for part, s in zip(parts, shifts)
        ]
        return [sent[shifts.index(areas - s)] for s in shifts]

    return len(shifts), lambda here, i: lax.rem(here + shifts[i], areas), by_shift


def by_flips(here, flip_3, flip_2):
    return jnp.where(here < 2, flip_3, flip_2), jnp.where(here < 2, flip_2, flip_3)


def block_facts(here, partner):
    low = partner > here
    distance = jnp.abs(partner - here)
    block = jnp.clip(distance - 1, 0, REACH - 1)
    in_reach = (distance >= 1) & (distance <= REACH)
    return low, jnp.minimum(here, partner), block, in_reach


def fold(x):
    half = x.shape[0] // 2
    low = lax.broadcasted_iota(jnp.int32, (half, LANES), 1) < LANES // 2
    shared = jnp.where(low, x[0:half, LANES : 2 * LANES], x[half:, LANES : 2 * LANES])
    return jnp.concatenate([x[:, 0:LANES], shared], axis=0)


def unfold(packed):
    rows = 2 * packed.shape[0] // 3
    shared = packed[rows:, :]
    low = lax.broadcasted_iota(jnp.int32, shared.shape, 1) < LANES // 2
    turned = pltpu.roll(shared, LANES // 2, 1)
    rest = jnp.concatenate([jnp.where(low, shared, turned), jnp.where(low, turned, shared)], axis=0)
    return jnp.concatenate([packed[0:rows, :], rest], axis=1)


def repeat_rest(inject_ref, width):
    inject_ref[width:, :] = inject_ref[width - LANES // 2 : width, :]


def split_3(x):
    high = x.astype(jnp.bfloat16)
    rest = x - high.astype(jnp.float32)
    middle = rest.astype(jnp.bfloat16)
    rest = rest - middle.astype(jnp.float32)
    return jnp.concatenate([high, middle, rest.astype(jnp.bfloat16)], axis=0)


def put_row(packed_ref, hours, h, row):
    for j in range(row.shape[1] // LANES):
        packed_ref[j * hours + h : j * hours + h + 1, :] = row[:, j * LANES : (j + 1) * LANES]


def clear_rest(packed_ref, used):
    rows = packed_ref.shape[0]
    if used < rows:
        packed_ref[used:, :] = jnp.zeros((rows - used, LANES), jnp.float32)


def agree(mean_ref, sum_refs, hours, scen_total):
    for j in range(mean_ref.shape[1] // LANES):
        parts = [ref[j * hours : (j + 1) * hours, :] for ref in sum_refs]
        mean_ref[0:hours, j * LANES : (j + 1) * LANES] = functools.reduce(jnp.add, parts) / scen_total


def excess(diffs, limit):
    return diffs - jnp.clip(diffs, -limit, limit)


def write_ramp(mean_ref, beyond, limit, first_hour, padded_ref, excess_ref, ramp_ref):
    hours = ramp_ref.shape[0]
    padded_ref[0:1, :] = beyond
    padded_ref[1 : hours + 1, :] = mean_ref[0:hours, :]
    padded_ref[hours + 1 : hours + 2, :] = beyond
    diffs = padded_ref[1 : hours + 2, :] - padded_ref[0 : hours + 1, :]
    ids = first_hour + lax.broadcasted_iota(jnp.int32, diffs.shape, 0)
    valid = (ids >= 1) & (ids <= HOURS - 1)
    excess_ref[0 : hours + 1, :] = jnp.where(valid, excess(diffs, limit), 0.0)
    ramp_ref[...] = excess_ref[0:hours, :] - excess_ref[1 : hours + 1, :]


def line_work(inject_ref, ptdf_ref, line_max_ref, over_ref):
    inject = inject_ref[...]
    lines = ptdf_ref.shape[0]
    for at in range(0, lines, LINE_CHUNK):
        part = slice(at, at + LINE_CHUNK)
        flows = lax.dot_general(
            inject, ptdf_ref[part, :], CONTRACT_LAST, preferred_element_type=jnp.float32
        )
        limit = line_max_ref[:, part]
        over_ref[:, part] = (flows - jnp.clip(flows, -limit, limit)).astype(jnp.bfloat16)
    return jnp.dot(over_ref[...], ptdf_ref[...], preferred_element_type=jnp.float32)


def table_kernel(
    blocks,
    partner_of,
    hedge_in,
    start_in,
    count_in,
    low_bus_in,
    high_bus_in,
    susc_in,
    edge_hedge_ref,
    start_ref,
    onehot_ref,
    spread_ref,
    weight_ref,
    count_ref,
    low_bus_ref,
    high_bus_ref,
    susc_ref,
    copy_sems,
):
    hours, buses = start_ref.shape
    scens = hedge_in.shape[0] // hours
    here = lax.axis_index("area")
    last = (hours - 1) * scens
    edge_rows = pl.ds(pl.multiple_of((1 - lax.axis_index("hour")) * last, scens), scens)

    pairs = (
        (count_in, count_ref),
        (low_bus_in, low_bus_ref),
        (high_bus_in, high_bus_ref),
        (susc_in, susc_ref),
        (start_in, start_ref),
        (hedge_in.at[edge_rows], edge_hedge_ref),
    )
    copies = [pltpu.make_async_copy(src, dst, copy_sems.at[i]) for i, (src, dst) in enumerate(pairs)]
    for copy in copies:
        copy.start()
    for copy in copies[:4]:
        copy.wait()
    for i in range(blocks):
        partner = partner_of(here, i)
        low, row, block, in_reach = block_facts(here, partner)
        slots = slice(i * CAP, (i + 1) * CAP)
        pick = lax.broadcasted_iota(jnp.int32, (CAP, REACH * CAP), 1) == (
            block * CAP + lax.broadcasted_iota(jnp.int32, (CAP, REACH * CAP), 0)
        )
        table_row = pl.ds(row, 1)
        bus_row = jnp.where(low, low_bus_ref[table_row, :], high_bus_ref[table_row, :])
        bus = jnp.sum(jnp.where(pick, bus_row.astype(jnp.float32), 0.0), axis=1, keepdims=True)
        susc = jnp.sum(jnp.where(pick, susc_ref[table_row, :], 0.0), axis=1, keepdims=True)
        count_row = count_ref[table_row, :].astype(jnp.float32)
        is_block = lax.broadcasted_iota(jnp.int32, (CAP, REACH), 1) == block
        count = jnp.sum(jnp.where(is_block, count_row, 0.0), axis=1, keepdims=True)
        slot_ids = lax.broadcasted_iota(jnp.int32, (CAP, 1), 0).astype(jnp.float32)
        live = jnp.where((slot_ids < count) & in_reach, 1.0, 0.0)
        sign = jnp.where(low, 1.0, -1.0)
        bus_ids = lax.broadcasted_iota(jnp.int32, (CAP, buses), 1).astype(jnp.float32)
        onehot = jnp.where(bus_ids == bus, live, 0.0)
        onehot_ref[slots, :] = onehot.astype(jnp.bfloat16)
        spread_ref[slots, :] = (-sign * onehot).astype(jnp.bfloat16)
        weight_ref[slots, :] = jnp.broadcast_to(live * sign * susc, (CAP, 128))

    for copy in copies[4:]:
        copy.wait()


def angle_kernel(blocks, sens_ref, demand_ref, start_ref, onehot_ref, *refs):
    sent_refs, (own_ref, inject_ref, rows_ref) = refs[:blocks], refs[blocks:]
    hours = start_ref.shape[0]
    scens = demand_ref.shape[0] // hours
    rows = jnp.dot(onehot_ref[...], sens_ref[...], preferred_element_type=jnp.float32)
    rows_ref[...] = rows.astype(jnp.bfloat16)
    for h in range(hours):
        part = slice(h * scens, (h + 1) * scens)
        inject_ref[part, :] = (start_ref[h : h + 1, :] - demand_ref[part, :]).astype(jnp.bfloat16)
    repeat_rest(inject_ref, hours * scens)
    own = lax.dot_general(
        rows_ref[...], inject_ref[...], CONTRACT_LAST, preferred_element_type=jnp.float32
    )
    own_ref[...] = own
    for i in range(blocks):
        sent_refs[i][...] = fold(own[i * CAP : (i + 1) * CAP, :])


def edge_kernel(demand_ref, edge_hedge_ref, start_ref, edge_ref):
    scens = edge_hedge_ref.shape[0]
    hours = start_ref.shape[0]
    early = lax.axis_index("hour") == 0
    last = (hours - 1) * scens
    at = 2 * scens
    edge_ref[0:scens, :] = jnp.where(early, demand_ref[last:, :], demand_ref[0:scens, :])
    edge_ref[scens:at, :] = edge_hedge_ref[...]
    edge_ref[at : at + 1, :] = jnp.where(early, start_ref[hours - 1 : hours, :], start_ref[0:1, :])
    edge_ref[at + 1 : at + 2, :] = jnp.where(
        early, start_ref[hours - 2 : hours - 1, :], start_ref[1:2, :]
    )


def first_kernel(
    ptdf_ref,
    own_inject_ref,
    demand_ref,
    hedge_ref,
    start_ref,
    edge_ref,
    cost_ref,
    max_ref,
    limit_ref,
    line_max_ref,
    gen_ref,
    base_ref,
    hedged_ref,
    sums_ref,
    inject_ref,
    over_ref,
    back_ref,
    padded_ref,
    excess_ref,
    ramp_ref,
):
    hours, buses = start_ref.shape
    width = demand_ref.shape[0]
    scens = width // hours
    at = 2 * scens
    early = lax.axis_index("hour") == 0
    first_hour = lax.axis_index("hour") * hours
    beyond = edge_ref[at : at + 1, :]
    limit = limit_ref[...]
    cost = cost_ref[...]
    top = max_ref[...]

    inject_ref[0:width, :] = own_inject_ref[0:width, :]
    inject_ref[width : width + scens, :] = (beyond - edge_ref[0:scens, :]).astype(jnp.bfloat16)
    back_ref[...] = line_work(inject_ref, ptdf_ref, line_max_ref, over_ref)
    write_ramp(start_ref, beyond, limit, first_hour, padded_ref, excess_ref, ramp_ref)

    def step(mean, hedge, back, ramp):
        grad = cost + back + (mean - mean + hedge) + ramp
        gen = jnp.clip(mean - STEP_SIZE * grad, 0.0, top)
        return gen, gen + hedge

    for h in range(hours):
        part = slice(h * scens, (h + 1) * scens)
        mean = start_ref[h : h + 1, :]
        gen, hedged = step(mean, hedge_ref[part, :], back_ref[part, :], ramp_ref[h : h + 1, :])
        gen_ref[part, :] = gen
        base_ref[part, :] = gen - demand_ref[part, :]
        hedged_ref[part, :] = hedged
        put_row(sums_ref, hours + 1, h, jnp.sum(hedged, axis=0, keepdims=True))
    near = jnp.where(early, start_ref[hours - 1 : hours, :], start_ref[0:1, :])
    ramp = excess(beyond - near, limit) + excess(beyond - edge_ref[at + 1 : at + 2, :], limit)
    _, hedged = step(beyond, edge_ref[scens:at, :], back_ref[width : width + scens, :], ramp)
    put_row(sums_ref, hours + 1, hours, jnp.sum(hedged, axis=0, keepdims=True))
    clear_rest(sums_ref, (hours + 1) * (buses // LANES))


def tie_kernel(blocks, relayed, base_ref, spread_ref, rows_ref, weight_ref, own_ref, *refs):
    peer_refs, refs = refs[:blocks], refs[blocks:]
    *next_refs, inject_ref, mine_ref, theirs_ref = refs
    width = base_ref.shape[0]

    weight = weight_ref[:, 0:1]
    own = own_ref[...]
    peer = jnp.concatenate([unfold(ref[...]) for ref in peer_refs], axis=0)
    est_mine = weight * own
    est_theirs = -weight * peer
    flow = (est_mine + est_theirs) * 0.5
    dual_mine = est_mine - flow
    dual_theirs = est_theirs - flow
    spread = spread_ref[...]
    add = lax.dot_general(
        split_3(flow),
        jnp.concatenate([spread, spread, spread], axis=0),
        CONTRACT_FIRST,
        preferred_element_type=jnp.float32,
    )
    inject_ref[0:width, :] = (base_ref[...] + add[0:width, :]).astype(jnp.bfloat16)
    repeat_rest(inject_ref, width)

    own_next = lax.dot_general(
        rows_ref[...], inject_ref[...], CONTRACT_LAST, preferred_element_type=jnp.float32
    )
    parts = [own_next[i * CAP : (i + 1) * CAP, :] for i in range(blocks)]
    if relayed:
        far_ref, near_ref = next_refs
        flip_3, flip_2 = by_flips(lax.axis_index("area"), parts[0], parts[1])
        far_ref[...] = fold(jnp.concatenate([flip_2, flip_3], axis=0))
        near_ref[...] = parts[2]
    else:
        for ref, part in zip(next_refs, parts):
            ref[...] = fold(part)
    mine_ref[...] = weight * (own_next - peer) + dual_mine
    theirs_ref[...] = weight * own + dual_theirs


def second_kernel(
    terms,
    scen_total,
    ptdf_ref,
    inject_ref,
    gen_ref,
    hedged_ref,
    cost_ref,
    max_ref,
    limit_ref,
    line_max_ref,
    *refs,
):
    sum_refs, refs = refs[:terms], refs[terms:]
    (hedged_out_ref, sums_out_ref, over_ref, back_ref, mean_ref, padded_ref, excess_ref, ramp_ref) = refs
    hours, buses = ramp_ref.shape
    width = back_ref.shape[0]
    scens = width // hours
    first_hour = lax.axis_index("hour") * hours

    back_ref[...] = line_work(inject_ref.at[0:width, :], ptdf_ref, line_max_ref, over_ref)
    agree(mean_ref, sum_refs, hours + 1, scen_total)
    write_ramp(
        mean_ref, mean_ref[hours : hours + 1, :], limit_ref[...], first_hour, padded_ref, excess_ref, ramp_ref
    )
    cost = cost_ref[...]
    top = max_ref[...]
    for h in range(hours):
        part = slice(h * scens, (h + 1) * scens)
        mean = mean_ref[h : h + 1, :]
        gen = gen_ref[part, :]
        hedge = hedged_ref[part, :] - mean
        grad = cost + back_ref[part, :] + (gen - mean + hedge) + ramp_ref[h : h + 1, :]
        gen = jnp.clip(gen - STEP_SIZE * grad, 0.0, top)
        hedged = gen + hedge
        hedged_out_ref[part, :] = hedged
        put_row(sums_out_ref, hours, h, jnp.sum(hedged, axis=0, keepdims=True))
    clear_rest(sums_out_ref, hours * (buses // LANES))


def relay_kernel(near_ref, far_ref, both_ref):
    low = lax.broadcasted_iota(jnp.int32, (CAP, LANES), 1) < LANES // 2
    both_ref[0:CAP, :] = near_ref[:, 0:LANES]
    both_ref[CAP : 2 * CAP, :] = far_ref[CAP : 2 * CAP, :]
    both_ref[2 * CAP :, :] = jnp.where(low, near_ref[:, LANES:], far_ref[2 * CAP :, :])


def agree_kernel(scen_total, hedged_ref, *refs):
    sum_refs, (mean_ref, hedge_ref) = refs[:-2], refs[-2:]
    hours = mean_ref.shape[0]
    scens = hedged_ref.shape[0] // hours
    agree(mean_ref, sum_refs, hours, scen_total)
    for h in range(hours):
        part = slice(h * scens, (h + 1) * scens)
        hedge_ref[part, :] = hedged_ref[part, :] - mean_ref[h : h + 1, :]


def last_kernel(blocks, relayed, partner_of, hedge_ref, mean_ref, *refs):
    *peer_refs, weight_ref, mine_ref, theirs_ref = refs[:-6]
    hedge_out, mean_out, tie_out, tie_ref, placed_ref, copy_sems = refs[-6:]
    copies = []

    def send(src, dst):
        copies.append(pltpu.make_async_copy(src, dst, copy_sems.at[len(copies)]))
        copies[-1].start()

    send(hedge_ref, hedge_out)
    send(mean_ref, mean_out)
    here = lax.axis_index("area")
    placed_ref[...] = jnp.zeros_like(placed_ref)
    if relayed:
        far, both = (unfold(ref[...]) for ref in peer_refs)
        peers = [*by_flips(here, both[CAP:, :], far[0:CAP, :]), both[0:CAP, :]]
    else:
        peers = [unfold(ref[...]) for ref in peer_refs]
    for i in range(blocks):
        slots = slice(i * CAP, (i + 1) * CAP)
        flow = (mine_ref[slots, :] + (theirs_ref[slots, :] - weight_ref[slots, 0:1] * peers[i])) * 0.5
        low, _, block, in_reach = block_facts(here, partner_of(here, i))
        first = block * CAP + jnp.where(low, 0, REACH * CAP)

        @pl.when(in_reach)
        def _():
            placed_ref[pl.ds(pl.multiple_of(first, CAP), CAP), :] = flow

    tie_ref[...] = jnp.transpose(placed_ref[...])[0 : tie_ref.shape[0], :]
    send(tie_ref, tie_out)
    for copy in copies:
        copy.wait()


def call(kernel, name, args, outs, scratch, flops, in_place=(), outs_in_place=False):
    size = sum(x.size * x.dtype.itemsize for x in list(args) + list(outs))
    return pl.pallas_call(
        kernel,
        name=name,
        out_shape=outs,
        in_specs=[ANY if i in in_place else VMEM for i in range(len(args))],
        out_specs=[ANY if outs_in_place else VMEM] * len(outs),
        scratch_shapes=scratch,
        compiler_params=pltpu.CompilerParams(vmem_limit_bytes=32 * 1024 * 1024),
        cost_estimate=pl.CostEstimate(flops=flops, bytes_accessed=size, transcendentals=0),
    )(*(pltpu.with_memory_space_constraint(x, pltpu.HBM) if i in in_place else x for i, x in enumerate(args)))


def per_device(
    ptdf,
    angle_sens,
    demand,
    gen_start,
    hedge_dual,
    gen_cost,
    gen_max,
    gen_ramp,
    line_max,
    tie_count,
    tie_low_bus,
    tie_high_bus,
    tie_susc,
):
    hours, scens, buses = demand.shape
    lines = ptdf.shape[0]
    width = hours * scens
    areas = lax.axis_size("area")
    n_scen = lax.axis_size("scen")
    assert lax.axis_size("hour") == 2 and hours >= 2
    assert width % LANES == LANES // 2 and width < 2 * LANES
    columns = 2 * LANES
    block_rows = CAP * 3 // 2
    scen_total = scens * n_scen
    blocks, partner_of, from_partners = partner_plan(areas)
    slots = blocks * CAP
    pieces = buses // LANES
    sum_rows = 8 * pl.cdiv((hours + 1) * pieces, 8)
    f32, bf16 = jnp.float32, jnp.bfloat16

    def shape(*dims, dtype=f32):
        return jax.ShapeDtypeStruct(dims, dtype)

    def over_scens(sums):
        if n_scen == 2:
            return [sums, lax.ppermute(sums, "scen", [(0, 1), (1, 0)])]
        return [lax.psum(sums, "scen")]

    work = 4 * width * lines * buses

    def step_scratch(rows):
        return [
            pltpu.VMEM((rows, buses), bf16),
            pltpu.VMEM((rows, lines), bf16),
            pltpu.VMEM((rows, buses), f32),
        ]

    ramp_scratch = [
        pltpu.VMEM((hours + 4, buses), f32),
        pltpu.VMEM((hours + 4, buses), f32),
        pltpu.VMEM((hours, buses), f32),
    ]
    tables = (tie_count, tie_low_bus, tie_high_bus, tie_susc)
    vectors = [x.reshape(1, -1) for x in (gen_cost, gen_max, gen_ramp, line_max)]
    load = demand.reshape(width, buses)
    hedge = hedge_dual.reshape(width, buses)
    edge_hedge, start, onehot, spread, weight = call(
        functools.partial(table_kernel, blocks, partner_of),
        "tables",
        (hedge, gen_start, *tables),
        [
            shape(scens, buses),
            shape(hours, buses),
            shape(slots, buses, dtype=bf16),
            shape(slots, buses, dtype=bf16),
            shape(slots, LANES),
        ],
        [pltpu.VMEM(x.shape, x.dtype) for x in tables] + [pltpu.SemaphoreType.DMA((6,))],
        BETWEEN,
        range(6),
    )
    *sent, own, inject, rows = call(
        functools.partial(angle_kernel, blocks),
        "angles",
        (angle_sens, load, start, onehot),
        [shape(block_rows, LANES)] * blocks
        + [shape(slots, columns), shape(columns, buses, dtype=bf16), shape(slots, buses, dtype=bf16)],
        [],
        2 * slots * buses * (width + buses),
    )
    edge_hedge, own = lax.optimization_barrier((edge_hedge, own))
    (edge,) = call(edge_kernel, "edge", (load, edge_hedge, start), [shape(2 * scens + 8, buses)], [], BETWEEN)
    edge = lax.ppermute(edge, "hour", [(0, 1), (1, 0)])
    peer = from_partners(sent)
    gen, base, hedged, sums = call(
        first_kernel,
        "first",
        (ptdf, inject, load, hedge, start, edge, *vectors),
        [
            shape(width, buses),
            shape(width, buses),
            shape(width, buses),
            shape(sum_rows, LANES),
        ],
        step_scratch(width + scens) + ramp_scratch,
        work,
    )
    sum_terms = over_scens(sums)
    terms = len(sum_terms)
    relayed = areas == 4
    tied = call(
        functools.partial(tie_kernel, blocks, relayed),
        "ties",
        (base, spread, rows, weight, own, *peer),
        (
            [shape(2 * block_rows, LANES), shape(CAP, columns)]
            if relayed
            else [shape(block_rows, LANES)] * blocks
        )
        + [shape(columns, buses, dtype=bf16), shape(slots, columns), shape(slots, columns)],
        [],
        BETWEEN,
    )
    *sent, inject, mine, theirs = tied
    hedged, sums = call(
        functools.partial(second_kernel, terms, scen_total),
        "second",
        (ptdf, inject, gen, hedged, *vectors, *sum_terms),
        [shape(width, buses), shape(sum_rows, LANES)],
        step_scratch(width)[1:] + [pltpu.VMEM((8 * pl.cdiv(hours + 1, 8), buses), f32)] + ramp_scratch,
        work,
    )
    sum_terms = over_scens(sums)
    if relayed:
        far, near = sent
        far = lax.ppermute(far, "area", [(a, a ^ 2) for a in range(areas)])
        arrived, _ = lax.optimization_barrier((far, sums))
        (both,) = call(relay_kernel, "relay", (near, arrived), [shape(2 * block_rows, LANES)], [], BETWEEN)
        peer = [far, lax.ppermute(both, "area", [(a, a ^ 1) for a in range(areas)])]
    else:
        peer = from_partners(sent)
    gen_mean, hedge = call(
        functools.partial(agree_kernel, scen_total),
        "agree",
        (hedged, *sum_terms),
        [shape(hours, buses), shape(width, buses)],
        [],
        BETWEEN,
    )
    tie_shape = shape(width, 2 * REACH * CAP)
    hedge, gen_mean, tie_flow = call(
        functools.partial(last_kernel, blocks, relayed, partner_of),
        "last",
        (hedge, gen_mean, *peer, weight, mine, theirs),
        [shape(width, buses), shape(hours, buses), tie_shape],
        [
            pltpu.VMEM(tie_shape.shape, f32),
            pltpu.VMEM((2 * REACH * CAP, columns), f32),
            pltpu.SemaphoreType.DMA((3,)),
        ],
        slots * columns,
        outs_in_place=True,
    )
    return (
        gen_mean,
        hedge.reshape(hours, scens, buses),
        tie_flow.reshape(hours, scens, 2 * REACH * CAP),
    )


def solution(mesh):
    return jax.shard_map(
        per_device,
        mesh=mesh,
        in_specs=(
            P(("group", "area"), None),
            P(("group", "area"), None),
            P(("group", "hour"), "scen", "area"),
            P(("group", "hour"), "area"),
            P(("group", "hour"), "scen", "area"),
            P(("group", "area")),
            P(("group", "area")),
            P(("group", "area")),
            P(("group", "area")),
            P("group", None),
            P("group", None),
            P("group", None),
            P("group", None),
        ),
        out_specs=(
            P(("group", "hour"), "area"),
            P(("group", "hour"), "scen", "area"),
            P(("group", "hour"), "scen", "area"),
        ),
        check_vma=False,
    )
```

```python
import functools

import jax
import jax.numpy as jnp
from jax import lax
from jax.experimental import pallas as pl
from jax.experimental.pallas import tpu as pltpu
from jax.sharding import PartitionSpec as P

HOURS = 24
REACH = 4
CAP = 16

STEP_SIZE = 0.5
LINE_CHUNK = 1024
LANES = 128
BETWEEN = 20_000_000_000

CONTRACT_LAST = (((1,), (1,)), ((), ()))
CONTRACT_FIRST = (((0,), (0,)), ((), ()))
VMEM = pl.BlockSpec(memory_space=pltpu.VMEM)
ANY = pl.BlockSpec(memory_space=pltpu.HBM)


TARGETS = ((3, 2, 0, 1), (2, 3, 1, 0), (1, 0, 3, 2))


def partner_plan(areas):
    if areas == 4:

        def partner_of(here, i):
            return sum(jnp.where(here == a, target, 0) for a, target in enumerate(TARGETS[i]))

        def by_target(parts):
            out, back, pair = (
                lax.ppermute(part, "area", list(enumerate(target))) for part, target in zip(parts, TARGETS)
            )
            return [back, out, pair]

        return len(TARGETS), partner_of, by_target
    reach = min(REACH, areas - 1)
    shifts = sorted({s % areas for d in range(1, reach + 1) for s in (d, -d)})

    def by_shift(parts):
        sent = [
            lax.ppermute(part, "area", [(a, (a + s) % areas) for a in range(areas)])
            for part, s in zip(parts, shifts)
        ]
        return [sent[shifts.index(areas - s)] for s in shifts]

    return len(shifts), lambda here, i: lax.rem(here + shifts[i], areas), by_shift


def by_flips(here, flip_3, flip_2):
    return jnp.where(here < 2, flip_3, flip_2), jnp.where(here < 2, flip_2, flip_3)


def block_facts(here, partner):
    low = partner > here
    distance = jnp.abs(partner - here)
    block = jnp.clip(distance - 1, 0, REACH - 1)
    in_reach = (distance >= 1) & (distance <= REACH)
    return low, jnp.minimum(here, partner), block, in_reach


def fold(x):
    half = x.shape[0] // 2
    low = lax.broadcasted_iota(jnp.int32, (half, LANES), 1) < LANES // 2
    shared = jnp.where(low, x[0:half, LANES : 2 * LANES], x[half:, LANES : 2 * LANES])
    return jnp.concatenate([x[:, 0:LANES], shared], axis=0)


def unfold(packed):
    rows = 2 * packed.shape[0] // 3
    shared = packed[rows:, :]
    low = lax.broadcasted_iota(jnp.int32, shared.shape, 1) < LANES // 2
    turned = pltpu.roll(shared, LANES // 2, 1)
    rest = jnp.concatenate([jnp.where(low, shared, turned), jnp.where(low, turned, shared)], axis=0)
    return jnp.concatenate([packed[0:rows, :], rest], axis=1)


def repeat_rest(inject_ref, width):
    inject_ref[width:, :] = inject_ref[width - LANES // 2 : width, :]


def split_3(x):
    high = x.astype(jnp.bfloat16)
    rest = x - high.astype(jnp.float32)
    middle = rest.astype(jnp.bfloat16)
    rest = rest - middle.astype(jnp.float32)
    return jnp.concatenate([high, middle, rest.astype(jnp.bfloat16)], axis=0)


def put_row(packed_ref, hours, h, row):
    for j in range(row.shape[1] // LANES):
        packed_ref[j * hours + h : j * hours + h + 1, :] = row[:, j * LANES : (j + 1) * LANES]


def clear_rest(packed_ref, used):
    rows = packed_ref.shape[0]
    if used < rows:
        packed_ref[used:, :] = jnp.zeros((rows - used, LANES), jnp.float32)


def agree(mean_ref, sum_refs, hours, scen_total):
    for j in range(mean_ref.shape[1] // LANES):
        parts = [ref[j * hours : (j + 1) * hours, :] for ref in sum_refs]
        mean_ref[0:hours, j * LANES : (j + 1) * LANES] = functools.reduce(jnp.add, parts) / scen_total


def excess(diffs, limit):
    return diffs - jnp.clip(diffs, -limit, limit)


def write_ramp(mean_ref, beyond, limit, first_hour, padded_ref, excess_ref, ramp_ref):
    hours = ramp_ref.shape[0]
    padded_ref[0:1, :] = beyond
    padded_ref[1 : hours + 1, :] = mean_ref[0:hours, :]
    padded_ref[hours + 1 : hours + 2, :] = beyond
    diffs = padded_ref[1 : hours + 2, :] - padded_ref[0 : hours + 1, :]
    ids = first_hour + lax.broadcasted_iota(jnp.int32, diffs.shape, 0)
    valid = (ids >= 1) & (ids <= HOURS - 1)
    excess_ref[0 : hours + 1, :] = jnp.where(valid, excess(diffs, limit), 0.0)
    ramp_ref[...] = excess_ref[0:hours, :] - excess_ref[1 : hours + 1, :]


def line_work(inject_ref, ptdf_ref, line_max_ref, over_ref):
    inject = inject_ref[...]
    lines = ptdf_ref.shape[0]
    for at in range(0, lines, LINE_CHUNK):
        part = slice(at, at + LINE_CHUNK)
        flows = lax.dot_general(
            inject, ptdf_ref[part, :], CONTRACT_LAST, preferred_element_type=jnp.float32
        )
        limit = line_max_ref[:, part]
        over_ref[:, part] = (flows - jnp.clip(flows, -limit, limit)).astype(jnp.bfloat16)
    return jnp.dot(over_ref[...], ptdf_ref[...], preferred_element_type=jnp.float32)


def table_kernel(
    blocks,
    partner_of,
    hedge_in,
    start_in,
    count_in,
    low_bus_in,
    high_bus_in,
    susc_in,
    edge_hedge_ref,
    start_ref,
    onehot_ref,
    spread_ref,
    weight_ref,
    count_ref,
    low_bus_ref,
    high_bus_ref,
    susc_ref,
    copy_sems,
):
    hours, buses = start_ref.shape
    scens = hedge_in.shape[0] // hours
    here = lax.axis_index("area")
    last = (hours - 1) * scens
    edge_rows = pl.ds(pl.multiple_of((1 - lax.axis_index("hour")) * last, scens), scens)

    pairs = (
        (count_in, count_ref),
        (low_bus_in, low_bus_ref),
        (high_bus_in, high_bus_ref),
        (susc_in, susc_ref),
        (start_in, start_ref),
        (hedge_in.at[edge_rows], edge_hedge_ref),
    )
    copies = [pltpu.make_async_copy(src, dst, copy_sems.at[i]) for i, (src, dst) in enumerate(pairs)]
    for copy in copies:
        copy.start()
    for copy in copies[:4]:
        copy.wait()
    for i in range(blocks):
        partner = partner_of(here, i)
        low, row, block, in_reach = block_facts(here, partner)
        slots = slice(i * CAP, (i + 1) * CAP)
        pick = lax.broadcasted_iota(jnp.int32, (CAP, REACH * CAP), 1) == (
            block * CAP + lax.broadcasted_iota(jnp.int32, (CAP, REACH * CAP), 0)
        )
        table_row = pl.ds(row, 1)
        bus_row = jnp.where(low, low_bus_ref[table_row, :], high_bus_ref[table_row, :])
        bus = jnp.sum(jnp.where(pick, bus_row.astype(jnp.float32), 0.0), axis=1, keepdims=True)
        susc = jnp.sum(jnp.where(pick, susc_ref[table_row, :], 0.0), axis=1, keepdims=True)
        count_row = count_ref[table_row, :].astype(jnp.float32)
        is_block = lax.broadcasted_iota(jnp.int32, (CAP, REACH), 1) == block
        count = jnp.sum(jnp.where(is_block, count_row, 0.0), axis=1, keepdims=True)
        slot_ids = lax.broadcasted_iota(jnp.int32, (CAP, 1), 0).astype(jnp.float32)
        live = jnp.where((slot_ids < count) & in_reach, 1.0, 0.0)
        sign = jnp.where(low, 1.0, -1.0)
        bus_ids = lax.broadcasted_iota(jnp.int32, (CAP, buses), 1).astype(jnp.float32)
        onehot = jnp.where(bus_ids == bus, live, 0.0)
        onehot_ref[slots, :] = onehot.astype(jnp.bfloat16)
        spread_ref[slots, :] = (-sign * onehot).astype(jnp.bfloat16)
        weight_ref[slots, :] = jnp.broadcast_to(live * sign * susc, (CAP, 128))

    for copy in copies[4:]:
        copy.wait()


def angle_kernel(blocks, sens_ref, demand_ref, start_ref, onehot_ref, *refs):
    sent_refs, (own_ref, inject_ref, rows_ref) = refs[:blocks], refs[blocks:]
    hours = start_ref.shape[0]
    scens = demand_ref.shape[0] // hours
    rows = jnp.dot(onehot_ref[...], sens_ref[...], preferred_element_type=jnp.float32)
    rows_ref[...] = rows.astype(jnp.bfloat16)
    for h in range(hours):
        part = slice(h * scens, (h + 1) * scens)
        inject_ref[part, :] = (start_ref[h : h + 1, :] - demand_ref[part, :]).astype(jnp.bfloat16)
    repeat_rest(inject_ref, hours * scens)
    own = lax.dot_general(
        rows_ref[...], inject_ref[...], CONTRACT_LAST, preferred_element_type=jnp.float32
    )
    own_ref[...] = own
    for i in range(blocks):
        sent_refs[i][...] = fold(own[i * CAP : (i + 1) * CAP, :])


def edge_kernel(demand_ref, edge_hedge_ref, start_ref, edge_ref):
    scens = edge_hedge_ref.shape[0]
    hours = start_ref.shape[0]
    early = lax.axis_index("hour") == 0
    last = (hours - 1) * scens
    at = 2 * scens
    edge_ref[0:scens, :] = jnp.where(early, demand_ref[last:, :], demand_ref[0:scens, :])
    edge_ref[scens:at, :] = edge_hedge_ref[...]
    edge_ref[at : at + 1, :] = jnp.where(early, start_ref[hours - 1 : hours, :], start_ref[0:1, :])
    edge_ref[at + 1 : at + 2, :] = jnp.where(
        early, start_ref[hours - 2 : hours - 1, :], start_ref[1:2, :]
    )


def first_kernel(
    ptdf_ref,
    own_inject_ref,
    demand_ref,
    hedge_ref,
    start_ref,
    edge_ref,
    cost_ref,
    max_ref,
    limit_ref,
    line_max_ref,
    gen_ref,
    base_ref,
    hedged_ref,
    sums_ref,
    inject_ref,
    over_ref,
    back_ref,
    padded_ref,
    excess_ref,
    ramp_ref,
):
    hours, buses = start_ref.shape
    width = demand_ref.shape[0]
    scens = width // hours
    at = 2 * scens
    early = lax.axis_index("hour") == 0
    first_hour = lax.axis_index("hour") * hours
    beyond = edge_ref[at : at + 1, :]
    limit = limit_ref[...]
    cost = cost_ref[...]
    top = max_ref[...]

    inject_ref[0:width, :] = own_inject_ref[0:width, :]
    inject_ref[width : width + scens, :] = (beyond - edge_ref[0:scens, :]).astype(jnp.bfloat16)
    back_ref[...] = line_work(inject_ref, ptdf_ref, line_max_ref, over_ref)
    write_ramp(start_ref, beyond, limit, first_hour, padded_ref, excess_ref, ramp_ref)

    def step(mean, hedge, back, ramp):
        grad = cost + back + (mean - mean + hedge) + ramp
        gen = jnp.clip(mean - STEP_SIZE * grad, 0.0, top)
        return gen, gen + hedge

    for h in range(hours):
        part = slice(h * scens, (h + 1) * scens)
        mean = start_ref[h : h + 1, :]
        gen, hedged = step(mean, hedge_ref[part, :], back_ref[part, :], ramp_ref[h : h + 1, :])
        gen_ref[part, :] = gen
        base_ref[part, :] = gen - demand_ref[part, :]
        hedged_ref[part, :] = hedged
        put_row(sums_ref, hours + 1, h, jnp.sum(hedged, axis=0, keepdims=True))
    near = jnp.where(early, start_ref[hours - 1 : hours, :], start_ref[0:1, :])
    ramp = excess(beyond - near, limit) + excess(beyond - edge_ref[at + 1 : at + 2, :], limit)
    _, hedged = step(beyond, edge_ref[scens:at, :], back_ref[width : width + scens, :], ramp)
    put_row(sums_ref, hours + 1, hours, jnp.sum(hedged, axis=0, keepdims=True))
    clear_rest(sums_ref, (hours + 1) * (buses // LANES))


def tie_kernel(blocks, relayed, base_ref, spread_ref, rows_ref, weight_ref, own_ref, *refs):
    peer_refs, refs = refs[:blocks], refs[blocks:]
    *next_refs, inject_ref, mine_ref, theirs_ref = refs
    width = base_ref.shape[0]

    weight = jnp.concatenate([weight_ref[...], weight_ref[...]], axis=1)
    own = own_ref[...]
    peer = jnp.concatenate([unfold(ref[...]) for ref in peer_refs], axis=0)
    est_mine = weight * own
    est_theirs = -weight * peer
    flow = (est_mine + est_theirs) * 0.5
    dual_mine = est_mine - flow
    dual_theirs = est_theirs - flow
    spread = spread_ref[...]
    add = lax.dot_general(
        split_3(flow),
        jnp.concatenate([spread, spread, spread], axis=0),
        CONTRACT_FIRST,
        preferred_element_type=jnp.float32,
    )
    inject_ref[0:width, :] = (base_ref[...] + add[0:width, :]).astype(jnp.bfloat16)
    repeat_rest(inject_ref, width)

    own_next = lax.dot_general(
        rows_ref[...], inject_ref[...], CONTRACT_LAST, preferred_element_type=jnp.float32
    )
    parts = [own_next[i * CAP : (i + 1) * CAP, :] for i in range(blocks)]
    if relayed:
        far_ref, near_ref = next_refs
        flip_3, flip_2 = by_flips(lax.axis_index("area"), parts[0], parts[1])
        far_ref[...] = fold(jnp.concatenate([flip_2, flip_3], axis=0))
        near_ref[...] = parts[2]
    else:
        for ref, part in zip(next_refs, parts):
            ref[...] = fold(part)
    mine_ref[...] = weight * (own_next - peer) + dual_mine
    theirs_ref[...] = weight * own + dual_theirs


def second_kernel(
    terms,
    scen_total,
    ptdf_ref,
    inject_ref,
    gen_ref,
    hedged_ref,
    cost_ref,
    max_ref,
    limit_ref,
    line_max_ref,
    *refs,
):
    sum_refs, refs = refs[:terms], refs[terms:]
    (hedged_out_ref, sums_out_ref, over_ref, back_ref, mean_ref, padded_ref, excess_ref, ramp_ref) = refs
    hours, buses = ramp_ref.shape
    width = back_ref.shape[0]
    scens = width // hours
    first_hour = lax.axis_index("hour") * hours

    back_ref[...] = line_work(inject_ref.at[0:width, :], ptdf_ref, line_max_ref, over_ref)
    agree(mean_ref, sum_refs, hours + 1, scen_total)
    write_ramp(
        mean_ref, mean_ref[hours : hours + 1, :], limit_ref[...], first_hour, padded_ref, excess_ref, ramp_ref
    )
    cost = cost_ref[...]
    top = max_ref[...]
    for h in range(hours):
        part = slice(h * scens, (h + 1) * scens)
        mean = mean_ref[h : h + 1, :]
        gen = gen_ref[part, :]
        hedge = hedged_ref[part, :] - mean
        grad = cost + back_ref[part, :] + (gen - mean + hedge) + ramp_ref[h : h + 1, :]
        gen = jnp.clip(gen - STEP_SIZE * grad, 0.0, top)
        hedged = gen + hedge
        hedged_out_ref[part, :] = hedged
        put_row(sums_out_ref, hours, h, jnp.sum(hedged, axis=0, keepdims=True))
    clear_rest(sums_out_ref, hours * (buses // LANES))


def relay_kernel(near_ref, far_ref, both_ref):
    low = lax.broadcasted_iota(jnp.int32, (CAP, LANES), 1) < LANES // 2
    both_ref[0:CAP, :] = near_ref[:, 0:LANES]
    both_ref[CAP : 2 * CAP, :] = far_ref[CAP : 2 * CAP, :]
    both_ref[2 * CAP :, :] = jnp.where(low, near_ref[:, LANES:], far_ref[2 * CAP :, :])


def agree_kernel(scen_total, hedged_ref, *refs):
    sum_refs, (mean_ref, hedge_ref) = refs[:-2], refs[-2:]
    hours = mean_ref.shape[0]
    scens = hedged_ref.shape[0] // hours
    agree(mean_ref, sum_refs, hours, scen_total)
    for h in range(hours):
        part = slice(h * scens, (h + 1) * scens)
        hedge_ref[part, :] = hedged_ref[part, :] - mean_ref[h : h + 1, :]


def last_kernel(blocks, relayed, partner_of, hedge_ref, mean_ref, *refs):
    *peer_refs, weight_ref, mine_ref, theirs_ref = refs[:-6]
    hedge_out, mean_out, tie_out, tie_ref, placed_ref, copy_sems = refs[-6:]
    copies = []

    def send(src, dst):
        copies.append(pltpu.make_async_copy(src, dst, copy_sems.at[len(copies)]))
        copies[-1].start()

    send(hedge_ref, hedge_out)
    send(mean_ref, mean_out)
    here = lax.axis_index("area")
    placed_ref[...] = jnp.zeros_like(placed_ref)
    if relayed:
        far, both = (unfold(ref[...]) for ref in peer_refs)
        peers = [*by_flips(here, both[CAP:, :], far[0:CAP, :]), both[0:CAP, :]]
    else:
        peers = [unfold(ref[...]) for ref in peer_refs]
    for i in range(blocks):
        slots = slice(i * CAP, (i + 1) * CAP)
        weight = jnp.concatenate([weight_ref[slots, :], weight_ref[slots, :]], axis=1)
        flow = (mine_ref[slots, :] + (theirs_ref[slots, :] - weight * peers[i])) * 0.5
        low, _, block, in_reach = block_facts(here, partner_of(here, i))
        first = block * CAP + jnp.where(low, 0, REACH * CAP)

        @pl.when(in_reach)
        def _():
            placed_ref[pl.ds(pl.multiple_of(first, CAP), CAP), :] = flow

    tie_ref[...] = jnp.transpose(placed_ref[...])[0 : tie_ref.shape[0], :]
    send(tie_ref, tie_out)
    for copy in copies:
        copy.wait()


def call(kernel, name, args, outs, scratch, flops, in_place=(), outs_in_place=False):
    size = sum(x.size * x.dtype.itemsize for x in list(args) + list(outs))
    return pl.pallas_call(
        kernel,
        name=name,
        out_shape=outs,
        in_specs=[ANY if i in in_place else VMEM for i in range(len(args))],
        out_specs=[ANY if outs_in_place else VMEM] * len(outs),
        scratch_shapes=scratch,
        compiler_params=pltpu.CompilerParams(vmem_limit_bytes=32 * 1024 * 1024),
        cost_estimate=pl.CostEstimate(flops=flops, bytes_accessed=size, transcendentals=0),
    )(*(pltpu.with_memory_space_constraint(x, pltpu.HBM) if i in in_place else x for i, x in enumerate(args)))


def per_device(
    ptdf,
    angle_sens,
    demand,
    gen_start,
    hedge_dual,
    gen_cost,
    gen_max,
    gen_ramp,
    line_max,
    tie_count,
    tie_low_bus,
    tie_high_bus,
    tie_susc,
):
    hours, scens, buses = demand.shape
    lines = ptdf.shape[0]
    width = hours * scens
    areas = lax.axis_size("area")
    n_scen = lax.axis_size("scen")
    assert lax.axis_size("hour") == 2 and hours >= 2
    assert width % LANES == LANES // 2 and width < 2 * LANES
    columns = 2 * LANES
    block_rows = CAP * 3 // 2
    scen_total = scens * n_scen
    blocks, partner_of, from_partners = partner_plan(areas)
    slots = blocks * CAP
    pieces = buses // LANES
    sum_rows = 8 * pl.cdiv((hours + 1) * pieces, 8)
    f32, bf16 = jnp.float32, jnp.bfloat16

    def shape(*dims, dtype=f32):
        return jax.ShapeDtypeStruct(dims, dtype)

    def over_scens(sums):
        if n_scen == 2:
            return [sums, lax.ppermute(sums, "scen", [(0, 1), (1, 0)])]
        return [lax.psum(sums, "scen")]

    work = 4 * width * lines * buses

    def step_scratch(rows):
        return [
            pltpu.VMEM((rows, buses), bf16),
            pltpu.VMEM((rows, lines), bf16),
            pltpu.VMEM((rows, buses), f32),
        ]

    ramp_scratch = [
        pltpu.VMEM((hours + 4, buses), f32),
        pltpu.VMEM((hours + 4, buses), f32),
        pltpu.VMEM((hours, buses), f32),
    ]
    tables = (tie_count, tie_low_bus, tie_high_bus, tie_susc)
    vectors = [x.reshape(1, -1) for x in (gen_cost, gen_max, gen_ramp, line_max)]
    load = demand.reshape(width, buses)
    hedge = hedge_dual.reshape(width, buses)
    edge_hedge, start, onehot, spread, weight = call(
        functools.partial(table_kernel, blocks, partner_of),
        "tables",
        (hedge, gen_start, *tables),
        [
            shape(scens, buses),
            shape(hours, buses),
            shape(slots, buses, dtype=bf16),
            shape(slots, buses, dtype=bf16),
            shape(slots, LANES),
        ],
        [pltpu.VMEM(x.shape, x.dtype) for x in tables] + [pltpu.SemaphoreType.DMA((6,))],
        BETWEEN,
        range(6),
    )
    *sent, own, inject, rows = call(
        functools.partial(angle_kernel, blocks),
        "angles",
        (angle_sens, load, start, onehot),
        [shape(block_rows, LANES)] * blocks
        + [shape(slots, columns), shape(columns, buses, dtype=bf16), shape(slots, buses, dtype=bf16)],
        [],
        2 * slots * buses * (width + buses),
    )
    edge_hedge, own = lax.optimization_barrier((edge_hedge, own))
    (edge,) = call(edge_kernel, "edge", (load, edge_hedge, start), [shape(2 * scens + 8, buses)], [], BETWEEN)
    edge = lax.ppermute(edge, "hour", [(0, 1), (1, 0)])
    peer = from_partners(sent)
    gen, base, hedged, sums = call(
        first_kernel,
        "first",
        (ptdf, inject, load, hedge, start, edge, *vectors),
        [
            shape(width, buses),
            shape(width, buses),
            shape(width, buses),
            shape(sum_rows, LANES),
        ],
        step_scratch(width + scens) + ramp_scratch,
        work,
    )
    sum_terms = over_scens(sums)
    terms = len(sum_terms)
    relayed = areas == 4
    tied = call(
        functools.partial(tie_kernel, blocks, relayed),
        "ties",
        (base, spread, rows, weight, own, *peer),
        (
            [shape(2 * block_rows, LANES), shape(CAP, columns)]
            if relayed
            else [shape(block_rows, LANES)] * blocks
        )
        + [shape(columns, buses, dtype=bf16), shape(slots, columns), shape(slots, columns)],
        [],
        BETWEEN,
    )
    *sent, inject, mine, theirs = tied
    hedged, sums = call(
        functools.partial(second_kernel, terms, scen_total),
        "second",
        (ptdf, inject, gen, hedged, *vectors, *sum_terms),
        [shape(width, buses), shape(sum_rows, LANES)],
        step_scratch(width)[1:] + [pltpu.VMEM((8 * pl.cdiv(hours + 1, 8), buses), f32)] + ramp_scratch,
        work,
    )
    sum_terms = over_scens(sums)
    if relayed:
        far, near = sent
        far = lax.ppermute(far, "area", [(a, a ^ 2) for a in range(areas)])
        arrived, _ = lax.optimization_barrier((far, sums))
        (both,) = call(relay_kernel, "relay", (near, arrived), [shape(2 * block_rows, LANES)], [], BETWEEN)
        peer = [far, lax.ppermute(both, "area", [(a, a ^ 1) for a in range(areas)])]
    else:
        peer = from_partners(sent)
    gen_mean, hedge = call(
        functools.partial(agree_kernel, scen_total),
        "agree",
        (hedged, *sum_terms),
        [shape(hours, buses), shape(width, buses)],
        [],
        BETWEEN,
    )
    tie_shape = shape(width, 2 * REACH * CAP)
    hedge, gen_mean, tie_flow = call(
        functools.partial(last_kernel, blocks, relayed, partner_of),
        "last",
        (hedge, gen_mean, *peer, weight, mine, theirs),
        [shape(width, buses), shape(hours, buses), tie_shape],
        [
            pltpu.VMEM(tie_shape.shape, f32),
            pltpu.VMEM((2 * REACH * CAP, columns), f32),
            pltpu.SemaphoreType.DMA((3,)),
        ],
        slots * columns,
        outs_in_place=True,
    )
    return (
        gen_mean,
        hedge.reshape(hours, scens, buses),
        tie_flow.reshape(hours, scens, 2 * REACH * CAP),
    )


def solution(mesh):
    return jax.shard_map(
        per_device,
        mesh=mesh,
        in_specs=(
            P(("group", "area"), None),
            P(("group", "area"), None),
            P(("group", "hour"), "scen", "area"),
            P(("group", "hour"), "area"),
            P(("group", "hour"), "scen", "area"),
            P(("group", "area")),
            P(("group", "area")),
            P(("group", "area")),
            P(("group", "area")),
            P("group", None),
            P("group", None),
            P("group", None),
            P("group", None),
        ),
        out_specs=(
            P(("group", "hour"), "area"),
            P(("group", "hour"), "scen", "area"),
            P(("group", "hour"), "scen", "area"),
        ),
        check_vma=False,
    )
```

```python
import functools

import jax
import jax.numpy as jnp
from jax import lax
from jax.experimental import pallas as pl
from jax.experimental.pallas import tpu as pltpu
from jax.sharding import PartitionSpec as P

HOURS = 24
REACH = 4
CAP = 16

STEP_SIZE = 0.5
LINE_CHUNK = 1024
LANES = 128
BETWEEN = 20_000_000_000

CONTRACT_LAST = (((1,), (1,)), ((), ()))
CONTRACT_FIRST = (((0,), (0,)), ((), ()))
VMEM = pl.BlockSpec(memory_space=pltpu.VMEM)
ANY = pl.BlockSpec(memory_space=pltpu.HBM)


TARGETS = ((3, 2, 0, 1), (2, 3, 1, 0), (1, 0, 3, 2))


def partner_plan(areas):
    if areas == 4:

        def partner_of(here, i):
            return sum(jnp.where(here == a, target, 0) for a, target in enumerate(TARGETS[i]))

        def by_target(parts):
            out, back, pair = (
                lax.ppermute(part, "area", list(enumerate(target))) for part, target in zip(parts, TARGETS)
            )
            return [back, out, pair]

        return len(TARGETS), partner_of, by_target
    reach = min(REACH, areas - 1)
    shifts = sorted({s % areas for d in range(1, reach + 1) for s in (d, -d)})

    def by_shift(parts):
        sent = [
            lax.ppermute(part, "area", [(a, (a + s) % areas) for a in range(areas)])
            for part, s in zip(parts, shifts)
        ]
        return [sent[shifts.index(areas - s)] for s in shifts]

    return len(shifts), lambda here, i: lax.rem(here + shifts[i], areas), by_shift


def by_flips(here, flip_3, flip_2):
    return jnp.where(here < 2, flip_3, flip_2), jnp.where(here < 2, flip_2, flip_3)


def block_facts(here, partner):
    low = partner > here
    distance = jnp.abs(partner - here)
    block = jnp.clip(distance - 1, 0, REACH - 1)
    in_reach = (distance >= 1) & (distance <= REACH)
    return low, jnp.minimum(here, partner), block, in_reach


def fold(x):
    half = x.shape[0] // 2
    low = lax.broadcasted_iota(jnp.int32, (half, LANES), 1) < LANES // 2
    shared = jnp.where(low, x[0:half, LANES : 2 * LANES], x[half:, LANES : 2 * LANES])
    return jnp.concatenate([x[:, 0:LANES], shared], axis=0)


def unfold(packed):
    rows = 2 * packed.shape[0] // 3
    shared = packed[rows:, :]
    low = lax.broadcasted_iota(jnp.int32, shared.shape, 1) < LANES // 2
    turned = pltpu.roll(shared, LANES // 2, 1)
    rest = jnp.concatenate([jnp.where(low, shared, turned), jnp.where(low, turned, shared)], axis=0)
    return jnp.concatenate([packed[0:rows, :], rest], axis=1)


def repeat_rest(inject_ref, width):
    inject_ref[width:, :] = inject_ref[width - LANES // 2 : width, :]


def split_3(x):
    high = x.astype(jnp.bfloat16)
    rest = x - high.astype(jnp.float32)
    middle = rest.astype(jnp.bfloat16)
    rest = rest - middle.astype(jnp.float32)
    return jnp.concatenate([high, middle, rest.astype(jnp.bfloat16)], axis=0)


def put_row(packed_ref, hours, h, row):
    for j in range(row.shape[1] // LANES):
        packed_ref[j * hours + h : j * hours + h + 1, :] = row[:, j * LANES : (j + 1) * LANES]


def clear_rest(packed_ref, used):
    rows = packed_ref.shape[0]
    if used < rows:
        packed_ref[used:, :] = jnp.zeros((rows - used, LANES), jnp.float32)


def agree(mean_ref, sum_refs, hours, scen_total):
    for j in range(mean_ref.shape[1] // LANES):
        parts = [ref[j * hours : (j + 1) * hours, :] for ref in sum_refs]
        mean_ref[0:hours, j * LANES : (j + 1) * LANES] = functools.reduce(jnp.add, parts) / scen_total


def excess(diffs, limit):
    return diffs - jnp.clip(diffs, -limit, limit)


def write_ramp(mean_ref, beyond, limit, first_hour, padded_ref, excess_ref, ramp_ref):
    hours = ramp_ref.shape[0]
    padded_ref[0:1, :] = beyond
    padded_ref[1 : hours + 1, :] = mean_ref[0:hours, :]
    padded_ref[hours + 1 : hours + 2, :] = beyond
    diffs = padded_ref[1 : hours + 2, :] - padded_ref[0 : hours + 1, :]
    ids = first_hour + lax.broadcasted_iota(jnp.int32, diffs.shape, 0)
    valid = (ids >= 1) & (ids <= HOURS - 1)
    excess_ref[0 : hours + 1, :] = jnp.where(valid, excess(diffs, limit), 0.0)
    ramp_ref[...] = excess_ref[0:hours, :] - excess_ref[1 : hours + 1, :]


def line_work(inject_ref, ptdf_ref, line_max_ref, over_ref):
    inject = inject_ref[...]
    lines = ptdf_ref.shape[0]
    for at in range(0, lines, LINE_CHUNK):
        part = slice(at, at + LINE_CHUNK)
        flows = lax.dot_general(
            inject, ptdf_ref[part, :], CONTRACT_LAST, preferred_element_type=jnp.float32
        )
        limit = line_max_ref[:, part]
        over_ref[:, part] = (flows - jnp.clip(flows, -limit, limit)).astype(jnp.bfloat16)
    return jnp.dot(over_ref[...], ptdf_ref[...], preferred_element_type=jnp.float32)


def table_kernel(
    blocks,
    partner_of,
    hedge_in,
    start_in,
    count_in,
    low_bus_in,
    high_bus_in,
    susc_in,
    edge_hedge_ref,
    start_ref,
    onehot_ref,
    spread_ref,
    weight_ref,
    count_ref,
    low_bus_ref,
    high_bus_ref,
    susc_ref,
    copy_sems,
):
    hours, buses = start_ref.shape
    scens = hedge_in.shape[0] // hours
    here = lax.axis_index("area")
    last = (hours - 1) * scens
    edge_rows = pl.ds(pl.multiple_of((1 - lax.axis_index("hour")) * last, scens), scens)

    pairs = (
        (count_in, count_ref),
        (low_bus_in, low_bus_ref),
        (high_bus_in, high_bus_ref),
        (susc_in, susc_ref),
        (start_in, start_ref),
        (hedge_in.at[edge_rows], edge_hedge_ref),
    )
    copies = [pltpu.make_async_copy(src, dst, copy_sems.at[i]) for i, (src, dst) in enumerate(pairs)]
    for copy in copies:
        copy.start()
    for copy in copies[:4]:
        copy.wait()
    for i in range(blocks):
        partner = partner_of(here, i)
        low, row, block, in_reach = block_facts(here, partner)
        slots = slice(i * CAP, (i + 1) * CAP)
        pick = lax.broadcasted_iota(jnp.int32, (CAP, REACH * CAP), 1) == (
            block * CAP + lax.broadcasted_iota(jnp.int32, (CAP, REACH * CAP), 0)
        )
        table_row = pl.ds(row, 1)
        bus_row = jnp.where(low, low_bus_ref[table_row, :], high_bus_ref[table_row, :])
        bus = jnp.sum(jnp.where(pick, bus_row.astype(jnp.float32), 0.0), axis=1, keepdims=True)
        susc = jnp.sum(jnp.where(pick, susc_ref[table_row, :], 0.0), axis=1, keepdims=True)
        count_row = count_ref[table_row, :].astype(jnp.float32)
        is_block = lax.broadcasted_iota(jnp.int32, (CAP, REACH), 1) == block
        count = jnp.sum(jnp.where(is_block, count_row, 0.0), axis=1, keepdims=True)
        slot_ids = lax.broadcasted_iota(jnp.int32, (CAP, 1), 0).astype(jnp.float32)
        live = jnp.where((slot_ids < count) & in_reach, 1.0, 0.0)
        sign = jnp.where(low, 1.0, -1.0)
        bus_ids = lax.broadcasted_iota(jnp.int32, (CAP, buses), 1).astype(jnp.float32)
        onehot = jnp.where(bus_ids == bus, live, 0.0)
        onehot_ref[slots, :] = onehot.astype(jnp.bfloat16)
        spread_ref[slots, :] = (-sign * onehot).astype(jnp.bfloat16)
        weight_ref[slots, :] = jnp.broadcast_to(live * sign * susc, (CAP, 128))

    for copy in copies[4:]:
        copy.wait()


def row_kernel(sens_ref, onehot_ref, rows_ref):
    rows = jnp.dot(onehot_ref[...], sens_ref[...], preferred_element_type=jnp.float32)
    rows_ref[...] = rows.astype(jnp.bfloat16)


def angle_kernel(blocks, demand_ref, start_ref, rows_ref, *refs):
    sent_refs, (own_ref, inject_ref) = refs[:blocks], refs[blocks:]
    hours = start_ref.shape[0]
    scens = demand_ref.shape[0] // hours
    for h in range(hours):
        part = slice(h * scens, (h + 1) * scens)
        inject_ref[part, :] = (start_ref[h : h + 1, :] - demand_ref[part, :]).astype(jnp.bfloat16)
    repeat_rest(inject_ref, hours * scens)
    own = lax.dot_general(
        rows_ref[...], inject_ref[...], CONTRACT_LAST, preferred_element_type=jnp.float32
    )
    own_ref[...] = own
    for i in range(blocks):
        sent_refs[i][...] = fold(own[i * CAP : (i + 1) * CAP, :])


def edge_kernel(demand_ref, edge_hedge_ref, start_ref, edge_ref):
    scens = edge_hedge_ref.shape[0]
    hours = start_ref.shape[0]
    early = lax.axis_index("hour") == 0
    last = (hours - 1) * scens
    at = 2 * scens
    edge_ref[0:scens, :] = jnp.where(early, demand_ref[last:, :], demand_ref[0:scens, :])
    edge_ref[scens:at, :] = edge_hedge_ref[...]
    edge_ref[at : at + 1, :] = jnp.where(early, start_ref[hours - 1 : hours, :], start_ref[0:1, :])
    edge_ref[at + 1 : at + 2, :] = jnp.where(
        early, start_ref[hours - 2 : hours - 1, :], start_ref[1:2, :]
    )


def first_kernel(
    ptdf_ref,
    own_inject_ref,
    demand_ref,
    hedge_ref,
    start_ref,
    edge_ref,
    cost_ref,
    max_ref,
    limit_ref,
    line_max_ref,
    gen_ref,
    base_ref,
    hedged_ref,
    sums_ref,
    inject_ref,
    over_ref,
    back_ref,
    padded_ref,
    excess_ref,
    ramp_ref,
):
    hours, buses = start_ref.shape
    width = demand_ref.shape[0]
    scens = width // hours
    at = 2 * scens
    early = lax.axis_index("hour") == 0
    first_hour = lax.axis_index("hour") * hours
    beyond = edge_ref[at : at + 1, :]
    limit = limit_ref[...]
    cost = cost_ref[...]
    top = max_ref[...]

    inject_ref[0:width, :] = own_inject_ref[0:width, :]
    inject_ref[width : width + scens, :] = (beyond - edge_ref[0:scens, :]).astype(jnp.bfloat16)
    back_ref[...] = line_work(inject_ref, ptdf_ref, line_max_ref, over_ref)
    write_ramp(start_ref, beyond, limit, first_hour, padded_ref, excess_ref, ramp_ref)

    def step(mean, hedge, back, ramp):
        grad = cost + back + (mean - mean + hedge) + ramp
        gen = jnp.clip(mean - STEP_SIZE * grad, 0.0, top)
        return gen, gen + hedge

    for h in range(hours):
        part = slice(h * scens, (h + 1) * scens)
        mean = start_ref[h : h + 1, :]
        gen, hedged = step(mean, hedge_ref[part, :], back_ref[part, :], ramp_ref[h : h + 1, :])
        gen_ref[part, :] = gen
        base_ref[part, :] = gen - demand_ref[part, :]
        hedged_ref[part, :] = hedged
        put_row(sums_ref, hours + 1, h, jnp.sum(hedged, axis=0, keepdims=True))
    near = jnp.where(early, start_ref[hours - 1 : hours, :], start_ref[0:1, :])
    ramp = excess(beyond - near, limit) + excess(beyond - edge_ref[at + 1 : at + 2, :], limit)
    _, hedged = step(beyond, edge_ref[scens:at, :], back_ref[width : width + scens, :], ramp)
    put_row(sums_ref, hours + 1, hours, jnp.sum(hedged, axis=0, keepdims=True))
    clear_rest(sums_ref, (hours + 1) * (buses // LANES))


def tie_kernel(blocks, relayed, base_ref, spread_ref, rows_ref, weight_ref, own_ref, *refs):
    peer_refs, refs = refs[:blocks], refs[blocks:]
    *next_refs, inject_ref, mine_ref, theirs_ref = refs
    width = base_ref.shape[0]

    weight = jnp.concatenate([weight_ref[...], weight_ref[...]], axis=1)
    own = own_ref[...]
    peer = jnp.concatenate([unfold(ref[...]) for ref in peer_refs], axis=0)
    est_mine = weight * own
    est_theirs = -weight * peer
    flow = (est_mine + est_theirs) * 0.5
    dual_mine = est_mine - flow
    dual_theirs = est_theirs - flow
    spread = spread_ref[...]
    add = lax.dot_general(
        split_3(flow),
        jnp.concatenate([spread, spread, spread], axis=0),
        CONTRACT_FIRST,
        preferred_element_type=jnp.float32,
    )
    inject_ref[0:width, :] = (base_ref[...] + add[0:width, :]).astype(jnp.bfloat16)
    repeat_rest(inject_ref, width)

    own_next = lax.dot_general(
        rows_ref[...], inject_ref[...], CONTRACT_LAST, preferred_element_type=jnp.float32
    )
    parts = [own_next[i * CAP : (i + 1) * CAP, :] for i in range(blocks)]
    if relayed:
        far_ref, near_ref = next_refs
        flip_3, flip_2 = by_flips(lax.axis_index("area"), parts[0], parts[1])
        far_ref[...] = fold(jnp.concatenate([flip_2, flip_3], axis=0))
        near_ref[...] = parts[2]
    else:
        for ref, part in zip(next_refs, parts):
            ref[...] = fold(part)
    mine_ref[...] = weight * (own_next - peer) + dual_mine
    theirs_ref[...] = weight * own + dual_theirs


def second_kernel(
    terms,
    scen_total,
    ptdf_ref,
    inject_ref,
    gen_ref,
    hedged_ref,
    cost_ref,
    max_ref,
    limit_ref,
    line_max_ref,
    *refs,
):
    sum_refs, refs = refs[:terms], refs[terms:]
    (hedged_out_ref, sums_out_ref, over_ref, back_ref, mean_ref, padded_ref, excess_ref, ramp_ref) = refs
    hours, buses = ramp_ref.shape
    width = back_ref.shape[0]
    scens = width // hours
    first_hour = lax.axis_index("hour") * hours

    back_ref[...] = line_work(inject_ref.at[0:width, :], ptdf_ref, line_max_ref, over_ref)
    agree(mean_ref, sum_refs, hours + 1, scen_total)
    write_ramp(
        mean_ref, mean_ref[hours : hours + 1, :], limit_ref[...], first_hour, padded_ref, excess_ref, ramp_ref
    )
    cost = cost_ref[...]
    top = max_ref[...]
    for h in range(hours):
        part = slice(h * scens, (h + 1) * scens)
        mean = mean_ref[h : h + 1, :]
        gen = gen_ref[part, :]
        hedge = hedged_ref[part, :] - mean
        grad = cost + back_ref[part, :] + (gen - mean + hedge) + ramp_ref[h : h + 1, :]
        gen = jnp.clip(gen - STEP_SIZE * grad, 0.0, top)
        hedged = gen + hedge
        hedged_out_ref[part, :] = hedged
        put_row(sums_out_ref, hours, h, jnp.sum(hedged, axis=0, keepdims=True))
    clear_rest(sums_out_ref, hours * (buses // LANES))


def relay_kernel(near_ref, far_ref, both_ref):
    low = lax.broadcasted_iota(jnp.int32, (CAP, LANES), 1) < LANES // 2
    both_ref[0:CAP, :] = near_ref[:, 0:LANES]
    both_ref[CAP : 2 * CAP, :] = far_ref[CAP : 2 * CAP, :]
    both_ref[2 * CAP :, :] = jnp.where(low, near_ref[:, LANES:], far_ref[2 * CAP :, :])


def agree_kernel(scen_total, hedged_ref, *refs):
    sum_refs, (mean_ref, hedge_ref) = refs[:-2], refs[-2:]
    hours = mean_ref.shape[0]
    scens = hedged_ref.shape[0] // hours
    agree(mean_ref, sum_refs, hours, scen_total)
    for h in range(hours):
        part = slice(h * scens, (h + 1) * scens)
        hedge_ref[part, :] = hedged_ref[part, :] - mean_ref[h : h + 1, :]


def last_kernel(blocks, relayed, partner_of, hedge_ref, mean_ref, *refs):
    *peer_refs, weight_ref, mine_ref, theirs_ref = refs[:-6]
    hedge_out, mean_out, tie_out, tie_ref, placed_ref, copy_sems = refs[-6:]
    copies = []

    def send(src, dst):
        copies.append(pltpu.make_async_copy(src, dst, copy_sems.at[len(copies)]))
        copies[-1].start()

    send(hedge_ref, hedge_out)
    send(mean_ref, mean_out)
    here = lax.axis_index("area")
    placed_ref[...] = jnp.zeros_like(placed_ref)
    if relayed:
        far, both = (unfold(ref[...]) for ref in peer_refs)
        peers = [*by_flips(here, both[CAP:, :], far[0:CAP, :]), both[0:CAP, :]]
    else:
        peers = [unfold(ref[...]) for ref in peer_refs]
    for i in range(blocks):
        slots = slice(i * CAP, (i + 1) * CAP)
        weight = jnp.concatenate([weight_ref[slots, :], weight_ref[slots, :]], axis=1)
        flow = (mine_ref[slots, :] + (theirs_ref[slots, :] - weight * peers[i])) * 0.5
        low, _, block, in_reach = block_facts(here, partner_of(here, i))
        first = block * CAP + jnp.where(low, 0, REACH * CAP)

        @pl.when(in_reach)
        def _():
            placed_ref[pl.ds(pl.multiple_of(first, CAP), CAP), :] = flow

    for first in range(0, tie_ref.shape[0], LANES):
        count = min(LANES, tie_ref.shape[0] - first)
        tie_ref[first : first + count, :] = jnp.transpose(placed_ref[:, first : first + LANES])[0:count, :]
        send(tie_ref.at[pl.ds(first, count)], tie_out.at[pl.ds(first, count)])
    for copy in copies:
        copy.wait()


def call(kernel, name, args, outs, scratch, flops, in_place=(), outs_in_place=False):
    size = sum(x.size * x.dtype.itemsize for x in list(args) + list(outs))
    return pl.pallas_call(
        kernel,
        name=name,
        out_shape=outs,
        in_specs=[ANY if i in in_place else VMEM for i in range(len(args))],
        out_specs=[ANY if outs_in_place else VMEM] * len(outs),
        scratch_shapes=scratch,
        compiler_params=pltpu.CompilerParams(vmem_limit_bytes=32 * 1024 * 1024),
        cost_estimate=pl.CostEstimate(flops=flops, bytes_accessed=size, transcendentals=0),
    )(*(pltpu.with_memory_space_constraint(x, pltpu.HBM) if i in in_place else x for i, x in enumerate(args)))


def per_device(
    ptdf,
    angle_sens,
    demand,
    gen_start,
    hedge_dual,
    gen_cost,
    gen_max,
    gen_ramp,
    line_max,
    tie_count,
    tie_low_bus,
    tie_high_bus,
    tie_susc,
):
    hours, scens, buses = demand.shape
    lines = ptdf.shape[0]
    width = hours * scens
    areas = lax.axis_size("area")
    n_scen = lax.axis_size("scen")
    assert lax.axis_size("hour") == 2 and hours >= 2
    assert width % LANES == LANES // 2 and width < 2 * LANES
    columns = 2 * LANES
    block_rows = CAP * 3 // 2
    scen_total = scens * n_scen
    blocks, partner_of, from_partners = partner_plan(areas)
    slots = blocks * CAP
    pieces = buses // LANES
    sum_rows = 8 * pl.cdiv((hours + 1) * pieces, 8)
    f32, bf16 = jnp.float32, jnp.bfloat16

    def shape(*dims, dtype=f32):
        return jax.ShapeDtypeStruct(dims, dtype)

    def over_scens(sums):
        if n_scen == 2:
            return [sums, lax.ppermute(sums, "scen", [(0, 1), (1, 0)])]
        return [lax.psum(sums, "scen")]

    work = 4 * width * lines * buses

    def step_scratch(rows):
        return [
            pltpu.VMEM((rows, buses), bf16),
            pltpu.VMEM((rows, lines), bf16),
            pltpu.VMEM((rows, buses), f32),
        ]

    ramp_scratch = [
        pltpu.VMEM((hours + 4, buses), f32),
        pltpu.VMEM((hours + 4, buses), f32),
        pltpu.VMEM((hours, buses), f32),
    ]
    tables = (tie_count, tie_low_bus, tie_high_bus, tie_susc)
    vectors = [x.reshape(1, -1) for x in (gen_cost, gen_max, gen_ramp, line_max)]
    load = demand.reshape(width, buses)
    hedge = hedge_dual.reshape(width, buses)
    edge_hedge, start, onehot, spread, weight = call(
        functools.partial(table_kernel, blocks, partner_of),
        "tables",
        (hedge, gen_start, *tables),
        [
            shape(scens, buses),
            shape(hours, buses),
            shape(slots, buses, dtype=bf16),
            shape(slots, buses, dtype=bf16),
            shape(slots, LANES),
        ],
        [pltpu.VMEM(x.shape, x.dtype) for x in tables] + [pltpu.SemaphoreType.DMA((6,))],
        BETWEEN,
        range(6),
    )
    (rows,) = call(
        row_kernel,
        "rows",
        (angle_sens, onehot),
        [shape(slots, buses, dtype=bf16)],
        [],
        2 * slots * buses * buses,
    )
    *sent, own, inject = call(
        functools.partial(angle_kernel, blocks),
        "angles",
        (load, start, rows),
        [shape(block_rows, LANES)] * blocks
        + [shape(slots, columns), shape(columns, buses, dtype=bf16)],
        [],
        2 * slots * buses * width,
    )
    edge_hedge, own = lax.optimization_barrier((edge_hedge, own))
    (edge,) = call(edge_kernel, "edge", (load, edge_hedge, start), [shape(2 * scens + 8, buses)], [], BETWEEN)
    edge = lax.ppermute(edge, "hour", [(0, 1), (1, 0)])
    peer = from_partners(sent)
    gen, base, hedged, sums = call(
        first_kernel,
        "first",
        (ptdf, inject, load, hedge, start, edge, *vectors),
        [
            shape(width, buses),
            shape(width, buses),
            shape(width, buses),
            shape(sum_rows, LANES),
        ],
        step_scratch(width + scens) + ramp_scratch,
        work,
    )
    sum_terms = over_scens(sums)
    terms = len(sum_terms)
    relayed = areas == 4
    tied = call(
        functools.partial(tie_kernel, blocks, relayed),
        "ties",
        (base, spread, rows, weight, own, *peer),
        (
            [shape(2 * block_rows, LANES), shape(CAP, columns)]
            if relayed
            else [shape(block_rows, LANES)] * blocks
        )
        + [shape(columns, buses, dtype=bf16), shape(slots, columns), shape(slots, columns)],
        [],
        BETWEEN,
    )
    *sent, inject, mine, theirs = tied
    hedged, sums = call(
        functools.partial(second_kernel, terms, scen_total),
        "second",
        (ptdf, inject, gen, hedged, *vectors, *sum_terms),
        [shape(width, buses), shape(sum_rows, LANES)],
        step_scratch(width)[1:] + [pltpu.VMEM((8 * pl.cdiv(hours + 1, 8), buses), f32)] + ramp_scratch,
        work,
    )
    sum_terms = over_scens(sums)
    if relayed:
        far, near = sent
        far = lax.ppermute(far, "area", [(a, a ^ 2) for a in range(areas)])
        arrived, _ = lax.optimization_barrier((far, sums))
        (both,) = call(relay_kernel, "relay", (near, arrived), [shape(2 * block_rows, LANES)], [], BETWEEN)
        peer = [far, lax.ppermute(both, "area", [(a, a ^ 1) for a in range(areas)])]
    else:
        peer = from_partners(sent)
    gen_mean, hedge = call(
        functools.partial(agree_kernel, scen_total),
        "agree",
        (hedged, *sum_terms),
        [shape(hours, buses), shape(width, buses)],
        [],
        BETWEEN,
    )
    tie_shape = shape(width, 2 * REACH * CAP)
    hedge, gen_mean, tie_flow = call(
        functools.partial(last_kernel, blocks, relayed, partner_of),
        "last",
        (hedge, gen_mean, *peer, weight, mine, theirs),
        [shape(width, buses), shape(hours, buses), tie_shape],
        [
            pltpu.VMEM(tie_shape.shape, f32),
            pltpu.VMEM((2 * REACH * CAP, columns), f32),
            pltpu.SemaphoreType.DMA((2 + columns // LANES,)),
        ],
        slots * columns,
        outs_in_place=True,
    )
    return (
        gen_mean,
        hedge.reshape(hours, scens, buses),
        tie_flow.reshape(hours, scens, 2 * REACH * CAP),
    )


def solution(mesh):
    return jax.shard_map(
        per_device,
        mesh=mesh,
        in_specs=(
            P(("group", "area"), None),
            P(("group", "area"), None),
            P(("group", "hour"), "scen", "area"),
            P(("group", "hour"), "area"),
            P(("group", "hour"), "scen", "area"),
            P(("group", "area")),
            P(("group", "area")),
            P(("group", "area")),
            P(("group", "area")),
            P("group", None),
            P("group", None),
            P("group", None),
            P("group", None),
        ),
        out_specs=(
            P(("group", "hour"), "area"),
            P(("group", "hour"), "scen", "area"),
            P(("group", "hour"), "scen", "area"),
        ),
        check_vma=False,
    )
```

```python
import functools

import jax
import jax.numpy as jnp
from jax import lax
from jax.experimental import pallas as pl
from jax.experimental.pallas import tpu as pltpu
from jax.sharding import PartitionSpec as P

HOURS = 24
REACH = 4
CAP = 16

STEP_SIZE = 0.5
LINE_CHUNK = 1024
LANES = 128
BETWEEN = 20_000_000_000

CONTRACT_LAST = (((1,), (1,)), ((), ()))
CONTRACT_FIRST = (((0,), (0,)), ((), ()))
VMEM = pl.BlockSpec(memory_space=pltpu.VMEM)
ANY = pl.BlockSpec(memory_space=pltpu.HBM)


TARGETS = ((3, 2, 0, 1), (2, 3, 1, 0), (1, 0, 3, 2))


def partner_plan(areas):
    if areas == 4:

        def partner_of(here, i):
            return sum(jnp.where(here == a, target, 0) for a, target in enumerate(TARGETS[i]))

        def by_target(parts):
            out, back, pair = (
                lax.ppermute(part, "area", list(enumerate(target))) for part, target in zip(parts, TARGETS)
            )
            return [back, out, pair]

        return len(TARGETS), partner_of, by_target
    reach = min(REACH, areas - 1)
    shifts = sorted({s % areas for d in range(1, reach + 1) for s in (d, -d)})

    def by_shift(parts):
        sent = [
            lax.ppermute(part, "area", [(a, (a + s) % areas) for a in range(areas)])
            for part, s in zip(parts, shifts)
        ]
        return [sent[shifts.index(areas - s)] for s in shifts]

    return len(shifts), lambda here, i: lax.rem(here + shifts[i], areas), by_shift


def by_flips(here, flip_3, flip_2):
    return jnp.where(here < 2, flip_3, flip_2), jnp.where(here < 2, flip_2, flip_3)


def block_facts(here, partner):
    low = partner > here
    distance = jnp.abs(partner - here)
    block = jnp.clip(distance - 1, 0, REACH - 1)
    in_reach = (distance >= 1) & (distance <= REACH)
    return low, jnp.minimum(here, partner), block, in_reach


def fold(x):
    half = x.shape[0] // 2
    low = lax.broadcasted_iota(jnp.int32, (half, LANES), 1) < LANES // 2
    shared = jnp.where(low, x[0:half, LANES : 2 * LANES], x[half:, LANES : 2 * LANES])
    return jnp.concatenate([x[:, 0:LANES], shared], axis=0)


def unfold(packed):
    rows = 2 * packed.shape[0] // 3
    shared = packed[rows:, :]
    low = lax.broadcasted_iota(jnp.int32, shared.shape, 1) < LANES // 2
    turned = pltpu.roll(shared, LANES // 2, 1)
    rest = jnp.concatenate([jnp.where(low, shared, turned), jnp.where(low, turned, shared)], axis=0)
    return jnp.concatenate([packed[0:rows, :], rest], axis=1)


def repeat_rest(inject_ref, width):
    inject_ref[width:, :] = inject_ref[width - LANES // 2 : width, :]


def split_3(x):
    high = x.astype(jnp.bfloat16)
    rest = x - high.astype(jnp.float32)
    middle = rest.astype(jnp.bfloat16)
    rest = rest - middle.astype(jnp.float32)
    return jnp.concatenate([high, middle, rest.astype(jnp.bfloat16)], axis=0)


def put_row(packed_ref, hours, h, row):
    for j in range(row.shape[1] // LANES):
        packed_ref[j * hours + h : j * hours + h + 1, :] = row[:, j * LANES : (j + 1) * LANES]


def clear_rest(packed_ref, used):
    rows = packed_ref.shape[0]
    if used < rows:
        packed_ref[used:, :] = jnp.zeros((rows - used, LANES), jnp.float32)


def agree(mean_ref, sum_refs, hours, scen_total):
    for j in range(mean_ref.shape[1] // LANES):
        parts = [ref[j * hours : (j + 1) * hours, :] for ref in sum_refs]
        mean_ref[0:hours, j * LANES : (j + 1) * LANES] = functools.reduce(jnp.add, parts) / scen_total


def excess(diffs, limit):
    return diffs - jnp.clip(diffs, -limit, limit)


def write_ramp(mean_ref, beyond, limit, first_hour, padded_ref, excess_ref, ramp_ref):
    hours = ramp_ref.shape[0]
    padded_ref[0:1, :] = beyond
    padded_ref[1 : hours + 1, :] = mean_ref[0:hours, :]
    padded_ref[hours + 1 : hours + 2, :] = beyond
    diffs = padded_ref[1 : hours + 2, :] - padded_ref[0 : hours + 1, :]
    ids = first_hour + lax.broadcasted_iota(jnp.int32, diffs.shape, 0)
    valid = (ids >= 1) & (ids <= HOURS - 1)
    excess_ref[0 : hours + 1, :] = jnp.where(valid, excess(diffs, limit), 0.0)
    ramp_ref[...] = excess_ref[0:hours, :] - excess_ref[1 : hours + 1, :]


def line_work(inject_ref, ptdf_ref, line_max_ref, over_ref):
    inject = inject_ref[...]
    lines = ptdf_ref.shape[0]
    for at in range(0, lines, LINE_CHUNK):
        part = slice(at, at + LINE_CHUNK)
        flows = lax.dot_general(
            inject, ptdf_ref[part, :], CONTRACT_LAST, preferred_element_type=jnp.float32
        )
        limit = line_max_ref[:, part]
        over_ref[:, part] = (flows - jnp.clip(flows, -limit, limit)).astype(jnp.bfloat16)
    return jnp.dot(over_ref[...], ptdf_ref[...], preferred_element_type=jnp.float32)


def table_kernel(
    blocks,
    partner_of,
    sens_in,
    hedge_in,
    start_in,
    count_in,
    low_bus_in,
    high_bus_in,
    susc_in,
    edge_hedge_ref,
    start_ref,
    onehot_ref,
    spread_ref,
    weight_ref,
    sens_ref,
    count_ref,
    low_bus_ref,
    high_bus_ref,
    susc_ref,
    copy_sems,
):
    hours, buses = start_ref.shape
    scens = hedge_in.shape[0] // hours
    here = lax.axis_index("area")
    last = (hours - 1) * scens
    edge_rows = pl.ds(pl.multiple_of((1 - lax.axis_index("hour")) * last, scens), scens)

    half = buses // 2
    halves = (pl.ds(0, half), pl.ds(half, half))
    pairs = (
        (count_in, count_ref),
        (low_bus_in, low_bus_ref),
        (high_bus_in, high_bus_ref),
        (susc_in, susc_ref),
        (start_in, start_ref),
        (hedge_in.at[edge_rows], edge_hedge_ref),
        *((sens_in.at[rows], sens_ref.at[rows]) for rows in halves),
    )
    copies = [pltpu.make_async_copy(src, dst, copy_sems.at[i]) for i, (src, dst) in enumerate(pairs)]
    for copy in (*copies[6:], *copies[:6]):
        copy.start()
    for copy in copies[:4]:
        copy.wait()
    for i in range(blocks):
        partner = partner_of(here, i)
        low, row, block, in_reach = block_facts(here, partner)
        slots = slice(i * CAP, (i + 1) * CAP)
        pick = lax.broadcasted_iota(jnp.int32, (CAP, REACH * CAP), 1) == (
            block * CAP + lax.broadcasted_iota(jnp.int32, (CAP, REACH * CAP), 0)
        )
        table_row = pl.ds(row, 1)
        bus_row = jnp.where(low, low_bus_ref[table_row, :], high_bus_ref[table_row, :])
        bus = jnp.sum(jnp.where(pick, bus_row.astype(jnp.float32), 0.0), axis=1, keepdims=True)
        susc = jnp.sum(jnp.where(pick, susc_ref[table_row, :], 0.0), axis=1, keepdims=True)
        count_row = count_ref[table_row, :].astype(jnp.float32)
        is_block = lax.broadcasted_iota(jnp.int32, (CAP, REACH), 1) == block
        count = jnp.sum(jnp.where(is_block, count_row, 0.0), axis=1, keepdims=True)
        slot_ids = lax.broadcasted_iota(jnp.int32, (CAP, 1), 0).astype(jnp.float32)
        live = jnp.where((slot_ids < count) & in_reach, 1.0, 0.0)
        sign = jnp.where(low, 1.0, -1.0)
        bus_ids = lax.broadcasted_iota(jnp.int32, (CAP, buses), 1).astype(jnp.float32)
        onehot = jnp.where(bus_ids == bus, live, 0.0)
        onehot_ref[slots, :] = onehot.astype(jnp.bfloat16)
        spread_ref[slots, :] = (-sign * onehot).astype(jnp.bfloat16)
        weight_ref[slots, :] = jnp.broadcast_to(live * sign * susc, (CAP, 128))

    for copy in copies[4:]:
        copy.wait()


def row_kernel(sens_ref, onehot_ref, rows_ref):
    rows = jnp.dot(onehot_ref[...], sens_ref[...], preferred_element_type=jnp.float32)
    rows_ref[...] = rows.astype(jnp.bfloat16)


def angle_kernel(blocks, demand_ref, start_ref, rows_ref, *refs):
    sent_refs, (own_ref, inject_ref) = refs[:blocks], refs[blocks:]
    hours = start_ref.shape[0]
    scens = demand_ref.shape[0] // hours
    for h in range(hours):
        part = slice(h * scens, (h + 1) * scens)
        inject_ref[part, :] = (start_ref[h : h + 1, :] - demand_ref[part, :]).astype(jnp.bfloat16)
    repeat_rest(inject_ref, hours * scens)
    own = lax.dot_general(
        rows_ref[...], inject_ref[...], CONTRACT_LAST, preferred_element_type=jnp.float32
    )
    own_ref[...] = own
    for i in range(blocks):
        sent_refs[i][...] = fold(own[i * CAP : (i + 1) * CAP, :])


def edge_kernel(demand_ref, edge_hedge_ref, start_ref, edge_ref):
    scens = edge_hedge_ref.shape[0]
    hours = start_ref.shape[0]
    early = lax.axis_index("hour") == 0
    last = (hours - 1) * scens
    at = 2 * scens
    edge_ref[0:scens, :] = jnp.where(early, demand_ref[last:, :], demand_ref[0:scens, :])
    edge_ref[scens:at, :] = edge_hedge_ref[...]
    edge_ref[at : at + 1, :] = jnp.where(early, start_ref[hours - 1 : hours, :], start_ref[0:1, :])
    edge_ref[at + 1 : at + 2, :] = jnp.where(
        early, start_ref[hours - 2 : hours - 1, :], start_ref[1:2, :]
    )


def first_kernel(
    ptdf_ref,
    own_inject_ref,
    demand_ref,
    hedge_ref,
    start_ref,
    edge_ref,
    cost_ref,
    max_ref,
    limit_ref,
    line_max_ref,
    gen_ref,
    base_ref,
    hedged_ref,
    sums_ref,
    inject_ref,
    over_ref,
    back_ref,
    padded_ref,
    excess_ref,
    ramp_ref,
):
    hours, buses = start_ref.shape
    width = demand_ref.shape[0]
    scens = width // hours
    at = 2 * scens
    early = lax.axis_index("hour") == 0
    first_hour = lax.axis_index("hour") * hours
    beyond = edge_ref[at : at + 1, :]
    limit = limit_ref[...]
    cost = cost_ref[...]
    top = max_ref[...]

    inject_ref[0:width, :] = own_inject_ref[0:width, :]
    inject_ref[width : width + scens, :] = (beyond - edge_ref[0:scens, :]).astype(jnp.bfloat16)
    back_ref[...] = line_work(inject_ref, ptdf_ref, line_max_ref, over_ref)
    write_ramp(start_ref, beyond, limit, first_hour, padded_ref, excess_ref, ramp_ref)

    def step(mean, hedge, back, ramp):
        grad = cost + back + (mean - mean + hedge) + ramp
        gen = jnp.clip(mean - STEP_SIZE * grad, 0.0, top)
        return gen, gen + hedge

    for h in range(hours):
        part = slice(h * scens, (h + 1) * scens)
        mean = start_ref[h : h + 1, :]
        gen, hedged = step(mean, hedge_ref[part, :], back_ref[part, :], ramp_ref[h : h + 1, :])
        gen_ref[part, :] = gen
        base_ref[part, :] = gen - demand_ref[part, :]
        hedged_ref[part, :] = hedged
        put_row(sums_ref, hours + 1, h, jnp.sum(hedged, axis=0, keepdims=True))
    near = jnp.where(early, start_ref[hours - 1 : hours, :], start_ref[0:1, :])
    ramp = excess(beyond - near, limit) + excess(beyond - edge_ref[at + 1 : at + 2, :], limit)
    _, hedged = step(beyond, edge_ref[scens:at, :], back_ref[width : width + scens, :], ramp)
    put_row(sums_ref, hours + 1, hours, jnp.sum(hedged, axis=0, keepdims=True))
    clear_rest(sums_ref, (hours + 1) * (buses // LANES))


def tie_kernel(blocks, relayed, base_ref, spread_ref, rows_ref, weight_ref, own_ref, *refs):
    peer_refs, refs = refs[:blocks], refs[blocks:]
    *next_refs, inject_ref, mine_ref, theirs_ref = refs
    width = base_ref.shape[0]

    weight = jnp.concatenate([weight_ref[...], weight_ref[...]], axis=1)
    own = own_ref[...]
    peer = jnp.concatenate([unfold(ref[...]) for ref in peer_refs], axis=0)
    est_mine = weight * own
    est_theirs = -weight * peer
    flow = (est_mine + est_theirs) * 0.5
    dual_mine = est_mine - flow
    dual_theirs = est_theirs - flow
    spread = spread_ref[...]
    add = lax.dot_general(
        split_3(flow[:, 0:width]),
        jnp.concatenate([spread, spread, spread], axis=0),
        CONTRACT_FIRST,
        preferred_element_type=jnp.float32,
    )
    inject_ref[0:width, :] = (base_ref[...] + add).astype(jnp.bfloat16)
    repeat_rest(inject_ref, width)

    own_next = lax.dot_general(
        rows_ref[...], inject_ref[...], CONTRACT_LAST, preferred_element_type=jnp.float32
    )
    parts = [own_next[i * CAP : (i + 1) * CAP, :] for i in range(blocks)]
    if relayed:
        far_ref, near_ref = next_refs
        flip_3, flip_2 = by_flips(lax.axis_index("area"), parts[0], parts[1])
        far_ref[...] = fold(jnp.concatenate([flip_2, flip_3], axis=0))
        near_ref[...] = parts[2]
    else:
        for ref, part in zip(next_refs, parts):
            ref[...] = fold(part)
    mine_ref[...] = weight * (own_next - peer) + dual_mine
    theirs_ref[...] = weight * own + dual_theirs


def second_kernel(
    terms,
    scen_total,
    ptdf_ref,
    inject_ref,
    gen_ref,
    hedged_ref,
    cost_ref,
    max_ref,
    limit_ref,
    line_max_ref,
    *refs,
):
    sum_refs, refs = refs[:terms], refs[terms:]
    (hedged_out_ref, sums_out_ref, over_ref, back_ref, mean_ref, padded_ref, excess_ref, ramp_ref) = refs
    hours, buses = ramp_ref.shape
    width = back_ref.shape[0]
    scens = width // hours
    first_hour = lax.axis_index("hour") * hours

    back_ref[...] = line_work(inject_ref.at[0:width, :], ptdf_ref, line_max_ref, over_ref)
    agree(mean_ref, sum_refs, hours + 1, scen_total)
    write_ramp(
        mean_ref, mean_ref[hours : hours + 1, :], limit_ref[...], first_hour, padded_ref, excess_ref, ramp_ref
    )
    cost = cost_ref[...]
    top = max_ref[...]
    for h in range(hours):
        part = slice(h * scens, (h + 1) * scens)
        mean = mean_ref[h : h + 1, :]
        gen = gen_ref[part, :]
        hedge = hedged_ref[part, :] - mean
        grad = cost + back_ref[part, :] + (gen - mean + hedge) + ramp_ref[h : h + 1, :]
        gen = jnp.clip(gen - STEP_SIZE * grad, 0.0, top)
        hedged = gen + hedge
        hedged_out_ref[part, :] = hedged
        put_row(sums_out_ref, hours, h, jnp.sum(hedged, axis=0, keepdims=True))
    clear_rest(sums_out_ref, hours * (buses // LANES))


def relay_kernel(near_ref, far_ref, both_ref):
    low = lax.broadcasted_iota(jnp.int32, (CAP, LANES), 1) < LANES // 2
    both_ref[0:CAP, :] = near_ref[:, 0:LANES]
    both_ref[CAP : 2 * CAP, :] = far_ref[CAP : 2 * CAP, :]
    both_ref[2 * CAP :, :] = jnp.where(low, near_ref[:, LANES:], far_ref[2 * CAP :, :])


def agree_kernel(scen_total, hedged_ref, *refs):
    sum_refs, (mean_ref, hedge_ref) = refs[:-2], refs[-2:]
    hours = mean_ref.shape[0]
    scens = hedged_ref.shape[0] // hours
    agree(mean_ref, sum_refs, hours, scen_total)
    for h in range(hours):
        part = slice(h * scens, (h + 1) * scens)
        hedge_ref[part, :] = hedged_ref[part, :] - mean_ref[h : h + 1, :]


def last_kernel(blocks, relayed, partner_of, hedge_ref, mean_ref, *refs):
    *peer_refs, weight_ref, mine_ref, theirs_ref = refs[:-6]
    hedge_out, mean_out, tie_out, tie_ref, placed_ref, copy_sems = refs[-6:]
    copies = []

    def send(src, dst):
        copies.append(pltpu.make_async_copy(src, dst, copy_sems.at[len(copies)]))
        copies[-1].start()

    send(hedge_ref, hedge_out)
    send(mean_ref, mean_out)
    here = lax.axis_index("area")
    placed_ref[...] = jnp.zeros_like(placed_ref)
    if relayed:
        far, both = (unfold(ref[...]) for ref in peer_refs)
        peers = [*by_flips(here, both[CAP:, :], far[0:CAP, :]), both[0:CAP, :]]
    else:
        peers = [unfold(ref[...]) for ref in peer_refs]
    for i in range(blocks):
        slots = slice(i * CAP, (i + 1) * CAP)
        weight = jnp.concatenate([weight_ref[slots, :], weight_ref[slots, :]], axis=1)
        flow = (mine_ref[slots, :] + (theirs_ref[slots, :] - weight * peers[i])) * 0.5
        low, _, block, in_reach = block_facts(here, partner_of(here, i))
        first = block * CAP + jnp.where(low, 0, REACH * CAP)

        @pl.when(in_reach)
        def _():
            placed_ref[pl.ds(pl.multiple_of(first, CAP), CAP), :] = flow

    for first in range(0, tie_ref.shape[0], LANES):
        count = min(LANES, tie_ref.shape[0] - first)
        tie_ref[first : first + count, :] = jnp.transpose(placed_ref[:, first : first + LANES])[0:count, :]
        send(tie_ref.at[pl.ds(first, count)], tie_out.at[pl.ds(first, count)])
    for copy in copies:
        copy.wait()


def call(kernel, name, args, outs, scratch, flops, in_place=(), outs_in_place=False):
    size = sum(x.size * x.dtype.itemsize for x in list(args) + list(outs))
    return pl.pallas_call(
        kernel,
        name=name,
        out_shape=outs,
        in_specs=[ANY if i in in_place else VMEM for i in range(len(args))],
        out_specs=[ANY if outs_in_place else VMEM] * len(outs),
        scratch_shapes=scratch,
        compiler_params=pltpu.CompilerParams(vmem_limit_bytes=32 * 1024 * 1024),
        cost_estimate=pl.CostEstimate(flops=flops, bytes_accessed=size, transcendentals=0),
    )(*(pltpu.with_memory_space_constraint(x, pltpu.HBM) if i in in_place else x for i, x in enumerate(args)))


def per_device(
    ptdf,
    angle_sens,
    demand,
    gen_start,
    hedge_dual,
    gen_cost,
    gen_max,
    gen_ramp,
    line_max,
    tie_count,
    tie_low_bus,
    tie_high_bus,
    tie_susc,
):
    hours, scens, buses = demand.shape
    lines = ptdf.shape[0]
    width = hours * scens
    areas = lax.axis_size("area")
    n_scen = lax.axis_size("scen")
    assert lax.axis_size("hour") == 2 and hours >= 2
    assert width % LANES == LANES // 2 and width < 2 * LANES
    columns = 2 * LANES
    block_rows = CAP * 3 // 2
    scen_total = scens * n_scen
    blocks, partner_of, from_partners = partner_plan(areas)
    slots = blocks * CAP
    pieces = buses // LANES
    sum_rows = 8 * pl.cdiv((hours + 1) * pieces, 8)
    f32, bf16 = jnp.float32, jnp.bfloat16

    def shape(*dims, dtype=f32):
        return jax.ShapeDtypeStruct(dims, dtype)

    def over_scens(sums):
        if n_scen == 2:
            return [sums, lax.ppermute(sums, "scen", [(0, 1), (1, 0)])]
        return [lax.psum(sums, "scen")]

    work = 4 * width * lines * buses

    def step_scratch(rows):
        return [
            pltpu.VMEM((rows, buses), bf16),
            pltpu.VMEM((rows, lines), bf16),
            pltpu.VMEM((rows, buses), f32),
        ]

    ramp_scratch = [
        pltpu.VMEM((hours + 4, buses), f32),
        pltpu.VMEM((hours + 4, buses), f32),
        pltpu.VMEM((hours, buses), f32),
    ]
    tables = (tie_count, tie_low_bus, tie_high_bus, tie_susc)
    vectors = [x.reshape(1, -1) for x in (gen_cost, gen_max, gen_ramp, line_max)]
    load = demand.reshape(width, buses)
    hedge = hedge_dual.reshape(width, buses)
    edge_hedge, start, onehot, spread, weight, sens = call(
        functools.partial(table_kernel, blocks, partner_of),
        "tables",
        (angle_sens, hedge, gen_start, *tables),
        [
            shape(scens, buses),
            shape(hours, buses),
            shape(slots, buses, dtype=bf16),
            shape(slots, buses, dtype=bf16),
            shape(slots, LANES),
            shape(buses, buses, dtype=bf16),
        ],
        [pltpu.VMEM(x.shape, x.dtype) for x in tables] + [pltpu.SemaphoreType.DMA((8,))],
        BETWEEN,
        range(7),
    )
    (rows,) = call(
        row_kernel,
        "rows",
        (sens, onehot),
        [shape(slots, buses, dtype=bf16)],
        [],
        2 * slots * buses * buses,
    )
    *sent, own, inject = call(
        functools.partial(angle_kernel, blocks),
        "angles",
        (load, start, rows),
        [shape(block_rows, LANES)] * blocks
        + [shape(slots, columns), shape(columns, buses, dtype=bf16)],
        [],
        2 * slots * buses * width,
    )
    edge_hedge, own = lax.optimization_barrier((edge_hedge, own))
    (edge,) = call(edge_kernel, "edge", (load, edge_hedge, start), [shape(2 * scens + 8, buses)], [], BETWEEN)
    edge = lax.ppermute(edge, "hour", [(0, 1), (1, 0)])
    peer = from_partners(sent)
    gen, base, hedged, sums = call(
        first_kernel,
        "first",
        (ptdf, inject, load, hedge, start, edge, *vectors),
        [
            shape(width, buses),
            shape(width, buses),
            shape(width, buses),
            shape(sum_rows, LANES),
        ],
        step_scratch(width + scens) + ramp_scratch,
        work,
    )
    sum_terms = over_scens(sums)
    terms = len(sum_terms)
    relayed = areas == 4
    tied = call(
        functools.partial(tie_kernel, blocks, relayed),
        "ties",
        (base, spread, rows, weight, own, *peer),
        (
            [shape(2 * block_rows, LANES), shape(CAP, columns)]
            if relayed
            else [shape(block_rows, LANES)] * blocks
        )
        + [shape(columns, buses, dtype=bf16), shape(slots, columns), shape(slots, columns)],
        [],
        BETWEEN,
    )
    *sent, inject, mine, theirs = tied
    hedged, sums = call(
        functools.partial(second_kernel, terms, scen_total),
        "second",
        (ptdf, inject, gen, hedged, *vectors, *sum_terms),
        [shape(width, buses), shape(sum_rows, LANES)],
        step_scratch(width)[1:] + [pltpu.VMEM((8 * pl.cdiv(hours + 1, 8), buses), f32)] + ramp_scratch,
        work,
    )
    sum_terms = over_scens(sums)
    if relayed:
        far, near = sent
        far = lax.ppermute(far, "area", [(a, a ^ 2) for a in range(areas)])
        arrived, _ = lax.optimization_barrier((far, sums))
        (both,) = call(relay_kernel, "relay", (near, arrived), [shape(2 * block_rows, LANES)], [], BETWEEN)
        peer = [far, lax.ppermute(both, "area", [(a, a ^ 1) for a in range(areas)])]
    else:
        peer = from_partners(sent)
    gen_mean, hedge = call(
        functools.partial(agree_kernel, scen_total),
        "agree",
        (hedged, *sum_terms),
        [shape(hours, buses), shape(width, buses)],
        [],
        BETWEEN,
    )
    tie_shape = shape(width, 2 * REACH * CAP)
    hedge, gen_mean, tie_flow = call(
        functools.partial(last_kernel, blocks, relayed, partner_of),
        "last",
        (hedge, gen_mean, *peer, weight, mine, theirs),
        [shape(width, buses), shape(hours, buses), tie_shape],
        [
            pltpu.VMEM(tie_shape.shape, f32),
            pltpu.VMEM((2 * REACH * CAP, columns), f32),
            pltpu.SemaphoreType.DMA((2 + columns // LANES,)),
        ],
        slots * columns,
        outs_in_place=True,
    )
    return (
        gen_mean,
        hedge.reshape(hours, scens, buses),
        tie_flow.reshape(hours, scens, 2 * REACH * CAP),
    )


def solution(mesh):
    return jax.shard_map(
        per_device,
        mesh=mesh,
        in_specs=(
            P(("group", "area"), None),
            P(("group", "area"), None),
            P(("group", "hour"), "scen", "area"),
            P(("group", "hour"), "area"),
            P(("group", "hour"), "scen", "area"),
            P(("group", "area")),
            P(("group", "area")),
            P(("group", "area")),
            P(("group", "area")),
            P("group", None),
            P("group", None),
            P("group", None),
            P("group", None),
        ),
        out_specs=(
            P(("group", "hour"), "area"),
            P(("group", "hour"), "scen", "area"),
            P(("group", "hour"), "scen", "area"),
        ),
        check_vma=False,
    )
```

```python
import functools

import jax
import jax.numpy as jnp
from jax import lax
from jax.experimental import pallas as pl
from jax.experimental.pallas import tpu as pltpu
from jax.sharding import PartitionSpec as P

HOURS = 24
REACH = 4
CAP = 16

STEP_SIZE = 0.5
LINE_CHUNK = 1024
LANES = 128
BETWEEN = 20_000_000_000

CONTRACT_LAST = (((1,), (1,)), ((), ()))
CONTRACT_FIRST = (((0,), (0,)), ((), ()))
VMEM = pl.BlockSpec(memory_space=pltpu.VMEM)
ANY = pl.BlockSpec(memory_space=pltpu.HBM)


TARGETS = ((3, 2, 0, 1), (2, 3, 1, 0), (1, 0, 3, 2))


def partner_plan(areas):
    if areas == 4:

        def partner_of(here, i):
            return sum(jnp.where(here == a, target, 0) for a, target in enumerate(TARGETS[i]))

        def by_target(parts):
            out, back, pair = (
                lax.ppermute(part, "area", list(enumerate(target))) for part, target in zip(parts, TARGETS)
            )
            return [back, out, pair]

        return len(TARGETS), partner_of, by_target
    reach = min(REACH, areas - 1)
    shifts = sorted({s % areas for d in range(1, reach + 1) for s in (d, -d)})

    def by_shift(parts):
        sent = [
            lax.ppermute(part, "area", [(a, (a + s) % areas) for a in range(areas)])
            for part, s in zip(parts, shifts)
        ]
        return [sent[shifts.index(areas - s)] for s in shifts]

    return len(shifts), lambda here, i: lax.rem(here + shifts[i], areas), by_shift


def by_flips(here, flip_3, flip_2):
    return jnp.where(here < 2, flip_3, flip_2), jnp.where(here < 2, flip_2, flip_3)


def block_facts(here, partner):
    low = partner > here
    distance = jnp.abs(partner - here)
    block = jnp.clip(distance - 1, 0, REACH - 1)
    in_reach = (distance >= 1) & (distance <= REACH)
    return low, jnp.minimum(here, partner), block, in_reach


def fold(x):
    half = x.shape[0] // 2
    low = lax.broadcasted_iota(jnp.int32, (half, LANES), 1) < LANES // 2
    shared = jnp.where(low, x[0:half, LANES : 2 * LANES], x[half:, LANES : 2 * LANES])
    return jnp.concatenate([x[:, 0:LANES], shared], axis=0)


def unfold(packed):
    rows = 2 * packed.shape[0] // 3
    shared = packed[rows:, :]
    low = lax.broadcasted_iota(jnp.int32, shared.shape, 1) < LANES // 2
    turned = pltpu.roll(shared, LANES // 2, 1)
    rest = jnp.concatenate([jnp.where(low, shared, turned), jnp.where(low, turned, shared)], axis=0)
    return jnp.concatenate([packed[0:rows, :], rest], axis=1)


def repeat_rest(inject_ref, width):
    inject_ref[width:, :] = inject_ref[width - LANES // 2 : width, :]


def split_3(x):
    high = x.astype(jnp.bfloat16)
    rest = x - high.astype(jnp.float32)
    middle = rest.astype(jnp.bfloat16)
    rest = rest - middle.astype(jnp.float32)
    return jnp.concatenate([high, middle, rest.astype(jnp.bfloat16)], axis=0)


def put_row(packed_ref, hours, h, row):
    for j in range(row.shape[1] // LANES):
        packed_ref[j * hours + h : j * hours + h + 1, :] = row[:, j * LANES : (j + 1) * LANES]


def clear_rest(packed_ref, used):
    rows = packed_ref.shape[0]
    if used < rows:
        packed_ref[used:, :] = jnp.zeros((rows - used, LANES), jnp.float32)


def agree(mean_ref, sum_refs, hours, scen_total):
    for j in range(mean_ref.shape[1] // LANES):
        parts = [ref[j * hours : (j + 1) * hours, :] for ref in sum_refs]
        mean_ref[0:hours, j * LANES : (j + 1) * LANES] = functools.reduce(jnp.add, parts) / scen_total


def excess(diffs, limit):
    return diffs - jnp.clip(diffs, -limit, limit)


def write_ramp(mean_ref, beyond, limit, first_hour, padded_ref, excess_ref, ramp_ref):
    hours = ramp_ref.shape[0]
    padded_ref[0:1, :] = beyond
    padded_ref[1 : hours + 1, :] = mean_ref[0:hours, :]
    padded_ref[hours + 1 : hours + 2, :] = beyond
    diffs = padded_ref[1 : hours + 2, :] - padded_ref[0 : hours + 1, :]
    ids = first_hour + lax.broadcasted_iota(jnp.int32, diffs.shape, 0)
    valid = (ids >= 1) & (ids <= HOURS - 1)
    excess_ref[0 : hours + 1, :] = jnp.where(valid, excess(diffs, limit), 0.0)
    ramp_ref[...] = excess_ref[0:hours, :] - excess_ref[1 : hours + 1, :]


def line_work(inject_ref, ptdf_ref, line_max_ref, over_ref):
    inject = inject_ref[...]
    lines = ptdf_ref.shape[0]
    for at in range(0, lines, LINE_CHUNK):
        part = slice(at, at + LINE_CHUNK)
        flows = lax.dot_general(
            inject, ptdf_ref[part, :], CONTRACT_LAST, preferred_element_type=jnp.float32
        )
        limit = line_max_ref[:, part]
        over_ref[:, part] = (flows - jnp.clip(flows, -limit, limit)).astype(jnp.bfloat16)
    return jnp.dot(over_ref[...], ptdf_ref[...], preferred_element_type=jnp.float32)


def table_kernel(
    blocks,
    partner_of,
    hedge_in,
    start_in,
    count_in,
    low_bus_in,
    high_bus_in,
    susc_in,
    cost_in,
    max_in,
    limit_in,
    line_max_in,
    edge_hedge_ref,
    start_ref,
    cost_ref,
    max_ref,
    limit_ref,
    line_max_ref,
    onehot_ref,
    spread_ref,
    weight_ref,
    count_ref,
    low_bus_ref,
    high_bus_ref,
    susc_ref,
    copy_sems,
):
    hours, buses = start_ref.shape
    scens = hedge_in.shape[0] // hours
    here = lax.axis_index("area")
    last = (hours - 1) * scens
    edge_rows = pl.ds(pl.multiple_of((1 - lax.axis_index("hour")) * last, scens), scens)

    pairs = (
        (count_in, count_ref),
        (low_bus_in, low_bus_ref),
        (high_bus_in, high_bus_ref),
        (susc_in, susc_ref),
        (start_in, start_ref),
        (hedge_in.at[edge_rows], edge_hedge_ref),
        (cost_in, cost_ref),
        (max_in, max_ref),
        (limit_in, limit_ref),
        (line_max_in, line_max_ref),
    )
    copies = [pltpu.make_async_copy(src, dst, copy_sems.at[i]) for i, (src, dst) in enumerate(pairs)]
    for copy in copies:
        copy.start()
    for copy in copies[:4]:
        copy.wait()
    for i in range(blocks):
        partner = partner_of(here, i)
        low, row, block, in_reach = block_facts(here, partner)
        slots = slice(i * CAP, (i + 1) * CAP)
        pick = lax.broadcasted_iota(jnp.int32, (CAP, REACH * CAP), 1) == (
            block * CAP + lax.broadcasted_iota(jnp.int32, (CAP, REACH * CAP), 0)
        )
        table_row = pl.ds(row, 1)
        bus_row = jnp.where(low, low_bus_ref[table_row, :], high_bus_ref[table_row, :])
        bus = jnp.sum(jnp.where(pick, bus_row.astype(jnp.float32), 0.0), axis=1, keepdims=True)
        susc = jnp.sum(jnp.where(pick, susc_ref[table_row, :], 0.0), axis=1, keepdims=True)
        count_row = count_ref[table_row, :].astype(jnp.float32)
        is_block = lax.broadcasted_iota(jnp.int32, (CAP, REACH), 1) == block
        count = jnp.sum(jnp.where(is_block, count_row, 0.0), axis=1, keepdims=True)
        slot_ids = lax.broadcasted_iota(jnp.int32, (CAP, 1), 0).astype(jnp.float32)
        live = jnp.where((slot_ids < count) & in_reach, 1.0, 0.0)
        sign = jnp.where(low, 1.0, -1.0)
        bus_ids = lax.broadcasted_iota(jnp.int32, (CAP, buses), 1).astype(jnp.float32)
        onehot = jnp.where(bus_ids == bus, live, 0.0)
        onehot_ref[slots, :] = onehot.astype(jnp.bfloat16)
        spread_ref[slots, :] = (-sign * onehot).astype(jnp.bfloat16)
        weight_ref[slots, :] = jnp.broadcast_to(live * sign * susc, (CAP, 128))

    for copy in copies[4:]:
        copy.wait()


def row_kernel(sens_ref, onehot_ref, rows_ref):
    rows = jnp.dot(onehot_ref[...], sens_ref[...], preferred_element_type=jnp.float32)
    rows_ref[...] = rows.astype(jnp.bfloat16)


def angle_kernel(blocks, demand_ref, start_ref, rows_ref, *refs):
    sent_refs, (own_ref, inject_ref) = refs[:blocks], refs[blocks:]
    hours = start_ref.shape[0]
    scens = demand_ref.shape[0] // hours
    for h in range(hours):
        part = slice(h * scens, (h + 1) * scens)
        inject_ref[part, :] = (start_ref[h : h + 1, :] - demand_ref[part, :]).astype(jnp.bfloat16)
    repeat_rest(inject_ref, hours * scens)
    own = lax.dot_general(
        rows_ref[...], inject_ref[...], CONTRACT_LAST, preferred_element_type=jnp.float32
    )
    own_ref[...] = own
    for i in range(blocks):
        sent_refs[i][...] = fold(own[i * CAP : (i + 1) * CAP, :])


def edge_kernel(demand_ref, edge_hedge_ref, start_ref, edge_ref):
    scens = edge_hedge_ref.shape[0]
    hours = start_ref.shape[0]
    early = lax.axis_index("hour") == 0
    last = (hours - 1) * scens
    at = 2 * scens
    edge_ref[0:scens, :] = jnp.where(early, demand_ref[last:, :], demand_ref[0:scens, :])
    edge_ref[scens:at, :] = edge_hedge_ref[...]
    edge_ref[at : at + 1, :] = jnp.where(early, start_ref[hours - 1 : hours, :], start_ref[0:1, :])
    edge_ref[at + 1 : at + 2, :] = jnp.where(
        early, start_ref[hours - 2 : hours - 1, :], start_ref[1:2, :]
    )


def first_kernel(
    ptdf_ref,
    own_inject_ref,
    demand_ref,
    hedge_ref,
    start_ref,
    edge_ref,
    cost_ref,
    max_ref,
    limit_ref,
    line_max_ref,
    gen_ref,
    base_ref,
    hedged_ref,
    sums_ref,
    inject_ref,
    over_ref,
    back_ref,
    padded_ref,
    excess_ref,
    ramp_ref,
):
    hours, buses = start_ref.shape
    width = demand_ref.shape[0]
    scens = width // hours
    at = 2 * scens
    early = lax.axis_index("hour") == 0
    first_hour = lax.axis_index("hour") * hours
    beyond = edge_ref[at : at + 1, :]
    limit = limit_ref[...]
    cost = cost_ref[...]
    top = max_ref[...]

    inject_ref[0:width, :] = own_inject_ref[0:width, :]
    inject_ref[width : width + scens, :] = (beyond - edge_ref[0:scens, :]).astype(jnp.bfloat16)
    back_ref[...] = line_work(inject_ref, ptdf_ref, line_max_ref, over_ref)
    write_ramp(start_ref, beyond, limit, first_hour, padded_ref, excess_ref, ramp_ref)

    def step(mean, hedge, back, ramp):
        grad = cost + back + (mean - mean + hedge) + ramp
        gen = jnp.clip(mean - STEP_SIZE * grad, 0.0, top)
        return gen, gen + hedge

    for h in range(hours):
        part = slice(h * scens, (h + 1) * scens)
        mean = start_ref[h : h + 1, :]
        gen, hedged = step(mean, hedge_ref[part, :], back_ref[part, :], ramp_ref[h : h + 1, :])
        gen_ref[part, :] = gen
        base_ref[part, :] = gen - demand_ref[part, :]
        hedged_ref[part, :] = hedged
        put_row(sums_ref, hours + 1, h, jnp.sum(hedged, axis=0, keepdims=True))
    near = jnp.where(early, start_ref[hours - 1 : hours, :], start_ref[0:1, :])
    ramp = excess(beyond - near, limit) + excess(beyond - edge_ref[at + 1 : at + 2, :], limit)
    _, hedged = step(beyond, edge_ref[scens:at, :], back_ref[width : width + scens, :], ramp)
    put_row(sums_ref, hours + 1, hours, jnp.sum(hedged, axis=0, keepdims=True))
    clear_rest(sums_ref, (hours + 1) * (buses // LANES))


def tie_kernel(blocks, relayed, base_ref, spread_ref, rows_ref, weight_ref, own_ref, *refs):
    peer_refs, refs = refs[:blocks], refs[blocks:]
    *next_refs, inject_ref, mine_ref, theirs_ref = refs
    width = base_ref.shape[0]

    weight = jnp.concatenate([weight_ref[...], weight_ref[...]], axis=1)
    own = own_ref[...]
    peer = jnp.concatenate([unfold(ref[...]) for ref in peer_refs], axis=0)
    est_mine = weight * own
    est_theirs = -weight * peer
    flow = (est_mine + est_theirs) * 0.5
    dual_mine = est_mine - flow
    dual_theirs = est_theirs - flow
    spread = spread_ref[...]
    add = lax.dot_general(
        split_3(flow),
        jnp.concatenate([spread, spread, spread], axis=0),
        CONTRACT_FIRST,
        preferred_element_type=jnp.float32,
    )
    inject_ref[0:width, :] = (base_ref[...] + add[0:width, :]).astype(jnp.bfloat16)
    repeat_rest(inject_ref, width)

    own_next = lax.dot_general(
        rows_ref[...], inject_ref[...], CONTRACT_LAST, preferred_element_type=jnp.float32
    )
    parts = [own_next[i * CAP : (i + 1) * CAP, :] for i in range(blocks)]
    if relayed:
        far_ref, near_ref = next_refs
        flip_3, flip_2 = by_flips(lax.axis_index("area"), parts[0], parts[1])
        far_ref[...] = fold(jnp.concatenate([flip_2, flip_3], axis=0))
        near_ref[...] = parts[2]
    else:
        for ref, part in zip(next_refs, parts):
            ref[...] = fold(part)
    mine_ref[...] = weight * (own_next - peer) + dual_mine
    theirs_ref[...] = weight * own + dual_theirs


def second_kernel(
    terms,
    scen_total,
    ptdf_ref,
    inject_ref,
    gen_ref,
    hedged_ref,
    cost_ref,
    max_ref,
    limit_ref,
    line_max_ref,
    *refs,
):
    sum_refs, refs = refs[:terms], refs[terms:]
    (hedged_out_ref, sums_out_ref, over_ref, back_ref, mean_ref, padded_ref, excess_ref, ramp_ref) = refs
    hours, buses = ramp_ref.shape
    width = back_ref.shape[0]
    scens = width // hours
    first_hour = lax.axis_index("hour") * hours

    back_ref[...] = line_work(inject_ref.at[0:width, :], ptdf_ref, line_max_ref, over_ref)
    agree(mean_ref, sum_refs, hours + 1, scen_total)
    write_ramp(
        mean_ref, mean_ref[hours : hours + 1, :], limit_ref[...], first_hour, padded_ref, excess_ref, ramp_ref
    )
    cost = cost_ref[...]
    top = max_ref[...]
    for h in range(hours):
        part = slice(h * scens, (h + 1) * scens)
        mean = mean_ref[h : h + 1, :]
        gen = gen_ref[part, :]
        hedge = hedged_ref[part, :] - mean
        grad = cost + back_ref[part, :] + (gen - mean + hedge) + ramp_ref[h : h + 1, :]
        gen = jnp.clip(gen - STEP_SIZE * grad, 0.0, top)
        hedged = gen + hedge
        hedged_out_ref[part, :] = hedged
        put_row(sums_out_ref, hours, h, jnp.sum(hedged, axis=0, keepdims=True))
    clear_rest(sums_out_ref, hours * (buses // LANES))


def relay_kernel(near_ref, far_ref, both_ref):
    low = lax.broadcasted_iota(jnp.int32, (CAP, LANES), 1) < LANES // 2
    both_ref[0:CAP, :] = near_ref[:, 0:LANES]
    both_ref[CAP : 2 * CAP, :] = far_ref[CAP : 2 * CAP, :]
    both_ref[2 * CAP :, :] = jnp.where(low, near_ref[:, LANES:], far_ref[2 * CAP :, :])


def agree_kernel(scen_total, hedged_ref, *refs):
    sum_refs, (mean_ref, hedge_ref) = refs[:-2], refs[-2:]
    hours = mean_ref.shape[0]
    scens = hedged_ref.shape[0] // hours
    agree(mean_ref, sum_refs, hours, scen_total)
    for h in range(hours):
        part = slice(h * scens, (h + 1) * scens)
        hedge_ref[part, :] = hedged_ref[part, :] - mean_ref[h : h + 1, :]


def last_kernel(blocks, relayed, partner_of, hedge_ref, mean_ref, *refs):
    *peer_refs, weight_ref, mine_ref, theirs_ref = refs[:-6]
    hedge_out, mean_out, tie_out, tie_ref, placed_ref, copy_sems = refs[-6:]
    copies = []

    def send(src, dst):
        copies.append(pltpu.make_async_copy(src, dst, copy_sems.at[len(copies)]))
        copies[-1].start()

    send(hedge_ref, hedge_out)
    send(mean_ref, mean_out)
    here = lax.axis_index("area")
    placed_ref[...] = jnp.zeros_like(placed_ref)
    if relayed:
        far, both = (unfold(ref[...]) for ref in peer_refs)
        peers = [*by_flips(here, both[CAP:, :], far[0:CAP, :]), both[0:CAP, :]]
    else:
        peers = [unfold(ref[...]) for ref in peer_refs]
    for i in range(blocks):
        slots = slice(i * CAP, (i + 1) * CAP)
        weight = jnp.concatenate([weight_ref[slots, :], weight_ref[slots, :]], axis=1)
        flow = (mine_ref[slots, :] + (theirs_ref[slots, :] - weight * peers[i])) * 0.5
        low, _, block, in_reach = block_facts(here, partner_of(here, i))
        first = block * CAP + jnp.where(low, 0, REACH * CAP)

        @pl.when(in_reach)
        def _():
            placed_ref[pl.ds(pl.multiple_of(first, CAP), CAP), :] = flow

    for first in range(0, tie_ref.shape[0], LANES):
        count = min(LANES, tie_ref.shape[0] - first)
        tie_ref[first : first + count, :] = jnp.transpose(placed_ref[:, first : first + LANES])[0:count, :]
        send(tie_ref.at[pl.ds(first, count)], tie_out.at[pl.ds(first, count)])
    for copy in copies:
        copy.wait()


def call(kernel, name, args, outs, scratch, flops, in_place=(), outs_in_place=False):
    size = sum(x.size * x.dtype.itemsize for x in list(args) + list(outs))
    return pl.pallas_call(
        kernel,
        name=name,
        out_shape=outs,
        in_specs=[ANY if i in in_place else VMEM for i in range(len(args))],
        out_specs=[ANY if outs_in_place else VMEM] * len(outs),
        scratch_shapes=scratch,
        compiler_params=pltpu.CompilerParams(vmem_limit_bytes=32 * 1024 * 1024),
        cost_estimate=pl.CostEstimate(flops=flops, bytes_accessed=size, transcendentals=0),
    )(*(pltpu.with_memory_space_constraint(x, pltpu.HBM) if i in in_place else x for i, x in enumerate(args)))


def per_device(
    ptdf,
    angle_sens,
    demand,
    gen_start,
    hedge_dual,
    gen_cost,
    gen_max,
    gen_ramp,
    line_max,
    tie_count,
    tie_low_bus,
    tie_high_bus,
    tie_susc,
):
    hours, scens, buses = demand.shape
    lines = ptdf.shape[0]
    width = hours * scens
    areas = lax.axis_size("area")
    n_scen = lax.axis_size("scen")
    assert lax.axis_size("hour") == 2 and hours >= 2
    assert width % LANES == LANES // 2 and width < 2 * LANES
    columns = 2 * LANES
    block_rows = CAP * 3 // 2
    scen_total = scens * n_scen
    blocks, partner_of, from_partners = partner_plan(areas)
    slots = blocks * CAP
    pieces = buses // LANES
    sum_rows = 8 * pl.cdiv((hours + 1) * pieces, 8)
    f32, bf16 = jnp.float32, jnp.bfloat16

    def shape(*dims, dtype=f32):
        return jax.ShapeDtypeStruct(dims, dtype)

    def over_scens(sums):
        if n_scen == 2:
            return [sums, lax.ppermute(sums, "scen", [(0, 1), (1, 0)])]
        return [lax.psum(sums, "scen")]

    work = 4 * width * lines * buses

    def step_scratch(rows):
        return [
            pltpu.VMEM((rows, buses), bf16),
            pltpu.VMEM((rows, lines), bf16),
            pltpu.VMEM((rows, buses), f32),
        ]

    ramp_scratch = [
        pltpu.VMEM((hours + 4, buses), f32),
        pltpu.VMEM((hours + 4, buses), f32),
        pltpu.VMEM((hours, buses), f32),
    ]
    tables = (tie_count, tie_low_bus, tie_high_bus, tie_susc)
    vectors = [x.reshape(1, -1) for x in (gen_cost, gen_max, gen_ramp, line_max)]
    load = demand.reshape(width, buses)
    hedge = hedge_dual.reshape(width, buses)
    edge_hedge, start, *vectors, onehot, spread, weight = call(
        functools.partial(table_kernel, blocks, partner_of),
        "tables",
        (hedge, gen_start, *tables, *vectors),
        [
            shape(scens, buses),
            shape(hours, buses),
            *(shape(*x.shape) for x in vectors),
            shape(slots, buses, dtype=bf16),
            shape(slots, buses, dtype=bf16),
            shape(slots, LANES),
        ],
        [pltpu.VMEM(x.shape, x.dtype) for x in tables] + [pltpu.SemaphoreType.DMA((10,))],
        BETWEEN,
        range(10),
    )
    (rows,) = call(
        row_kernel,
        "rows",
        (angle_sens, onehot),
        [shape(slots, buses, dtype=bf16)],
        [],
        2 * slots * buses * buses,
    )
    *sent, own, inject = call(
        functools.partial(angle_kernel, blocks),
        "angles",
        (load, start, rows),
        [shape(block_rows, LANES)] * blocks
        + [shape(slots, columns), shape(columns, buses, dtype=bf16)],
        [],
        2 * slots * buses * width,
    )
    edge_hedge, own = lax.optimization_barrier((edge_hedge, own))
    (edge,) = call(edge_kernel, "edge", (load, edge_hedge, start), [shape(2 * scens + 8, buses)], [], BETWEEN)
    edge = lax.ppermute(edge, "hour", [(0, 1), (1, 0)])
    peer = from_partners(sent)
    gen, base, hedged, sums = call(
        first_kernel,
        "first",
        (ptdf, inject, load, hedge, start, edge, *vectors),
        [
            shape(width, buses),
            shape(width, buses),
            shape(width, buses),
            shape(sum_rows, LANES),
        ],
        step_scratch(width + scens) + ramp_scratch,
        work,
    )
    sum_terms = over_scens(sums)
    terms = len(sum_terms)
    relayed = areas == 4
    tied = call(
        functools.partial(tie_kernel, blocks, relayed),
        "ties",
        (base, spread, rows, weight, own, *peer),
        (
            [shape(2 * block_rows, LANES), shape(CAP, columns)]
            if relayed
            else [shape(block_rows, LANES)] * blocks
        )
        + [shape(columns, buses, dtype=bf16), shape(slots, columns), shape(slots, columns)],
        [],
        BETWEEN,
    )
    *sent, inject, mine, theirs = tied
    hedged, sums = call(
        functools.partial(second_kernel, terms, scen_total),
        "second",
        (ptdf, inject, gen, hedged, *vectors, *sum_terms),
        [shape(width, buses), shape(sum_rows, LANES)],
        step_scratch(width)[1:] + [pltpu.VMEM((8 * pl.cdiv(hours + 1, 8), buses), f32)] + ramp_scratch,
        work,
    )
    sum_terms = over_scens(sums)
    if relayed:
        far, near = sent
        far = lax.ppermute(far, "area", [(a, a ^ 2) for a in range(areas)])
        arrived, _ = lax.optimization_barrier((far, sums))
        (both,) = call(relay_kernel, "relay", (near, arrived), [shape(2 * block_rows, LANES)], [], BETWEEN)
        peer = [far, lax.ppermute(both, "area", [(a, a ^ 1) for a in range(areas)])]
    else:
        peer = from_partners(sent)
    gen_mean, hedge = call(
        functools.partial(agree_kernel, scen_total),
        "agree",
        (hedged, *sum_terms),
        [shape(hours, buses), shape(width, buses)],
        [],
        BETWEEN,
    )
    tie_shape = shape(width, 2 * REACH * CAP)
    hedge, gen_mean, tie_flow = call(
        functools.partial(last_kernel, blocks, relayed, partner_of),
        "last",
        (hedge, gen_mean, *peer, weight, mine, theirs),
        [shape(width, buses), shape(hours, buses), tie_shape],
        [
            pltpu.VMEM(tie_shape.shape, f32),
            pltpu.VMEM((2 * REACH * CAP, columns), f32),
            pltpu.SemaphoreType.DMA((2 + columns // LANES,)),
        ],
        slots * columns,
        outs_in_place=True,
    )
    return (
        gen_mean,
        hedge.reshape(hours, scens, buses),
        tie_flow.reshape(hours, scens, 2 * REACH * CAP),
    )


def solution(mesh):
    return jax.shard_map(
        per_device,
        mesh=mesh,
        in_specs=(
            P(("group", "area"), None),
            P(("group", "area"), None),
            P(("group", "hour"), "scen", "area"),
            P(("group", "hour"), "area"),
            P(("group", "hour"), "scen", "area"),
            P(("group", "area")),
            P(("group", "area")),
            P(("group", "area")),
            P(("group", "area")),
            P("group", None),
            P("group", None),
            P("group", None),
            P("group", None),
        ),
        out_specs=(
            P(("group", "hour"), "area"),
            P(("group", "hour"), "scen", "area"),
            P(("group", "hour"), "scen", "area"),
        ),
        check_vma=False,
    )
```

```python
import functools

import jax
import jax.numpy as jnp
from jax import lax
from jax.experimental import pallas as pl
from jax.experimental.pallas import tpu as pltpu
from jax.sharding import PartitionSpec as P

HOURS = 24
REACH = 4
CAP = 16

STEP_SIZE = 0.5
LINE_CHUNK = 1024
LANES = 128
HEDGE_PIECES = 3
BETWEEN = 20_000_000_000

CONTRACT_LAST = (((1,), (1,)), ((), ()))
CONTRACT_FIRST = (((0,), (0,)), ((), ()))
VMEM = pl.BlockSpec(memory_space=pltpu.VMEM)
ANY = pl.BlockSpec(memory_space=pltpu.HBM)


TARGETS = ((3, 2, 0, 1), (2, 3, 1, 0), (1, 0, 3, 2))


def partner_plan(areas):
    if areas == 4:

        def partner_of(here, i):
            return sum(jnp.where(here == a, target, 0) for a, target in enumerate(TARGETS[i]))

        def by_target(parts):
            out, back, pair = (
                lax.ppermute(part, "area", list(enumerate(target))) for part, target in zip(parts, TARGETS)
            )
            return [back, out, pair]

        return len(TARGETS), partner_of, by_target
    reach = min(REACH, areas - 1)
    shifts = sorted({s % areas for d in range(1, reach + 1) for s in (d, -d)})

    def by_shift(parts):
        sent = [
            lax.ppermute(part, "area", [(a, (a + s) % areas) for a in range(areas)])
            for part, s in zip(parts, shifts)
        ]
        return [sent[shifts.index(areas - s)] for s in shifts]

    return len(shifts), lambda here, i: lax.rem(here + shifts[i], areas), by_shift


def by_flips(here, flip_3, flip_2):
    return jnp.where(here < 2, flip_3, flip_2), jnp.where(here < 2, flip_2, flip_3)


def block_facts(here, partner):
    low = partner > here
    distance = jnp.abs(partner - here)
    block = jnp.clip(distance - 1, 0, REACH - 1)
    in_reach = (distance >= 1) & (distance <= REACH)
    return low, jnp.minimum(here, partner), block, in_reach


def fold(x):
    half = x.shape[0] // 2
    low = lax.broadcasted_iota(jnp.int32, (half, LANES), 1) < LANES // 2
    shared = jnp.where(low, x[0:half, LANES : 2 * LANES], x[half:, LANES : 2 * LANES])
    return jnp.concatenate([x[:, 0:LANES], shared], axis=0)


def unfold(packed):
    rows = 2 * packed.shape[0] // 3
    shared = packed[rows:, :]
    low = lax.broadcasted_iota(jnp.int32, shared.shape, 1) < LANES // 2
    turned = pltpu.roll(shared, LANES // 2, 1)
    rest = jnp.concatenate([jnp.where(low, shared, turned), jnp.where(low, turned, shared)], axis=0)
    return jnp.concatenate([packed[0:rows, :], rest], axis=1)


def repeat_rest(inject_ref, width):
    inject_ref[width:, :] = inject_ref[width - LANES // 2 : width, :]


def split_3(x):
    high = x.astype(jnp.bfloat16)
    rest = x - high.astype(jnp.float32)
    middle = rest.astype(jnp.bfloat16)
    rest = rest - middle.astype(jnp.float32)
    return jnp.concatenate([high, middle, rest.astype(jnp.bfloat16)], axis=0)


def put_row(packed_ref, hours, h, row):
    for j in range(row.shape[1] // LANES):
        packed_ref[j * hours + h : j * hours + h + 1, :] = row[:, j * LANES : (j + 1) * LANES]


def clear_rest(packed_ref, used):
    rows = packed_ref.shape[0]
    if used < rows:
        packed_ref[used:, :] = jnp.zeros((rows - used, LANES), jnp.float32)


def agree(mean_ref, sum_refs, hours, scen_total):
    for j in range(mean_ref.shape[1] // LANES):
        parts = [ref[j * hours : (j + 1) * hours, :] for ref in sum_refs]
        mean_ref[0:hours, j * LANES : (j + 1) * LANES] = functools.reduce(jnp.add, parts) / scen_total


def excess(diffs, limit):
    return diffs - jnp.clip(diffs, -limit, limit)


def write_ramp(mean_ref, beyond, limit, first_hour, padded_ref, excess_ref, ramp_ref):
    hours = ramp_ref.shape[0]
    padded_ref[0:1, :] = beyond
    padded_ref[1 : hours + 1, :] = mean_ref[0:hours, :]
    padded_ref[hours + 1 : hours + 2, :] = beyond
    diffs = padded_ref[1 : hours + 2, :] - padded_ref[0 : hours + 1, :]
    ids = first_hour + lax.broadcasted_iota(jnp.int32, diffs.shape, 0)
    valid = (ids >= 1) & (ids <= HOURS - 1)
    excess_ref[0 : hours + 1, :] = jnp.where(valid, excess(diffs, limit), 0.0)
    ramp_ref[...] = excess_ref[0:hours, :] - excess_ref[1 : hours + 1, :]


def line_work(inject_ref, ptdf_ref, line_max_ref, over_ref):
    inject = inject_ref[...]
    lines = ptdf_ref.shape[0]
    for at in range(0, lines, LINE_CHUNK):
        part = slice(at, at + LINE_CHUNK)
        flows = lax.dot_general(
            inject, ptdf_ref[part, :], CONTRACT_LAST, preferred_element_type=jnp.float32
        )
        limit = line_max_ref[:, part]
        over_ref[:, part] = (flows - jnp.clip(flows, -limit, limit)).astype(jnp.bfloat16)
    return jnp.dot(over_ref[...], ptdf_ref[...], preferred_element_type=jnp.float32)


def table_kernel(
    blocks,
    partner_of,
    demand_in,
    hedge_in,
    start_in,
    count_in,
    low_bus_in,
    high_bus_in,
    susc_in,
    cost_in,
    max_in,
    limit_in,
    line_max_in,
    demand_ref,
    edge_hedge_ref,
    start_ref,
    cost_ref,
    max_ref,
    limit_ref,
    line_max_ref,
    onehot_ref,
    spread_ref,
    weight_ref,
    count_ref,
    low_bus_ref,
    high_bus_ref,
    susc_ref,
    copy_sems,
):
    hours, buses = start_ref.shape
    scens = hedge_in.shape[0] // hours
    here = lax.axis_index("area")
    last = (hours - 1) * scens
    edge_rows = pl.ds(pl.multiple_of((1 - lax.axis_index("hour")) * last, scens), scens)

    pairs = (
        (count_in, count_ref),
        (low_bus_in, low_bus_ref),
        (high_bus_in, high_bus_ref),
        (susc_in, susc_ref),
        (start_in, start_ref),
        (demand_in, demand_ref),
        (hedge_in.at[edge_rows], edge_hedge_ref),
        (cost_in, cost_ref),
        (max_in, max_ref),
        (limit_in, limit_ref),
        (line_max_in, line_max_ref),
    )
    copies = [pltpu.make_async_copy(src, dst, copy_sems.at[i]) for i, (src, dst) in enumerate(pairs)]
    for copy in (copies[5], *copies[:5], *copies[6:]):
        copy.start()
    for copy in copies[:4]:
        copy.wait()
    for i in range(blocks):
        partner = partner_of(here, i)
        low, row, block, in_reach = block_facts(here, partner)
        slots = slice(i * CAP, (i + 1) * CAP)
        pick = lax.broadcasted_iota(jnp.int32, (CAP, REACH * CAP), 1) == (
            block * CAP + lax.broadcasted_iota(jnp.int32, (CAP, REACH * CAP), 0)
        )
        table_row = pl.ds(row, 1)
        bus_row = jnp.where(low, low_bus_ref[table_row, :], high_bus_ref[table_row, :])
        bus = jnp.sum(jnp.where(pick, bus_row.astype(jnp.float32), 0.0), axis=1, keepdims=True)
        susc = jnp.sum(jnp.where(pick, susc_ref[table_row, :], 0.0), axis=1, keepdims=True)
        count_row = count_ref[table_row, :].astype(jnp.float32)
        is_block = lax.broadcasted_iota(jnp.int32, (CAP, REACH), 1) == block
        count = jnp.sum(jnp.where(is_block, count_row, 0.0), axis=1, keepdims=True)
        slot_ids = lax.broadcasted_iota(jnp.int32, (CAP, 1), 0).astype(jnp.float32)
        live = jnp.where((slot_ids < count) & in_reach, 1.0, 0.0)
        sign = jnp.where(low, 1.0, -1.0)
        bus_ids = lax.broadcasted_iota(jnp.int32, (CAP, buses), 1).astype(jnp.float32)
        onehot = jnp.where(bus_ids == bus, live, 0.0)
        onehot_ref[slots, :] = onehot.astype(jnp.bfloat16)
        spread_ref[slots, :] = (-sign * onehot).astype(jnp.bfloat16)
        weight_ref[slots, :] = jnp.broadcast_to(live * sign * susc, (CAP, 128))

    for copy in copies[4:]:
        copy.wait()


def row_kernel(sens_ref, onehot_ref, rows_ref):
    rows = jnp.dot(onehot_ref[...], sens_ref[...], preferred_element_type=jnp.float32)
    rows_ref[...] = rows.astype(jnp.bfloat16)


def angle_kernel(blocks, demand_ref, start_ref, rows_ref, *refs):
    sent_refs, (own_ref, inject_ref) = refs[:blocks], refs[blocks:]
    hours = start_ref.shape[0]
    scens = demand_ref.shape[0] // hours
    for h in range(hours):
        part = slice(h * scens, (h + 1) * scens)
        inject_ref[part, :] = (start_ref[h : h + 1, :] - demand_ref[part, :]).astype(jnp.bfloat16)
    repeat_rest(inject_ref, hours * scens)
    own = lax.dot_general(
        rows_ref[...], inject_ref[...], CONTRACT_LAST, preferred_element_type=jnp.float32
    )
    own_ref[...] = own
    for i in range(blocks):
        sent_refs[i][...] = fold(own[i * CAP : (i + 1) * CAP, :])


def edge_kernel(demand_ref, edge_hedge_ref, start_ref, edge_ref):
    scens = edge_hedge_ref.shape[0]
    hours = start_ref.shape[0]
    early = lax.axis_index("hour") == 0
    last = (hours - 1) * scens
    at = 2 * scens
    edge_ref[0:scens, :] = jnp.where(early, demand_ref[last:, :], demand_ref[0:scens, :])
    edge_ref[scens:at, :] = edge_hedge_ref[...]
    edge_ref[at : at + 1, :] = jnp.where(early, start_ref[hours - 1 : hours, :], start_ref[0:1, :])
    edge_ref[at + 1 : at + 2, :] = jnp.where(
        early, start_ref[hours - 2 : hours - 1, :], start_ref[1:2, :]
    )


def first_kernel(
    ptdf_ref,
    own_inject_ref,
    demand_ref,
    hedge_ref,
    start_ref,
    edge_ref,
    cost_ref,
    max_ref,
    limit_ref,
    line_max_ref,
    gen_ref,
    base_ref,
    hedged_ref,
    sums_ref,
    inject_ref,
    over_ref,
    back_ref,
    padded_ref,
    excess_ref,
    ramp_ref,
):
    hours, buses = start_ref.shape
    width = demand_ref.shape[0]
    scens = width // hours
    at = 2 * scens
    early = lax.axis_index("hour") == 0
    first_hour = lax.axis_index("hour") * hours
    beyond = edge_ref[at : at + 1, :]
    limit = limit_ref[...]
    cost = cost_ref[...]
    top = max_ref[...]

    inject_ref[0:width, :] = own_inject_ref[0:width, :]
    inject_ref[width : width + scens, :] = (beyond - edge_ref[0:scens, :]).astype(jnp.bfloat16)
    back_ref[...] = line_work(inject_ref, ptdf_ref, line_max_ref, over_ref)
    write_ramp(start_ref, beyond, limit, first_hour, padded_ref, excess_ref, ramp_ref)

    def step(mean, hedge, back, ramp):
        grad = cost + back + (mean - mean + hedge) + ramp
        gen = jnp.clip(mean - STEP_SIZE * grad, 0.0, top)
        return gen, gen + hedge

    for h in range(hours):
        part = slice(h * scens, (h + 1) * scens)
        mean = start_ref[h : h + 1, :]
        gen, hedged = step(mean, hedge_ref[part, :], back_ref[part, :], ramp_ref[h : h + 1, :])
        gen_ref[part, :] = gen
        base_ref[part, :] = gen - demand_ref[part, :]
        hedged_ref[part, :] = hedged
        put_row(sums_ref, hours + 1, h, jnp.sum(hedged, axis=0, keepdims=True))
    near = jnp.where(early, start_ref[hours - 1 : hours, :], start_ref[0:1, :])
    ramp = excess(beyond - near, limit) + excess(beyond - edge_ref[at + 1 : at + 2, :], limit)
    _, hedged = step(beyond, edge_ref[scens:at, :], back_ref[width : width + scens, :], ramp)
    put_row(sums_ref, hours + 1, hours, jnp.sum(hedged, axis=0, keepdims=True))
    clear_rest(sums_ref, (hours + 1) * (buses // LANES))


def tie_kernel(blocks, relayed, base_ref, spread_ref, rows_ref, weight_ref, own_ref, *refs):
    peer_refs, refs = refs[:blocks], refs[blocks:]
    *next_refs, inject_ref, mine_ref, theirs_ref = refs
    width = base_ref.shape[0]

    weight = jnp.concatenate([weight_ref[...], weight_ref[...]], axis=1)
    own = own_ref[...]
    peer = jnp.concatenate([unfold(ref[...]) for ref in peer_refs], axis=0)
    est_mine = weight * own
    est_theirs = -weight * peer
    flow = (est_mine + est_theirs) * 0.5
    dual_mine = est_mine - flow
    dual_theirs = est_theirs - flow
    spread = spread_ref[...]
    add = lax.dot_general(
        split_3(flow),
        jnp.concatenate([spread, spread, spread], axis=0),
        CONTRACT_FIRST,
        preferred_element_type=jnp.float32,
    )
    inject_ref[0:width, :] = (base_ref[...] + add[0:width, :]).astype(jnp.bfloat16)
    repeat_rest(inject_ref, width)

    own_next = lax.dot_general(
        rows_ref[...], inject_ref[...], CONTRACT_LAST, preferred_element_type=jnp.float32
    )
    parts = [own_next[i * CAP : (i + 1) * CAP, :] for i in range(blocks)]
    if relayed:
        far_ref, near_ref = next_refs
        flip_3, flip_2 = by_flips(lax.axis_index("area"), parts[0], parts[1])
        far_ref[...] = fold(jnp.concatenate([flip_2, flip_3], axis=0))
        near_ref[...] = parts[2]
    else:
        for ref, part in zip(next_refs, parts):
            ref[...] = fold(part)
    mine_ref[...] = weight * (own_next - peer) + dual_mine
    theirs_ref[...] = weight * own + dual_theirs


def second_kernel(
    terms,
    scen_total,
    ptdf_ref,
    inject_ref,
    gen_ref,
    hedged_ref,
    cost_ref,
    max_ref,
    limit_ref,
    line_max_ref,
    *refs,
):
    sum_refs, refs = refs[:terms], refs[terms:]
    (hedged_out_ref, sums_out_ref, over_ref, back_ref, mean_ref, padded_ref, excess_ref, ramp_ref) = refs
    hours, buses = ramp_ref.shape
    width = back_ref.shape[0]
    scens = width // hours
    first_hour = lax.axis_index("hour") * hours

    back_ref[...] = line_work(inject_ref.at[0:width, :], ptdf_ref, line_max_ref, over_ref)
    agree(mean_ref, sum_refs, hours + 1, scen_total)
    write_ramp(
        mean_ref, mean_ref[hours : hours + 1, :], limit_ref[...], first_hour, padded_ref, excess_ref, ramp_ref
    )
    cost = cost_ref[...]
    top = max_ref[...]
    for h in range(hours):
        part = slice(h * scens, (h + 1) * scens)
        mean = mean_ref[h : h + 1, :]
        gen = gen_ref[part, :]
        hedge = hedged_ref[part, :] - mean
        grad = cost + back_ref[part, :] + (gen - mean + hedge) + ramp_ref[h : h + 1, :]
        gen = jnp.clip(gen - STEP_SIZE * grad, 0.0, top)
        hedged = gen + hedge
        hedged_out_ref[part, :] = hedged
        put_row(sums_out_ref, hours, h, jnp.sum(hedged, axis=0, keepdims=True))
    clear_rest(sums_out_ref, hours * (buses // LANES))


def relay_kernel(near_ref, far_ref, both_ref):
    low = lax.broadcasted_iota(jnp.int32, (CAP, LANES), 1) < LANES // 2
    both_ref[0:CAP, :] = near_ref[:, 0:LANES]
    both_ref[CAP : 2 * CAP, :] = far_ref[CAP : 2 * CAP, :]
    both_ref[2 * CAP :, :] = jnp.where(low, near_ref[:, LANES:], far_ref[2 * CAP :, :])


def agree_kernel(scen_total, hedged_ref, *refs):
    sum_refs, (mean_ref, hedge_ref) = refs[:-2], refs[-2:]
    hours = mean_ref.shape[0]
    scens = hedged_ref.shape[0] // hours
    agree(mean_ref, sum_refs, hours, scen_total)
    for h in range(hours):
        part = slice(h * scens, (h + 1) * scens)
        hedge_ref[part, :] = hedged_ref[part, :] - mean_ref[h : h + 1, :]


def last_kernel(blocks, relayed, partner_of, hedge_ref, mean_ref, *refs):
    *peer_refs, weight_ref, mine_ref, theirs_ref = refs[:-6]
    hedge_out, mean_out, tie_out, tie_ref, placed_ref, copy_sems = refs[-6:]
    copies = []

    def send(src, dst):
        copies.append(pltpu.make_async_copy(src, dst, copy_sems.at[len(copies)]))
        copies[-1].start()

    piece = hedge_ref.shape[0] // HEDGE_PIECES
    for first in range(0, hedge_ref.shape[0], piece):
        send(hedge_ref.at[pl.ds(first, piece)], hedge_out.at[pl.ds(first, piece)])
    send(mean_ref, mean_out)
    here = lax.axis_index("area")
    placed_ref[...] = jnp.zeros_like(placed_ref)
    if relayed:
        far, both = (unfold(ref[...]) for ref in peer_refs)
        peers = [*by_flips(here, both[CAP:, :], far[0:CAP, :]), both[0:CAP, :]]
    else:
        peers = [unfold(ref[...]) for ref in peer_refs]
    for i in range(blocks):
        slots = slice(i * CAP, (i + 1) * CAP)
        weight = jnp.concatenate([weight_ref[slots, :], weight_ref[slots, :]], axis=1)
        flow = (mine_ref[slots, :] + (theirs_ref[slots, :] - weight * peers[i])) * 0.5
        low, _, block, in_reach = block_facts(here, partner_of(here, i))
        first = block * CAP + jnp.where(low, 0, REACH * CAP)

        @pl.when(in_reach)
        def _():
            placed_ref[pl.ds(pl.multiple_of(first, CAP), CAP), :] = flow

    for first in range(0, tie_ref.shape[0], LANES):
        count = min(LANES, tie_ref.shape[0] - first)
        tie_ref[first : first + count, :] = jnp.transpose(placed_ref[:, first : first + LANES])[0:count, :]
        send(tie_ref.at[pl.ds(first, count)], tie_out.at[pl.ds(first, count)])
    for copy in copies:
        copy.wait()


def call(kernel, name, args, outs, scratch, flops, in_place=(), outs_in_place=False):
    size = sum(x.size * x.dtype.itemsize for x in list(args) + list(outs))
    return pl.pallas_call(
        kernel,
        name=name,
        out_shape=outs,
        in_specs=[ANY if i in in_place else VMEM for i in range(len(args))],
        out_specs=[ANY if outs_in_place else VMEM] * len(outs),
        scratch_shapes=scratch,
        compiler_params=pltpu.CompilerParams(vmem_limit_bytes=32 * 1024 * 1024),
        cost_estimate=pl.CostEstimate(flops=flops, bytes_accessed=size, transcendentals=0),
    )(*(pltpu.with_memory_space_constraint(x, pltpu.HBM) if i in in_place else x for i, x in enumerate(args)))


def per_device(
    ptdf,
    angle_sens,
    demand,
    gen_start,
    hedge_dual,
    gen_cost,
    gen_max,
    gen_ramp,
    line_max,
    tie_count,
    tie_low_bus,
    tie_high_bus,
    tie_susc,
):
    hours, scens, buses = demand.shape
    lines = ptdf.shape[0]
    width = hours * scens
    areas = lax.axis_size("area")
    n_scen = lax.axis_size("scen")
    assert lax.axis_size("hour") == 2 and hours >= 2
    assert width % (8 * HEDGE_PIECES) == 0
    assert width % LANES == LANES // 2 and width < 2 * LANES
    columns = 2 * LANES
    block_rows = CAP * 3 // 2
    scen_total = scens * n_scen
    blocks, partner_of, from_partners = partner_plan(areas)
    slots = blocks * CAP
    pieces = buses // LANES
    sum_rows = 8 * pl.cdiv((hours + 1) * pieces, 8)
    f32, bf16 = jnp.float32, jnp.bfloat16

    def shape(*dims, dtype=f32):
        return jax.ShapeDtypeStruct(dims, dtype)

    def over_scens(sums):
        if n_scen == 2:
            return [sums, lax.ppermute(sums, "scen", [(0, 1), (1, 0)])]
        return [lax.psum(sums, "scen")]

    work = 4 * width * lines * buses

    def step_scratch(rows):
        return [
            pltpu.VMEM((rows, buses), bf16),
            pltpu.VMEM((rows, lines), bf16),
            pltpu.VMEM((rows, buses), f32),
        ]

    ramp_scratch = [
        pltpu.VMEM((hours + 4, buses), f32),
        pltpu.VMEM((hours + 4, buses), f32),
        pltpu.VMEM((hours, buses), f32),
    ]
    tables = (tie_count, tie_low_bus, tie_high_bus, tie_susc)
    vectors = [x.reshape(1, -1) for x in (gen_cost, gen_max, gen_ramp, line_max)]
    hedge = hedge_dual.reshape(width, buses)
    load, edge_hedge, start, *vectors, onehot, spread, weight = call(
        functools.partial(table_kernel, blocks, partner_of),
        "tables",
        (demand.reshape(width, buses), hedge, gen_start, *tables, *vectors),
        [
            shape(width, buses),
            shape(scens, buses),
            shape(hours, buses),
            *(shape(*x.shape) for x in vectors),
            shape(slots, buses, dtype=bf16),
            shape(slots, buses, dtype=bf16),
            shape(slots, LANES),
        ],
        [pltpu.VMEM(x.shape, x.dtype) for x in tables] + [pltpu.SemaphoreType.DMA((11,))],
        BETWEEN,
        range(11),
    )
    (edge,) = call(edge_kernel, "edge", (load, edge_hedge, start), [shape(2 * scens + 8, buses)], [], width)
    (rows,) = call(
        row_kernel,
        "rows",
        (angle_sens, onehot),
        [shape(slots, buses, dtype=bf16)],
        [],
        BETWEEN,
    )
    *sent, own, inject = call(
        functools.partial(angle_kernel, blocks),
        "angles",
        (load, start, rows),
        [shape(block_rows, LANES)] * blocks
        + [shape(slots, columns), shape(columns, buses, dtype=bf16)],
        [],
        2 * slots * buses * width,
    )
    edge = lax.ppermute(edge, "hour", [(0, 1), (1, 0)])
    peer = from_partners(sent)
    gen, base, hedged, sums = call(
        first_kernel,
        "first",
        (ptdf, inject, load, hedge, start, edge, *vectors),
        [
            shape(width, buses),
            shape(width, buses),
            shape(width, buses),
            shape(sum_rows, LANES),
        ],
        step_scratch(width + scens) + ramp_scratch,
        work,
    )
    sum_terms = over_scens(sums)
    terms = len(sum_terms)
    relayed = areas == 4
    tied = call(
        functools.partial(tie_kernel, blocks, relayed),
        "ties",
        (base, spread, rows, weight, own, *peer),
        (
            [shape(2 * block_rows, LANES), shape(CAP, columns)]
            if relayed
            else [shape(block_rows, LANES)] * blocks
        )
        + [shape(columns, buses, dtype=bf16), shape(slots, columns), shape(slots, columns)],
        [],
        BETWEEN,
    )
    *sent, inject, mine, theirs = tied
    hedged, sums = call(
        functools.partial(second_kernel, terms, scen_total),
        "second",
        (ptdf, inject, gen, hedged, *vectors, *sum_terms),
        [shape(width, buses), shape(sum_rows, LANES)],
        step_scratch(width)[1:] + [pltpu.VMEM((8 * pl.cdiv(hours + 1, 8), buses), f32)] + ramp_scratch,
        work,
    )
    sum_terms = over_scens(sums)
    if relayed:
        far, near = sent
        far = lax.ppermute(far, "area", [(a, a ^ 2) for a in range(areas)])
        arrived, _ = lax.optimization_barrier((far, sums))
        (both,) = call(relay_kernel, "relay", (near, arrived), [shape(2 * block_rows, LANES)], [], BETWEEN)
        peer = [far, lax.ppermute(both, "area", [(a, a ^ 1) for a in range(areas)])]
    else:
        peer = from_partners(sent)
    gen_mean, hedge = call(
        functools.partial(agree_kernel, scen_total),
        "agree",
        (hedged, *sum_terms),
        [shape(hours, buses), shape(width, buses)],
        [],
        BETWEEN,
    )
    tie_shape = shape(width, 2 * REACH * CAP)
    hedge, gen_mean, tie_flow = call(
        functools.partial(last_kernel, blocks, relayed, partner_of),
        "last",
        (hedge, gen_mean, *peer, weight, mine, theirs),
        [shape(width, buses), shape(hours, buses), tie_shape],
        [
            pltpu.VMEM(tie_shape.shape, f32),
            pltpu.VMEM((2 * REACH * CAP, columns), f32),
            pltpu.SemaphoreType.DMA((1 + HEDGE_PIECES + columns // LANES,)),
        ],
        slots * columns,
        outs_in_place=True,
    )
    return (
        gen_mean,
        hedge.reshape(hours, scens, buses),
        tie_flow.reshape(hours, scens, 2 * REACH * CAP),
    )


def solution(mesh):
    return jax.shard_map(
        per_device,
        mesh=mesh,
        in_specs=(
            P(("group", "area"), None),
            P(("group", "area"), None),
            P(("group", "hour"), "scen", "area"),
            P(("group", "hour"), "area"),
            P(("group", "hour"), "scen", "area"),
            P(("group", "area")),
            P(("group", "area")),
            P(("group", "area")),
            P(("group", "area")),
            P("group", None),
            P("group", None),
            P("group", None),
            P("group", None),
        ),
        out_specs=(
            P(("group", "hour"), "area"),
            P(("group", "hour"), "scen", "area"),
            P(("group", "hour"), "scen", "area"),
        ),
        check_vma=False,
    )
```

```python
import functools

import jax
import jax.numpy as jnp
from jax import lax
from jax.experimental import pallas as pl
from jax.experimental.pallas import tpu as pltpu
from jax.sharding import PartitionSpec as P

HOURS = 24
REACH = 4
CAP = 16

STEP_SIZE = 0.5
LINE_CHUNK = 1024
LANES = 128
BETWEEN = 20_000_000_000

CONTRACT_LAST = (((1,), (1,)), ((), ()))
CONTRACT_FIRST = (((0,), (0,)), ((), ()))
VMEM = pl.BlockSpec(memory_space=pltpu.VMEM)
ANY = pl.BlockSpec(memory_space=pltpu.HBM)


TARGETS = ((3, 2, 0, 1), (2, 3, 1, 0), (1, 0, 3, 2))


def partner_plan(areas):
    if areas == 4:

        def partner_of(here, i):
            return sum(jnp.where(here == a, target, 0) for a, target in enumerate(TARGETS[i]))

        def by_target(parts):
            out, back, pair = (
                lax.ppermute(part, "area", list(enumerate(target))) for part, target in zip(parts, TARGETS)
            )
            return [back, out, pair]

        return len(TARGETS), partner_of, by_target
    reach = min(REACH, areas - 1)
    shifts = sorted({s % areas for d in range(1, reach + 1) for s in (d, -d)})

    def by_shift(parts):
        sent = [
            lax.ppermute(part, "area", [(a, (a + s) % areas) for a in range(areas)])
            for part, s in zip(parts, shifts)
        ]
        return [sent[shifts.index(areas - s)] for s in shifts]

    return len(shifts), lambda here, i: lax.rem(here + shifts[i], areas), by_shift


def by_flips(here, flip_3, flip_2):
    return jnp.where(here < 2, flip_3, flip_2), jnp.where(here < 2, flip_2, flip_3)


def block_facts(here, partner):
    low = partner > here
    distance = jnp.abs(partner - here)
    block = jnp.clip(distance - 1, 0, REACH - 1)
    in_reach = (distance >= 1) & (distance <= REACH)
    return low, jnp.minimum(here, partner), block, in_reach


def fold(x):
    half = x.shape[0] // 2
    low = lax.broadcasted_iota(jnp.int32, (half, LANES), 1) < LANES // 2
    shared = jnp.where(low, x[0:half, LANES : 2 * LANES], x[half:, LANES : 2 * LANES])
    return jnp.concatenate([x[:, 0:LANES], shared], axis=0)


def unfold(packed):
    rows = 2 * packed.shape[0] // 3
    shared = packed[rows:, :]
    low = lax.broadcasted_iota(jnp.int32, shared.shape, 1) < LANES // 2
    turned = pltpu.roll(shared, LANES // 2, 1)
    rest = jnp.concatenate([jnp.where(low, shared, turned), jnp.where(low, turned, shared)], axis=0)
    return jnp.concatenate([packed[0:rows, :], rest], axis=1)


def repeat_rest(inject_ref, width):
    inject_ref[width:, :] = inject_ref[width - LANES // 2 : width, :]


def split_3(x):
    high = x.astype(jnp.bfloat16)
    rest = x - high.astype(jnp.float32)
    middle = rest.astype(jnp.bfloat16)
    rest = rest - middle.astype(jnp.float32)
    return jnp.concatenate([high, middle, rest.astype(jnp.bfloat16)], axis=0)


def put_row(packed_ref, hours, h, row):
    for j in range(row.shape[1] // LANES):
        packed_ref[j * hours + h : j * hours + h + 1, :] = row[:, j * LANES : (j + 1) * LANES]


def clear_rest(packed_ref, used):
    rows = packed_ref.shape[0]
    if used < rows:
        packed_ref[used:, :] = jnp.zeros((rows - used, LANES), jnp.float32)


def agree(mean_ref, sum_refs, hours, scen_total):
    for j in range(mean_ref.shape[1] // LANES):
        parts = [ref[j * hours : (j + 1) * hours, :] for ref in sum_refs]
        mean_ref[0:hours, j * LANES : (j + 1) * LANES] = functools.reduce(jnp.add, parts) / scen_total


def excess(diffs, limit):
    return diffs - jnp.clip(diffs, -limit, limit)


def write_ramp(mean_ref, beyond, limit, first_hour, padded_ref, excess_ref, ramp_ref):
    hours = ramp_ref.shape[0]
    padded_ref[0:1, :] = beyond
    padded_ref[1 : hours + 1, :] = mean_ref[0:hours, :]
    padded_ref[hours + 1 : hours + 2, :] = beyond
    diffs = padded_ref[1 : hours + 2, :] - padded_ref[0 : hours + 1, :]
    ids = first_hour + lax.broadcasted_iota(jnp.int32, diffs.shape, 0)
    valid = (ids >= 1) & (ids <= HOURS - 1)
    excess_ref[0 : hours + 1, :] = jnp.where(valid, excess(diffs, limit), 0.0)
    ramp_ref[...] = excess_ref[0:hours, :] - excess_ref[1 : hours + 1, :]


def line_work(inject_ref, ptdf_ref, line_max_ref, over_ref):
    inject = inject_ref[...]
    lines = ptdf_ref.shape[0]
    for at in range(0, lines, LINE_CHUNK):
        part = slice(at, at + LINE_CHUNK)
        flows = lax.dot_general(
            inject, ptdf_ref[part, :], CONTRACT_LAST, preferred_element_type=jnp.float32
        )
        limit = line_max_ref[:, part]
        over_ref[:, part] = (flows - jnp.clip(flows, -limit, limit)).astype(jnp.bfloat16)
    return jnp.dot(over_ref[...], ptdf_ref[...], preferred_element_type=jnp.float32)


def table_kernel(
    blocks,
    partner_of,
    demand_in,
    hedge_in,
    start_in,
    count_in,
    low_bus_in,
    high_bus_in,
    susc_in,
    cost_in,
    max_in,
    limit_in,
    line_max_in,
    demand_ref,
    edge_hedge_ref,
    start_ref,
    cost_ref,
    max_ref,
    limit_ref,
    line_max_ref,
    onehot_ref,
    spread_ref,
    weight_ref,
    count_ref,
    low_bus_ref,
    high_bus_ref,
    susc_ref,
    copy_sems,
):
    hours, buses = start_ref.shape
    scens = hedge_in.shape[0] // hours
    here = lax.axis_index("area")
    last = (hours - 1) * scens
    edge_rows = pl.ds(pl.multiple_of((1 - lax.axis_index("hour")) * last, scens), scens)

    pairs = (
        (count_in, count_ref),
        (low_bus_in, low_bus_ref),
        (high_bus_in, high_bus_ref),
        (susc_in, susc_ref),
        (start_in, start_ref),
        (demand_in, demand_ref),
        (hedge_in.at[edge_rows], edge_hedge_ref),
        (cost_in, cost_ref),
        (max_in, max_ref),
        (limit_in, limit_ref),
        (line_max_in, line_max_ref),
    )
    copies = [pltpu.make_async_copy(src, dst, copy_sems.at[i]) for i, (src, dst) in enumerate(pairs)]
    for copy in (copies[5], *copies[:5], *copies[6:]):
        copy.start()
    for copy in copies[:4]:
        copy.wait()
    for i in range(blocks):
        partner = partner_of(here, i)
        low, row, block, in_reach = block_facts(here, partner)
        slots = slice(i * CAP, (i + 1) * CAP)
        pick = lax.broadcasted_iota(jnp.int32, (CAP, REACH * CAP), 1) == (
            block * CAP + lax.broadcasted_iota(jnp.int32, (CAP, REACH * CAP), 0)
        )
        table_row = pl.ds(row, 1)
        bus_row = jnp.where(low, low_bus_ref[table_row, :], high_bus_ref[table_row, :])
        bus = jnp.sum(jnp.where(pick, bus_row.astype(jnp.float32), 0.0), axis=1, keepdims=True)
        susc = jnp.sum(jnp.where(pick, susc_ref[table_row, :], 0.0), axis=1, keepdims=True)
        count_row = count_ref[table_row, :].astype(jnp.float32)
        is_block = lax.broadcasted_iota(jnp.int32, (CAP, REACH), 1) == block
        count = jnp.sum(jnp.where(is_block, count_row, 0.0), axis=1, keepdims=True)
        slot_ids = lax.broadcasted_iota(jnp.int32, (CAP, 1), 0).astype(jnp.float32)
        live = jnp.where((slot_ids < count) & in_reach, 1.0, 0.0)
        sign = jnp.where(low, 1.0, -1.0)
        bus_ids = lax.broadcasted_iota(jnp.int32, (CAP, buses), 1).astype(jnp.float32)
        onehot = jnp.where(bus_ids == bus, live, 0.0)
        onehot_ref[slots, :] = onehot.astype(jnp.bfloat16)
        spread_ref[slots, :] = (-sign * onehot).astype(jnp.bfloat16)
        weight_ref[slots, :] = jnp.broadcast_to(live * sign * susc, (CAP, 128))

    for copy in copies[4:]:
        copy.wait()


def angle_kernel(blocks, sens_ref, demand_ref, start_ref, onehot_ref, *refs):
    sent_refs, (own_ref, inject_ref, rows_ref) = refs[:blocks], refs[blocks:]
    hours = start_ref.shape[0]
    scens = demand_ref.shape[0] // hours
    rows = jnp.dot(onehot_ref[...], sens_ref[...], preferred_element_type=jnp.float32)
    rows_ref[...] = rows.astype(jnp.bfloat16)
    for h in range(hours):
        part = slice(h * scens, (h + 1) * scens)
        inject_ref[part, :] = (start_ref[h : h + 1, :] - demand_ref[part, :]).astype(jnp.bfloat16)
    repeat_rest(inject_ref, hours * scens)
    own = lax.dot_general(
        rows_ref[...], inject_ref[...], CONTRACT_LAST, preferred_element_type=jnp.float32
    )
    own_ref[...] = own
    for i in range(blocks):
        sent_refs[i][...] = fold(own[i * CAP : (i + 1) * CAP, :])


def edge_kernel(demand_ref, edge_hedge_ref, start_ref, edge_ref):
    scens = edge_hedge_ref.shape[0]
    hours = start_ref.shape[0]
    early = lax.axis_index("hour") == 0
    last = (hours - 1) * scens
    at = 2 * scens
    edge_ref[0:scens, :] = jnp.where(early, demand_ref[last:, :], demand_ref[0:scens, :])
    edge_ref[scens:at, :] = edge_hedge_ref[...]
    edge_ref[at : at + 1, :] = jnp.where(early, start_ref[hours - 1 : hours, :], start_ref[0:1, :])
    edge_ref[at + 1 : at + 2, :] = jnp.where(
        early, start_ref[hours - 2 : hours - 1, :], start_ref[1:2, :]
    )


def first_kernel(
    ptdf_ref,
    own_inject_ref,
    demand_ref,
    hedge_ref,
    start_ref,
    edge_ref,
    cost_ref,
    max_ref,
    limit_ref,
    line_max_ref,
    gen_ref,
    base_ref,
    hedged_ref,
    sums_ref,
    inject_ref,
    over_ref,
    back_ref,
    padded_ref,
    excess_ref,
    ramp_ref,
):
    hours, buses = start_ref.shape
    width = demand_ref.shape[0]
    scens = width // hours
    at = 2 * scens
    early = lax.axis_index("hour") == 0
    first_hour = lax.axis_index("hour") * hours
    beyond = edge_ref[at : at + 1, :]
    limit = limit_ref[...]
    cost = cost_ref[...]
    top = max_ref[...]

    inject_ref[0:width, :] = own_inject_ref[0:width, :]
    inject_ref[width : width + scens, :] = (beyond - edge_ref[0:scens, :]).astype(jnp.bfloat16)
    back_ref[...] = line_work(inject_ref, ptdf_ref, line_max_ref, over_ref)
    write_ramp(start_ref, beyond, limit, first_hour, padded_ref, excess_ref, ramp_ref)

    def step(mean, hedge, back, ramp):
        grad = cost + back + (mean - mean + hedge) + ramp
        gen = jnp.clip(mean - STEP_SIZE * grad, 0.0, top)
        return gen, gen + hedge

    for h in range(hours):
        part = slice(h * scens, (h + 1) * scens)
        mean = start_ref[h : h + 1, :]
        gen, hedged = step(mean, hedge_ref[part, :], back_ref[part, :], ramp_ref[h : h + 1, :])
        gen_ref[part, :] = gen
        base_ref[part, :] = gen - demand_ref[part, :]
        hedged_ref[part, :] = hedged
        put_row(sums_ref, hours + 1, h, jnp.sum(hedged, axis=0, keepdims=True))
    near = jnp.where(early, start_ref[hours - 1 : hours, :], start_ref[0:1, :])
    ramp = excess(beyond - near, limit) + excess(beyond - edge_ref[at + 1 : at + 2, :], limit)
    _, hedged = step(beyond, edge_ref[scens:at, :], back_ref[width : width + scens, :], ramp)
    put_row(sums_ref, hours + 1, hours, jnp.sum(hedged, axis=0, keepdims=True))
    clear_rest(sums_ref, (hours + 1) * (buses // LANES))


def tie_kernel(blocks, relayed, base_ref, spread_ref, rows_ref, weight_ref, own_ref, *refs):
    peer_refs, refs = refs[:blocks], refs[blocks:]
    *next_refs, inject_ref, mine_ref, theirs_ref = refs
    width = base_ref.shape[0]

    weight = jnp.concatenate([weight_ref[...], weight_ref[...]], axis=1)
    own = own_ref[...]
    peer = jnp.concatenate([unfold(ref[...]) for ref in peer_refs], axis=0)
    est_mine = weight * own
    est_theirs = -weight * peer
    flow = (est_mine + est_theirs) * 0.5
    dual_mine = est_mine - flow
    dual_theirs = est_theirs - flow
    spread = spread_ref[...]
    add = lax.dot_general(
        split_3(flow),
        jnp.concatenate([spread, spread, spread], axis=0),
        CONTRACT_FIRST,
        preferred_element_type=jnp.float32,
    )
    inject_ref[0:width, :] = (base_ref[...] + add[0:width, :]).astype(jnp.bfloat16)
    repeat_rest(inject_ref, width)

    own_next = lax.dot_general(
        rows_ref[...], inject_ref[...], CONTRACT_LAST, preferred_element_type=jnp.float32
    )
    parts = [own_next[i * CAP : (i + 1) * CAP, :] for i in range(blocks)]
    if relayed:
        far_ref, near_ref = next_refs
        flip_3, flip_2 = by_flips(lax.axis_index("area"), parts[0], parts[1])
        far_ref[...] = fold(jnp.concatenate([flip_2, flip_3], axis=0))
        near_ref[...] = parts[2]
    else:
        for ref, part in zip(next_refs, parts):
            ref[...] = fold(part)
    mine_ref[...] = weight * (own_next - peer) + dual_mine
    theirs_ref[...] = weight * own + dual_theirs


def second_kernel(
    terms,
    scen_total,
    ptdf_ref,
    inject_ref,
    gen_ref,
    hedged_ref,
    cost_ref,
    max_ref,
    limit_ref,
    line_max_ref,
    *refs,
):
    sum_refs, refs = refs[:terms], refs[terms:]
    (hedged_out_ref, sums_out_ref, over_ref, back_ref, mean_ref, padded_ref, excess_ref, ramp_ref) = refs
    hours, buses = ramp_ref.shape
    width = back_ref.shape[0]
    scens = width // hours
    first_hour = lax.axis_index("hour") * hours

    back_ref[...] = line_work(inject_ref.at[0:width, :], ptdf_ref, line_max_ref, over_ref)
    agree(mean_ref, sum_refs, hours + 1, scen_total)
    write_ramp(
        mean_ref, mean_ref[hours : hours + 1, :], limit_ref[...], first_hour, padded_ref, excess_ref, ramp_ref
    )
    cost = cost_ref[...]
    top = max_ref[...]
    for h in range(hours):
        part = slice(h * scens, (h + 1) * scens)
        mean = mean_ref[h : h + 1, :]
        gen = gen_ref[part, :]
        hedge = hedged_ref[part, :] - mean
        grad = cost + back_ref[part, :] + (gen - mean + hedge) + ramp_ref[h : h + 1, :]
        gen = jnp.clip(gen - STEP_SIZE * grad, 0.0, top)
        hedged = gen + hedge
        hedged_out_ref[part, :] = hedged
        put_row(sums_out_ref, hours, h, jnp.sum(hedged, axis=0, keepdims=True))
    clear_rest(sums_out_ref, hours * (buses // LANES))


def relay_kernel(near_ref, far_ref, both_ref):
    low = lax.broadcasted_iota(jnp.int32, (CAP, LANES), 1) < LANES // 2
    both_ref[0:CAP, :] = near_ref[:, 0:LANES]
    both_ref[CAP : 2 * CAP, :] = far_ref[CAP : 2 * CAP, :]
    both_ref[2 * CAP :, :] = jnp.where(low, near_ref[:, LANES:], far_ref[2 * CAP :, :])


def agree_kernel(scen_total, hedged_ref, *refs):
    sum_refs, (mean_ref, hedge_ref) = refs[:-2], refs[-2:]
    hours = mean_ref.shape[0]
    scens = hedged_ref.shape[0] // hours
    agree(mean_ref, sum_refs, hours, scen_total)
    for h in range(hours):
        part = slice(h * scens, (h + 1) * scens)
        hedge_ref[part, :] = hedged_ref[part, :] - mean_ref[h : h + 1, :]


def last_kernel(blocks, relayed, partner_of, hedge_ref, mean_ref, *refs):
    *peer_refs, weight_ref, mine_ref, theirs_ref = refs[:-6]
    hedge_out, mean_out, tie_out, tie_ref, placed_ref, copy_sems = refs[-6:]
    copies = []

    def send(src, dst):
        copies.append(pltpu.make_async_copy(src, dst, copy_sems.at[len(copies)]))
        copies[-1].start()

    send(hedge_ref, hedge_out)
    send(mean_ref, mean_out)
    here = lax.axis_index("area")
    placed_ref[...] = jnp.zeros_like(placed_ref)
    if relayed:
        far, both = (unfold(ref[...]) for ref in peer_refs)
        peers = [*by_flips(here, both[CAP:, :], far[0:CAP, :]), both[0:CAP, :]]
    else:
        peers = [unfold(ref[...]) for ref in peer_refs]
    for i in range(blocks):
        slots = slice(i * CAP, (i + 1) * CAP)
        weight = jnp.concatenate([weight_ref[slots, :], weight_ref[slots, :]], axis=1)
        flow = (mine_ref[slots, :] + (theirs_ref[slots, :] - weight * peers[i])) * 0.5
        low, _, block, in_reach = block_facts(here, partner_of(here, i))
        first = block * CAP + jnp.where(low, 0, REACH * CAP)

        @pl.when(in_reach)
        def _():
            placed_ref[pl.ds(pl.multiple_of(first, CAP), CAP), :] = flow

    for first in range(0, tie_ref.shape[0], LANES):
        count = min(LANES, tie_ref.shape[0] - first)
        tie_ref[first : first + count, :] = jnp.transpose(placed_ref[:, first : first + LANES])[0:count, :]
        send(tie_ref.at[pl.ds(first, count)], tie_out.at[pl.ds(first, count)])
    for copy in copies:
        copy.wait()


def call(kernel, name, args, outs, scratch, flops, in_place=(), outs_in_place=False):
    size = sum(x.size * x.dtype.itemsize for x in list(args) + list(outs))
    return pl.pallas_call(
        kernel,
        name=name,
        out_shape=outs,
        in_specs=[ANY if i in in_place else VMEM for i in range(len(args))],
        out_specs=[ANY if outs_in_place else VMEM] * len(outs),
        scratch_shapes=scratch,
        compiler_params=pltpu.CompilerParams(vmem_limit_bytes=32 * 1024 * 1024),
        cost_estimate=pl.CostEstimate(flops=flops, bytes_accessed=size, transcendentals=0),
    )(*(pltpu.with_memory_space_constraint(x, pltpu.HBM) if i in in_place else x for i, x in enumerate(args)))


def per_device(
    ptdf,
    angle_sens,
    demand,
    gen_start,
    hedge_dual,
    gen_cost,
    gen_max,
    gen_ramp,
    line_max,
    tie_count,
    tie_low_bus,
    tie_high_bus,
    tie_susc,
):
    hours, scens, buses = demand.shape
    lines = ptdf.shape[0]
    width = hours * scens
    areas = lax.axis_size("area")
    n_scen = lax.axis_size("scen")
    assert lax.axis_size("hour") == 2 and hours >= 2
    assert width % LANES == LANES // 2 and width < 2 * LANES
    columns = 2 * LANES
    block_rows = CAP * 3 // 2
    scen_total = scens * n_scen
    blocks, partner_of, from_partners = partner_plan(areas)
    slots = blocks * CAP
    pieces = buses // LANES
    sum_rows = 8 * pl.cdiv((hours + 1) * pieces, 8)
    f32, bf16 = jnp.float32, jnp.bfloat16

    def shape(*dims, dtype=f32):
        return jax.ShapeDtypeStruct(dims, dtype)

    def over_scens(sums):
        if n_scen == 2:
            return [sums, lax.ppermute(sums, "scen", [(0, 1), (1, 0)])]
        return [lax.psum(sums, "scen")]

    work = 4 * width * lines * buses

    def step_scratch(rows):
        return [
            pltpu.VMEM((rows, buses), bf16),
            pltpu.VMEM((rows, lines), bf16),
            pltpu.VMEM((rows, buses), f32),
        ]

    ramp_scratch = [
        pltpu.VMEM((hours + 4, buses), f32),
        pltpu.VMEM((hours + 4, buses), f32),
        pltpu.VMEM((hours, buses), f32),
    ]
    tables = (tie_count, tie_low_bus, tie_high_bus, tie_susc)
    vectors = [x.reshape(1, -1) for x in (gen_cost, gen_max, gen_ramp, line_max)]
    hedge = hedge_dual.reshape(width, buses)
    load, edge_hedge, start, *vectors, onehot, spread, weight = call(
        functools.partial(table_kernel, blocks, partner_of),
        "tables",
        (demand.reshape(width, buses), hedge, gen_start, *tables, *vectors),
        [
            shape(width, buses),
            shape(scens, buses),
            shape(hours, buses),
            *(shape(*x.shape) for x in vectors),
            shape(slots, buses, dtype=bf16),
            shape(slots, buses, dtype=bf16),
            shape(slots, LANES),
        ],
        [pltpu.VMEM(x.shape, x.dtype) for x in tables] + [pltpu.SemaphoreType.DMA((11,))],
        BETWEEN,
        range(11),
    )
    (edge,) = call(edge_kernel, "edge", (load, edge_hedge, start), [shape(2 * scens + 8, buses)], [], width)
    *sent, own, inject, rows = call(
        functools.partial(angle_kernel, blocks),
        "angles",
        (angle_sens, load, start, onehot),
        [shape(block_rows, LANES)] * blocks
        + [shape(slots, columns), shape(columns, buses, dtype=bf16), shape(slots, buses, dtype=bf16)],
        [],
        BETWEEN,
    )
    edge = lax.ppermute(edge, "hour", [(0, 1), (1, 0)])
    peer = from_partners(sent)
    gen, base, hedged, sums = call(
        first_kernel,
        "first",
        (ptdf, inject, load, hedge, start, edge, *vectors),
        [
            shape(width, buses),
            shape(width, buses),
            shape(width, buses),
            shape(sum_rows, LANES),
        ],
        step_scratch(width + scens) + ramp_scratch,
        work,
    )
    sum_terms = over_scens(sums)
    terms = len(sum_terms)
    relayed = areas == 4
    tied = call(
        functools.partial(tie_kernel, blocks, relayed),
        "ties",
        (base, spread, rows, weight, own, *peer),
        (
            [shape(2 * block_rows, LANES), shape(CAP, columns)]
            if relayed
            else [shape(block_rows, LANES)] * blocks
        )
        + [shape(columns, buses, dtype=bf16), shape(slots, columns), shape(slots, columns)],
        [],
        BETWEEN,
    )
    *sent, inject, mine, theirs = tied
    hedged, sums = call(
        functools.partial(second_kernel, terms, scen_total),
        "second",
        (ptdf, inject, gen, hedged, *vectors, *sum_terms),
        [shape(width, buses), shape(sum_rows, LANES)],
        step_scratch(width)[1:] + [pltpu.VMEM((8 * pl.cdiv(hours + 1, 8), buses), f32)] + ramp_scratch,
        work,
    )
    sum_terms = over_scens(sums)
    if relayed:
        far, near = sent
        far = lax.ppermute(far, "area", [(a, a ^ 2) for a in range(areas)])
        arrived, _ = lax.optimization_barrier((far, sums))
        (both,) = call(relay_kernel, "relay", (near, arrived), [shape(2 * block_rows, LANES)], [], BETWEEN)
        peer = [far, lax.ppermute(both, "area", [(a, a ^ 1) for a in range(areas)])]
    else:
        peer = from_partners(sent)
    gen_mean, hedge = call(
        functools.partial(agree_kernel, scen_total),
        "agree",
        (hedged, *sum_terms),
        [shape(hours, buses), shape(width, buses)],
        [],
        BETWEEN,
    )
    tie_shape = shape(width, 2 * REACH * CAP)
    hedge, gen_mean, tie_flow = call(
        functools.partial(last_kernel, blocks, relayed, partner_of),
        "last",
        (hedge, gen_mean, *peer, weight, mine, theirs),
        [shape(width, buses), shape(hours, buses), tie_shape],
        [
            pltpu.VMEM(tie_shape.shape, f32),
            pltpu.VMEM((2 * REACH * CAP, columns), f32),
            pltpu.SemaphoreType.DMA((2 + columns // LANES,)),
        ],
        slots * columns,
        outs_in_place=True,
    )
    return (
        gen_mean,
        hedge.reshape(hours, scens, buses),
        tie_flow.reshape(hours, scens, 2 * REACH * CAP),
    )


def solution(mesh):
    return jax.shard_map(
        per_device,
        mesh=mesh,
        in_specs=(
            P(("group", "area"), None),
            P(("group", "area"), None),
            P(("group", "hour"), "scen", "area"),
            P(("group", "hour"), "area"),
            P(("group", "hour"), "scen", "area"),
            P(("group", "area")),
            P(("group", "area")),
            P(("group", "area")),
            P(("group", "area")),
            P("group", None),
            P("group", None),
            P("group", None),
            P("group", None),
        ),
        out_specs=(
            P(("group", "hour"), "area"),
            P(("group", "hour"), "scen", "area"),
            P(("group", "hour"), "scen", "area"),
        ),
        check_vma=False,
    )
```

```python
import functools

import jax
import jax.numpy as jnp
from jax import lax
from jax.experimental import pallas as pl
from jax.experimental.pallas import tpu as pltpu
from jax.sharding import PartitionSpec as P

HOURS = 24
REACH = 4
CAP = 16

STEP_SIZE = 0.5
LINE_CHUNK = 512
LANES = 128
BETWEEN = 20_000_000_000

CONTRACT_LAST = (((1,), (1,)), ((), ()))
CONTRACT_FIRST = (((0,), (0,)), ((), ()))
VMEM = pl.BlockSpec(memory_space=pltpu.VMEM)
ANY = pl.BlockSpec(memory_space=pltpu.HBM)


TARGETS = ((3, 2, 0, 1), (2, 3, 1, 0), (1, 0, 3, 2))


def partner_plan(areas):
    if areas == 4:

        def partner_of(here, i):
            return sum(jnp.where(here == a, target, 0) for a, target in enumerate(TARGETS[i]))

        def by_target(parts):
            out, back, pair = (
                lax.ppermute(part, "area", list(enumerate(target))) for part, target in zip(parts, TARGETS)
            )
            return [back, out, pair]

        return len(TARGETS), partner_of, by_target
    reach = min(REACH, areas - 1)
    shifts = sorted({s % areas for d in range(1, reach + 1) for s in (d, -d)})

    def by_shift(parts):
        sent = [
            lax.ppermute(part, "area", [(a, (a + s) % areas) for a in range(areas)])
            for part, s in zip(parts, shifts)
        ]
        return [sent[shifts.index(areas - s)] for s in shifts]

    return len(shifts), lambda here, i: lax.rem(here + shifts[i], areas), by_shift


def by_flips(here, flip_3, flip_2):
    return jnp.where(here < 2, flip_3, flip_2), jnp.where(here < 2, flip_2, flip_3)


def block_facts(here, partner):
    low = partner > here
    distance = jnp.abs(partner - here)
    block = jnp.clip(distance - 1, 0, REACH - 1)
    in_reach = (distance >= 1) & (distance <= REACH)
    return low, jnp.minimum(here, partner), block, in_reach


def fold(x):
    half = x.shape[0] // 2
    low = lax.broadcasted_iota(jnp.int32, (half, LANES), 1) < LANES // 2
    shared = jnp.where(low, x[0:half, LANES : 2 * LANES], x[half:, LANES : 2 * LANES])
    return jnp.concatenate([x[:, 0:LANES], shared], axis=0)


def unfold(packed):
    rows = 2 * packed.shape[0] // 3
    shared = packed[rows:, :]
    low = lax.broadcasted_iota(jnp.int32, shared.shape, 1) < LANES // 2
    turned = pltpu.roll(shared, LANES // 2, 1)
    rest = jnp.concatenate([jnp.where(low, shared, turned), jnp.where(low, turned, shared)], axis=0)
    return jnp.concatenate([packed[0:rows, :], rest], axis=1)


def repeat_rest(inject_ref, width):
    inject_ref[width:, :] = inject_ref[width - LANES // 2 : width, :]


def split_3(x):
    high = x.astype(jnp.bfloat16)
    rest = x - high.astype(jnp.float32)
    middle = rest.astype(jnp.bfloat16)
    rest = rest - middle.astype(jnp.float32)
    return jnp.concatenate([high, middle, rest.astype(jnp.bfloat16)], axis=0)


def put_row(packed_ref, hours, h, row):
    for j in range(row.shape[1] // LANES):
        packed_ref[j * hours + h : j * hours + h + 1, :] = row[:, j * LANES : (j + 1) * LANES]


def clear_rest(packed_ref, used):
    rows = packed_ref.shape[0]
    if used < rows:
        packed_ref[used:, :] = jnp.zeros((rows - used, LANES), jnp.float32)


def agree(mean_ref, sum_refs, hours, scen_total):
    for j in range(mean_ref.shape[1] // LANES):
        parts = [ref[j * hours : (j + 1) * hours, :] for ref in sum_refs]
        mean_ref[0:hours, j * LANES : (j + 1) * LANES] = functools.reduce(jnp.add, parts) / scen_total


def excess(diffs, limit):
    return diffs - jnp.clip(diffs, -limit, limit)


def write_ramp(mean_ref, beyond, limit, first_hour, padded_ref, excess_ref, ramp_ref):
    hours = ramp_ref.shape[0]
    padded_ref[0:1, :] = beyond
    padded_ref[1 : hours + 1, :] = mean_ref[0:hours, :]
    padded_ref[hours + 1 : hours + 2, :] = beyond
    diffs = padded_ref[1 : hours + 2, :] - padded_ref[0 : hours + 1, :]
    ids = first_hour + lax.broadcasted_iota(jnp.int32, diffs.shape, 0)
    valid = (ids >= 1) & (ids <= HOURS - 1)
    excess_ref[0 : hours + 1, :] = jnp.where(valid, excess(diffs, limit), 0.0)
    ramp_ref[...] = excess_ref[0:hours, :] - excess_ref[1 : hours + 1, :]


def line_work(inject_ref, ptdf_ref, line_max_ref):
    inject = inject_ref[...]
    lines = ptdf_ref.shape[0]
    back = 0.0
    for at in range(0, lines, LINE_CHUNK):
        part = slice(at, at + LINE_CHUNK)
        weights = ptdf_ref[part, :]
        flows = lax.dot_general(inject, weights, CONTRACT_LAST, preferred_element_type=jnp.float32)
        limit = line_max_ref[:, part]
        over = (flows - jnp.clip(flows, -limit, limit)).astype(jnp.bfloat16)
        back = back + jnp.dot(over, weights, preferred_element_type=jnp.float32)
    return back


def table_kernel(
    blocks,
    partner_of,
    hedge_in,
    start_in,
    count_in,
    low_bus_in,
    high_bus_in,
    susc_in,
    cost_in,
    max_in,
    limit_in,
    line_max_in,
    edge_hedge_ref,
    start_ref,
    cost_ref,
    max_ref,
    limit_ref,
    line_max_ref,
    onehot_ref,
    spread_ref,
    weight_ref,
    count_ref,
    low_bus_ref,
    high_bus_ref,
    susc_ref,
    copy_sems,
):
    hours, buses = start_ref.shape
    scens = hedge_in.shape[0] // hours
    here = lax.axis_index("area")
    last = (hours - 1) * scens
    edge_rows = pl.ds(pl.multiple_of((1 - lax.axis_index("hour")) * last, scens), scens)

    pairs = (
        (count_in, count_ref),
        (low_bus_in, low_bus_ref),
        (high_bus_in, high_bus_ref),
        (susc_in, susc_ref),
        (start_in, start_ref),
        (hedge_in.at[edge_rows], edge_hedge_ref),
        (cost_in, cost_ref),
        (max_in, max_ref),
        (limit_in, limit_ref),
        (line_max_in, line_max_ref),
    )
    copies = [pltpu.make_async_copy(src, dst, copy_sems.at[i]) for i, (src, dst) in enumerate(pairs)]
    for copy in copies:
        copy.start()
    for copy in copies[:4]:
        copy.wait()
    for i in range(blocks):
        partner = partner_of(here, i)
        low, row, block, in_reach = block_facts(here, partner)
        slots = slice(i * CAP, (i + 1) * CAP)
        pick = lax.broadcasted_iota(jnp.int32, (CAP, REACH * CAP), 1) == (
            block * CAP + lax.broadcasted_iota(jnp.int32, (CAP, REACH * CAP), 0)
        )
        table_row = pl.ds(row, 1)
        bus_row = jnp.where(low, low_bus_ref[table_row, :], high_bus_ref[table_row, :])
        bus = jnp.sum(jnp.where(pick, bus_row.astype(jnp.float32), 0.0), axis=1, keepdims=True)
        susc = jnp.sum(jnp.where(pick, susc_ref[table_row, :], 0.0), axis=1, keepdims=True)
        count_row = count_ref[table_row, :].astype(jnp.float32)
        is_block = lax.broadcasted_iota(jnp.int32, (CAP, REACH), 1) == block
        count = jnp.sum(jnp.where(is_block, count_row, 0.0), axis=1, keepdims=True)
        slot_ids = lax.broadcasted_iota(jnp.int32, (CAP, 1), 0).astype(jnp.float32)
        live = jnp.where((slot_ids < count) & in_reach, 1.0, 0.0)
        sign = jnp.where(low, 1.0, -1.0)
        bus_ids = lax.broadcasted_iota(jnp.int32, (CAP, buses), 1).astype(jnp.float32)
        onehot = jnp.where(bus_ids == bus, live, 0.0)
        onehot_ref[slots, :] = onehot.astype(jnp.bfloat16)
        spread_ref[slots, :] = (-sign * onehot).astype(jnp.bfloat16)
        weight_ref[slots, :] = jnp.broadcast_to(live * sign * susc, (CAP, 128))

    for copy in copies[4:]:
        copy.wait()


def row_kernel(sens_ref, onehot_ref, rows_ref):
    rows = jnp.dot(onehot_ref[...], sens_ref[...], preferred_element_type=jnp.float32)
    rows_ref[...] = rows.astype(jnp.bfloat16)


def angle_kernel(blocks, demand_ref, start_ref, rows_ref, *refs):
    sent_refs, (own_ref, inject_ref) = refs[:blocks], refs[blocks:]
    hours = start_ref.shape[0]
    scens = demand_ref.shape[0] // hours
    for h in range(hours):
        part = slice(h * scens, (h + 1) * scens)
        inject_ref[part, :] = (start_ref[h : h + 1, :] - demand_ref[part, :]).astype(jnp.bfloat16)
    repeat_rest(inject_ref, hours * scens)
    own = lax.dot_general(
        rows_ref[...], inject_ref[...], CONTRACT_LAST, preferred_element_type=jnp.float32
    )
    own_ref[...] = own
    for i in range(blocks):
        sent_refs[i][...] = fold(own[i * CAP : (i + 1) * CAP, :])


def edge_kernel(demand_ref, edge_hedge_ref, start_ref, edge_ref):
    scens = edge_hedge_ref.shape[0]
    hours = start_ref.shape[0]
    early = lax.axis_index("hour") == 0
    last = (hours - 1) * scens
    at = 2 * scens
    edge_ref[0:scens, :] = jnp.where(early, demand_ref[last:, :], demand_ref[0:scens, :])
    edge_ref[scens:at, :] = edge_hedge_ref[...]
    edge_ref[at : at + 1, :] = jnp.where(early, start_ref[hours - 1 : hours, :], start_ref[0:1, :])
    edge_ref[at + 1 : at + 2, :] = jnp.where(
        early, start_ref[hours - 2 : hours - 1, :], start_ref[1:2, :]
    )


def first_kernel(
    ptdf_ref,
    own_inject_ref,
    demand_ref,
    hedge_ref,
    start_ref,
    edge_ref,
    cost_ref,
    max_ref,
    limit_ref,
    line_max_ref,
    gen_ref,
    base_ref,
    hedged_ref,
    sums_ref,
    inject_ref,
    back_ref,
    padded_ref,
    excess_ref,
    ramp_ref,
):
    hours, buses = start_ref.shape
    width = demand_ref.shape[0]
    scens = width // hours
    at = 2 * scens
    early = lax.axis_index("hour") == 0
    first_hour = lax.axis_index("hour") * hours
    beyond = edge_ref[at : at + 1, :]
    limit = limit_ref[...]
    cost = cost_ref[...]
    top = max_ref[...]

    inject_ref[0:width, :] = own_inject_ref[0:width, :]
    inject_ref[width : width + scens, :] = (beyond - edge_ref[0:scens, :]).astype(jnp.bfloat16)
    back_ref[...] = line_work(inject_ref, ptdf_ref, line_max_ref)
    write_ramp(start_ref, beyond, limit, first_hour, padded_ref, excess_ref, ramp_ref)

    def step(mean, hedge, back, ramp):
        grad = cost + back + (mean - mean + hedge) + ramp
        gen = jnp.clip(mean - STEP_SIZE * grad, 0.0, top)
        return gen, gen + hedge

    for h in range(hours):
        part = slice(h * scens, (h + 1) * scens)
        mean = start_ref[h : h + 1, :]
        gen, hedged = step(mean, hedge_ref[part, :], back_ref[part, :], ramp_ref[h : h + 1, :])
        gen_ref[part, :] = gen
        base_ref[part, :] = gen - demand_ref[part, :]
        hedged_ref[part, :] = hedged
        put_row(sums_ref, hours + 1, h, jnp.sum(hedged, axis=0, keepdims=True))
    near = jnp.where(early, start_ref[hours - 1 : hours, :], start_ref[0:1, :])
    ramp = excess(beyond - near, limit) + excess(beyond - edge_ref[at + 1 : at + 2, :], limit)
    _, hedged = step(beyond, edge_ref[scens:at, :], back_ref[width : width + scens, :], ramp)
    put_row(sums_ref, hours + 1, hours, jnp.sum(hedged, axis=0, keepdims=True))
    clear_rest(sums_ref, (hours + 1) * (buses // LANES))


def tie_kernel(blocks, relayed, base_ref, spread_ref, rows_ref, weight_ref, own_ref, *refs):
    peer_refs, refs = refs[:blocks], refs[blocks:]
    *next_refs, inject_ref, mine_ref, theirs_ref = refs
    width = base_ref.shape[0]

    weight = jnp.concatenate([weight_ref[...], weight_ref[...]], axis=1)
    own = own_ref[...]
    peer = jnp.concatenate([unfold(ref[...]) for ref in peer_refs], axis=0)
    est_mine = weight * own
    est_theirs = -weight * peer
    flow = (est_mine + est_theirs) * 0.5
    dual_mine = est_mine - flow
    dual_theirs = est_theirs - flow
    spread = spread_ref[...]
    add = lax.dot_general(
        split_3(flow),
        jnp.concatenate([spread, spread, spread], axis=0),
        CONTRACT_FIRST,
        preferred_element_type=jnp.float32,
    )
    inject_ref[0:width, :] = (base_ref[...] + add[0:width, :]).astype(jnp.bfloat16)
    repeat_rest(inject_ref, width)

    own_next = lax.dot_general(
        rows_ref[...], inject_ref[...], CONTRACT_LAST, preferred_element_type=jnp.float32
    )
    parts = [own_next[i * CAP : (i + 1) * CAP, :] for i in range(blocks)]
    if relayed:
        far_ref, near_ref = next_refs
        flip_3, flip_2 = by_flips(lax.axis_index("area"), parts[0], parts[1])
        far_ref[...] = fold(jnp.concatenate([flip_2, flip_3], axis=0))
        near_ref[...] = parts[2]
    else:
        for ref, part in zip(next_refs, parts):
            ref[...] = fold(part)
    mine_ref[...] = weight * (own_next - peer) + dual_mine
    theirs_ref[...] = weight * own + dual_theirs


def second_kernel(
    terms,
    scen_total,
    ptdf_ref,
    inject_ref,
    gen_ref,
    hedged_ref,
    cost_ref,
    max_ref,
    limit_ref,
    line_max_ref,
    *refs,
):
    sum_refs, refs = refs[:terms], refs[terms:]
    (hedged_out_ref, sums_out_ref, back_ref, mean_ref, padded_ref, excess_ref, ramp_ref) = refs
    hours, buses = ramp_ref.shape
    width = back_ref.shape[0]
    scens = width // hours
    first_hour = lax.axis_index("hour") * hours

    back_ref[...] = line_work(inject_ref.at[0:width, :], ptdf_ref, line_max_ref)
    agree(mean_ref, sum_refs, hours + 1, scen_total)
    write_ramp(
        mean_ref, mean_ref[hours : hours + 1, :], limit_ref[...], first_hour, padded_ref, excess_ref, ramp_ref
    )
    cost = cost_ref[...]
    top = max_ref[...]
    for h in range(hours):
        part = slice(h * scens, (h + 1) * scens)
        mean = mean_ref[h : h + 1, :]
        gen = gen_ref[part, :]
        hedge = hedged_ref[part, :] - mean
        grad = cost + back_ref[part, :] + (gen - mean + hedge) + ramp_ref[h : h + 1, :]
        gen = jnp.clip(gen - STEP_SIZE * grad, 0.0, top)
        hedged = gen + hedge
        hedged_out_ref[part, :] = hedged
        put_row(sums_out_ref, hours, h, jnp.sum(hedged, axis=0, keepdims=True))
    clear_rest(sums_out_ref, hours * (buses // LANES))


def relay_kernel(near_ref, far_ref, both_ref):
    low = lax.broadcasted_iota(jnp.int32, (CAP, LANES), 1) < LANES // 2
    both_ref[0:CAP, :] = near_ref[:, 0:LANES]
    both_ref[CAP : 2 * CAP, :] = far_ref[CAP : 2 * CAP, :]
    both_ref[2 * CAP :, :] = jnp.where(low, near_ref[:, LANES:], far_ref[2 * CAP :, :])


def agree_kernel(scen_total, hedged_ref, *refs):
    sum_refs, (mean_ref, hedge_ref) = refs[:-2], refs[-2:]
    hours = mean_ref.shape[0]
    scens = hedged_ref.shape[0] // hours
    agree(mean_ref, sum_refs, hours, scen_total)
    for h in range(hours):
        part = slice(h * scens, (h + 1) * scens)
        hedge_ref[part, :] = hedged_ref[part, :] - mean_ref[h : h + 1, :]


def last_kernel(blocks, relayed, partner_of, hedge_ref, mean_ref, *refs):
    *peer_refs, weight_ref, mine_ref, theirs_ref = refs[:-6]
    hedge_out, mean_out, tie_out, tie_ref, placed_ref, copy_sems = refs[-6:]
    copies = []

    def send(src, dst):
        copies.append(pltpu.make_async_copy(src, dst, copy_sems.at[len(copies)]))
        copies[-1].start()

    send(hedge_ref, hedge_out)
    send(mean_ref, mean_out)
    here = lax.axis_index("area")
    placed_ref[...] = jnp.zeros_like(placed_ref)
    if relayed:
        far, both = (unfold(ref[...]) for ref in peer_refs)
        peers = [*by_flips(here, both[CAP:, :], far[0:CAP, :]), both[0:CAP, :]]
    else:
        peers = [unfold(ref[...]) for ref in peer_refs]
    for i in range(blocks):
        slots = slice(i * CAP, (i + 1) * CAP)
        weight = jnp.concatenate([weight_ref[slots, :], weight_ref[slots, :]], axis=1)
        flow = (mine_ref[slots, :] + (theirs_ref[slots, :] - weight * peers[i])) * 0.5
        low, _, block, in_reach = block_facts(here, partner_of(here, i))
        first = block * CAP + jnp.where(low, 0, REACH * CAP)

        @pl.when(in_reach)
        def _():
            placed_ref[pl.ds(pl.multiple_of(first, CAP), CAP), :] = flow

    for first in range(0, tie_ref.shape[0], LANES):
        count = min(LANES, tie_ref.shape[0] - first)
        tie_ref[first : first + count, :] = jnp.transpose(placed_ref[:, first : first + LANES])[0:count, :]
        send(tie_ref.at[pl.ds(first, count)], tie_out.at[pl.ds(first, count)])
    for copy in copies:
        copy.wait()


def call(kernel, name, args, outs, scratch, flops, in_place=(), outs_in_place=False):
    size = sum(x.size * x.dtype.itemsize for x in list(args) + list(outs))
    return pl.pallas_call(
        kernel,
        name=name,
        out_shape=outs,
        in_specs=[ANY if i in in_place else VMEM for i in range(len(args))],
        out_specs=[ANY if outs_in_place else VMEM] * len(outs),
        scratch_shapes=scratch,
        compiler_params=pltpu.CompilerParams(vmem_limit_bytes=32 * 1024 * 1024),
        cost_estimate=pl.CostEstimate(flops=flops, bytes_accessed=size, transcendentals=0),
    )(*(pltpu.with_memory_space_constraint(x, pltpu.HBM) if i in in_place else x for i, x in enumerate(args)))


def per_device(
    ptdf,
    angle_sens,
    demand,
    gen_start,
    hedge_dual,
    gen_cost,
    gen_max,
    gen_ramp,
    line_max,
    tie_count,
    tie_low_bus,
    tie_high_bus,
    tie_susc,
):
    hours, scens, buses = demand.shape
    lines = ptdf.shape[0]
    width = hours * scens
    areas = lax.axis_size("area")
    n_scen = lax.axis_size("scen")
    assert lax.axis_size("hour") == 2 and hours >= 2
    assert width % LANES == LANES // 2 and width < 2 * LANES
    columns = 2 * LANES
    block_rows = CAP * 3 // 2
    scen_total = scens * n_scen
    blocks, partner_of, from_partners = partner_plan(areas)
    slots = blocks * CAP
    pieces = buses // LANES
    sum_rows = 8 * pl.cdiv((hours + 1) * pieces, 8)
    f32, bf16 = jnp.float32, jnp.bfloat16

    def shape(*dims, dtype=f32):
        return jax.ShapeDtypeStruct(dims, dtype)

    def over_scens(sums):
        if n_scen == 2:
            return [sums, lax.ppermute(sums, "scen", [(0, 1), (1, 0)])]
        return [lax.psum(sums, "scen")]

    work = 4 * width * lines * buses

    def step_scratch(rows):
        return [
            pltpu.VMEM((rows, buses), bf16),
            pltpu.VMEM((rows, buses), f32),
        ]

    ramp_scratch = [
        pltpu.VMEM((hours + 4, buses), f32),
        pltpu.VMEM((hours + 4, buses), f32),
        pltpu.VMEM((hours, buses), f32),
    ]
    tables = (tie_count, tie_low_bus, tie_high_bus, tie_susc)
    vectors = [x.reshape(1, -1) for x in (gen_cost, gen_max, gen_ramp, line_max)]
    load = demand.reshape(width, buses)
    hedge = hedge_dual.reshape(width, buses)
    edge_hedge, start, *vectors, onehot, spread, weight = call(
        functools.partial(table_kernel, blocks, partner_of),
        "tables",
        (hedge, gen_start, *tables, *vectors),
        [
            shape(scens, buses),
            shape(hours, buses),
            *(shape(*x.shape) for x in vectors),
            shape(slots, buses, dtype=bf16),
            shape(slots, buses, dtype=bf16),
            shape(slots, LANES),
        ],
        [pltpu.VMEM(x.shape, x.dtype) for x in tables] + [pltpu.SemaphoreType.DMA((10,))],
        BETWEEN,
        range(10),
    )
    (rows,) = call(
        row_kernel,
        "rows",
        (angle_sens, onehot),
        [shape(slots, buses, dtype=bf16)],
        [],
        2 * slots * buses * buses,
    )
    *sent, own, inject = call(
        functools.partial(angle_kernel, blocks),
        "angles",
        (load, start, rows),
        [shape(block_rows, LANES)] * blocks
        + [shape(slots, columns), shape(columns, buses, dtype=bf16)],
        [],
        2 * slots * buses * width,
    )
    edge_hedge, own = lax.optimization_barrier((edge_hedge, own))
    (edge,) = call(edge_kernel, "edge", (load, edge_hedge, start), [shape(2 * scens + 8, buses)], [], BETWEEN)
    edge = lax.ppermute(edge, "hour", [(0, 1), (1, 0)])
    peer = from_partners(sent)
    gen, base, hedged, sums = call(
        first_kernel,
        "first",
        (ptdf, inject, load, hedge, start, edge, *vectors),
        [
            shape(width, buses),
            shape(width, buses),
            shape(width, buses),
            shape(sum_rows, LANES),
        ],
        step_scratch(width + scens) + ramp_scratch,
        work,
    )
    sum_terms = over_scens(sums)
    terms = len(sum_terms)
    relayed = areas == 4
    tied = call(
        functools.partial(tie_kernel, blocks, relayed),
        "ties",
        (base, spread, rows, weight, own, *peer),
        (
            [shape(2 * block_rows, LANES), shape(CAP, columns)]
            if relayed
            else [shape(block_rows, LANES)] * blocks
        )
        + [shape(columns, buses, dtype=bf16), shape(slots, columns), shape(slots, columns)],
        [],
        BETWEEN,
    )
    *sent, inject, mine, theirs = tied
    hedged, sums = call(
        functools.partial(second_kernel, terms, scen_total),
        "second",
        (ptdf, inject, gen, hedged, *vectors, *sum_terms),
        [shape(width, buses), shape(sum_rows, LANES)],
        step_scratch(width)[1:] + [pltpu.VMEM((8 * pl.cdiv(hours + 1, 8), buses), f32)] + ramp_scratch,
        work,
    )
    sum_terms = over_scens(sums)
    if relayed:
        far, near = sent
        far = lax.ppermute(far, "area", [(a, a ^ 2) for a in range(areas)])
        arrived, _ = lax.optimization_barrier((far, sums))
        (both,) = call(relay_kernel, "relay", (near, arrived), [shape(2 * block_rows, LANES)], [], BETWEEN)
        peer = [far, lax.ppermute(both, "area", [(a, a ^ 1) for a in range(areas)])]
    else:
        peer = from_partners(sent)
    gen_mean, hedge = call(
        functools.partial(agree_kernel, scen_total),
        "agree",
        (hedged, *sum_terms),
        [shape(hours, buses), shape(width, buses)],
        [],
        BETWEEN,
    )
    tie_shape = shape(width, 2 * REACH * CAP)
    hedge, gen_mean, tie_flow = call(
        functools.partial(last_kernel, blocks, relayed, partner_of),
        "last",
        (hedge, gen_mean, *peer, weight, mine, theirs),
        [shape(width, buses), shape(hours, buses), tie_shape],
        [
            pltpu.VMEM(tie_shape.shape, f32),
            pltpu.VMEM((2 * REACH * CAP, columns), f32),
            pltpu.SemaphoreType.DMA((2 + columns // LANES,)),
        ],
        slots * columns,
        outs_in_place=True,
    )
    return (
        gen_mean,
        hedge.reshape(hours, scens, buses),
        tie_flow.reshape(hours, scens, 2 * REACH * CAP),
    )


def solution(mesh):
    return jax.shard_map(
        per_device,
        mesh=mesh,
        in_specs=(
            P(("group", "area"), None),
            P(("group", "area"), None),
            P(("group", "hour"), "scen", "area"),
            P(("group", "hour"), "area"),
            P(("group", "hour"), "scen", "area"),
            P(("group", "area")),
            P(("group", "area")),
            P(("group", "area")),
            P(("group", "area")),
            P("group", None),
            P("group", None),
            P("group", None),
            P("group", None),
        ),
        out_specs=(
            P(("group", "hour"), "area"),
            P(("group", "hour"), "scen", "area"),
            P(("group", "hour"), "scen", "area"),
        ),
        check_vma=False,
    )
```

```python
import functools

import jax
import jax.numpy as jnp
from jax import lax
from jax.experimental import pallas as pl
from jax.experimental.pallas import tpu as pltpu
from jax.sharding import PartitionSpec as P

HOURS = 24
REACH = 4
CAP = 16

STEP_SIZE = 0.5
LINE_CHUNK = 1024
LANES = 128
BETWEEN = 20_000_000_000

CONTRACT_LAST = (((1,), (1,)), ((), ()))
CONTRACT_FIRST = (((0,), (0,)), ((), ()))
VMEM = pl.BlockSpec(memory_space=pltpu.VMEM)
ANY = pl.BlockSpec(memory_space=pltpu.HBM)


TARGETS = ((3, 2, 0, 1), (2, 3, 1, 0), (1, 0, 3, 2))


def partner_plan(areas):
    if areas == 4:

        def partner_of(here, i):
            return sum(jnp.where(here == a, target, 0) for a, target in enumerate(TARGETS[i]))

        def by_target(parts):
            out, back, pair = (
                lax.ppermute(part, "area", list(enumerate(target))) for part, target in zip(parts, TARGETS)
            )
            return [back, out, pair]

        return len(TARGETS), partner_of, by_target
    reach = min(REACH, areas - 1)
    shifts = sorted({s % areas for d in range(1, reach + 1) for s in (d, -d)})

    def by_shift(parts):
        sent = [
            lax.ppermute(part, "area", [(a, (a + s) % areas) for a in range(areas)])
            for part, s in zip(parts, shifts)
        ]
        return [sent[shifts.index(areas - s)] for s in shifts]

    return len(shifts), lambda here, i: lax.rem(here + shifts[i], areas), by_shift


def by_flips(here, flip_3, flip_2):
    return jnp.where(here < 2, flip_3, flip_2), jnp.where(here < 2, flip_2, flip_3)


def block_facts(here, partner):
    low = partner > here
    distance = jnp.abs(partner - here)
    block = jnp.clip(distance - 1, 0, REACH - 1)
    in_reach = (distance >= 1) & (distance <= REACH)
    return low, jnp.minimum(here, partner), block, in_reach


def fold(x):
    half = x.shape[0] // 2
    low = lax.broadcasted_iota(jnp.int32, (half, LANES), 1) < LANES // 2
    shared = jnp.where(low, x[0:half, LANES : 2 * LANES], x[half:, LANES : 2 * LANES])
    return jnp.concatenate([x[:, 0:LANES], shared], axis=0)


def unfold(packed):
    rows = 2 * packed.shape[0] // 3
    shared = packed[rows:, :]
    low = lax.broadcasted_iota(jnp.int32, shared.shape, 1) < LANES // 2
    turned = pltpu.roll(shared, LANES // 2, 1)
    rest = jnp.concatenate([jnp.where(low, shared, turned), jnp.where(low, turned, shared)], axis=0)
    return jnp.concatenate([packed[0:rows, :], rest], axis=1)


def repeat_rest(inject_ref, width):
    inject_ref[width:, :] = inject_ref[width - LANES // 2 : width, :]


def split_3(x):
    high = x.astype(jnp.bfloat16)
    rest = x - high.astype(jnp.float32)
    middle = rest.astype(jnp.bfloat16)
    rest = rest - middle.astype(jnp.float32)
    return jnp.concatenate([high, middle, rest.astype(jnp.bfloat16)], axis=0)


def put_row(packed_ref, hours, h, row):
    for j in range(row.shape[1] // LANES):
        packed_ref[j * hours + h : j * hours + h + 1, :] = row[:, j * LANES : (j + 1) * LANES]


def clear_rest(packed_ref, used):
    rows = packed_ref.shape[0]
    if used < rows:
        packed_ref[used:, :] = jnp.zeros((rows - used, LANES), jnp.float32)


def agree(mean_ref, sum_refs, hours, scen_total):
    for j in range(mean_ref.shape[1] // LANES):
        parts = [ref[j * hours : (j + 1) * hours, :] for ref in sum_refs]
        mean_ref[0:hours, j * LANES : (j + 1) * LANES] = functools.reduce(jnp.add, parts) / scen_total


def excess(diffs, limit):
    return diffs - jnp.clip(diffs, -limit, limit)


def write_ramp(mean_ref, beyond, limit, first_hour, padded_ref, excess_ref, ramp_ref):
    hours = ramp_ref.shape[0]
    padded_ref[0:1, :] = beyond
    padded_ref[1 : hours + 1, :] = mean_ref[0:hours, :]
    padded_ref[hours + 1 : hours + 2, :] = beyond
    diffs = padded_ref[1 : hours + 2, :] - padded_ref[0 : hours + 1, :]
    ids = first_hour + lax.broadcasted_iota(jnp.int32, diffs.shape, 0)
    valid = (ids >= 1) & (ids <= HOURS - 1)
    excess_ref[0 : hours + 1, :] = jnp.where(valid, excess(diffs, limit), 0.0)
    ramp_ref[...] = excess_ref[0:hours, :] - excess_ref[1 : hours + 1, :]


def line_work(inject_ref, ptdf_ref, line_max_ref, over_ref):
    inject = inject_ref[...]
    lines = ptdf_ref.shape[0]
    for at in range(0, lines, LINE_CHUNK):
        part = slice(at, at + LINE_CHUNK)
        flows = lax.dot_general(
            inject, ptdf_ref[part, :], CONTRACT_LAST, preferred_element_type=jnp.float32
        )
        limit = line_max_ref[:, part]
        over_ref[:, part] = (flows - jnp.clip(flows, -limit, limit)).astype(jnp.bfloat16)
    return jnp.dot(over_ref[...], ptdf_ref[...], preferred_element_type=jnp.float32)


def table_kernel(
    blocks,
    partner_of,
    demand_in,
    hedge_in,
    start_in,
    count_in,
    low_bus_in,
    high_bus_in,
    susc_in,
    cost_in,
    max_in,
    limit_in,
    line_max_in,
    demand_ref,
    edge_hedge_ref,
    start_ref,
    cost_ref,
    max_ref,
    limit_ref,
    line_max_ref,
    onehot_ref,
    spread_ref,
    weight_ref,
    count_ref,
    low_bus_ref,
    high_bus_ref,
    susc_ref,
    copy_sems,
):
    hours, buses = start_ref.shape
    scens = hedge_in.shape[0] // hours
    here = lax.axis_index("area")
    last = (hours - 1) * scens
    edge_rows = pl.ds(pl.multiple_of((1 - lax.axis_index("hour")) * last, scens), scens)

    pairs = (
        (count_in, count_ref),
        (low_bus_in, low_bus_ref),
        (high_bus_in, high_bus_ref),
        (susc_in, susc_ref),
        (start_in, start_ref),
        (demand_in, demand_ref),
        (hedge_in.at[edge_rows], edge_hedge_ref),
        (cost_in, cost_ref),
        (max_in, max_ref),
        (limit_in, limit_ref),
        (line_max_in, line_max_ref),
    )
    copies = [pltpu.make_async_copy(src, dst, copy_sems.at[i]) for i, (src, dst) in enumerate(pairs)]
    for copy in (copies[5], *copies[:5], *copies[6:]):
        copy.start()
    for copy in copies[:4]:
        copy.wait()
    for i in range(blocks):
        partner = partner_of(here, i)
        low, row, block, in_reach = block_facts(here, partner)
        slots = slice(i * CAP, (i + 1) * CAP)
        pick = lax.broadcasted_iota(jnp.int32, (CAP, REACH * CAP), 1) == (
            block * CAP + lax.broadcasted_iota(jnp.int32, (CAP, REACH * CAP), 0)
        )
        table_row = pl.ds(row, 1)
        bus_row = jnp.where(low, low_bus_ref[table_row, :], high_bus_ref[table_row, :])
        bus = jnp.sum(jnp.where(pick, bus_row.astype(jnp.float32), 0.0), axis=1, keepdims=True)
        susc = jnp.sum(jnp.where(pick, susc_ref[table_row, :], 0.0), axis=1, keepdims=True)
        count_row = count_ref[table_row, :].astype(jnp.float32)
        is_block = lax.broadcasted_iota(jnp.int32, (CAP, REACH), 1) == block
        count = jnp.sum(jnp.where(is_block, count_row, 0.0), axis=1, keepdims=True)
        slot_ids = lax.broadcasted_iota(jnp.int32, (CAP, 1), 0).astype(jnp.float32)
        live = jnp.where((slot_ids < count) & in_reach, 1.0, 0.0)
        sign = jnp.where(low, 1.0, -1.0)
        bus_ids = lax.broadcasted_iota(jnp.int32, (CAP, buses), 1).astype(jnp.float32)
        onehot = jnp.where(bus_ids == bus, live, 0.0)
        onehot_ref[slots, :] = onehot.astype(jnp.bfloat16)
        spread_ref[slots, :] = (-sign * onehot).astype(jnp.bfloat16)
        weight_ref[slots, :] = jnp.broadcast_to(live * sign * susc, (CAP, 128))

    for copy in copies[4:]:
        copy.wait()


def angle_kernel(blocks, sens_ref, demand_ref, start_ref, onehot_ref, *refs):
    sent_refs, (own_ref, inject_ref, rows_ref) = refs[:blocks], refs[blocks:]
    hours = start_ref.shape[0]
    scens = demand_ref.shape[0] // hours
    rows = jnp.dot(onehot_ref[...], sens_ref[...], preferred_element_type=jnp.float32)
    rows_ref[...] = rows.astype(jnp.bfloat16)
    for h in range(hours):
        part = slice(h * scens, (h + 1) * scens)
        inject_ref[part, :] = (start_ref[h : h + 1, :] - demand_ref[part, :]).astype(jnp.bfloat16)
    repeat_rest(inject_ref, hours * scens)
    own = lax.dot_general(
        rows_ref[...], inject_ref[...], CONTRACT_LAST, preferred_element_type=jnp.float32
    )
    own_ref[...] = own
    for i in range(blocks):
        sent_refs[i][...] = fold(own[i * CAP : (i + 1) * CAP, :])


def edge_kernel(demand_ref, edge_hedge_ref, start_ref, edge_ref):
    scens = edge_hedge_ref.shape[0]
    hours = start_ref.shape[0]
    early = lax.axis_index("hour") == 0
    last = (hours - 1) * scens
    at = 2 * scens
    edge_ref[0:scens, :] = jnp.where(early, demand_ref[last:, :], demand_ref[0:scens, :])
    edge_ref[scens:at, :] = edge_hedge_ref[...]
    edge_ref[at : at + 1, :] = jnp.where(early, start_ref[hours - 1 : hours, :], start_ref[0:1, :])
    edge_ref[at + 1 : at + 2, :] = jnp.where(
        early, start_ref[hours - 2 : hours - 1, :], start_ref[1:2, :]
    )


def first_kernel(
    ptdf_ref,
    own_inject_ref,
    demand_ref,
    hedge_ref,
    start_ref,
    edge_ref,
    cost_ref,
    max_ref,
    limit_ref,
    line_max_ref,
    gen_ref,
    base_ref,
    hedged_ref,
    sums_ref,
    inject_ref,
    over_ref,
    back_ref,
    padded_ref,
    excess_ref,
    ramp_ref,
):
    hours, buses = start_ref.shape
    width = demand_ref.shape[0]
    scens = width // hours
    at = 2 * scens
    early = lax.axis_index("hour") == 0
    first_hour = lax.axis_index("hour") * hours
    beyond = edge_ref[at : at + 1, :]
    limit = limit_ref[...]
    cost = cost_ref[...]
    top = max_ref[...]

    inject_ref[0:width, :] = own_inject_ref[0:width, :]
    inject_ref[width : width + scens, :] = (beyond - edge_ref[0:scens, :]).astype(jnp.bfloat16)
    back_ref[...] = line_work(inject_ref, ptdf_ref, line_max_ref, over_ref)
    write_ramp(start_ref, beyond, limit, first_hour, padded_ref, excess_ref, ramp_ref)

    def step(mean, hedge, back, ramp):
        grad = cost + back + (mean - mean + hedge) + ramp
        gen = jnp.clip(mean - STEP_SIZE * grad, 0.0, top)
        return gen, gen + hedge

    for h in range(hours):
        part = slice(h * scens, (h + 1) * scens)
        mean = start_ref[h : h + 1, :]
        gen, hedged = step(mean, hedge_ref[part, :], back_ref[part, :], ramp_ref[h : h + 1, :])
        gen_ref[part, :] = gen
        base_ref[part, :] = gen - demand_ref[part, :]
        hedged_ref[part, :] = hedged
        put_row(sums_ref, hours + 1, h, jnp.sum(hedged, axis=0, keepdims=True))
    near = jnp.where(early, start_ref[hours - 1 : hours, :], start_ref[0:1, :])
    ramp = excess(beyond - near, limit) + excess(beyond - edge_ref[at + 1 : at + 2, :], limit)
    _, hedged = step(beyond, edge_ref[scens:at, :], back_ref[width : width + scens, :], ramp)
    put_row(sums_ref, hours + 1, hours, jnp.sum(hedged, axis=0, keepdims=True))
    clear_rest(sums_ref, (hours + 1) * (buses // LANES))


def first_flow(weight, own, peer):
    est_mine = weight * own
    est_theirs = -weight * peer
    return est_mine, est_theirs, (est_mine + est_theirs) * 0.5


def tie_kernel(blocks, relayed, base_ref, spread_ref, rows_ref, weight_ref, own_ref, *refs):
    peer_refs, refs = refs[:blocks], refs[blocks:]
    *next_refs, inject_ref, own_next_ref = refs
    width = base_ref.shape[0]

    weight = jnp.concatenate([weight_ref[...], weight_ref[...]], axis=1)
    own = own_ref[...]
    peer = jnp.concatenate([unfold(ref[...]) for ref in peer_refs], axis=0)
    flow = first_flow(weight, own, peer)[2]
    spread = spread_ref[...]
    add = lax.dot_general(
        split_3(flow),
        jnp.concatenate([spread, spread, spread], axis=0),
        CONTRACT_FIRST,
        preferred_element_type=jnp.float32,
    )
    inject_ref[0:width, :] = (base_ref[...] + add[0:width, :]).astype(jnp.bfloat16)
    repeat_rest(inject_ref, width)

    own_next = lax.dot_general(
        rows_ref[...], inject_ref[...], CONTRACT_LAST, preferred_element_type=jnp.float32
    )
    parts = [own_next[i * CAP : (i + 1) * CAP, :] for i in range(blocks)]
    if relayed:
        far_ref, near_ref = next_refs
        flip_3, flip_2 = by_flips(lax.axis_index("area"), parts[0], parts[1])
        far_ref[...] = fold(jnp.concatenate([flip_2, flip_3], axis=0))
        near_ref[...] = parts[2]
    else:
        for ref, part in zip(next_refs, parts):
            ref[...] = fold(part)
    own_next_ref[...] = own_next


def second_kernel(
    terms,
    scen_total,
    ptdf_ref,
    inject_ref,
    gen_ref,
    hedged_ref,
    cost_ref,
    max_ref,
    limit_ref,
    line_max_ref,
    *refs,
):
    sum_refs, refs = refs[:terms], refs[terms:]
    (hedged_out_ref, sums_out_ref, over_ref, back_ref, mean_ref, padded_ref, excess_ref, ramp_ref) = refs
    hours, buses = ramp_ref.shape
    width = back_ref.shape[0]
    scens = width // hours
    first_hour = lax.axis_index("hour") * hours

    back_ref[...] = line_work(inject_ref.at[0:width, :], ptdf_ref, line_max_ref, over_ref)
    agree(mean_ref, sum_refs, hours + 1, scen_total)
    write_ramp(
        mean_ref, mean_ref[hours : hours + 1, :], limit_ref[...], first_hour, padded_ref, excess_ref, ramp_ref
    )
    cost = cost_ref[...]
    top = max_ref[...]
    for h in range(hours):
        part = slice(h * scens, (h + 1) * scens)
        mean = mean_ref[h : h + 1, :]
        gen = gen_ref[part, :]
        hedge = hedged_ref[part, :] - mean
        grad = cost + back_ref[part, :] + (gen - mean + hedge) + ramp_ref[h : h + 1, :]
        gen = jnp.clip(gen - STEP_SIZE * grad, 0.0, top)
        hedged = gen + hedge
        hedged_out_ref[part, :] = hedged
        put_row(sums_out_ref, hours, h, jnp.sum(hedged, axis=0, keepdims=True))
    clear_rest(sums_out_ref, hours * (buses // LANES))


def relay_kernel(near_ref, far_ref, both_ref):
    low = lax.broadcasted_iota(jnp.int32, (CAP, LANES), 1) < LANES // 2
    both_ref[0:CAP, :] = near_ref[:, 0:LANES]
    both_ref[CAP : 2 * CAP, :] = far_ref[CAP : 2 * CAP, :]
    both_ref[2 * CAP :, :] = jnp.where(low, near_ref[:, LANES:], far_ref[2 * CAP :, :])


def agree_kernel(blocks, scen_total, hedged_ref, weight_ref, own_ref, own_next_ref, *refs):
    peer_refs, refs = refs[:blocks], refs[blocks:]
    sum_refs, (mean_ref, hedge_ref, mine_ref, theirs_ref) = refs[:-4], refs[-4:]
    hours = mean_ref.shape[0]
    scens = hedged_ref.shape[0] // hours
    agree(mean_ref, sum_refs, hours, scen_total)
    for h in range(hours):
        part = slice(h * scens, (h + 1) * scens)
        hedge_ref[part, :] = hedged_ref[part, :] - mean_ref[h : h + 1, :]

    weight = jnp.concatenate([weight_ref[...], weight_ref[...]], axis=1)
    own = own_ref[...]
    peer = jnp.concatenate([unfold(ref[...]) for ref in peer_refs], axis=0)
    est_mine, est_theirs, flow = first_flow(weight, own, peer)
    mine_ref[...] = weight * (own_next_ref[...] - peer) + (est_mine - flow)
    theirs_ref[...] = weight * own + (est_theirs - flow)


def last_kernel(blocks, relayed, partner_of, hedge_ref, mean_ref, *refs):
    *peer_refs, weight_ref, mine_ref, theirs_ref = refs[:-6]
    hedge_out, mean_out, tie_out, tie_ref, placed_ref, copy_sems = refs[-6:]
    copies = []

    def send(src, dst):
        copies.append(pltpu.make_async_copy(src, dst, copy_sems.at[len(copies)]))
        copies[-1].start()

    send(hedge_ref, hedge_out)
    send(mean_ref, mean_out)
    here = lax.axis_index("area")
    placed_ref[...] = jnp.zeros_like(placed_ref)
    if relayed:
        far, both = (unfold(ref[...]) for ref in peer_refs)
        peers = [*by_flips(here, both[CAP:, :], far[0:CAP, :]), both[0:CAP, :]]
    else:
        peers = [unfold(ref[...]) for ref in peer_refs]
    for i in range(blocks):
        slots = slice(i * CAP, (i + 1) * CAP)
        weight = jnp.concatenate([weight_ref[slots, :], weight_ref[slots, :]], axis=1)
        flow = (mine_ref[slots, :] + (theirs_ref[slots, :] - weight * peers[i])) * 0.5
        low, _, block, in_reach = block_facts(here, partner_of(here, i))
        first = block * CAP + jnp.where(low, 0, REACH * CAP)

        @pl.when(in_reach)
        def _():
            placed_ref[pl.ds(pl.multiple_of(first, CAP), CAP), :] = flow

    for first in range(0, tie_ref.shape[0], LANES):
        count = min(LANES, tie_ref.shape[0] - first)
        tie_ref[first : first + count, :] = jnp.transpose(placed_ref[:, first : first + LANES])[0:count, :]
        send(tie_ref.at[pl.ds(first, count)], tie_out.at[pl.ds(first, count)])
    for copy in copies:
        copy.wait()


def call(kernel, name, args, outs, scratch, flops, in_place=(), outs_in_place=False):
    size = sum(x.size * x.dtype.itemsize for x in list(args) + list(outs))
    return pl.pallas_call(
        kernel,
        name=name,
        out_shape=outs,
        in_specs=[ANY if i in in_place else VMEM for i in range(len(args))],
        out_specs=[ANY if outs_in_place else VMEM] * len(outs),
        scratch_shapes=scratch,
        compiler_params=pltpu.CompilerParams(vmem_limit_bytes=32 * 1024 * 1024),
        cost_estimate=pl.CostEstimate(flops=flops, bytes_accessed=size, transcendentals=0),
    )(*(pltpu.with_memory_space_constraint(x, pltpu.HBM) if i in in_place else x for i, x in enumerate(args)))


def per_device(
    ptdf,
    angle_sens,
    demand,
    gen_start,
    hedge_dual,
    gen_cost,
    gen_max,
    gen_ramp,
    line_max,
    tie_count,
    tie_low_bus,
    tie_high_bus,
    tie_susc,
):
    hours, scens, buses = demand.shape
    lines = ptdf.shape[0]
    width = hours * scens
    areas = lax.axis_size("area")
    n_scen = lax.axis_size("scen")
    assert lax.axis_size("hour") == 2 and hours >= 2
    assert width % LANES == LANES // 2 and width < 2 * LANES
    columns = 2 * LANES
    block_rows = CAP * 3 // 2
    scen_total = scens * n_scen
    blocks, partner_of, from_partners = partner_plan(areas)
    slots = blocks * CAP
    pieces = buses // LANES
    sum_rows = 8 * pl.cdiv((hours + 1) * pieces, 8)
    f32, bf16 = jnp.float32, jnp.bfloat16

    def shape(*dims, dtype=f32):
        return jax.ShapeDtypeStruct(dims, dtype)

    def over_scens(sums):
        if n_scen == 2:
            return [sums, lax.ppermute(sums, "scen", [(0, 1), (1, 0)])]
        return [lax.psum(sums, "scen")]

    work = 4 * width * lines * buses

    def step_scratch(rows):
        return [
            pltpu.VMEM((rows, buses), bf16),
            pltpu.VMEM((rows, lines), bf16),
            pltpu.VMEM((rows, buses), f32),
        ]

    ramp_scratch = [
        pltpu.VMEM((hours + 4, buses), f32),
        pltpu.VMEM((hours + 4, buses), f32),
        pltpu.VMEM((hours, buses), f32),
    ]
    tables = (tie_count, tie_low_bus, tie_high_bus, tie_susc)
    vectors = [x.reshape(1, -1) for x in (gen_cost, gen_max, gen_ramp, line_max)]
    hedge = hedge_dual.reshape(width, buses)
    load, edge_hedge, start, *vectors, onehot, spread, weight = call(
        functools.partial(table_kernel, blocks, partner_of),
        "tables",
        (demand.reshape(width, buses), hedge, gen_start, *tables, *vectors),
        [
            shape(width, buses),
            shape(scens, buses),
            shape(hours, buses),
            *(shape(*x.shape) for x in vectors),
            shape(slots, buses, dtype=bf16),
            shape(slots, buses, dtype=bf16),
            shape(slots, LANES),
        ],
        [pltpu.VMEM(x.shape, x.dtype) for x in tables] + [pltpu.SemaphoreType.DMA((11,))],
        BETWEEN,
        range(11),
    )
    (edge,) = call(edge_kernel, "edge", (load, edge_hedge, start), [shape(2 * scens + 8, buses)], [], width)
    *sent, own, inject, rows = call(
        functools.partial(angle_kernel, blocks),
        "angles",
        (angle_sens, load, start, onehot),
        [shape(block_rows, LANES)] * blocks
        + [shape(slots, columns), shape(columns, buses, dtype=bf16), shape(slots, buses, dtype=bf16)],
        [],
        BETWEEN,
    )
    edge = lax.ppermute(edge, "hour", [(0, 1), (1, 0)])
    peer = from_partners(sent)
    gen, base, hedged, sums = call(
        first_kernel,
        "first",
        (ptdf, inject, load, hedge, start, edge, *vectors),
        [
            shape(width, buses),
            shape(width, buses),
            shape(width, buses),
            shape(sum_rows, LANES),
        ],
        step_scratch(width + scens) + ramp_scratch,
        work,
    )
    sum_terms = over_scens(sums)
    terms = len(sum_terms)
    relayed = areas == 4
    tied = call(
        functools.partial(tie_kernel, blocks, relayed),
        "ties",
        (base, spread, rows, weight, own, *peer),
        (
            [shape(2 * block_rows, LANES), shape(CAP, columns)]
            if relayed
            else [shape(block_rows, LANES)] * blocks
        )
        + [shape(columns, buses, dtype=bf16), shape(slots, columns)],
        [],
        BETWEEN,
    )
    *sent, inject, own_next = tied
    first_peer = peer
    hedged, sums = call(
        functools.partial(second_kernel, terms, scen_total),
        "second",
        (ptdf, inject, gen, hedged, *vectors, *sum_terms),
        [shape(width, buses), shape(sum_rows, LANES)],
        step_scratch(width)[1:] + [pltpu.VMEM((8 * pl.cdiv(hours + 1, 8), buses), f32)] + ramp_scratch,
        work,
    )
    sum_terms = over_scens(sums)
    if relayed:
        far, near = sent
        far = lax.ppermute(far, "area", [(a, a ^ 2) for a in range(areas)])
        arrived, _ = lax.optimization_barrier((far, sums))
        (both,) = call(relay_kernel, "relay", (near, arrived), [shape(2 * block_rows, LANES)], [], BETWEEN)
        peer = [far, lax.ppermute(both, "area", [(a, a ^ 1) for a in range(areas)])]
    else:
        peer = from_partners(sent)
    gen_mean, hedge, mine, theirs = call(
        functools.partial(agree_kernel, blocks, scen_total),
        "agree",
        (hedged, weight, own, own_next, *first_peer, *sum_terms),
        [shape(hours, buses), shape(width, buses), shape(slots, columns), shape(slots, columns)],
        [],
        BETWEEN,
    )
    tie_shape = shape(width, 2 * REACH * CAP)
    hedge, gen_mean, tie_flow = call(
        functools.partial(last_kernel, blocks, relayed, partner_of),
        "last",
        (hedge, gen_mean, *peer, weight, mine, theirs),
        [shape(width, buses), shape(hours, buses), tie_shape],
        [
            pltpu.VMEM(tie_shape.shape, f32),
            pltpu.VMEM((2 * REACH * CAP, columns), f32),
            pltpu.SemaphoreType.DMA((2 + columns // LANES,)),
        ],
        slots * columns,
        outs_in_place=True,
    )
    return (
        gen_mean,
        hedge.reshape(hours, scens, buses),
        tie_flow.reshape(hours, scens, 2 * REACH * CAP),
    )


def solution(mesh):
    return jax.shard_map(
        per_device,
        mesh=mesh,
        in_specs=(
            P(("group", "area"), None),
            P(("group", "area"), None),
            P(("group", "hour"), "scen", "area"),
            P(("group", "hour"), "area"),
            P(("group", "hour"), "scen", "area"),
            P(("group", "area")),
            P(("group", "area")),
            P(("group", "area")),
            P(("group", "area")),
            P("group", None),
            P("group", None),
            P("group", None),
            P("group", None),
        ),
        out_specs=(
            P(("group", "hour"), "area"),
            P(("group", "hour"), "scen", "area"),
            P(("group", "hour"), "scen", "area"),
        ),
        check_vma=False,
    )
```

```python
import functools

import jax
import jax.numpy as jnp
from jax import lax
from jax.experimental import pallas as pl
from jax.experimental.pallas import tpu as pltpu
from jax.sharding import PartitionSpec as P

HOURS = 24
REACH = 4
CAP = 16

STEP_SIZE = 0.5
LINE_CHUNK = 2048
LANES = 128
BETWEEN = 20_000_000_000

CONTRACT_LAST = (((1,), (1,)), ((), ()))
CONTRACT_FIRST = (((0,), (0,)), ((), ()))
VMEM = pl.BlockSpec(memory_space=pltpu.VMEM)
ANY = pl.BlockSpec(memory_space=pltpu.HBM)


TARGETS = ((3, 2, 0, 1), (2, 3, 1, 0), (1, 0, 3, 2))


def partner_plan(areas):
    if areas == 4:

        def partner_of(here, i):
            return sum(jnp.where(here == a, target, 0) for a, target in enumerate(TARGETS[i]))

        def by_target(parts):
            out, back, pair = (
                lax.ppermute(part, "area", list(enumerate(target))) for part, target in zip(parts, TARGETS)
            )
            return [back, out, pair]

        return len(TARGETS), partner_of, by_target
    reach = min(REACH, areas - 1)
    shifts = sorted({s % areas for d in range(1, reach + 1) for s in (d, -d)})

    def by_shift(parts):
        sent = [
            lax.ppermute(part, "area", [(a, (a + s) % areas) for a in range(areas)])
            for part, s in zip(parts, shifts)
        ]
        return [sent[shifts.index(areas - s)] for s in shifts]

    return len(shifts), lambda here, i: lax.rem(here + shifts[i], areas), by_shift


def by_flips(here, flip_3, flip_2):
    return jnp.where(here < 2, flip_3, flip_2), jnp.where(here < 2, flip_2, flip_3)


def block_facts(here, partner):
    low = partner > here
    distance = jnp.abs(partner - here)
    block = jnp.clip(distance - 1, 0, REACH - 1)
    in_reach = (distance >= 1) & (distance <= REACH)
    return low, jnp.minimum(here, partner), block, in_reach


def fold(x):
    half = x.shape[0] // 2
    low = lax.broadcasted_iota(jnp.int32, (half, LANES), 1) < LANES // 2
    shared = jnp.where(low, x[0:half, LANES : 2 * LANES], x[half:, LANES : 2 * LANES])
    return jnp.concatenate([x[:, 0:LANES], shared], axis=0)


def unfold(packed):
    rows = 2 * packed.shape[0] // 3
    shared = packed[rows:, :]
    low = lax.broadcasted_iota(jnp.int32, shared.shape, 1) < LANES // 2
    turned = pltpu.roll(shared, LANES // 2, 1)
    rest = jnp.concatenate([jnp.where(low, shared, turned), jnp.where(low, turned, shared)], axis=0)
    return jnp.concatenate([packed[0:rows, :], rest], axis=1)


def repeat_rest(inject_ref, width):
    inject_ref[width:, :] = inject_ref[width - LANES // 2 : width, :]


def split_3(x):
    high = x.astype(jnp.bfloat16)
    rest = x - high.astype(jnp.float32)
    middle = rest.astype(jnp.bfloat16)
    rest = rest - middle.astype(jnp.float32)
    return jnp.concatenate([high, middle, rest.astype(jnp.bfloat16)], axis=0)


def put_row(packed_ref, hours, h, row):
    for j in range(row.shape[1] // LANES):
        packed_ref[j * hours + h : j * hours + h + 1, :] = row[:, j * LANES : (j + 1) * LANES]


def clear_rest(packed_ref, used):
    rows = packed_ref.shape[0]
    if used < rows:
        packed_ref[used:, :] = jnp.zeros((rows - used, LANES), jnp.float32)


def agree(mean_ref, sum_refs, hours, scen_total):
    for j in range(mean_ref.shape[1] // LANES):
        parts = [ref[j * hours : (j + 1) * hours, :] for ref in sum_refs]
        mean_ref[0:hours, j * LANES : (j + 1) * LANES] = functools.reduce(jnp.add, parts) / scen_total


def excess(diffs, limit):
    return diffs - jnp.clip(diffs, -limit, limit)


def write_ramp(mean_ref, beyond, limit, first_hour, padded_ref, excess_ref, ramp_ref):
    hours = ramp_ref.shape[0]
    padded_ref[0:1, :] = beyond
    padded_ref[1 : hours + 1, :] = mean_ref[0:hours, :]
    padded_ref[hours + 1 : hours + 2, :] = beyond
    diffs = padded_ref[1 : hours + 2, :] - padded_ref[0 : hours + 1, :]
    ids = first_hour + lax.broadcasted_iota(jnp.int32, diffs.shape, 0)
    valid = (ids >= 1) & (ids <= HOURS - 1)
    excess_ref[0 : hours + 1, :] = jnp.where(valid, excess(diffs, limit), 0.0)
    ramp_ref[...] = excess_ref[0:hours, :] - excess_ref[1 : hours + 1, :]


def line_work(inject_ref, ptdf_ref, line_max_ref, over_ref):
    inject = inject_ref[...]
    lines = ptdf_ref.shape[0]
    for at in range(0, lines, LINE_CHUNK):
        part = slice(at, at + LINE_CHUNK)
        flows = lax.dot_general(
            inject, ptdf_ref[part, :], CONTRACT_LAST, preferred_element_type=jnp.float32
        )
        limit = line_max_ref[:, part]
        over_ref[:, part] = (flows - jnp.clip(flows, -limit, limit)).astype(jnp.bfloat16)
    return jnp.dot(over_ref[...], ptdf_ref[...], preferred_element_type=jnp.float32)


def table_kernel(
    blocks,
    partner_of,
    demand_in,
    hedge_in,
    start_in,
    count_in,
    low_bus_in,
    high_bus_in,
    susc_in,
    cost_in,
    max_in,
    limit_in,
    line_max_in,
    demand_ref,
    edge_hedge_ref,
    start_ref,
    cost_ref,
    max_ref,
    limit_ref,
    line_max_ref,
    onehot_ref,
    spread_ref,
    weight_ref,
    count_ref,
    low_bus_ref,
    high_bus_ref,
    susc_ref,
    copy_sems,
):
    hours, buses = start_ref.shape
    scens = hedge_in.shape[0] // hours
    here = lax.axis_index("area")
    last = (hours - 1) * scens
    edge_rows = pl.ds(pl.multiple_of((1 - lax.axis_index("hour")) * last, scens), scens)

    pairs = (
        (count_in, count_ref),
        (low_bus_in, low_bus_ref),
        (high_bus_in, high_bus_ref),
        (susc_in, susc_ref),
        (start_in, start_ref),
        (demand_in, demand_ref),
        (hedge_in.at[edge_rows], edge_hedge_ref),
        (cost_in, cost_ref),
        (max_in, max_ref),
        (limit_in, limit_ref),
        (line_max_in, line_max_ref),
    )
    copies = [pltpu.make_async_copy(src, dst, copy_sems.at[i]) for i, (src, dst) in enumerate(pairs)]
    for copy in (copies[5], *copies[:5], *copies[6:]):
        copy.start()
    for copy in copies[:4]:
        copy.wait()
    for i in range(blocks):
        partner = partner_of(here, i)
        low, row, block, in_reach = block_facts(here, partner)
        slots = slice(i * CAP, (i + 1) * CAP)
        pick = lax.broadcasted_iota(jnp.int32, (CAP, REACH * CAP), 1) == (
            block * CAP + lax.broadcasted_iota(jnp.int32, (CAP, REACH * CAP), 0)
        )
        table_row = pl.ds(row, 1)
        bus_row = jnp.where(low, low_bus_ref[table_row, :], high_bus_ref[table_row, :])
        bus = jnp.sum(jnp.where(pick, bus_row.astype(jnp.float32), 0.0), axis=1, keepdims=True)
        susc = jnp.sum(jnp.where(pick, susc_ref[table_row, :], 0.0), axis=1, keepdims=True)
        count_row = count_ref[table_row, :].astype(jnp.float32)
        is_block = lax.broadcasted_iota(jnp.int32, (CAP, REACH), 1) == block
        count = jnp.sum(jnp.where(is_block, count_row, 0.0), axis=1, keepdims=True)
        slot_ids = lax.broadcasted_iota(jnp.int32, (CAP, 1), 0).astype(jnp.float32)
        live = jnp.where((slot_ids < count) & in_reach, 1.0, 0.0)
        sign = jnp.where(low, 1.0, -1.0)
        bus_ids = lax.broadcasted_iota(jnp.int32, (CAP, buses), 1).astype(jnp.float32)
        onehot = jnp.where(bus_ids == bus, live, 0.0)
        onehot_ref[slots, :] = onehot.astype(jnp.bfloat16)
        spread_ref[slots, :] = (-sign * onehot).astype(jnp.bfloat16)
        weight_ref[slots, :] = jnp.broadcast_to(live * sign * susc, (CAP, 128))

    for copy in copies[4:]:
        copy.wait()


def angle_kernel(blocks, sens_ref, demand_ref, start_ref, onehot_ref, *refs):
    sent_refs, (own_ref, inject_ref, rows_ref) = refs[:blocks], refs[blocks:]
    hours = start_ref.shape[0]
    scens = demand_ref.shape[0] // hours
    rows = jnp.dot(onehot_ref[...], sens_ref[...], preferred_element_type=jnp.float32)
    rows_ref[...] = rows.astype(jnp.bfloat16)
    for h in range(hours):
        part = slice(h * scens, (h + 1) * scens)
        inject_ref[part, :] = (start_ref[h : h + 1, :] - demand_ref[part, :]).astype(jnp.bfloat16)
    repeat_rest(inject_ref, hours * scens)
    own = lax.dot_general(
        rows_ref[...], inject_ref[...], CONTRACT_LAST, preferred_element_type=jnp.float32
    )
    own_ref[...] = own
    for i in range(blocks):
        sent_refs[i][...] = fold(own[i * CAP : (i + 1) * CAP, :])


def edge_kernel(demand_ref, edge_hedge_ref, start_ref, edge_ref):
    scens = edge_hedge_ref.shape[0]
    hours = start_ref.shape[0]
    early = lax.axis_index("hour") == 0
    last = (hours - 1) * scens
    at = 2 * scens
    edge_ref[0:scens, :] = jnp.where(early, demand_ref[last:, :], demand_ref[0:scens, :])
    edge_ref[scens:at, :] = edge_hedge_ref[...]
    edge_ref[at : at + 1, :] = jnp.where(early, start_ref[hours - 1 : hours, :], start_ref[0:1, :])
    edge_ref[at + 1 : at + 2, :] = jnp.where(
        early, start_ref[hours - 2 : hours - 1, :], start_ref[1:2, :]
    )


def first_kernel(
    ptdf_ref,
    own_inject_ref,
    demand_ref,
    hedge_ref,
    start_ref,
    edge_ref,
    cost_ref,
    max_ref,
    limit_ref,
    line_max_ref,
    gen_ref,
    base_ref,
    hedged_ref,
    sums_ref,
    inject_ref,
    over_ref,
    back_ref,
    padded_ref,
    excess_ref,
    ramp_ref,
):
    hours, buses = start_ref.shape
    width = demand_ref.shape[0]
    scens = width // hours
    at = 2 * scens
    early = lax.axis_index("hour") == 0
    first_hour = lax.axis_index("hour") * hours
    beyond = edge_ref[at : at + 1, :]
    limit = limit_ref[...]
    cost = cost_ref[...]
    top = max_ref[...]

    inject_ref[0:width, :] = own_inject_ref[0:width, :]
    inject_ref[width : width + scens, :] = (beyond - edge_ref[0:scens, :]).astype(jnp.bfloat16)
    back_ref[...] = line_work(inject_ref, ptdf_ref, line_max_ref, over_ref)
    write_ramp(start_ref, beyond, limit, first_hour, padded_ref, excess_ref, ramp_ref)

    def step(mean, hedge, back, ramp):
        grad = cost + back + (mean - mean + hedge) + ramp
        gen = jnp.clip(mean - STEP_SIZE * grad, 0.0, top)
        return gen, gen + hedge

    for h in range(hours):
        part = slice(h * scens, (h + 1) * scens)
        mean = start_ref[h : h + 1, :]
        gen, hedged = step(mean, hedge_ref[part, :], back_ref[part, :], ramp_ref[h : h + 1, :])
        gen_ref[part, :] = gen
        base_ref[part, :] = gen - demand_ref[part, :]
        hedged_ref[part, :] = hedged
        put_row(sums_ref, hours + 1, h, jnp.sum(hedged, axis=0, keepdims=True))
    near = jnp.where(early, start_ref[hours - 1 : hours, :], start_ref[0:1, :])
    ramp = excess(beyond - near, limit) + excess(beyond - edge_ref[at + 1 : at + 2, :], limit)
    _, hedged = step(beyond, edge_ref[scens:at, :], back_ref[width : width + scens, :], ramp)
    put_row(sums_ref, hours + 1, hours, jnp.sum(hedged, axis=0, keepdims=True))
    clear_rest(sums_ref, (hours + 1) * (buses // LANES))


def first_flow(weight, own, peer):
    est_mine = weight * own
    est_theirs = -weight * peer
    return est_mine, est_theirs, (est_mine + est_theirs) * 0.5


def tie_kernel(blocks, relayed, base_ref, spread_ref, rows_ref, weight_ref, own_ref, *refs):
    peer_refs, refs = refs[:blocks], refs[blocks:]
    *next_refs, inject_ref, own_next_ref = refs
    width = base_ref.shape[0]

    weight = jnp.concatenate([weight_ref[...], weight_ref[...]], axis=1)
    own = own_ref[...]
    peer = jnp.concatenate([unfold(ref[...]) for ref in peer_refs], axis=0)
    flow = first_flow(weight, own, peer)[2]
    spread = spread_ref[...]
    add = lax.dot_general(
        split_3(flow),
        jnp.concatenate([spread, spread, spread], axis=0),
        CONTRACT_FIRST,
        preferred_element_type=jnp.float32,
    )
    inject_ref[0:width, :] = (base_ref[...] + add[0:width, :]).astype(jnp.bfloat16)
    repeat_rest(inject_ref, width)

    own_next = lax.dot_general(
        rows_ref[...], inject_ref[...], CONTRACT_LAST, preferred_element_type=jnp.float32
    )
    parts = [own_next[i * CAP : (i + 1) * CAP, :] for i in range(blocks)]
    if relayed:
        far_ref, near_ref = next_refs
        flip_3, flip_2 = by_flips(lax.axis_index("area"), parts[0], parts[1])
        far_ref[...] = fold(jnp.concatenate([flip_2, flip_3], axis=0))
        near_ref[...] = parts[2]
    else:
        for ref, part in zip(next_refs, parts):
            ref[...] = fold(part)
    own_next_ref[...] = own_next


def second_kernel(
    terms,
    scen_total,
    ptdf_ref,
    inject_ref,
    gen_ref,
    hedged_ref,
    cost_ref,
    max_ref,
    limit_ref,
    line_max_ref,
    *refs,
):
    sum_refs, refs = refs[:terms], refs[terms:]
    (hedged_out_ref, sums_out_ref, over_ref, back_ref, mean_ref, padded_ref, excess_ref, ramp_ref) = refs
    hours, buses = ramp_ref.shape
    width = back_ref.shape[0]
    scens = width // hours
    first_hour = lax.axis_index("hour") * hours

    back_ref[...] = line_work(inject_ref.at[0:width, :], ptdf_ref, line_max_ref, over_ref)
    agree(mean_ref, sum_refs, hours + 1, scen_total)
    write_ramp(
        mean_ref, mean_ref[hours : hours + 1, :], limit_ref[...], first_hour, padded_ref, excess_ref, ramp_ref
    )
    cost = cost_ref[...]
    top = max_ref[...]
    for h in range(hours):
        part = slice(h * scens, (h + 1) * scens)
        mean = mean_ref[h : h + 1, :]
        gen = gen_ref[part, :]
        hedge = hedged_ref[part, :] - mean
        grad = cost + back_ref[part, :] + (gen - mean + hedge) + ramp_ref[h : h + 1, :]
        gen = jnp.clip(gen - STEP_SIZE * grad, 0.0, top)
        hedged = gen + hedge
        hedged_out_ref[part, :] = hedged
        put_row(sums_out_ref, hours, h, jnp.sum(hedged, axis=0, keepdims=True))
    clear_rest(sums_out_ref, hours * (buses // LANES))


def relay_kernel(near_ref, far_ref, both_ref):
    low = lax.broadcasted_iota(jnp.int32, (CAP, LANES), 1) < LANES // 2
    both_ref[0:CAP, :] = near_ref[:, 0:LANES]
    both_ref[CAP : 2 * CAP, :] = far_ref[CAP : 2 * CAP, :]
    both_ref[2 * CAP :, :] = jnp.where(low, near_ref[:, LANES:], far_ref[2 * CAP :, :])


def agree_kernel(blocks, scen_total, hedged_ref, weight_ref, own_ref, own_next_ref, *refs):
    peer_refs, refs = refs[:blocks], refs[blocks:]
    sum_refs, (mean_ref, hedge_ref, mine_ref, theirs_ref) = refs[:-4], refs[-4:]
    hours = mean_ref.shape[0]
    scens = hedged_ref.shape[0] // hours
    agree(mean_ref, sum_refs, hours, scen_total)
    for h in range(hours):
        part = slice(h * scens, (h + 1) * scens)
        hedge_ref[part, :] = hedged_ref[part, :] - mean_ref[h : h + 1, :]

    weight = jnp.concatenate([weight_ref[...], weight_ref[...]], axis=1)
    own = own_ref[...]
    peer = jnp.concatenate([unfold(ref[...]) for ref in peer_refs], axis=0)
    est_mine, est_theirs, flow = first_flow(weight, own, peer)
    mine_ref[...] = weight * (own_next_ref[...] - peer) + (est_mine - flow)
    theirs_ref[...] = weight * own + (est_theirs - flow)


def last_kernel(blocks, relayed, partner_of, hedge_ref, mean_ref, *refs):
    *peer_refs, weight_ref, mine_ref, theirs_ref = refs[:-6]
    hedge_out, mean_out, tie_out, tie_ref, placed_ref, copy_sems = refs[-6:]
    copies = []

    def send(src, dst):
        copies.append(pltpu.make_async_copy(src, dst, copy_sems.at[len(copies)]))
        copies[-1].start()

    send(hedge_ref, hedge_out)
    send(mean_ref, mean_out)
    here = lax.axis_index("area")
    placed_ref[...] = jnp.zeros_like(placed_ref)
    if relayed:
        far, both = (unfold(ref[...]) for ref in peer_refs)
        peers = [*by_flips(here, both[CAP:, :], far[0:CAP, :]), both[0:CAP, :]]
    else:
        peers = [unfold(ref[...]) for ref in peer_refs]
    for i in range(blocks):
        slots = slice(i * CAP, (i + 1) * CAP)
        weight = jnp.concatenate([weight_ref[slots, :], weight_ref[slots, :]], axis=1)
        flow = (mine_ref[slots, :] + (theirs_ref[slots, :] - weight * peers[i])) * 0.5
        low, _, block, in_reach = block_facts(here, partner_of(here, i))
        first = block * CAP + jnp.where(low, 0, REACH * CAP)

        @pl.when(in_reach)
        def _():
            placed_ref[pl.ds(pl.multiple_of(first, CAP), CAP), :] = flow

    for first in range(0, tie_ref.shape[0], LANES):
        count = min(LANES, tie_ref.shape[0] - first)
        tie_ref[first : first + count, :] = jnp.transpose(placed_ref[:, first : first + LANES])[0:count, :]
        send(tie_ref.at[pl.ds(first, count)], tie_out.at[pl.ds(first, count)])
    for copy in copies:
        copy.wait()


def call(kernel, name, args, outs, scratch, flops, in_place=(), outs_in_place=False):
    size = sum(x.size * x.dtype.itemsize for x in list(args) + list(outs))
    return pl.pallas_call(
        kernel,
        name=name,
        out_shape=outs,
        in_specs=[ANY if i in in_place else VMEM for i in range(len(args))],
        out_specs=[ANY if outs_in_place else VMEM] * len(outs),
        scratch_shapes=scratch,
        compiler_params=pltpu.CompilerParams(vmem_limit_bytes=32 * 1024 * 1024),
        cost_estimate=pl.CostEstimate(flops=flops, bytes_accessed=size, transcendentals=0),
    )(*(pltpu.with_memory_space_constraint(x, pltpu.HBM) if i in in_place else x for i, x in enumerate(args)))


def per_device(
    ptdf,
    angle_sens,
    demand,
    gen_start,
    hedge_dual,
    gen_cost,
    gen_max,
    gen_ramp,
    line_max,
    tie_count,
    tie_low_bus,
    tie_high_bus,
    tie_susc,
):
    hours, scens, buses = demand.shape
    lines = ptdf.shape[0]
    width = hours * scens
    areas = lax.axis_size("area")
    n_scen = lax.axis_size("scen")
    assert lax.axis_size("hour") == 2 and hours >= 2
    assert width % LANES == LANES // 2 and width < 2 * LANES
    columns = 2 * LANES
    block_rows = CAP * 3 // 2
    scen_total = scens * n_scen
    blocks, partner_of, from_partners = partner_plan(areas)
    slots = blocks * CAP
    pieces = buses // LANES
    sum_rows = 8 * pl.cdiv((hours + 1) * pieces, 8)
    f32, bf16 = jnp.float32, jnp.bfloat16

    def shape(*dims, dtype=f32):
        return jax.ShapeDtypeStruct(dims, dtype)

    def over_scens(sums):
        if n_scen == 2:
            return [sums, lax.ppermute(sums, "scen", [(0, 1), (1, 0)])]
        return [lax.psum(sums, "scen")]

    work = 4 * width * lines * buses

    def step_scratch(rows):
        return [
            pltpu.VMEM((rows, buses), bf16),
            pltpu.VMEM((rows, lines), bf16),
            pltpu.VMEM((rows, buses), f32),
        ]

    ramp_scratch = [
        pltpu.VMEM((hours + 4, buses), f32),
        pltpu.VMEM((hours + 4, buses), f32),
        pltpu.VMEM((hours, buses), f32),
    ]
    tables = (tie_count, tie_low_bus, tie_high_bus, tie_susc)
    vectors = [x.reshape(1, -1) for x in (gen_cost, gen_max, gen_ramp, line_max)]
    hedge = hedge_dual.reshape(width, buses)
    load, edge_hedge, start, *vectors, onehot, spread, weight = call(
        functools.partial(table_kernel, blocks, partner_of),
        "tables",
        (demand.reshape(width, buses), hedge, gen_start, *tables, *vectors),
        [
            shape(width, buses),
            shape(scens, buses),
            shape(hours, buses),
            *(shape(*x.shape) for x in vectors),
            shape(slots, buses, dtype=bf16),
            shape(slots, buses, dtype=bf16),
            shape(slots, LANES),
        ],
        [pltpu.VMEM(x.shape, x.dtype) for x in tables] + [pltpu.SemaphoreType.DMA((11,))],
        BETWEEN,
        range(11),
    )
    (edge,) = call(edge_kernel, "edge", (load, edge_hedge, start), [shape(2 * scens + 8, buses)], [], width)
    *sent, own, inject, rows = call(
        functools.partial(angle_kernel, blocks),
        "angles",
        (angle_sens, load, start, onehot),
        [shape(block_rows, LANES)] * blocks
        + [shape(slots, columns), shape(columns, buses, dtype=bf16), shape(slots, buses, dtype=bf16)],
        [],
        BETWEEN,
    )
    edge = lax.ppermute(edge, "hour", [(0, 1), (1, 0)])
    peer = from_partners(sent)
    gen, base, hedged, sums = call(
        first_kernel,
        "first",
        (ptdf, inject, load, hedge, start, edge, *vectors),
        [
            shape(width, buses),
            shape(width, buses),
            shape(width, buses),
            shape(sum_rows, LANES),
        ],
        step_scratch(width + scens) + ramp_scratch,
        work,
    )
    sum_terms = over_scens(sums)
    terms = len(sum_terms)
    relayed = areas == 4
    tied = call(
        functools.partial(tie_kernel, blocks, relayed),
        "ties",
        (base, spread, rows, weight, own, *peer),
        (
            [shape(2 * block_rows, LANES), shape(CAP, columns)]
            if relayed
            else [shape(block_rows, LANES)] * blocks
        )
        + [shape(columns, buses, dtype=bf16), shape(slots, columns)],
        [],
        BETWEEN,
    )
    *sent, inject, own_next = tied
    first_peer = peer
    hedged, sums = call(
        functools.partial(second_kernel, terms, scen_total),
        "second",
        (ptdf, inject, gen, hedged, *vectors, *sum_terms),
        [shape(width, buses), shape(sum_rows, LANES)],
        step_scratch(width)[1:] + [pltpu.VMEM((8 * pl.cdiv(hours + 1, 8), buses), f32)] + ramp_scratch,
        work,
    )
    sum_terms = over_scens(sums)
    if relayed:
        far, near = sent
        far = lax.ppermute(far, "area", [(a, a ^ 2) for a in range(areas)])
        arrived, _ = lax.optimization_barrier((far, sums))
        (both,) = call(relay_kernel, "relay", (near, arrived), [shape(2 * block_rows, LANES)], [], BETWEEN)
        peer = [far, lax.ppermute(both, "area", [(a, a ^ 1) for a in range(areas)])]
    else:
        peer = from_partners(sent)
    gen_mean, hedge, mine, theirs = call(
        functools.partial(agree_kernel, blocks, scen_total),
        "agree",
        (hedged, weight, own, own_next, *first_peer, *sum_terms),
        [shape(hours, buses), shape(width, buses), shape(slots, columns), shape(slots, columns)],
        [],
        BETWEEN,
    )
    tie_shape = shape(width, 2 * REACH * CAP)
    hedge, gen_mean, tie_flow = call(
        functools.partial(last_kernel, blocks, relayed, partner_of),
        "last",
        (hedge, gen_mean, *peer, weight, mine, theirs),
        [shape(width, buses), shape(hours, buses), tie_shape],
        [
            pltpu.VMEM(tie_shape.shape, f32),
            pltpu.VMEM((2 * REACH * CAP, columns), f32),
            pltpu.SemaphoreType.DMA((2 + columns // LANES,)),
        ],
        slots * columns,
        outs_in_place=True,
    )
    return (
        gen_mean,
        hedge.reshape(hours, scens, buses),
        tie_flow.reshape(hours, scens, 2 * REACH * CAP),
    )


def solution(mesh):
    return jax.shard_map(
        per_device,
        mesh=mesh,
        in_specs=(
            P(("group", "area"), None),
            P(("group", "area"), None),
            P(("group", "hour"), "scen", "area"),
            P(("group", "hour"), "area"),
            P(("group", "hour"), "scen", "area"),
            P(("group", "area")),
            P(("group", "area")),
            P(("group", "area")),
            P(("group", "area")),
            P("group", None),
            P("group", None),
            P("group", None),
            P("group", None),
        ),
        out_specs=(
            P(("group", "hour"), "area"),
            P(("group", "hour"), "scen", "area"),
            P(("group", "hour"), "scen", "area"),
        ),
        check_vma=False,
    )
```

```python
import functools

import jax
import jax.numpy as jnp
from jax import lax
from jax.experimental import pallas as pl
from jax.experimental.pallas import tpu as pltpu
from jax.sharding import PartitionSpec as P

HOURS = 24
REACH = 4
CAP = 16

STEP_SIZE = 0.5
LINE_CHUNK = 1024
LANES = 128
BETWEEN = 20_000_000_000

CONTRACT_LAST = (((1,), (1,)), ((), ()))
CONTRACT_FIRST = (((0,), (0,)), ((), ()))
VMEM = pl.BlockSpec(memory_space=pltpu.VMEM)
ANY = pl.BlockSpec(memory_space=pltpu.HBM)


TARGETS = ((3, 2, 0, 1), (2, 3, 1, 0), (1, 0, 3, 2))


def partner_plan(areas):
    if areas == 4:

        def partner_of(here, i):
            return sum(jnp.where(here == a, target, 0) for a, target in enumerate(TARGETS[i]))

        def by_target(parts):
            out, back, pair = (
                lax.ppermute(part, "area", list(enumerate(target))) for part, target in zip(parts, TARGETS)
            )
            return [back, out, pair]

        return len(TARGETS), partner_of, by_target
    reach = min(REACH, areas - 1)
    shifts = sorted({s % areas for d in range(1, reach + 1) for s in (d, -d)})

    def by_shift(parts):
        sent = [
            lax.ppermute(part, "area", [(a, (a + s) % areas) for a in range(areas)])
            for part, s in zip(parts, shifts)
        ]
        return [sent[shifts.index(areas - s)] for s in shifts]

    return len(shifts), lambda here, i: lax.rem(here + shifts[i], areas), by_shift


def by_flips(here, flip_3, flip_2):
    return jnp.where(here < 2, flip_3, flip_2), jnp.where(here < 2, flip_2, flip_3)


def block_facts(here, partner):
    low = partner > here
    distance = jnp.abs(partner - here)
    block = jnp.clip(distance - 1, 0, REACH - 1)
    in_reach = (distance >= 1) & (distance <= REACH)
    return low, jnp.minimum(here, partner), block, in_reach


def fold(x):
    half = x.shape[0] // 2
    low = lax.broadcasted_iota(jnp.int32, (half, LANES), 1) < LANES // 2
    shared = jnp.where(low, x[0:half, LANES : 2 * LANES], x[half:, LANES : 2 * LANES])
    return jnp.concatenate([x[:, 0:LANES], shared], axis=0)


def unfold(packed):
    rows = 2 * packed.shape[0] // 3
    shared = packed[rows:, :]
    low = lax.broadcasted_iota(jnp.int32, shared.shape, 1) < LANES // 2
    turned = pltpu.roll(shared, LANES // 2, 1)
    rest = jnp.concatenate([jnp.where(low, shared, turned), jnp.where(low, turned, shared)], axis=0)
    return jnp.concatenate([packed[0:rows, :], rest], axis=1)


def repeat_rest(inject_ref, width):
    inject_ref[width:, :] = inject_ref[width - LANES // 2 : width, :]


def split_3(x):
    high = x.astype(jnp.bfloat16)
    rest = x - high.astype(jnp.float32)
    middle = rest.astype(jnp.bfloat16)
    rest = rest - middle.astype(jnp.float32)
    return jnp.concatenate([high, middle, rest.astype(jnp.bfloat16)], axis=0)


def put_row(packed_ref, hours, h, row):
    for j in range(row.shape[1] // LANES):
        packed_ref[j * hours + h : j * hours + h + 1, :] = row[:, j * LANES : (j + 1) * LANES]


def clear_rest(packed_ref, used):
    rows = packed_ref.shape[0]
    if used < rows:
        packed_ref[used:, :] = jnp.zeros((rows - used, LANES), jnp.float32)


def agree(mean_ref, sum_refs, hours, scen_total):
    for j in range(mean_ref.shape[1] // LANES):
        parts = [ref[j * hours : (j + 1) * hours, :] for ref in sum_refs]
        mean_ref[0:hours, j * LANES : (j + 1) * LANES] = functools.reduce(jnp.add, parts) / scen_total


def excess(diffs, limit):
    return diffs - jnp.clip(diffs, -limit, limit)


def write_ramp(mean_ref, beyond, limit, first_hour, padded_ref, excess_ref, ramp_ref):
    hours = ramp_ref.shape[0]
    padded_ref[0:1, :] = beyond
    padded_ref[1 : hours + 1, :] = mean_ref[0:hours, :]
    padded_ref[hours + 1 : hours + 2, :] = beyond
    diffs = padded_ref[1 : hours + 2, :] - padded_ref[0 : hours + 1, :]
    ids = first_hour + lax.broadcasted_iota(jnp.int32, diffs.shape, 0)
    valid = (ids >= 1) & (ids <= HOURS - 1)
    excess_ref[0 : hours + 1, :] = jnp.where(valid, excess(diffs, limit), 0.0)
    ramp_ref[...] = excess_ref[0:hours, :] - excess_ref[1 : hours + 1, :]


def line_work(inject_ref, ptdf_ref, line_max_ref, over_ref):
    inject = inject_ref[...]
    lines = ptdf_ref.shape[0]
    for at in range(0, lines, LINE_CHUNK):
        part = slice(at, at + LINE_CHUNK)
        flows = lax.dot_general(
            inject, ptdf_ref[part, :], CONTRACT_LAST, preferred_element_type=jnp.float32
        )
        limit = line_max_ref[:, part]
        over_ref[:, part] = (flows - jnp.clip(flows, -limit, limit)).astype(jnp.bfloat16)
    return jnp.dot(over_ref[...], ptdf_ref[...], preferred_element_type=jnp.float32)


def table_kernel(
    blocks,
    partner_of,
    demand_in,
    hedge_in,
    start_in,
    count_in,
    low_bus_in,
    high_bus_in,
    susc_in,
    cost_in,
    max_in,
    limit_in,
    line_max_in,
    demand_ref,
    edge_hedge_ref,
    start_ref,
    cost_ref,
    max_ref,
    limit_ref,
    line_max_ref,
    onehot_ref,
    spread_ref,
    weight_ref,
    count_ref,
    low_bus_ref,
    high_bus_ref,
    susc_ref,
    copy_sems,
):
    hours, buses = start_ref.shape
    scens = hedge_in.shape[0] // hours
    here = lax.axis_index("area")
    last = (hours - 1) * scens
    edge_rows = pl.ds(pl.multiple_of((1 - lax.axis_index("hour")) * last, scens), scens)

    pairs = (
        (count_in, count_ref),
        (low_bus_in, low_bus_ref),
        (high_bus_in, high_bus_ref),
        (susc_in, susc_ref),
        (start_in, start_ref),
        (demand_in, demand_ref),
        (hedge_in.at[edge_rows], edge_hedge_ref),
        (cost_in, cost_ref),
        (max_in, max_ref),
        (limit_in, limit_ref),
        (line_max_in, line_max_ref),
    )
    copies = [pltpu.make_async_copy(src, dst, copy_sems.at[i]) for i, (src, dst) in enumerate(pairs)]
    for copy in (*copies[:4], copies[5], copies[4], *copies[6:]):
        copy.start()
    for copy in copies[:4]:
        copy.wait()
    for i in range(blocks):
        partner = partner_of(here, i)
        low, row, block, in_reach = block_facts(here, partner)
        slots = slice(i * CAP, (i + 1) * CAP)
        pick = lax.broadcasted_iota(jnp.int32, (CAP, REACH * CAP), 1) == (
            block * CAP + lax.broadcasted_iota(jnp.int32, (CAP, REACH * CAP), 0)
        )
        table_row = pl.ds(row, 1)
        bus_row = jnp.where(low, low_bus_ref[table_row, :], high_bus_ref[table_row, :])
        bus = jnp.sum(jnp.where(pick, bus_row.astype(jnp.float32), 0.0), axis=1, keepdims=True)
        susc = jnp.sum(jnp.where(pick, susc_ref[table_row, :], 0.0), axis=1, keepdims=True)
        count_row = count_ref[table_row, :].astype(jnp.float32)
        is_block = lax.broadcasted_iota(jnp.int32, (CAP, REACH), 1) == block
        count = jnp.sum(jnp.where(is_block, count_row, 0.0), axis=1, keepdims=True)
        slot_ids = lax.broadcasted_iota(jnp.int32, (CAP, 1), 0).astype(jnp.float32)
        live = jnp.where((slot_ids < count) & in_reach, 1.0, 0.0)
        sign = jnp.where(low, 1.0, -1.0)
        bus_ids = lax.broadcasted_iota(jnp.int32, (CAP, buses), 1).astype(jnp.float32)
        onehot = jnp.where(bus_ids == bus, live, 0.0)
        onehot_ref[slots, :] = onehot.astype(jnp.bfloat16)
        spread_ref[slots, :] = (-sign * onehot).astype(jnp.bfloat16)
        weight_ref[slots, :] = jnp.broadcast_to(live * sign * susc, (CAP, 128))

    for copy in copies[4:]:
        copy.wait()


def angle_kernel(blocks, sens_ref, demand_ref, start_ref, onehot_ref, *refs):
    sent_refs, (own_ref, inject_ref, rows_ref) = refs[:blocks], refs[blocks:]
    hours = start_ref.shape[0]
    scens = demand_ref.shape[0] // hours
    rows = jnp.dot(onehot_ref[...], sens_ref[...], preferred_element_type=jnp.float32)
    rows_ref[...] = rows.astype(jnp.bfloat16)
    for h in range(hours):
        part = slice(h * scens, (h + 1) * scens)
        inject_ref[part, :] = (start_ref[h : h + 1, :] - demand_ref[part, :]).astype(jnp.bfloat16)
    repeat_rest(inject_ref, hours * scens)
    own = lax.dot_general(
        rows_ref[...], inject_ref[...], CONTRACT_LAST, preferred_element_type=jnp.float32
    )
    own_ref[...] = own
    for i in range(blocks):
        sent_refs[i][...] = fold(own[i * CAP : (i + 1) * CAP, :])


def edge_kernel(demand_ref, edge_hedge_ref, start_ref, edge_ref):
    scens = edge_hedge_ref.shape[0]
    hours = start_ref.shape[0]
    early = lax.axis_index("hour") == 0
    last = (hours - 1) * scens
    at = 2 * scens
    edge_ref[0:scens, :] = jnp.where(early, demand_ref[last:, :], demand_ref[0:scens, :])
    edge_ref[scens:at, :] = edge_hedge_ref[...]
    edge_ref[at : at + 1, :] = jnp.where(early, start_ref[hours - 1 : hours, :], start_ref[0:1, :])
    edge_ref[at + 1 : at + 2, :] = jnp.where(
        early, start_ref[hours - 2 : hours - 1, :], start_ref[1:2, :]
    )


def first_kernel(
    ptdf_ref,
    own_inject_ref,
    demand_ref,
    hedge_ref,
    start_ref,
    edge_ref,
    cost_ref,
    max_ref,
    limit_ref,
    line_max_ref,
    gen_ref,
    base_ref,
    hedged_ref,
    sums_ref,
    inject_ref,
    over_ref,
    back_ref,
    padded_ref,
    excess_ref,
    ramp_ref,
):
    hours, buses = start_ref.shape
    width = demand_ref.shape[0]
    scens = width // hours
    at = 2 * scens
    early = lax.axis_index("hour") == 0
    first_hour = lax.axis_index("hour") * hours
    beyond = edge_ref[at : at + 1, :]
    limit = limit_ref[...]
    cost = cost_ref[...]
    top = max_ref[...]

    inject_ref[0:width, :] = own_inject_ref[0:width, :]
    inject_ref[width : width + scens, :] = (beyond - edge_ref[0:scens, :]).astype(jnp.bfloat16)
    back_ref[...] = line_work(inject_ref, ptdf_ref, line_max_ref, over_ref)
    write_ramp(start_ref, beyond, limit, first_hour, padded_ref, excess_ref, ramp_ref)

    def step(mean, hedge, back, ramp):
        grad = cost + back + (mean - mean + hedge) + ramp
        gen = jnp.clip(mean - STEP_SIZE * grad, 0.0, top)
        return gen, gen + hedge

    for h in range(hours):
        part = slice(h * scens, (h + 1) * scens)
        mean = start_ref[h : h + 1, :]
        gen, hedged = step(mean, hedge_ref[part, :], back_ref[part, :], ramp_ref[h : h + 1, :])
        gen_ref[part, :] = gen
        base_ref[part, :] = gen - demand_ref[part, :]
        hedged_ref[part, :] = hedged
        put_row(sums_ref, hours + 1, h, jnp.sum(hedged, axis=0, keepdims=True))
    near = jnp.where(early, start_ref[hours - 1 : hours, :], start_ref[0:1, :])
    ramp = excess(beyond - near, limit) + excess(beyond - edge_ref[at + 1 : at + 2, :], limit)
    _, hedged = step(beyond, edge_ref[scens:at, :], back_ref[width : width + scens, :], ramp)
    put_row(sums_ref, hours + 1, hours, jnp.sum(hedged, axis=0, keepdims=True))
    clear_rest(sums_ref, (hours + 1) * (buses // LANES))


def first_flow(weight, own, peer):
    est_mine = weight * own
    est_theirs = -weight * peer
    return est_mine, est_theirs, (est_mine + est_theirs) * 0.5


def tie_kernel(blocks, relayed, base_ref, spread_ref, rows_ref, weight_ref, own_ref, *refs):
    peer_refs, refs = refs[:blocks], refs[blocks:]
    *next_refs, inject_ref, own_next_ref = refs
    width = base_ref.shape[0]

    weight = jnp.concatenate([weight_ref[...], weight_ref[...]], axis=1)
    own = own_ref[...]
    peer = jnp.concatenate([unfold(ref[...]) for ref in peer_refs], axis=0)
    flow = first_flow(weight, own, peer)[2]
    spread = spread_ref[...]
    add = lax.dot_general(
        split_3(flow),
        jnp.concatenate([spread, spread, spread], axis=0),
        CONTRACT_FIRST,
        preferred_element_type=jnp.float32,
    )
    inject_ref[0:width, :] = (base_ref[...] + add[0:width, :]).astype(jnp.bfloat16)
    repeat_rest(inject_ref, width)

    own_next = lax.dot_general(
        rows_ref[...], inject_ref[...], CONTRACT_LAST, preferred_element_type=jnp.float32
    )
    parts = [own_next[i * CAP : (i + 1) * CAP, :] for i in range(blocks)]
    if relayed:
        far_ref, near_ref = next_refs
        flip_3, flip_2 = by_flips(lax.axis_index("area"), parts[0], parts[1])
        far_ref[...] = fold(jnp.concatenate([flip_2, flip_3], axis=0))
        near_ref[...] = parts[2]
    else:
        for ref, part in zip(next_refs, parts):
            ref[...] = fold(part)
    own_next_ref[...] = own_next


def second_kernel(
    terms,
    scen_total,
    ptdf_ref,
    inject_ref,
    gen_ref,
    hedged_ref,
    cost_ref,
    max_ref,
    limit_ref,
    line_max_ref,
    *refs,
):
    sum_refs, refs = refs[:terms], refs[terms:]
    (hedged_out_ref, sums_out_ref, over_ref, back_ref, mean_ref, padded_ref, excess_ref, ramp_ref) = refs
    hours, buses = ramp_ref.shape
    width = back_ref.shape[0]
    scens = width // hours
    first_hour = lax.axis_index("hour") * hours

    back_ref[...] = line_work(inject_ref.at[0:width, :], ptdf_ref, line_max_ref, over_ref)
    agree(mean_ref, sum_refs, hours + 1, scen_total)
    write_ramp(
        mean_ref, mean_ref[hours : hours + 1, :], limit_ref[...], first_hour, padded_ref, excess_ref, ramp_ref
    )
    cost = cost_ref[...]
    top = max_ref[...]
    for h in range(hours):
        part = slice(h * scens, (h + 1) * scens)
        mean = mean_ref[h : h + 1, :]
        gen = gen_ref[part, :]
        hedge = hedged_ref[part, :] - mean
        grad = cost + back_ref[part, :] + (gen - mean + hedge) + ramp_ref[h : h + 1, :]
        gen = jnp.clip(gen - STEP_SIZE * grad, 0.0, top)
        hedged = gen + hedge
        hedged_out_ref[part, :] = hedged
        put_row(sums_out_ref, hours, h, jnp.sum(hedged, axis=0, keepdims=True))
    clear_rest(sums_out_ref, hours * (buses // LANES))


def relay_kernel(near_ref, far_ref, both_ref):
    low = lax.broadcasted_iota(jnp.int32, (CAP, LANES), 1) < LANES // 2
    both_ref[0:CAP, :] = near_ref[:, 0:LANES]
    both_ref[CAP : 2 * CAP, :] = far_ref[CAP : 2 * CAP, :]
    both_ref[2 * CAP :, :] = jnp.where(low, near_ref[:, LANES:], far_ref[2 * CAP :, :])


def agree_kernel(blocks, scen_total, hedged_ref, weight_ref, own_ref, own_next_ref, *refs):
    peer_refs, refs = refs[:blocks], refs[blocks:]
    sum_refs, (mean_ref, hedge_ref, mine_ref, theirs_ref) = refs[:-4], refs[-4:]
    hours = mean_ref.shape[0]
    scens = hedged_ref.shape[0] // hours
    agree(mean_ref, sum_refs, hours, scen_total)
    for h in range(hours):
        part = slice(h * scens, (h + 1) * scens)
        hedge_ref[part, :] = hedged_ref[part, :] - mean_ref[h : h + 1, :]

    weight = jnp.concatenate([weight_ref[...], weight_ref[...]], axis=1)
    own = own_ref[...]
    peer = jnp.concatenate([unfold(ref[...]) for ref in peer_refs], axis=0)
    est_mine, est_theirs, flow = first_flow(weight, own, peer)
    mine_ref[...] = weight * (own_next_ref[...] - peer) + (est_mine - flow)
    theirs_ref[...] = weight * own + (est_theirs - flow)


def last_kernel(blocks, relayed, partner_of, hedge_ref, mean_ref, *refs):
    *peer_refs, weight_ref, mine_ref, theirs_ref = refs[:-6]
    hedge_out, mean_out, tie_out, tie_ref, placed_ref, copy_sems = refs[-6:]
    copies = []

    def send(src, dst):
        copies.append(pltpu.make_async_copy(src, dst, copy_sems.at[len(copies)]))
        copies[-1].start()

    send(hedge_ref, hedge_out)
    send(mean_ref, mean_out)
    here = lax.axis_index("area")
    placed_ref[...] = jnp.zeros_like(placed_ref)
    if relayed:
        far, both = (unfold(ref[...]) for ref in peer_refs)
        peers = [*by_flips(here, both[CAP:, :], far[0:CAP, :]), both[0:CAP, :]]
    else:
        peers = [unfold(ref[...]) for ref in peer_refs]
    for i in range(blocks):
        slots = slice(i * CAP, (i + 1) * CAP)
        weight = jnp.concatenate([weight_ref[slots, :], weight_ref[slots, :]], axis=1)
        flow = (mine_ref[slots, :] + (theirs_ref[slots, :] - weight * peers[i])) * 0.5
        low, _, block, in_reach = block_facts(here, partner_of(here, i))
        first = block * CAP + jnp.where(low, 0, REACH * CAP)

        @pl.when(in_reach)
        def _():
            placed_ref[pl.ds(pl.multiple_of(first, CAP), CAP), :] = flow

    for first in range(0, tie_ref.shape[0], LANES):
        count = min(LANES, tie_ref.shape[0] - first)
        tie_ref[first : first + count, :] = jnp.transpose(placed_ref[:, first : first + LANES])[0:count, :]
        send(tie_ref.at[pl.ds(first, count)], tie_out.at[pl.ds(first, count)])
    for copy in copies:
        copy.wait()


def call(kernel, name, args, outs, scratch, flops, in_place=(), outs_in_place=False):
    size = sum(x.size * x.dtype.itemsize for x in list(args) + list(outs))
    return pl.pallas_call(
        kernel,
        name=name,
        out_shape=outs,
        in_specs=[ANY if i in in_place else VMEM for i in range(len(args))],
        out_specs=[ANY if outs_in_place else VMEM] * len(outs),
        scratch_shapes=scratch,
        compiler_params=pltpu.CompilerParams(vmem_limit_bytes=32 * 1024 * 1024),
        cost_estimate=pl.CostEstimate(flops=flops, bytes_accessed=size, transcendentals=0),
    )(*(pltpu.with_memory_space_constraint(x, pltpu.HBM) if i in in_place else x for i, x in enumerate(args)))


def per_device(
    ptdf,
    angle_sens,
    demand,
    gen_start,
    hedge_dual,
    gen_cost,
    gen_max,
    gen_ramp,
    line_max,
    tie_count,
    tie_low_bus,
    tie_high_bus,
    tie_susc,
):
    hours, scens, buses = demand.shape
    lines = ptdf.shape[0]
    width = hours * scens
    areas = lax.axis_size("area")
    n_scen = lax.axis_size("scen")
    assert lax.axis_size("hour") == 2 and hours >= 2
    assert width % LANES == LANES // 2 and width < 2 * LANES
    columns = 2 * LANES
    block_rows = CAP * 3 // 2
    scen_total = scens * n_scen
    blocks, partner_of, from_partners = partner_plan(areas)
    slots = blocks * CAP
    pieces = buses // LANES
    sum_rows = 8 * pl.cdiv((hours + 1) * pieces, 8)
    f32, bf16 = jnp.float32, jnp.bfloat16

    def shape(*dims, dtype=f32):
        return jax.ShapeDtypeStruct(dims, dtype)

    def over_scens(sums):
        if n_scen == 2:
            return [sums, lax.ppermute(sums, "scen", [(0, 1), (1, 0)])]
        return [lax.psum(sums, "scen")]

    work = 4 * width * lines * buses

    def step_scratch(rows):
        return [
            pltpu.VMEM((rows, buses), bf16),
            pltpu.VMEM((rows, lines), bf16),
            pltpu.VMEM((rows, buses), f32),
        ]

    ramp_scratch = [
        pltpu.VMEM((hours + 4, buses), f32),
        pltpu.VMEM((hours + 4, buses), f32),
        pltpu.VMEM((hours, buses), f32),
    ]
    tables = (tie_count, tie_low_bus, tie_high_bus, tie_susc)
    vectors = [x.reshape(1, -1) for x in (gen_cost, gen_max, gen_ramp, line_max)]
    hedge = hedge_dual.reshape(width, buses)
    load, edge_hedge, start, *vectors, onehot, spread, weight = call(
        functools.partial(table_kernel, blocks, partner_of),
        "tables",
        (demand.reshape(width, buses), hedge, gen_start, *tables, *vectors),
        [
            shape(width, buses),
            shape(scens, buses),
            shape(hours, buses),
            *(shape(*x.shape) for x in vectors),
            shape(slots, buses, dtype=bf16),
            shape(slots, buses, dtype=bf16),
            shape(slots, LANES),
        ],
        [pltpu.VMEM(x.shape, x.dtype) for x in tables] + [pltpu.SemaphoreType.DMA((11,))],
        BETWEEN,
        range(11),
    )
    (edge,) = call(edge_kernel, "edge", (load, edge_hedge, start), [shape(2 * scens + 8, buses)], [], width)
    *sent, own, inject, rows = call(
        functools.partial(angle_kernel, blocks),
        "angles",
        (angle_sens, load, start, onehot),
        [shape(block_rows, LANES)] * blocks
        + [shape(slots, columns), shape(columns, buses, dtype=bf16), shape(slots, buses, dtype=bf16)],
        [],
        BETWEEN,
    )
    edge = lax.ppermute(edge, "hour", [(0, 1), (1, 0)])
    peer = from_partners(sent)
    gen, base, hedged, sums = call(
        first_kernel,
        "first",
        (ptdf, inject, load, hedge, start, edge, *vectors),
        [
            shape(width, buses),
            shape(width, buses),
            shape(width, buses),
            shape(sum_rows, LANES),
        ],
        step_scratch(width + scens) + ramp_scratch,
        work,
    )
    sum_terms = over_scens(sums)
    terms = len(sum_terms)
    relayed = areas == 4
    tied = call(
        functools.partial(tie_kernel, blocks, relayed),
        "ties",
        (base, spread, rows, weight, own, *peer),
        (
            [shape(2 * block_rows, LANES), shape(CAP, columns)]
            if relayed
            else [shape(block_rows, LANES)] * blocks
        )
        + [shape(columns, buses, dtype=bf16), shape(slots, columns)],
        [],
        BETWEEN,
    )
    *sent, inject, own_next = tied
    first_peer = peer
    hedged, sums = call(
        functools.partial(second_kernel, terms, scen_total),
        "second",
        (ptdf, inject, gen, hedged, *vectors, *sum_terms),
        [shape(width, buses), shape(sum_rows, LANES)],
        step_scratch(width)[1:] + [pltpu.VMEM((8 * pl.cdiv(hours + 1, 8), buses), f32)] + ramp_scratch,
        work,
    )
    sum_terms = over_scens(sums)
    if relayed:
        far, near = sent
        far = lax.ppermute(far, "area", [(a, a ^ 2) for a in range(areas)])
        arrived, _ = lax.optimization_barrier((far, sums))
        (both,) = call(relay_kernel, "relay", (near, arrived), [shape(2 * block_rows, LANES)], [], BETWEEN)
        peer = [far, lax.ppermute(both, "area", [(a, a ^ 1) for a in range(areas)])]
    else:
        peer = from_partners(sent)
    gen_mean, hedge, mine, theirs = call(
        functools.partial(agree_kernel, blocks, scen_total),
        "agree",
        (hedged, weight, own, own_next, *first_peer, *sum_terms),
        [shape(hours, buses), shape(width, buses), shape(slots, columns), shape(slots, columns)],
        [],
        BETWEEN,
    )
    tie_shape = shape(width, 2 * REACH * CAP)
    hedge, gen_mean, tie_flow = call(
        functools.partial(last_kernel, blocks, relayed, partner_of),
        "last",
        (hedge, gen_mean, *peer, weight, mine, theirs),
        [shape(width, buses), shape(hours, buses), tie_shape],
        [
            pltpu.VMEM(tie_shape.shape, f32),
            pltpu.VMEM((2 * REACH * CAP, columns), f32),
            pltpu.SemaphoreType.DMA((2 + columns // LANES,)),
        ],
        slots * columns,
        outs_in_place=True,
    )
    return (
        gen_mean,
        hedge.reshape(hours, scens, buses),
        tie_flow.reshape(hours, scens, 2 * REACH * CAP),
    )


def solution(mesh):
    return jax.shard_map(
        per_device,
        mesh=mesh,
        in_specs=(
            P(("group", "area"), None),
            P(("group", "area"), None),
            P(("group", "hour"), "scen", "area"),
            P(("group", "hour"), "area"),
            P(("group", "hour"), "scen", "area"),
            P(("group", "area")),
            P(("group", "area")),
            P(("group", "area")),
            P(("group", "area")),
            P("group", None),
            P("group", None),
            P("group", None),
            P("group", None),
        ),
        out_specs=(
            P(("group", "hour"), "area"),
            P(("group", "hour"), "scen", "area"),
            P(("group", "hour"), "scen", "area"),
        ),
        check_vma=False,
    )
```
